32 devices in a mesh: dp: 8 (over z, x), mp: 4 (over y, core).
Axes of the slice: x: 2, y: 2, z: 4, core: 2. Of those that a mesh axis runs over, the one named last changes fastest.
Arguments:
- tokens: bfloat16 [16384, 768], P('dp'), may hold values from -6 to 6
- out_grad: bfloat16 [16384, 768], P('dp'), may hold values from -6 to 6
- w_qkv: bfloat16 [768, 3, 768], P('dp', None, 'mp'), may hold values from -0.21875 to 0.21875
- w_out: bfloat16 [768, 768], P('mp', 'dp'), may hold values from -3.5 to 3.5
- w_gu: bfloat16 [768, 2, 1152], P('dp', None, 'mp'), may hold values from -0.21875 to 0.21875
- w_down: bfloat16 [1152, 768], P('mp', 'dp'), may hold values from -0.1875 to 0.1875
- gain_attn: bfloat16 [768], P('dp'), may hold values from 0.25 to 1.75
- gain_mlp: bfloat16 [768], P('dp'), may hold values from 0.25 to 1.75
- doc_lengths: int32 [8, 8], P('dp'), may hold values from 0 to 2048, as said below
Outputs:
- layer_out: bfloat16 [16384, 768], P('dp')
- input_grad: float32 [16384, 768], P('dp')
- grad_w_qkv: float32 [768, 3, 768], P('dp', None, 'mp')
- grad_w_out: float32 [768, 768], P('mp', 'dp')
- grad_w_gu: float32 [768, 2, 1152], P('dp', None, 'mp')
- grad_w_down: float32 [1152, 768], P('mp', 'dp')
- grad_gain_attn: float32 [768], P('dp')
- grad_gain_mlp: float32 [768], P('dp')
The draws below stay inside these ranges and needn't reach their ends.
Inputs may be any that keep to these rules, and one draw needn't show every extreme that they name: `doc_lengths`: each row of a group's lengths sums to between 1024 and 2048; the token slots after that sum are padding. Lengths may be zero. In every draw one group holds a single document of exactly 2048 tokens.
All inputs are finite; a program needn't handle non-finite values.
Results may differ from the reference program's by a relative error of at most 0.022.
Values may be sent and summed in bfloat16 or wider, within the bound.
A program may use at most 128 MiB of HBM per device.

```python
import jax
import jax.numpy as jnp
from jax import lax

D = 768
HEADS = 12
HDIM = 64
FF = 1152
TOK_DEV = 2048
DOCS = 8
TOKENS = 16384
N_DP = 8
N_MP = 4


def draw_doc_lengths(key, part):
    key_count, key_full, key_cuts = jax.random.split(key, 3)
    totals = jax.random.randint(key_count, (N_DP,), TOK_DEV // 2, TOK_DEV + 1)
    full_group = jax.random.randint(key_full, (), 0, N_DP)
    cut_points = jnp.sort(jax.random.randint(key_cuts, (N_DP, DOCS - 1), 0, TOK_DEV + 1), axis=1)
    cut_points = jnp.minimum(cut_points, totals[:, None])
    edge_points = jnp.concatenate([jnp.zeros((N_DP, 1), jnp.int32), cut_points.astype(jnp.int32), totals[:, None].astype(jnp.int32)], axis=1)
    lengths = edge_points[:, 1:] - edge_points[:, :-1]
    single = jnp.where(jnp.arange(DOCS) == 0, TOK_DEV, 0)
    chosen = jnp.arange(N_DP)[:, None] == full_group
    return jnp.where(chosen, single[None, :], lengths).astype(jnp.int32)


def shard_levels(rng, extent, cuts, least, top_value):
    level, own = 1.0, jax.random.fold_in(rng, 6)
    for dim, blocks in cuts:
        heights = jnp.exp(jax.random.uniform(jax.random.fold_in(own, dim), (blocks,), jnp.float32, least / len(cuts), top_value / len(cuts)))
        level = level * jnp.repeat(heights, extent[dim] // blocks).reshape([-1 if axis == dim else 1 for axis in range(len(extent))])
    return level


def noise(own_key, dims, deviation, limit, cuts=(), held_as=jnp.bfloat16):
    result = deviation * jax.random.normal(own_key, dims, jnp.float32)
    if cuts:
        result = result * shard_levels(own_key, dims, cuts, -0.22, 0.18)
    return jnp.clip(result, -limit, limit).astype(held_as)


def setup_inputs(seed: int = 0) -> dict:
    splits = jax.random.split(jax.random.key(seed), 10)
    return {
        "tokens": noise(splits[0], (TOKENS, D), 1.0, 6.0, ((0, 8),)),
        "out_grad": noise(splits[1], (TOKENS, D), 1.0, 6.0, ((0, 8),)),
        "w_qkv": noise(splits[2], (D, 3, D), D ** -0.5, 0.21875, ((0, 8), (2, 4))),
        "w_out": noise(splits[3], (D, D), (max(D // 256, 1)) ** -0.5, 3.5, ((0, 4), (1, 8))),
        "w_gu": noise(splits[4], (D, 2, FF), D ** -0.5, 0.21875, ((0, 8), (2, 4))),
        "w_down": noise(splits[5], (FF, D), FF ** -0.5, 0.1875, ((0, 4), (1, 8))),
        "gain_attn": jnp.clip(1.0 + 0.15 * jax.random.normal(splits[6], (D,), jnp.float32), 0.25, 1.75).astype(jnp.bfloat16),
        "gain_mlp": jnp.clip(1.0 + 0.15 * jax.random.normal(splits[7], (D,), jnp.float32), 0.25, 1.75).astype(jnp.bfloat16),
        "doc_lengths": draw_doc_lengths(jax.random.fold_in(splits[9], 71), 0),
    }


@jax.custom_vjp
def low(v):
    return lax.optimization_barrier(v.astype(jnp.bfloat16)).astype(jnp.float32)

@jax.custom_vjp
def low_back(v):
    return v

def low_keep(v):
    return (low(v), None)

def low_pass(kept, grad):
    return (grad,)

def back_keep(v):
    return (v, None)

def back_low(kept, grad):
    return (low(grad),)
low.defvjp(low_keep, low_pass)
low_back.defvjp(back_keep, back_low)
epsilon = 1e-05
rope_base = 160000.0
highest = lax.Precision.HIGHEST

def layout(lengths):
    doc_ends = jnp.cumsum(lengths, dtype=jnp.int32)
    row_index = jnp.arange(TOK_DEV, dtype=jnp.int32)
    past_end = row_index[:, None] >= doc_ends[None, :]
    segment = lax.optimization_barrier(jnp.sum(past_end.astype(jnp.int32), axis=1, dtype=jnp.int32))
    doc_start = lax.optimization_barrier(jnp.max(jnp.where(past_end, doc_ends[None, :], 0), axis=1))
    return (segment, row_index - doc_start, row_index < doc_ends[-1])

def tables(position):
    half_dim = HDIM // 2
    frequency = rope_base ** (-(jnp.arange(half_dim, dtype=jnp.float32) * (2.0 / HDIM)))
    angles = position.astype(jnp.float32)[:, None] * frequency[None, :]
    cosine_table = jnp.concatenate([jnp.cos(angles), jnp.cos(angles)], axis=1)
    sine_table = jnp.concatenate([jnp.sin(angles), jnp.sin(angles)], axis=1)
    return (cosine_table, sine_table)

def rotate(vectors, cosine_table, sine_table):
    half_dim = vectors.shape[-1] // 2
    turned = jnp.concatenate([-vectors[..., half_dim:], vectors[..., :half_dim]], axis=-1)
    return vectors * cosine_table[:, None, :] + turned * sine_table[:, None, :]

def layer_norm(vectors, gain):
    row_mean = lax.optimization_barrier(jnp.mean(vectors, axis=-1, keepdims=True))
    centered = vectors - row_mean
    row_var = lax.optimization_barrier(jnp.mean(centered * centered, axis=-1, keepdims=True))
    return centered * lax.rsqrt(row_var + epsilon) * gain

def geglu(gate_up):
    return jax.nn.gelu(gate_up[:, 0], approximate=False) * gate_up[:, 1]

def group_layer(weights, inputs, lengths):
    w_qkv, w_out, w_gu, w_down, gain_attn, gain_mlp = weights
    segment, position, live_rows = layout(lengths)
    cosine_table, sine_table = tables(position)
    normed_one = low(layer_norm(inputs, gain_attn))
    proj_qkv = low_back(jnp.einsum('td,dcf->tcf', normed_one, w_qkv, precision=highest))
    shaped = proj_qkv.reshape(TOK_DEV, 3, HEADS, HDIM)
    queries = low(rotate(shaped[:, 0], cosine_table, sine_table))
    keys_rot = low(rotate(shaped[:, 1], cosine_table, sine_table))
    values = low(shaped[:, 2])
    scores = low_back(jnp.einsum('qhe,khe->hqk', queries, keys_rot, precision=highest) * HDIM ** (-0.5))
    same_doc = (segment[:, None] == segment[None, :])[None]
    masked = jnp.where(same_doc, scores, -jnp.inf)
    row_top = lax.optimization_barrier(jnp.max(masked, axis=-1, keepdims=True))
    exp_terms = jnp.exp(masked - row_top)
    prob_rows = low(exp_terms / lax.optimization_barrier(jnp.sum(exp_terms, axis=-1, keepdims=True)))
    heads_out = low(low_back(jnp.einsum('hqk,khe->qhe', prob_rows, values, precision=highest)))
    heads_out = heads_out.reshape(TOK_DEV, N_MP, D // N_MP)
    attn_parts = jnp.einsum('tmf,mfd->mtd', heads_out, w_out.reshape(N_MP, D // N_MP, D), precision=highest)
    attn_sum = low_back(lax.optimization_barrier(jnp.sum(low(attn_parts), axis=0)))
    middle = inputs + attn_sum
    normed_two = low(layer_norm(middle, gain_mlp))
    gate_up = low_back(jnp.einsum('td,dcf->tcf', normed_two, w_gu, precision=highest))
    hidden = low(geglu(gate_up)).reshape(TOK_DEV, N_MP, FF // N_MP)
    mlp_parts = jnp.einsum('tmf,mfd->mtd', hidden, w_down.reshape(N_MP, FF // N_MP, D), precision=highest)
    mlp_sum = low_back(lax.optimization_barrier(jnp.sum(low(mlp_parts), axis=0)))
    return middle + mlp_sum

def live_of(lengths):
    return layout(lengths)[2]

def reference(tokens, out_grad, w_qkv, w_out, w_gu, w_down, gain_attn, gain_mlp, doc_lengths):
    params = (w_qkv.astype(jnp.float32), w_out.astype(jnp.float32), w_gu.astype(jnp.float32), w_down.astype(jnp.float32), gain_attn.astype(jnp.float32), gain_mlp.astype(jnp.float32))
    grouped = tokens.astype(jnp.float32).reshape(N_DP, TOK_DEV, D)

    def forward(weights, inputs):

        def one_group(pieces):
            return group_layer(weights, pieces[0], pieces[1])
        return lax.map(jax.checkpoint(one_group), (inputs, doc_lengths))
    outputs, pull_back = jax.vjp(forward, params, grouped)
    live_rows = jax.vmap(live_of)(doc_lengths).astype(jnp.float32)
    out_cot = out_grad.astype(jnp.float32).reshape(N_DP, TOK_DEV, D) * live_rows[:, :, None]
    weight_grads, input_grad = pull_back(out_cot)
    return (outputs.reshape(TOKENS, D).astype(jnp.bfloat16), input_grad.reshape(TOKENS, D), weight_grads[0], weight_grads[1], weight_grads[2], weight_grads[3], weight_grads[4], weight_grads[5])
```

```python
import functools
import math

import jax
import jax.numpy as jnp
from jax import lax
from jax.experimental import pallas as pl
from jax.experimental.pallas import tpu as pltpu
from jax.sharding import PartitionSpec as P

HDIM = 64
HALF = HDIM // 2
AUG = HDIM + 16
EPS = 1e-05
ROPE_BASE = 160000.0
LOG2E = math.log2(math.e)
LN2 = math.log(2.0)
SCALE = HDIM ** (-0.5)
FAR = -1e30
BF16 = jnp.bfloat16
F32 = jnp.float32
VMEM_BYTES = 60 << 20
NN = (((1,), (0,)), ((), ()))
NT = (((1,), (1,)), ((), ()))
TN = (((0,), (0,)), ((), ()))


def dot(a, b, dims):
    return lax.dot_general(a, b, dims, preferred_element_type=F32)


def params(*semantics):
    return pltpu.CompilerParams(
        dimension_semantics=semantics or None, vmem_limit_bytes=VMEM_BYTES
    )


def whole(*shape):
    return pl.BlockSpec(shape, lambda *i: (0,) * len(shape))


def layout_rows(len_ref, docs, first, rows):
    index = first + lax.broadcasted_iota(jnp.int32, (1, rows), 1)
    segment = jnp.zeros((1, rows), jnp.int32)
    start = jnp.zeros((1, rows), jnp.int32)
    end = jnp.int32(0)
    for j in range(docs):
        end = end + len_ref[0, j]
        past = index >= end
        segment = segment + jnp.where(past, 1, 0)
        start = jnp.where(past, jnp.maximum(start, end), start)
    return segment, index - start, index < end


def normalize(columns):
    mean = jnp.mean(columns, axis=0, keepdims=True)
    centered = columns - mean
    var = jnp.mean(centered * centered, axis=0, keepdims=True)
    inv = lax.rsqrt(var + EPS)
    return centered * inv, inv


def turn(block, cos, sin, heads, back=False):
    out = []
    for h in range(heads):
        one = block[h * HDIM : h * HDIM + HALF]
        two = block[h * HDIM + HALF : (h + 1) * HDIM]
        if back:
            out += [one * cos + two * sin, two * cos - one * sin]
        else:
            out += [one * cos - two * sin, two * cos + one * sin]
    return jnp.concatenate(out, axis=0)


def prep_kernel(own_axis, own, len_ref, tok_ref, gain_ref, w_ref, n1_ref, q_ref, k_ref, v_ref, cos_ref, sin_ref):
    features, rows = n1_ref.shape
    width = w_ref.shape[2] // 3
    heads = width // HDIM
    chunk = own

    @pl.when(pl.program_id(0) == 0)
    def _():
        gain = gain_ref[...]

        def norm(i, carry):
            at = pl.ds(pl.multiple_of(i * chunk, chunk), chunk)
            hat, _ = normalize(tok_ref[at, :].T.astype(F32))
            n1_ref[:, at] = (hat * gain).astype(BF16)
            return carry

        lax.fori_loop(0, rows // chunk, norm, 0)
        _, position, _ = layout_rows(len_ref, len_ref.shape[1], 0, rows)
        power = lax.broadcasted_iota(jnp.int32, (HALF, 1), 0).astype(F32) * (-2.0 / HDIM * math.log2(ROPE_BASE))
        angle = position.astype(F32) * jnp.exp2(power)
        cos_ref[...] = jnp.cos(angle)
        sin_ref[...] = jnp.sin(angle)

    def project(i, carry):
        at = pl.ds(pl.multiple_of(i * chunk, chunk), chunk)
        made = dot(w_ref[0, :, width:], n1_ref[:, at], TN)
        k_ref[:, at] = turn(made[:width], cos_ref[:, at], sin_ref[:, at], heads).astype(BF16)
        v_ref[:, at] = made[width:].astype(BF16)
        return carry

    lax.fori_loop(0, rows // chunk, project, 0)
    mine = pl.ds(pl.multiple_of(lax.axis_index(own_axis) * own, own), own)
    made = dot(w_ref[0, :, :width], n1_ref[:, mine], TN) * (SCALE * LOG2E)
    q_ref[...] = turn(made, cos_ref[:, mine], sin_ref[:, mine], heads).astype(BF16)


def prep(lengths, tokens, gain, w_qkv, n_mp, own_axis="mp"):
    rows, features = tokens.shape
    own = rows // n_mp
    width = w_qkv.shape[2] // 3
    return pl.pallas_call(
        functools.partial(prep_kernel, own_axis, own),
        grid=(n_mp,),
        in_specs=[
            pl.BlockSpec(memory_space=pltpu.SMEM),
            whole(rows, features),
            whole(features, 1),
            pl.BlockSpec((1,) + w_qkv.shape[1:], lambda m: (m, 0, 0)),
        ],
        out_specs=[
            whole(features, rows),
            pl.BlockSpec((width, own), lambda m: (m, 0)),
            pl.BlockSpec((width, rows), lambda m: (m, 0)),
            pl.BlockSpec((width, rows), lambda m: (m, 0)),
            whole(HALF, rows),
            whole(HALF, rows),
        ],
        out_shape=[
            jax.ShapeDtypeStruct((features, rows), BF16),
            jax.ShapeDtypeStruct((features, own), BF16),
            jax.ShapeDtypeStruct((features, rows), BF16),
            jax.ShapeDtypeStruct((features, rows), BF16),
            jax.ShapeDtypeStruct((HALF, rows), F32),
            jax.ShapeDtypeStruct((HALF, rows), F32),
        ],
        compiler_params=params("arbitrary"),
        name="prep",
    )(lengths, tokens, gain, w_qkv)


def attend_kernel(own_axis, len_ref, q_ref, k_ref, v_ref, o_ref, p_ref, inv_ref, ka_ref, qa_ref, va_ref):
    rows, own = k_ref.shape[1], q_ref.shape[1]
    docs = len_ref.shape[1]

    @pl.when(pl.program_id(0) == 0)
    def _():
        keys, _, _ = layout_rows(len_ref, docs, 0, rows)
        queries, _, _ = layout_rows(len_ref, docs, lax.axis_index(own_axis) * own, own)
        kind = lax.broadcasted_iota(jnp.int32, (AUG - HDIM, 1), 0)
        ka_ref[HDIM:] = jnp.where(kind == keys, 1.0, 0.0).astype(BF16)
        qa_ref[HDIM:] = jnp.where(kind == queries, 0.0, FAR).astype(BF16)
        va_ref[HDIM:] = jnp.ones((AUG - HDIM, rows), BF16)

    ka_ref[:HDIM] = k_ref[...]
    qa_ref[:HDIM] = q_ref[...]
    va_ref[:HDIM] = v_ref[...]
    step = 256
    for c in range(own // step):
        at = slice(c * step, (c + 1) * step)
        scores = dot(ka_ref[...], qa_ref[:, at], TN)
        top = jnp.max(scores, axis=0, keepdims=True)
        probs = jnp.exp2(scores - top).astype(BF16)
        p_ref[0, :, at] = probs
        out = dot(va_ref[...], probs, NN)
        inv = 1.0 / out[HDIM : HDIM + 1]
        o_ref[:, at] = (out[:HDIM] * inv).astype(BF16)
        inv_ref[0, :, at] = inv


def attend(lengths, q, k, v, own_axis="mp"):
    (features, own), rows = q.shape, k.shape[1]
    heads = features // HDIM
    return pl.pallas_call(
        functools.partial(attend_kernel, own_axis),
        grid=(heads,),
        in_specs=[
            pl.BlockSpec(memory_space=pltpu.SMEM),
            pl.BlockSpec((HDIM, own), lambda h: (h, 0)),
            pl.BlockSpec((HDIM, rows), lambda h: (h, 0)),
            pl.BlockSpec((HDIM, rows), lambda h: (h, 0)),
        ],
        out_specs=[
            pl.BlockSpec((HDIM, own), lambda h: (h, 0)),
            pl.BlockSpec((1, rows, own), lambda h: (h, 0, 0)),
            pl.BlockSpec((1, 1, own), lambda h: (h, 0, 0)),
        ],
        out_shape=[
            jax.ShapeDtypeStruct((features, own), BF16),
            jax.ShapeDtypeStruct((heads, rows, own), BF16),
            jax.ShapeDtypeStruct((heads, 1, own), F32),
        ],
        scratch_shapes=[
            pltpu.VMEM((AUG, rows), BF16),
            pltpu.VMEM((AUG, own), BF16),
            pltpu.VMEM((AUG, rows), BF16),
        ],
        compiler_params=params("arbitrary"),
        name="attend",
    )(lengths, q, k, v)


def gelu_parts(gate):
    phi = 0.5 * (1.0 + lax.erf(gate * math.sqrt(0.5)))
    density = jnp.exp2(gate * gate * (-0.5 * LOG2E)) * (1.0 / math.sqrt(2.0 * math.pi))
    return phi, gate * density


def mid_kernel(
    own_axis, len_ref, tok_ref, cot_ref, gain_ref, heads_ref, inv_ref, wo_ref, wg_ref, wd_ref,
    out_ref, mcot_ref, do_ref, go_ref, gg_ref, gd_ref, gain_cot_ref,
    up_ref, hid_ref,
):
    own, features = tok_ref.shape
    parts, _, width = wo_ref.shape
    units = wd_ref.shape[2]
    heads = width // HDIM
    _, _, live = layout_rows(len_ref, len_ref.shape[1], lax.axis_index(own_axis) * own, own)
    total = dot(wo_ref[0], heads_ref[:width], NN)
    for m in range(1, parts):
        total += dot(wo_ref[m], heads_ref[m * width : (m + 1) * width], NN)
    middle = tok_ref[...].T.astype(F32) + total
    gain = gain_ref[...]
    hat, inv_sigma = normalize(middle)
    normed = (hat * gain).astype(BF16)
    branch = jnp.where(live, cot_ref[...].T.astype(F32), 0.0).astype(BF16)
    total = middle
    back = jnp.zeros((features, own), F32)
    for m in range(parts):
        gate_up = dot(wg_ref[m], normed, TN)
        gate, up = gate_up[:units], gate_up[units:]
        phi, slope = gelu_parts(gate)
        act = gate * phi
        hidden = (act * up).astype(BF16)
        total += dot(wd_ref[m], hidden, NN)
        hidden_cot = dot(wd_ref[m], branch, TN)
        gd_ref[m] = dot(branch, hidden, NT).astype(BF16)
        cots = jnp.concatenate([hidden_cot * up * (phi + slope), hidden_cot * act], axis=0).astype(BF16)
        gg_ref[m] = dot(normed, cots, NT).astype(BF16)
        back += dot(wg_ref[m], cots, NN)
    out_ref[...] = total.astype(BF16).T
    gain_cot_ref[...] = jnp.sum(back * hat, axis=1, keepdims=True)
    d = back * gain
    middle_cot = branch.astype(F32) + inv_sigma * (
        d - jnp.mean(d, axis=0, keepdims=True) - hat * jnp.mean(d * hat, axis=0, keepdims=True)
    )
    mcot_ref[...] = middle_cot
    attn_cot = middle_cot.astype(BF16)
    for m in range(parts):
        part = heads_ref[m * width : (m + 1) * width]
        go_ref[m] = dot(attn_cot, part, NT).astype(BF16)
        back_heads = dot(wo_ref[m], attn_cot, TN)
        for h in range(heads):
            head = m * heads + h
            rows = slice(h * HDIM, (h + 1) * HDIM)
            inv = inv_ref[head]
            cot = back_heads[rows] * inv
            inner = jnp.sum(cot * part[rows].astype(F32), axis=0, keepdims=True)
            high = inner.astype(BF16).astype(F32)
            pad = jnp.zeros((AUG - HDIM - 2, own), F32)
            do_ref[head] = jnp.concatenate([cot, high, inner - high, pad], axis=0).astype(BF16)


def mid(lengths, tokens, out_grad, gain, heads_out, inv, w_out, w_gu, w_down, own_axis="mp"):
    features, own = heads_out.shape
    heads = inv.shape[0]
    mine = lambda: (lax.axis_index(own_axis), 0)
    args = (tokens, out_grad, gain, heads_out, inv, w_out, w_gu, w_down)
    tok = lax.dynamic_slice_in_dim(tokens, lax.axis_index(own_axis) * own, own, 0)
    cot = lax.dynamic_slice_in_dim(out_grad, lax.axis_index(own_axis) * own, own, 0)
    vm = pl.BlockSpec(memory_space=pltpu.VMEM)
    units = w_down.shape[2]
    return pl.pallas_call(
        functools.partial(mid_kernel, own_axis),
        in_specs=[pl.BlockSpec(memory_space=pltpu.SMEM)] + [vm] * 8,
        out_specs=[vm] * 7,
        out_shape=[
            jax.ShapeDtypeStruct((own, features), BF16),
            jax.ShapeDtypeStruct((features, own), F32),
            jax.ShapeDtypeStruct((heads, AUG, own), BF16),
            jax.ShapeDtypeStruct(w_out.shape, BF16),
            jax.ShapeDtypeStruct(w_gu.shape, BF16),
            jax.ShapeDtypeStruct(w_down.shape, BF16),
            jax.ShapeDtypeStruct((features, 1), F32),
        ],
        scratch_shapes=[
            pltpu.VMEM((8, 128), F32),
            pltpu.VMEM((8, 128), F32),
        ],
        compiler_params=params(),
        name="mid",
    )(lengths, tok, cot, gain, heads_out, inv, w_out, w_gu, w_down)


def attend_back_kernel(q_ref, k_ref, v_ref, do_ref, p_ref, dq_ref, dk_ref, dv_ref, va_ref):
    rows, own = k_ref.shape[1], q_ref.shape[1]

    @pl.when(pl.program_id(0) == 0)
    def _():
        va_ref[HDIM:] = jnp.full((AUG - HDIM, rows), -1.0, BF16)

    va_ref[:HDIM] = v_ref[...]
    cot = dot(va_ref[...], do_ref[0], TN)
    probs = p_ref[0]
    score_cot = probs * cot.astype(BF16)
    dv_ref[...] = dot(do_ref[0, :HDIM], probs, NT)
    dk_ref[...] = dot(q_ref[...], score_cot, NT) * LN2
    dq_ref[...] = dot(k_ref[...], score_cot, NN) * SCALE


def last_kernel(own_axis, q_ref, k_ref, v_ref, do_ref, p_ref, cos_ref, sin_ref, n1_ref, w_ref, gq_ref, nc_ref, gc_ref, dq_ref, dk_ref, dv_ref, pc_ref, acc_ref, va_ref):
    step, head = pl.program_id(0), pl.program_id(1)
    per = pl.num_programs(1)
    features, rows = n1_ref.shape
    own = q_ref.shape[1]
    width = per * HDIM
    mine = pl.ds(pl.multiple_of(lax.axis_index(own_axis) * own, own), own)

    @pl.when((step == 0) & (head == 0))
    def _():
        va_ref[HDIM:] = jnp.full((AUG - HDIM, rows), -1.0, BF16)
        acc_ref[...] = jnp.zeros_like(acc_ref)
        gc_ref[...] = jnp.zeros_like(gc_ref)

    va_ref[:HDIM] = v_ref[...]
    cot = dot(va_ref[...], do_ref[0], TN)
    probs = p_ref[0]
    score_cot = probs * cot.astype(BF16)
    at = pl.ds(pl.multiple_of(head * HDIM, HDIM), HDIM)
    dv = dot(do_ref[0, :HDIM], probs, NT)
    dk = dot(q_ref[...], score_cot, NT) * LN2
    dq = dot(k_ref[...], score_cot, NN) * SCALE
    pc_ref[pl.ds(pl.multiple_of(width + head * HDIM, HDIM), HDIM)] = dv.astype(BF16)
    pc_ref[at] = turn(dk, cos_ref[...], sin_ref[...], 1, True).astype(BF16)
    dq_ref[at] = turn(dq, cos_ref[:, mine], sin_ref[:, mine], 1, True).astype(BF16)

    @pl.when(head == per - 1)
    def _():
        kv = dot(n1_ref[...], pc_ref[...], NT)
        q = dot(n1_ref[:, mine], dq_ref[...], NT)
        gq_ref[0, :, :width] = q.astype(BF16)
        gq_ref[0, :, width:] = kv.astype(BF16)
        gc_ref[...] += jnp.sum(q * w_ref[0, :, :width].astype(F32), axis=1, keepdims=True) + jnp.sum(
            kv * w_ref[0, :, width:].astype(F32), axis=1, keepdims=True
        )

        def spread(i, carry):
            cols = pl.ds(pl.multiple_of(i * own, own), own)
            acc_ref[:, cols] += dot(w_ref[0, :, width:], pc_ref[:, cols], NN)
            return carry

        lax.fori_loop(0, rows // own, spread, 0)
        acc_ref[:, mine] += dot(w_ref[0, :, :width], dq_ref[...], NN)

    @pl.when((step == pl.num_programs(0) - 1) & (head == per - 1))
    def _():
        nc_ref[...] = acc_ref[...].astype(BF16)


def last(q, k, v, do, p, cos, sin, n1, w_qkv, own_axis="mp"):
    (features, own), rows = q.shape, k.shape[1]
    parts = w_qkv.shape[0]
    per = features // parts // HDIM
    width = per * HDIM
    head = lambda m, h: (m * per + h, 0)
    return pl.pallas_call(
        functools.partial(last_kernel, own_axis),
        grid=(parts, per),
        in_specs=[
            pl.BlockSpec((HDIM, own), head),
            pl.BlockSpec((HDIM, rows), head),
            pl.BlockSpec((HDIM, rows), head),
            pl.BlockSpec((1, AUG, own), lambda m, h: (m * per + h, 0, 0)),
            pl.BlockSpec((1, rows, own), lambda m, h: (m * per + h, 0, 0)),
            whole(HALF, rows),
            whole(HALF, rows),
            whole(features, rows),
            pl.BlockSpec((1,) + w_qkv.shape[1:], lambda m, h: (m, 0, 0)),
        ],
        out_specs=[
            pl.BlockSpec((1,) + w_qkv.shape[1:], lambda m, h: (m, 0, 0)),
            whole(features, rows),
            whole(features, 1),
        ],
        out_shape=[
            jax.ShapeDtypeStruct(w_qkv.shape, BF16),
            jax.ShapeDtypeStruct((features, rows), BF16),
            jax.ShapeDtypeStruct((features, 1), F32),
        ],
        scratch_shapes=[
            pltpu.VMEM((width, own), BF16),
            pltpu.VMEM((8, 128), F32),
            pltpu.VMEM((8, 128), F32),
            pltpu.VMEM((2 * width, rows), BF16),
            pltpu.VMEM((features, rows), F32),
            pltpu.VMEM((AUG, rows), BF16),
        ],
        compiler_params=params("arbitrary", "arbitrary"),
        name="last",
    )(q, k, v, do, p, cos, sin, n1, w_qkv)


def finish_kernel(tok_ref, gain_ref, nc_ref, mcot_ref, out_ref):
    hat, inv_sigma = normalize(tok_ref[...].T.astype(F32))
    d = nc_ref[...].astype(F32) * gain_ref[...]
    made = mcot_ref[...] + inv_sigma * (
        d - jnp.mean(d, axis=0, keepdims=True) - hat * jnp.mean(d * hat, axis=0, keepdims=True)
    )
    out_ref[...] = made.T.astype(BF16)


def finish(tokens, gain, nc, middle_cot, own_axis="mp"):
    features, own = middle_cot.shape
    tok = lax.dynamic_slice_in_dim(tokens, lax.axis_index(own_axis) * own, own, 0)
    vm = pl.BlockSpec(memory_space=pltpu.VMEM)
    return pl.pallas_call(
        finish_kernel,
        in_specs=[vm] * 4,
        out_specs=vm,
        out_shape=jax.ShapeDtypeStruct((own, features), BF16),
        compiler_params=params(),
        name="finish",
    )(tok, gain, nc, middle_cot)


def per_device(n_dp, n_mp, tokens, out_grad, w_qkv, w_out, w_gu, w_down, gain_attn, gain_mlp, lengths):
    rows, features = tokens.shape
    depth = w_qkv.shape[0]
    everyone = ("mp", "dp")

    def gather(shard):
        full = lax.all_gather(shard, everyone, axis=0, tiled=True)
        return full.reshape(n_mp, features, shard.shape[1])

    full_qkv = gather(w_qkv.reshape(depth, -1))
    full_out = gather(w_out.T)
    full_gu = gather(w_gu.reshape(depth, -1))
    full_down = gather(w_down.T)
    gain_one = lax.all_gather(gain_attn, "dp", axis=0, tiled=True).astype(F32)[:, None]
    gain_two = lax.all_gather(gain_mlp, "dp", axis=0, tiled=True).astype(F32)[:, None]
    n1, q, k, v, cos, sin = prep(lengths, tokens, gain_one, full_qkv, n_mp)
    heads_out, probs, inv = attend(lengths, q, k, v)
    out_own, middle_cot, do, g_out, g_gu, g_down, gain_two_cot = mid(
        lengths, tokens, out_grad, gain_two, heads_out, inv, full_out, full_gu, full_down
    )
    g_qkv, nc, gain_one_cot = last(q, k, v, do, probs, cos, sin, n1, full_qkv)
    nc_own = lax.psum_scatter(nc, "mp", scatter_dimension=1, tiled=True)
    in_own = finish(tokens, gain_one, nc_own, middle_cot)
    layer_out = lax.all_gather(out_own, "mp", axis=0, tiled=True)
    input_grad = lax.all_gather(in_own, "mp", axis=0, tiled=True).astype(F32)

    def scatter(grad):
        flat = grad.reshape(n_mp * features, grad.shape[2])
        return lax.psum_scatter(flat, everyone, scatter_dimension=0, tiled=True).astype(F32)

    def gain_grad(partial):
        full = lax.psum(partial[:, 0], ("dp", "mp"))
        return lax.dynamic_slice_in_dim(full, lax.axis_index("dp") * depth, depth, 0)

    return (
        layer_out,
        input_grad,
        scatter(g_qkv).reshape(w_qkv.shape),
        scatter(g_out).T,
        scatter(g_gu).reshape(w_gu.shape),
        scatter(g_down).T,
        gain_grad(gain_one_cot / gain_one),
        gain_grad(gain_two_cot),
    )


def solution(mesh):
    n_dp, n_mp = mesh.shape["dp"], mesh.shape["mp"]
    return jax.shard_map(
        functools.partial(per_device, n_dp, n_mp),
        mesh=mesh,
        in_specs=(
            P("dp", None),
            P("dp", None),
            P("dp", None, "mp"),
            P("mp", "dp"),
            P("dp", None, "mp"),
            P("mp", "dp"),
            P("dp"),
            P("dp"),
            P("dp", None),
        ),
        out_specs=(
            P("dp", None),
            P("dp", None),
            P("dp", None, "mp"),
            P("mp", "dp"),
            P("dp", None, "mp"),
            P("mp", "dp"),
            P("dp"),
            P("dp"),
        ),
        check_vma=False,
    )
```

```python
import functools
import math

import jax
import jax.numpy as jnp
from jax import lax
from jax.experimental import pallas as pl
from jax.experimental.pallas import tpu as pltpu
from jax.sharding import PartitionSpec as P

HDIM = 64
HALF = HDIM // 2
AUG = HDIM + 16
EPS = 1e-05
ROPE_BASE = 160000.0
LOG2E = math.log2(math.e)
LN2 = math.log(2.0)
SCALE = HDIM ** (-0.5)
FAR = -1e30
BF16 = jnp.bfloat16
F32 = jnp.float32
VMEM_BYTES = 60 << 20
NN = (((1,), (0,)), ((), ()))
NT = (((1,), (1,)), ((), ()))
TN = (((0,), (0,)), ((), ()))


def dot(a, b, dims):
    return lax.dot_general(a, b, dims, preferred_element_type=F32)


def params(*semantics):
    return pltpu.CompilerParams(
        dimension_semantics=semantics or None, vmem_limit_bytes=VMEM_BYTES
    )


def whole(*shape):
    return pl.BlockSpec(shape, lambda *i: (0,) * len(shape))


def layout_rows(len_ref, docs, first, rows):
    index = first + lax.broadcasted_iota(jnp.int32, (1, rows), 1)
    segment = jnp.zeros((1, rows), jnp.int32)
    start = jnp.zeros((1, rows), jnp.int32)
    end = jnp.int32(0)
    for j in range(docs):
        end = end + len_ref[0, j]
        past = index >= end
        segment = segment + jnp.where(past, 1, 0)
        start = jnp.where(past, jnp.maximum(start, end), start)
    return segment, index - start, index < end


def normalize(columns):
    mean = jnp.mean(columns, axis=0, keepdims=True)
    centered = columns - mean
    var = jnp.mean(centered * centered, axis=0, keepdims=True)
    inv = lax.rsqrt(var + EPS)
    return centered * inv, inv


def turn(block, cos, sin, heads, back=False):
    out = []
    for h in range(heads):
        one = block[h * HDIM : h * HDIM + HALF]
        two = block[h * HDIM + HALF : (h + 1) * HDIM]
        if back:
            out += [one * cos + two * sin, two * cos - one * sin]
        else:
            out += [one * cos - two * sin, two * cos + one * sin]
    return jnp.concatenate(out, axis=0)


def prep_kernel(own_axis, own, len_ref, tok_ref, w_ref, n1_ref, q_ref, k_ref, v_ref, cos_ref, sin_ref):
    features, rows = n1_ref.shape
    width = q_ref.shape[0]
    heads = width // HDIM
    chunk = own

    @pl.when(pl.program_id(0) == 0)
    def _():
        gain = w_ref[0, :, 3 * width :].astype(F32)

        def norm(i, carry):
            at = pl.ds(pl.multiple_of(i * chunk, chunk), chunk)
            hat, _ = normalize(tok_ref[at, :].T.astype(F32))
            n1_ref[:, at] = (hat * gain).astype(BF16)
            return carry

        lax.fori_loop(0, rows // chunk, norm, 0)
        _, position, _ = layout_rows(len_ref, len_ref.shape[1], 0, rows)
        power = lax.broadcasted_iota(jnp.int32, (HALF, 1), 0).astype(F32) * (-2.0 / HDIM * math.log2(ROPE_BASE))
        angle = position.astype(F32) * jnp.exp2(power)
        cos_ref[...] = jnp.cos(angle)
        sin_ref[...] = jnp.sin(angle)

    def project(i, carry):
        at = pl.ds(pl.multiple_of(i * chunk, chunk), chunk)
        made = dot(w_ref[0, :, width : 3 * width], n1_ref[:, at], TN)
        k_ref[:, at] = turn(made[:width], cos_ref[:, at], sin_ref[:, at], heads).astype(BF16)
        v_ref[:, at] = made[width:].astype(BF16)
        return carry

    lax.fori_loop(0, rows // chunk, project, 0)
    mine = pl.ds(pl.multiple_of(lax.axis_index(own_axis) * own, own), own)
    made = dot(w_ref[0, :, :width], n1_ref[:, mine], TN) * (SCALE * LOG2E)
    q_ref[...] = turn(made, cos_ref[:, mine], sin_ref[:, mine], heads).astype(BF16)


def prep(lengths, tokens, w_qkv, n_mp, own_axis="mp"):
    rows, features = tokens.shape
    own = rows // n_mp
    width = features // n_mp
    return pl.pallas_call(
        functools.partial(prep_kernel, own_axis, own),
        grid=(n_mp,),
        in_specs=[
            pl.BlockSpec(memory_space=pltpu.SMEM),
            whole(rows, features),
            pl.BlockSpec((1,) + w_qkv.shape[1:], lambda m: (m, 0, 0)),
        ],
        out_specs=[
            whole(features, rows),
            pl.BlockSpec((width, own), lambda m: (m, 0)),
            pl.BlockSpec((width, rows), lambda m: (m, 0)),
            pl.BlockSpec((width, rows), lambda m: (m, 0)),
            whole(HALF, rows),
            whole(HALF, rows),
        ],
        out_shape=[
            jax.ShapeDtypeStruct((features, rows), BF16),
            jax.ShapeDtypeStruct((features, own), BF16),
            jax.ShapeDtypeStruct((features, rows), BF16),
            jax.ShapeDtypeStruct((features, rows), BF16),
            jax.ShapeDtypeStruct((HALF, rows), F32),
            jax.ShapeDtypeStruct((HALF, rows), F32),
        ],
        compiler_params=params("arbitrary"),
        name="prep",
    )(lengths, tokens, w_qkv)


def attend_kernel(own_axis, len_ref, q_ref, k_ref, v_ref, o_ref, p_ref, inv_ref, ka_ref, qa_ref, va_ref):
    rows, own = k_ref.shape[1], q_ref.shape[1]
    docs = len_ref.shape[1]

    @pl.when(pl.program_id(0) == 0)
    def _():
        keys, _, _ = layout_rows(len_ref, docs, 0, rows)
        queries, _, _ = layout_rows(len_ref, docs, lax.axis_index(own_axis) * own, own)
        kind = lax.broadcasted_iota(jnp.int32, (AUG - HDIM, 1), 0)
        ka_ref[HDIM:] = jnp.where(kind == keys, 1.0, 0.0).astype(BF16)
        qa_ref[HDIM:] = jnp.where(kind == queries, 0.0, FAR).astype(BF16)
        va_ref[HDIM:] = jnp.ones((AUG - HDIM, rows), BF16)

    ka_ref[:HDIM] = k_ref[...]
    qa_ref[:HDIM] = q_ref[...]
    va_ref[:HDIM] = v_ref[...]
    step = 256
    for c in range(own // step):
        at = slice(c * step, (c + 1) * step)
        scores = dot(ka_ref[...], qa_ref[:, at], TN)
        top = jnp.max(scores, axis=0, keepdims=True)
        probs = jnp.exp2(scores - top).astype(BF16)
        p_ref[0, :, at] = probs
        out = dot(va_ref[...], probs, NN)
        inv = 1.0 / out[HDIM : HDIM + 1]
        o_ref[:, at] = (out[:HDIM] * inv).astype(BF16)
        inv_ref[0, :, at] = inv


def attend(lengths, q, k, v, own_axis="mp"):
    (features, own), rows = q.shape, k.shape[1]
    heads = features // HDIM
    return pl.pallas_call(
        functools.partial(attend_kernel, own_axis),
        grid=(heads,),
        in_specs=[
            pl.BlockSpec(memory_space=pltpu.SMEM),
            pl.BlockSpec((HDIM, own), lambda h: (h, 0)),
            pl.BlockSpec((HDIM, rows), lambda h: (h, 0)),
            pl.BlockSpec((HDIM, rows), lambda h: (h, 0)),
        ],
        out_specs=[
            pl.BlockSpec((HDIM, own), lambda h: (h, 0)),
            pl.BlockSpec((1, rows, own), lambda h: (h, 0, 0)),
            pl.BlockSpec((1, 1, own), lambda h: (h, 0, 0)),
        ],
        out_shape=[
            jax.ShapeDtypeStruct((features, own), BF16),
            jax.ShapeDtypeStruct((heads, rows, own), BF16),
            jax.ShapeDtypeStruct((heads, 1, own), F32),
        ],
        scratch_shapes=[
            pltpu.VMEM((AUG, rows), BF16),
            pltpu.VMEM((AUG, own), BF16),
            pltpu.VMEM((AUG, rows), BF16),
        ],
        compiler_params=params("arbitrary"),
        name="attend",
    )(lengths, q, k, v)


def gelu_parts(gate):
    phi = 0.5 * (1.0 + lax.erf(gate * math.sqrt(0.5)))
    density = jnp.exp2(gate * gate * (-0.5 * LOG2E)) * (1.0 / math.sqrt(2.0 * math.pi))
    return phi, gate * density


def mid_kernel(
    own_axis, units, len_ref, tok_ref, cot_ref, heads_ref, inv_ref, w_ref,
    out_ref, mcot_ref, do_ref, g_ref,
):
    own, features = tok_ref.shape
    parts = w_ref.shape[0]
    width = features // parts
    heads = width // HDIM
    pair = 2 * units
    _, _, live = layout_rows(len_ref, len_ref.shape[1], lax.axis_index(own_axis) * own, own)

    def w_gu(m):
        return w_ref[m, :, :pair]

    def w_out(m):
        return w_ref[m, :, pair : pair + width]

    def w_down(m):
        return w_ref[m, :, pair + width : pair + width + units]

    total = dot(w_out(0), heads_ref[:width], NN)
    for m in range(1, parts):
        total += dot(w_out(m), heads_ref[m * width : (m + 1) * width], NN)
    middle = tok_ref[...].T.astype(F32) + total
    gain = w_ref[0, :, pair + width + units :].astype(F32)
    hat, inv_sigma = normalize(middle)
    normed = (hat * gain).astype(BF16)
    branch = jnp.where(live, cot_ref[...].T.astype(F32), 0.0).astype(BF16)
    total = middle
    back = jnp.zeros((features, own), F32)
    for m in range(parts):
        gate_up = dot(w_gu(m), normed, TN)
        gate, up = gate_up[:units], gate_up[units:]
        phi, slope = gelu_parts(gate)
        act = gate * phi
        hidden = (act * up).astype(BF16)
        total += dot(w_down(m), hidden, NN)
        hidden_cot = dot(w_down(m), branch, TN)
        g_ref[m, :, pair + width : pair + width + units] = dot(branch, hidden, NT).astype(BF16)
        cots = jnp.concatenate([hidden_cot * up * (phi + slope), hidden_cot * act], axis=0).astype(BF16)
        g_ref[m, :, :pair] = dot(normed, cots, NT).astype(BF16)
        back += dot(w_gu(m), cots, NN)
    out_ref[...] = total.astype(BF16).T
    gain_cot = jnp.sum(back * hat, axis=1, keepdims=True).astype(BF16)
    d = back * gain
    middle_cot = branch.astype(F32) + inv_sigma * (
        d - jnp.mean(d, axis=0, keepdims=True) - hat * jnp.mean(d * hat, axis=0, keepdims=True)
    )
    mcot_ref[...] = middle_cot
    attn_cot = middle_cot.astype(BF16)
    for m in range(parts):
        g_ref[m, :, pair + width + units :] = gain_cot
        part = heads_ref[m * width : (m + 1) * width]
        g_ref[m, :, pair : pair + width] = dot(attn_cot, part, NT).astype(BF16)
        back_heads = dot(w_out(m), attn_cot, TN)
        for h in range(heads):
            head = m * heads + h
            rows = slice(h * HDIM, (h + 1) * HDIM)
            cot = back_heads[rows] * inv_ref[head]
            inner = jnp.sum(cot * part[rows].astype(F32), axis=0, keepdims=True)
            high = inner.astype(BF16).astype(F32)
            pad = jnp.zeros((AUG - HDIM - 2, own), F32)
            do_ref[head] = jnp.concatenate([cot, high, inner - high, pad], axis=0).astype(BF16)


def mid(lengths, tokens, out_grad, heads_out, inv, w_rest, units, own_axis="mp"):
    features, own = heads_out.shape
    heads = inv.shape[0]
    tok = lax.dynamic_slice_in_dim(tokens, lax.axis_index(own_axis) * own, own, 0)
    cot = lax.dynamic_slice_in_dim(out_grad, lax.axis_index(own_axis) * own, own, 0)
    vm = pl.BlockSpec(memory_space=pltpu.VMEM)
    return pl.pallas_call(
        functools.partial(mid_kernel, own_axis, units),
        in_specs=[pl.BlockSpec(memory_space=pltpu.SMEM)] + [vm] * 5,
        out_specs=[vm] * 4,
        out_shape=[
            jax.ShapeDtypeStruct((own, features), BF16),
            jax.ShapeDtypeStruct((features, own), F32),
            jax.ShapeDtypeStruct((heads, AUG, own), BF16),
            jax.ShapeDtypeStruct(w_rest.shape, BF16),
        ],
        compiler_params=params(),
        name="mid",
    )(lengths, tok, cot, heads_out, inv, w_rest)


def last_kernel(own_axis, q_ref, k_ref, v_ref, do_ref, p_ref, cos_ref, sin_ref, n1_ref, w_ref, gq_ref, nc_ref, gc_ref, dq_ref, pc_ref, acc_ref, va_ref):
    step, head = pl.program_id(0), pl.program_id(1)
    per = pl.num_programs(1)
    features, rows = n1_ref.shape
    own = q_ref.shape[1]
    width = per * HDIM
    mine = pl.ds(pl.multiple_of(lax.axis_index(own_axis) * own, own), own)

    @pl.when((step == 0) & (head == 0))
    def _():
        va_ref[HDIM:] = jnp.full((AUG - HDIM, rows), -1.0, BF16)
        acc_ref[...] = jnp.zeros_like(acc_ref)
        gc_ref[...] = jnp.zeros_like(gc_ref)

    va_ref[:HDIM] = v_ref[...]
    cot = dot(va_ref[...], do_ref[0], TN)
    probs = p_ref[0]
    score_cot = probs * cot.astype(BF16)
    at = pl.ds(pl.multiple_of(head * HDIM, HDIM), HDIM)
    dv = dot(do_ref[0, :HDIM], probs, NT)
    dk = dot(q_ref[...], score_cot, NT) * LN2
    dq = dot(k_ref[...], score_cot, NN) * SCALE
    pc_ref[pl.ds(pl.multiple_of(width + head * HDIM, HDIM), HDIM)] = dv.astype(BF16)
    pc_ref[at] = turn(dk, cos_ref[...], sin_ref[...], 1, True).astype(BF16)
    dq_ref[at] = turn(dq, cos_ref[:, mine], sin_ref[:, mine], 1, True).astype(BF16)

    @pl.when(head == per - 1)
    def _():
        kv = dot(n1_ref[...], pc_ref[...], NT)
        q = dot(n1_ref[:, mine], dq_ref[...], NT)
        gq_ref[step, :, :width] = q.astype(BF16)
        gq_ref[step, :, width : 3 * width] = kv.astype(BF16)
        gc_ref[...] += jnp.sum(q * w_ref[0, :, :width].astype(F32), axis=1, keepdims=True) + jnp.sum(
            kv * w_ref[0, :, width : 3 * width].astype(F32), axis=1, keepdims=True
        )

        def spread(i, carry):
            cols = pl.ds(pl.multiple_of(i * own, own), own)
            acc_ref[:, cols] += dot(w_ref[0, :, width : 3 * width], pc_ref[:, cols], NN)
            return carry

        lax.fori_loop(0, rows // own, spread, 0)
        acc_ref[:, mine] += dot(w_ref[0, :, :width], dq_ref[...], NN)

    @pl.when((step == pl.num_programs(0) - 1) & (head == per - 1))
    def _():
        gain_cot = (gc_ref[...] / w_ref[0, :, 3 * width :].astype(F32)).astype(BF16)
        for m in range(gq_ref.shape[0]):
            nc_ref[m] = acc_ref[:, m * own : (m + 1) * own].astype(BF16)
            gq_ref[m, :, 3 * width :] = gain_cot


def last(q, k, v, do, p, cos, sin, n1, w_qkv, own_axis="mp"):
    (features, own), rows = q.shape, k.shape[1]
    parts = w_qkv.shape[0]
    per = features // parts // HDIM
    width = per * HDIM
    head = lambda m, h: (m * per + h, 0)
    return pl.pallas_call(
        functools.partial(last_kernel, own_axis),
        grid=(parts, per),
        in_specs=[
            pl.BlockSpec((HDIM, own), head),
            pl.BlockSpec((HDIM, rows), head),
            pl.BlockSpec((HDIM, rows), head),
            pl.BlockSpec((1, AUG, own), lambda m, h: (m * per + h, 0, 0)),
            pl.BlockSpec((1, rows, own), lambda m, h: (m * per + h, 0, 0)),
            whole(HALF, rows),
            whole(HALF, rows),
            whole(features, rows),
            pl.BlockSpec((1,) + w_qkv.shape[1:], lambda m, h: (m, 0, 0)),
        ],
        out_specs=[
            whole(*w_qkv.shape),
            whole(parts, features, own),
        ],
        out_shape=[
            jax.ShapeDtypeStruct(w_qkv.shape, BF16),
            jax.ShapeDtypeStruct((parts, features, own), BF16),
        ],
        scratch_shapes=[
            pltpu.VMEM((features, 1), F32),
            pltpu.VMEM((width, own), BF16),
            pltpu.VMEM((2 * width, rows), BF16),
            pltpu.VMEM((features, rows), F32),
            pltpu.VMEM((AUG, rows), BF16),
        ],
        compiler_params=params("arbitrary", "arbitrary"),
        name="last",
    )(q, k, v, do, p, cos, sin, n1, w_qkv)


def place():
    dp, mp = lax.axis_index("dp"), lax.axis_index("mp")
    return dp // 2, lax.rem(dp, 2), mp // 2, lax.rem(mp, 2)


def device(z, x, y, c):
    return (2 * z + x, 2 * y + c)


def remote(src, dst, send, recv, target):
    return pltpu.make_async_remote_copy(
        src_ref=src, dst_ref=dst, send_sem=send, recv_sem=recv,
        device_id=target, device_id_type=pl.DeviceIdType.MESH,
    )


def greet(targets):
    barrier = pltpu.get_barrier_semaphore()
    for target in targets:
        pl.semaphore_signal(barrier, inc=1, device_id=target, device_id_type=pl.DeviceIdType.MESH)
    pl.semaphore_wait(barrier, len(targets))


def peers(nz):
    z, x, y, c = place()
    across = [device(z, 1 - x, y, c), device(z, x, 1 - y, c), device(z, x, y, 1 - c)]
    return across + [device(lax.rem(z + d, nz), x, y, c) for d in range(1, nz)]


class Gather:
    def __init__(self, nz, src, full, send, recv, local):
        self.nz, self.src, self.full, self.send, self.recv, self.local = nz, src, full, send, recv, local
        self.depth = src.shape[0]
        self.index = {}
        for kind in ("Z", "X", "Y", "S", "YA", "XB", "SX", "SY", "SA", "SB"):
            for d in range(1 if kind == "Z" else 0, nz):
                self.index[kind, d] = len(self.index)

    @staticmethod
    def count(nz):
        return nz - 1 + 9 * nz

    def block(self, z, x, y, c, half=None):
        first, size = (0, self.depth) if half is None else (half * self.depth // 2, self.depth // 2)
        return self.full.at[2 * y + c, pl.ds(pl.multiple_of((2 * z + x) * self.depth + first, 16), size)]

    def message(self, kind, d, sending):
        z, x, y, c = place()
        nz = self.nz
        back = z if d == 0 else lax.rem(z - d + nz, nz)
        ahead = lax.rem(z + d, nz)
        sx, sy, sib = device(z, 1 - x, y, c), device(z, x, 1 - y, c), device(z, x, y, 1 - c)
        sent, got, half, target = {
            "Z": ((z, x, y, c), (back, x, y, c), None, device(ahead, x, y, c)),
            "X": ((back, x, y, c), (back, 1 - x, y, c), None, sx),
            "Y": ((back, x, y, c), (back, x, 1 - y, c), None, sy),
            "S": ((back, x, y, c), (back, x, y, 1 - c), None, sib),
            "YA": ((back, 1 - x, y, c), (back, 1 - x, 1 - y, c), 0, sy),
            "XB": ((back, x, 1 - y, c), (back, 1 - x, 1 - y, c), 1, sx),
            "SX": ((back, 1 - x, y, c), (back, 1 - x, y, 1 - c), None, sib),
            "SY": ((back, x, 1 - y, c), (back, x, 1 - y, 1 - c), None, sib),
            "SA": ((back, 1 - x, 1 - y, c), (back, 1 - x, 1 - y, 1 - c), 0, sib),
            "SB": ((back, 1 - x, 1 - y, c), (back, 1 - x, 1 - y, 1 - c), 1, sib),
        }[kind]
        i = self.index[kind, d]
        at = self.block(*(sent if sending else got), half)
        own = sending and (kind == "Z" or (d == 0 and kind in ("X", "Y", "S")))
        return remote(self.src if own else at, at, self.send.at[i], self.recv.at[i], target)

    def start(self, kind, d):
        self.message(kind, d, True).start()

    def arrived(self, kind, d):
        self.message(kind, d, False).wait_recv()

    def own(self):
        z, x, y, c = place()
        return pltpu.make_async_copy(self.src, self.block(z, x, y, c), self.local)

    def begin(self):
        for d in range(1, self.nz):
            self.start("Z", d)
        for kind in ("X", "Y", "S"):
            self.start(kind, 0)
        self.own().start()

    def along(self, d):
        self.arrived("Z", d)
        for kind in ("X", "Y", "S"):
            self.start(kind, d)

    def over(self, d):
        self.arrived("X", d)
        self.start("YA", d)
        self.start("SX", d)
        self.arrived("Y", d)
        self.start("XB", d)
        self.start("SY", d)

    def corner(self, d):
        self.arrived("YA", d)
        self.start("SA", d)
        self.arrived("XB", d)
        self.start("SB", d)

    def end(self):
        self.own().wait()
        for d in range(self.nz):
            for kind in ("S", "SX", "SY", "SA", "SB"):
                self.arrived(kind, d)
        for kind, d in self.index:
            self.message(kind, d, True).wait_send()

    def order(self):
        nz = self.nz
        near = sorted(range(1, nz), key=lambda d: min(d, nz - d))
        steps = [functools.partial(self.begin)]
        for d in [0] + near:
            if d:
                steps.append(functools.partial(self.along, d))
            steps.append(functools.partial(self.over, d))
        for d in [0] + near:
            steps.append(functools.partial(self.corner, d))
        return steps + [self.end]


def gather_kernel(nz, count, *refs):
    srcs, fulls, sems = refs[:count], refs[count : 2 * count], refs[2 * count :]
    greet(peers(nz))
    gathers = [Gather(nz, srcs[i], fulls[i], *sems[3 * i : 3 * i + 3]) for i in range(count)]
    for steps in zip(*[g.order() for g in gathers]):
        for step in steps:
            step()


def gather_all(nz, n_mp, shards):
    hbm = pl.BlockSpec(memory_space=pl.ANY)
    n = Gather.count(nz)
    dma = pltpu.SemaphoreType.DMA
    return pl.pallas_call(
        functools.partial(gather_kernel, nz, len(shards)),
        in_specs=[hbm] * len(shards),
        out_specs=[hbm] * len(shards),
        out_shape=[jax.ShapeDtypeStruct((n_mp, 2 * nz * s.shape[0], s.shape[1]), BF16) for s in shards],
        scratch_shapes=[dma((n,)), dma((n,)), dma] * len(shards),
        compiler_params=pltpu.CompilerParams(collective_id=1, has_side_effects=True),
        name="gather_all",
    )(*shards)


class Scatter:
    def __init__(self, nz, part, out, core, side, line, last, send, recv):
        self.nz, self.part, self.out, self.core, self.side, self.line, self.last = nz, part, out, core, side, line, last
        self.send, self.recv = send, recv
        self.depth = out.shape[0]

    @staticmethod
    def scratch(nz, depth, columns):
        count = 2 * nz + nz + nz
        return [
            pltpu.VMEM((2, 2 * nz * depth, columns), BF16),
            pltpu.VMEM((2, nz * depth, columns), BF16),
            pltpu.VMEM((nz, 2, depth, columns), BF16),
            pltpu.VMEM((depth, columns), BF16),
            pltpu.SemaphoreType.DMA((count,)),
            pltpu.SemaphoreType.DMA((count,)),
        ]

    def row(self, d):
        z, _, _, _ = place()
        return z if d == 0 else lax.rem(z + d, self.nz)

    def rows(self, d, x):
        return pl.ds(pl.multiple_of((2 * self.row(d) + x) * self.depth, 16), self.depth)

    def both(self, d):
        return pl.ds(pl.multiple_of(2 * self.row(d) * self.depth, 16), 2 * self.depth)

    def lane(self, d):
        return pl.ds(pl.multiple_of(self.row(d) * self.depth, 16), self.depth)

    def message(self, kind, d, up=0):
        z, x, y, c = place()
        nz = self.nz
        i = {"C": up * nz + d, "X": 2 * nz + d, "Z": 3 * nz + d, "Y": 3 * nz}[kind]
        sems = self.send.at[i], self.recv.at[i]
        if kind == "C":
            both = self.both(d)
            return remote(self.part.at[2 * up + 1 - c, both], self.core.at[up, both], *sems, device(z, x, y, 1 - c))
        if kind == "X":
            return remote(
                self.core.at[:, self.rows(d, 1 - x)], self.side.at[:, self.lane(d)], *sems, device(z, 1 - x, y, c)
            )
        if kind == "Z":
            return remote(self.side.at[:, self.lane(d)], self.line.at[d], *sems, device(self.row(d), x, y, c))
        return remote(self.line.at[0, 1 - y], self.last, *sems, device(z, x, 1 - y, c))

    def begin(self):
        for d in [*range(1, self.nz), 0]:
            for up in range(2):
                self.message("C", d, up).start()

    def chip(self, d):
        _, x, _, c = place()
        for up in range(2):
            self.message("C", d, up).wait_recv()
        for side in (1 - x, x):
            rows = self.rows(d, side)
            for up in range(2):
                made = self.part[2 * up + c, rows].astype(F32) + self.core[up, rows].astype(F32)
                self.core[up, rows] = made.astype(BF16)
            if side is not x:
                self.message("X", d).start()

    def over(self, d):
        _, x, _, _ = place()
        self.message("X", d).wait_recv()
        rows, lane = self.rows(d, x), self.lane(d)
        for up in range(2):
            made = self.core[up, rows].astype(F32) + self.side[up, lane].astype(F32)
            self.side[up, lane] = made.astype(BF16)
        if d:
            self.message("Z", d).start()

    def along(self):
        _, _, y, _ = place()
        for d in range(1, self.nz):
            self.message("Z", d).wait_recv()
        lane = self.lane(0)
        for up in range(2):
            made = self.side[up, lane].astype(F32)
            for d in range(1, self.nz):
                made += self.line[d, up].astype(F32)
            self.line[0, up] = made.astype(BF16)
        self.message("Y", 0).start()

    def end(self):
        _, _, y, _ = place()
        self.message("Y", 0).wait_recv()
        self.out[...] = self.line[0, y].astype(F32) + self.last[...].astype(F32)
        for d in range(self.nz):
            for up in range(2):
                self.message("C", d, up).wait_send()
            self.message("X", d).wait_send()
            if d:
                self.message("Z", d).wait_send()
        self.message("Y", 0).wait_send()

    def order(self):
        far = [*range(1, self.nz), 0]
        return (
            [self.begin]
            + [functools.partial(self.chip, d) for d in far]
            + [functools.partial(self.over, d) for d in far]
            + [self.along, self.end]
        )


class Share:
    def __init__(self, src, full, send, recv, local, pieces=1):
        self.src, self.full, self.send, self.recv, self.local, self.pieces = src, full, send, recv, local, pieces
        self.size = src.shape[0] // pieces

    @staticmethod
    def sems(pieces):
        dma = pltpu.SemaphoreType.DMA
        return [dma((3 * pieces,)), dma((3 * pieces,)), dma((pieces,))]

    def rows(self, y, c, i):
        own = self.size * self.pieces
        return pl.ds(pl.multiple_of((2 * y + c) * own + i * self.size, 16), self.size)

    def message(self, kind, i):
        z, x, y, c = place()
        n = self.pieces
        piece = self.src.at[pl.ds(i * self.size, self.size)]
        if kind == "own":
            return pltpu.make_async_copy(piece, self.full.at[self.rows(y, c, i)], self.local.at[i])
        k = {"Y": 0, "C": 1, "F": 2}[kind] * n + i
        sems = self.send.at[k], self.recv.at[k]
        sib = device(z, x, y, 1 - c)
        if kind == "Y":
            return remote(piece, self.full.at[self.rows(y, c, i)], *sems, device(z, x, 1 - y, c))
        if kind == "C":
            return remote(piece, self.full.at[self.rows(y, c, i)], *sems, sib)
        at = self.full.at[self.rows(1 - y, c, i)]
        return remote(at, at, *sems, sib)

    def begin(self, i):
        for kind in ("Y", "C", "own"):
            self.message(kind, i).start()

    def on(self, i):
        self.message("Y", i).wait_recv()
        self.message("F", i).start()

    def end(self):
        for i in range(self.pieces):
            self.message("own", i).wait()
            self.message("C", i).wait_recv()
            self.message("F", i).wait_recv()
            for kind in ("Y", "C", "F"):
                self.message(kind, i).wait_send()


class Fold:
    def __init__(self, part, near, far, send, recv, pieces):
        self.part, self.near, self.far, self.send, self.recv, self.pieces = part, near, far, send, recv, pieces
        self.size = part.shape[1] // pieces

    @staticmethod
    def scratch(features, own, pieces):
        dma = pltpu.SemaphoreType.DMA
        return [pltpu.VMEM((2, features, own), BF16), pltpu.VMEM((features, own), BF16), dma((3 * pieces,)), dma((3 * pieces,))]

    def rows(self, i):
        return pl.ds(i * self.size, self.size)

    def message(self, kind, i):
        z, x, y, c = place()
        k = {"far": 0, "near": 1, "Y": 2}[kind] * self.pieces + i
        sems = self.send.at[k], self.recv.at[k]
        rows = self.rows(i)
        if kind == "Y":
            return remote(self.near.at[1 - y, rows], self.far.at[rows], *sems, device(z, x, 1 - y, c))
        up = 1 - y if kind == "far" else y
        return remote(self.part.at[2 * up + 1 - c, rows], self.near.at[up, rows], *sems, device(z, x, y, 1 - c))

    def begin(self):
        for kind in ("far", "near"):
            for i in range(self.pieces):
                self.message(kind, i).start()

    def chip(self, i):
        _, _, y, c = place()
        self.message("far", i).wait_recv()
        rows = self.rows(i)
        made = self.part[2 * (1 - y) + c, rows].astype(F32) + self.near[1 - y, rows].astype(F32)
        self.near[1 - y, rows] = made.astype(BF16)
        self.message("Y", i).start()

    def end(self):
        _, _, y, c = place()
        for i in range(self.pieces):
            self.message("near", i).wait_recv()
            self.message("Y", i).wait_recv()
        made = self.part[2 * y + c].astype(F32) + self.near[y].astype(F32) + self.far[...].astype(F32)
        for i in range(self.pieces):
            for kind in ("far", "near", "Y"):
                self.message(kind, i).wait_send()
        return made


def finish(tokens, gain, cot, middle_cot):
    hat, inv_sigma = normalize(tokens.T.astype(F32))
    d = cot * gain
    made = middle_cot + inv_sigma * (
        d - jnp.mean(d, axis=0, keepdims=True) - hat * jnp.mean(d * hat, axis=0, keepdims=True)
    )
    return made.T.astype(BF16)


FOLD_PIECES = 4


def tail_kernel(nz, *refs):
    tok_ref, gain_ref, nc_ref, mcot_ref, out_own, gq_ref, gr_ref = refs[:7]
    out_full, in_full, dq_ref, dr_ref = refs[7:11]
    in_own = refs[11]
    a, b = Scatter(nz, gq_ref, dq_ref, *refs[12:18]), Scatter(nz, gr_ref, dr_ref, *refs[18:24])
    fold = Fold(nc_ref, *refs[24:28], FOLD_PIECES)
    out_share, in_share = Share(out_own, out_full, *refs[28:31]), Share(in_own, in_full, *refs[31:34])
    greet(peers(nz))
    fold.begin()
    for i in range(FOLD_PIECES):
        fold.chip(i)
    a.begin()
    b.begin()
    a_steps, b_steps = a.order()[1:], b.order()[1:]
    for i in range(nz):
        a_steps[i]()
        b_steps[i]()
    in_own[...] = finish(tok_ref[...], gain_ref[...], fold.end(), mcot_ref[...])
    in_share.begin(0)
    out_share.begin(0)
    for i in range(nz, len(a_steps)):
        a_steps[i]()
        b_steps[i]()
    for share in (in_share, out_share):
        share.on(0)
    for share in (in_share, out_share):
        share.end()


def tail(nz, n_mp, tokens, gain, nc, middle_cot, out_own, g_qkv, g_rest):
    features, own = middle_cot.shape
    tok = lax.dynamic_slice_in_dim(tokens, lax.axis_index("mp") * own, own, 0)
    vm = pl.BlockSpec(memory_space=pltpu.VMEM)
    hbm = pl.BlockSpec(memory_space=pl.ANY)
    depth = features // (2 * nz)
    return pl.pallas_call(
        functools.partial(tail_kernel, nz),
        in_specs=[vm] * 7,
        out_specs=[hbm, hbm, vm, vm],
        out_shape=[
            jax.ShapeDtypeStruct((n_mp * own, features), BF16),
            jax.ShapeDtypeStruct((n_mp * own, features), BF16),
            jax.ShapeDtypeStruct((depth, g_qkv.shape[2]), F32),
            jax.ShapeDtypeStruct((depth, g_rest.shape[2]), F32),
        ],
        scratch_shapes=[pltpu.VMEM((own, features), BF16)]
        + Scatter.scratch(nz, depth, g_qkv.shape[2])
        + Scatter.scratch(nz, depth, g_rest.shape[2])
        + Fold.scratch(features, own, FOLD_PIECES)
        + Share.sems(1)
        + Share.sems(1),
        compiler_params=pltpu.CompilerParams(
            collective_id=2, has_side_effects=True, vmem_limit_bytes=VMEM_BYTES
        ),
        name="tail",
    )(tok, gain, nc, middle_cot, out_own, g_qkv, g_rest)


def per_device(n_dp, n_mp, tokens, out_grad, w_qkv, w_out, w_gu, w_down, gain_attn, gain_mlp, lengths):
    rows, features = tokens.shape
    depth = w_qkv.shape[0]
    units, width = w_down.shape[0], w_out.shape[0]
    everyone = ("mp", "dp")
    linked = n_mp == 4 and n_dp % 2 == 0 and depth % 32 == 0
    shards = [
        jnp.concatenate([w_qkv.reshape(depth, -1), gain_attn[:, None]], axis=1),
        jnp.concatenate([w_gu.reshape(depth, -1), w_out.T, w_down.T, gain_mlp[:, None]], axis=1),
    ]
    if linked:
        full_qkv, full_rest = gather_all(n_dp // 2, n_mp, shards)
    else:
        full_qkv, full_rest = (
            lax.all_gather(s, everyone, axis=0, tiled=True).reshape(n_mp, features, s.shape[1]) for s in shards
        )
    n1, q, k, v, cos, sin = prep(lengths, tokens, full_qkv, n_mp)
    heads_out, probs, inv = attend(lengths, q, k, v)
    out_own, middle_cot, do, g_rest = mid(lengths, tokens, out_grad, heads_out, inv, full_rest, units)
    g_qkv, nc = last(q, k, v, do, probs, cos, sin, n1, full_qkv)
    gain_one = full_qkv[0, :, 3 * width :].astype(F32)
    if linked:
        layer_out, input_grad, d_qkv, d_rest = tail(
            n_dp // 2, n_mp, tokens, gain_one, nc, middle_cot, out_own, g_qkv, g_rest
        )
    else:
        own = middle_cot.shape[1]
        tok = lax.dynamic_slice_in_dim(tokens, lax.axis_index("mp") * own, own, 0)
        nc_own = lax.psum_scatter(nc, "mp", scatter_dimension=0, tiled=True)[0]
        in_own = finish(tok, gain_one, nc_own.astype(F32), middle_cot)
        layer_out, input_grad = (lax.all_gather(v, "mp", axis=0, tiled=True) for v in (out_own, in_own))
        d_qkv, d_rest = (
            lax.psum_scatter(
                g.reshape(n_mp * features, -1), everyone, scatter_dimension=0, tiled=True
            ).astype(F32)
            for g in (g_qkv, g_rest)
        )
    pair = 2 * units
    gains = [d_qkv[:, 3 * width], d_rest[:, pair + width + units]]
    if not linked:
        gains = [lax.all_gather(g, "mp")[0] for g in gains]
    return (
        layer_out,
        input_grad.astype(F32),
        d_qkv[:, : 3 * width].reshape(w_qkv.shape),
        d_rest[:, pair : pair + width].T,
        d_rest[:, :pair].reshape(w_gu.shape),
        d_rest[:, pair + width : pair + width + units].T,
        gains[0],
        gains[1],
    )


def solution(mesh):
    n_dp, n_mp = mesh.shape["dp"], mesh.shape["mp"]
    return jax.shard_map(
        functools.partial(per_device, n_dp, n_mp),
        mesh=mesh,
        in_specs=(
            P("dp", None),
            P("dp", None),
            P("dp", None, "mp"),
            P("mp", "dp"),
            P("dp", None, "mp"),
            P("mp", "dp"),
            P("dp"),
            P("dp"),
            P("dp", None),
        ),
        out_specs=(
            P("dp", None),
            P("dp", None),
            P("dp", None, "mp"),
            P("mp", "dp"),
            P("dp", None, "mp"),
            P("mp", "dp"),
            P("dp"),
            P("dp"),
        ),
        check_vma=False,
    )
```

```python
import functools
import math

import jax
import jax.numpy as jnp
from jax import lax
from jax.experimental import pallas as pl
from jax.experimental.pallas import tpu as pltpu
from jax.sharding import PartitionSpec as P

HDIM = 64
HALF = HDIM // 2
AUG = HDIM + 16
EPS = 1e-05
ROPE_BASE = 160000.0
LOG2E = math.log2(math.e)
LN2 = math.log(2.0)
SCALE = HDIM ** (-0.5)
FAR = -1e30
BF16 = jnp.bfloat16
F32 = jnp.float32
VMEM_BYTES = 60 << 20
NN = (((1,), (0,)), ((), ()))
NT = (((1,), (1,)), ((), ()))
TN = (((0,), (0,)), ((), ()))


def dot(a, b, dims):
    return lax.dot_general(a, b, dims, preferred_element_type=F32)


def params(*semantics):
    return pltpu.CompilerParams(
        dimension_semantics=semantics or None, vmem_limit_bytes=VMEM_BYTES
    )


def whole(*shape):
    return pl.BlockSpec(shape, lambda *i: (0,) * len(shape))


def layout_rows(len_ref, docs, first, rows):
    index = first + lax.broadcasted_iota(jnp.int32, (1, rows), 1)
    segment = jnp.zeros((1, rows), jnp.int32)
    start = jnp.zeros((1, rows), jnp.int32)
    end = jnp.int32(0)
    for j in range(docs):
        end = end + len_ref[0, j]
        past = index >= end
        segment = segment + jnp.where(past, 1, 0)
        start = jnp.where(past, jnp.maximum(start, end), start)
    return segment, index - start, index < end


def normalize(columns):
    mean = jnp.mean(columns, axis=0, keepdims=True)
    centered = columns - mean
    var = jnp.mean(centered * centered, axis=0, keepdims=True)
    inv = lax.rsqrt(var + EPS)
    return centered * inv, inv


def turn(block, cos, sin, heads, back=False):
    out = []
    for h in range(heads):
        one = block[h * HDIM : h * HDIM + HALF]
        two = block[h * HDIM + HALF : (h + 1) * HDIM]
        if back:
            out += [one * cos + two * sin, two * cos - one * sin]
        else:
            out += [one * cos - two * sin, two * cos + one * sin]
    return jnp.concatenate(out, axis=0)


def gelu_parts(gate):
    phi = 0.5 * (1.0 + lax.erf(gate * math.sqrt(0.5)))
    density = jnp.exp2(gate * gate * (-0.5 * LOG2E)) * (1.0 / math.sqrt(2.0 * math.pi))
    return phi, gate * density


def last_kernel(own_axis, q_ref, k_ref, v_ref, do_ref, p_ref, cos_ref, sin_ref, n1_ref, w_ref, gq_ref, nc_ref, gc_ref, dq_ref, pc_ref, acc_ref, va_ref):
    step, head = pl.program_id(0), pl.program_id(1)
    per = pl.num_programs(1)
    features, rows = n1_ref.shape
    own = q_ref.shape[1]
    width = per * HDIM
    mine = pl.ds(pl.multiple_of(lax.axis_index(own_axis) * own, own), own)

    @pl.when((step == 0) & (head == 0))
    def _():
        va_ref[HDIM:] = jnp.full((AUG - HDIM, rows), -1.0, BF16)
        acc_ref[...] = jnp.zeros_like(acc_ref)
        gc_ref[...] = jnp.zeros_like(gc_ref)

    va_ref[:HDIM] = v_ref[...]
    cot = dot(va_ref[...], do_ref[0], TN)
    probs = p_ref[0]
    score_cot = probs * cot.astype(BF16)
    at = pl.ds(pl.multiple_of(head * HDIM, HDIM), HDIM)
    dv = dot(do_ref[0, :HDIM], probs, NT)
    dk = dot(q_ref[...], score_cot, NT) * LN2
    dq = dot(k_ref[...], score_cot, NN) * SCALE
    pc_ref[pl.ds(pl.multiple_of(width + head * HDIM, HDIM), HDIM)] = dv.astype(BF16)
    pc_ref[at] = turn(dk, cos_ref[...], sin_ref[...], 1, True).astype(BF16)
    dq_ref[at] = turn(dq, cos_ref[:, mine], sin_ref[:, mine], 1, True).astype(BF16)

    @pl.when(head == per - 1)
    def _():
        kv = dot(n1_ref[...], pc_ref[...], NT)
        q = dot(n1_ref[:, mine], dq_ref[...], NT)
        gq_ref[step, :, :width] = q.astype(BF16)
        gq_ref[step, :, width : 3 * width] = kv.astype(BF16)
        gc_ref[...] += jnp.sum(q * w_ref[0, :, :width].astype(F32), axis=1, keepdims=True) + jnp.sum(
            kv * w_ref[0, :, width : 3 * width].astype(F32), axis=1, keepdims=True
        )

        def spread(i, carry):
            cols = pl.ds(pl.multiple_of(i * own, own), own)
            acc_ref[:, cols] += dot(w_ref[0, :, width : 3 * width], pc_ref[:, cols], NN)
            return carry

        lax.fori_loop(0, rows // own, spread, 0)
        acc_ref[:, mine] += dot(w_ref[0, :, :width], dq_ref[...], NN)

    @pl.when((step == pl.num_programs(0) - 1) & (head == per - 1))
    def _():
        gain_cot = (gc_ref[...] / w_ref[0, :, 3 * width :].astype(F32)).astype(BF16)
        for m in range(gq_ref.shape[0]):
            nc_ref[m] = acc_ref[:, m * own : (m + 1) * own].astype(BF16)
            gq_ref[m, :, 3 * width :] = gain_cot


def last(q, k, v, do, p, cos, sin, n1, w_qkv, own_axis="mp"):
    (features, own), rows = q.shape, k.shape[1]
    parts = w_qkv.shape[0]
    per = features // parts // HDIM
    width = per * HDIM
    head = lambda m, h: (m * per + h, 0)
    return pl.pallas_call(
        functools.partial(last_kernel, own_axis),
        grid=(parts, per),
        in_specs=[
            pl.BlockSpec((HDIM, own), head),
            pl.BlockSpec((HDIM, rows), head),
            pl.BlockSpec((HDIM, rows), head),
            pl.BlockSpec((1, AUG, own), lambda m, h: (m * per + h, 0, 0)),
            pl.BlockSpec((1, rows, own), lambda m, h: (m * per + h, 0, 0)),
            whole(HALF, rows),
            whole(HALF, rows),
            whole(features, rows),
            pl.BlockSpec((1,) + w_qkv.shape[1:], lambda m, h: (m, 0, 0)),
        ],
        out_specs=[
            whole(*w_qkv.shape),
            whole(parts, features, own),
        ],
        out_shape=[
            jax.ShapeDtypeStruct(w_qkv.shape, BF16),
            jax.ShapeDtypeStruct((parts, features, own), BF16),
        ],
        scratch_shapes=[
            pltpu.VMEM((features, 1), F32),
            pltpu.VMEM((width, own), BF16),
            pltpu.VMEM((2 * width, rows), BF16),
            pltpu.VMEM((features, rows), F32),
            pltpu.VMEM((AUG, rows), BF16),
        ],
        compiler_params=params("arbitrary", "arbitrary"),
        name="last",
    )(q, k, v, do, p, cos, sin, n1, w_qkv)


def place():
    dp, mp = lax.axis_index("dp"), lax.axis_index("mp")
    return dp // 2, lax.rem(dp, 2), mp // 2, lax.rem(mp, 2)


def device(z, x, y, c):
    return (2 * z + x, 2 * y + c)


def remote(src, dst, send, recv, target):
    return pltpu.make_async_remote_copy(
        src_ref=src, dst_ref=dst, send_sem=send, recv_sem=recv,
        device_id=target, device_id_type=pl.DeviceIdType.MESH,
    )


def greet(targets):
    barrier = pltpu.get_barrier_semaphore()
    for target in targets:
        pl.semaphore_signal(barrier, inc=1, device_id=target, device_id_type=pl.DeviceIdType.MESH)
    pl.semaphore_wait(barrier, len(targets))


def peers(nz):
    z, x, y, c = place()
    across = [device(z, 1 - x, y, c), device(z, x, 1 - y, c), device(z, x, y, 1 - c)]
    return across + [device(lax.rem(z + d, nz), x, y, c) for d in range(1, nz)]


class Gather:
    def __init__(self, nz, src, full, send, recv, local):
        self.nz, self.src, self.full, self.send, self.recv, self.local = nz, src, full, send, recv, local
        self.depth = src.shape[0]
        self.index = {}
        for kind in ("Z", "X", "Y", "S", "YA", "XB", "SX", "SY", "SA", "SB"):
            for d in range(1 if kind == "Z" else 0, nz):
                self.index[kind, d] = len(self.index)

    @staticmethod
    def count(nz):
        return nz - 1 + 9 * nz

    def block(self, z, x, y, c, half=None):
        first, size = (0, self.depth) if half is None else (half * self.depth // 2, self.depth // 2)
        return self.full.at[2 * y + c, pl.ds(pl.multiple_of((2 * z + x) * self.depth + first, 16), size)]

    def message(self, kind, d, sending):
        z, x, y, c = place()
        nz = self.nz
        back = z if d == 0 else lax.rem(z - d + nz, nz)
        ahead = lax.rem(z + d, nz)
        sx, sy, sib = device(z, 1 - x, y, c), device(z, x, 1 - y, c), device(z, x, y, 1 - c)
        sent, got, half, target = {
            "Z": ((z, x, y, c), (back, x, y, c), None, device(ahead, x, y, c)),
            "X": ((back, x, y, c), (back, 1 - x, y, c), None, sx),
            "Y": ((back, x, y, c), (back, x, 1 - y, c), None, sy),
            "S": ((back, x, y, c), (back, x, y, 1 - c), None, sib),
            "YA": ((back, 1 - x, y, c), (back, 1 - x, 1 - y, c), 0, sy),
            "XB": ((back, x, 1 - y, c), (back, 1 - x, 1 - y, c), 1, sx),
            "SX": ((back, 1 - x, y, c), (back, 1 - x, y, 1 - c), None, sib),
            "SY": ((back, x, 1 - y, c), (back, x, 1 - y, 1 - c), None, sib),
            "SA": ((back, 1 - x, 1 - y, c), (back, 1 - x, 1 - y, 1 - c), 0, sib),
            "SB": ((back, 1 - x, 1 - y, c), (back, 1 - x, 1 - y, 1 - c), 1, sib),
        }[kind]
        i = self.index[kind, d]
        at = self.block(*(sent if sending else got), half)
        own = sending and (kind == "Z" or (d == 0 and kind in ("X", "Y", "S")))
        return remote(self.src if own else at, at, self.send.at[i], self.recv.at[i], target)

    def start(self, kind, d):
        self.message(kind, d, True).start()

    def arrived(self, kind, d):
        self.message(kind, d, False).wait_recv()

    def own(self):
        z, x, y, c = place()
        return pltpu.make_async_copy(self.src, self.block(z, x, y, c), self.local)

    def begin(self):
        for d in range(1, self.nz):
            self.start("Z", d)
        for kind in ("X", "Y", "S"):
            self.start(kind, 0)
        self.own().start()

    def along(self, d):
        self.arrived("Z", d)
        for kind in ("X", "Y", "S"):
            self.start(kind, d)

    def over(self, d):
        self.arrived("X", d)
        self.start("YA", d)
        self.start("SX", d)
        self.arrived("Y", d)
        self.start("XB", d)
        self.start("SY", d)

    def corner(self, d):
        self.arrived("YA", d)
        self.start("SA", d)
        self.arrived("XB", d)
        self.start("SB", d)

    def end(self):
        self.own().wait()
        for d in range(self.nz):
            for kind in ("S", "SX", "SY", "SA", "SB"):
                self.arrived(kind, d)
        for kind, d in self.index:
            self.message(kind, d, True).wait_send()

    def order(self):
        nz = self.nz
        near = sorted(range(1, nz), key=lambda d: min(d, nz - d))
        steps = [functools.partial(self.begin)]
        for d in [0] + near:
            if d:
                steps.append(functools.partial(self.along, d))
            steps.append(functools.partial(self.over, d))
        for d in [0] + near:
            steps.append(functools.partial(self.corner, d))
        return steps + [self.end]


class Share:
    def __init__(self, src, full, send, recv, local, pieces=1):
        self.src, self.full, self.send, self.recv, self.local, self.pieces = src, full, send, recv, local, pieces
        self.size = src.shape[0] // pieces

    @staticmethod
    def sems(pieces):
        dma = pltpu.SemaphoreType.DMA
        return [dma((3 * pieces,)), dma((3 * pieces,)), dma((pieces,))]

    def rows(self, y, c, i):
        own = self.size * self.pieces
        return pl.ds(pl.multiple_of((2 * y + c) * own + i * self.size, 16), self.size)

    def message(self, kind, i):
        z, x, y, c = place()
        n = self.pieces
        piece = self.src.at[pl.ds(i * self.size, self.size)]
        if kind == "own":
            return pltpu.make_async_copy(piece, self.full.at[self.rows(y, c, i)], self.local.at[i])
        k = {"Y": 0, "C": 1, "F": 2}[kind] * n + i
        sems = self.send.at[k], self.recv.at[k]
        sib = device(z, x, y, 1 - c)
        if kind == "Y":
            return remote(piece, self.full.at[self.rows(y, c, i)], *sems, device(z, x, 1 - y, c))
        if kind == "C":
            return remote(piece, self.full.at[self.rows(y, c, i)], *sems, sib)
        at = self.full.at[self.rows(1 - y, c, i)]
        return remote(at, at, *sems, sib)

    def begin(self, i):
        for kind in ("Y", "C", "own"):
            self.message(kind, i).start()

    def on(self, i):
        self.message("Y", i).wait_recv()
        self.message("F", i).start()

    def end(self):
        for i in range(self.pieces):
            self.message("own", i).wait()
            self.message("C", i).wait_recv()
            self.message("F", i).wait_recv()
            for kind in ("Y", "C", "F"):
                self.message(kind, i).wait_send()


def finish(tokens, gain, cot, middle_cot):
    hat, inv_sigma = normalize(tokens.T.astype(F32))
    d = cot * gain
    made = middle_cot + inv_sigma * (
        d - jnp.mean(d, axis=0, keepdims=True) - hat * jnp.mean(d * hat, axis=0, keepdims=True)
    )
    return made.T.astype(BF16)


class Scatter:
    def __init__(self, nz, ups, src, part, out, core, side, line, last, send, recv, shared=None):
        self.nz, self.ups, self.src, self.part, self.out, self.shared = nz, ups, src, part, out, shared
        self.core, self.side, self.line, self.last, self.send, self.recv = core, side, line, last, send, recv
        self.depth = out.shape[0]

    @staticmethod
    def scratch(nz, ups, depth, columns):
        count = len(ups) * nz + 2 * nz
        return [
            pltpu.VMEM((len(ups), 2 * nz * depth, columns), BF16),
            pltpu.VMEM((len(ups), nz * depth, columns), BF16),
            pltpu.VMEM((nz, len(ups), depth, columns), BF16),
            pltpu.VMEM((depth, columns), BF16),
            pltpu.SemaphoreType.DMA((count,)),
            pltpu.SemaphoreType.DMA((count,)),
        ]

    def row(self, d):
        z, _, _, _ = place()
        return z if d == 0 else lax.rem(z + d, self.nz)

    def rows(self, d, x):
        return pl.ds(pl.multiple_of((2 * self.row(d) + x) * self.depth, 16), self.depth)

    def both(self, d):
        return pl.ds(pl.multiple_of(2 * self.row(d) * self.depth, 16), 2 * self.depth)

    def lane(self, d):
        return pl.ds(pl.multiple_of(self.row(d) * self.depth, 16), self.depth)

    def message(self, kind, d, u=0):
        z, x, y, c = place()
        nz, n = self.nz, len(self.ups)
        i = {"C": u * nz + d, "X": n * nz + d, "Z": n * nz + nz + d, "Y": n * nz + nz}[kind]
        sems = self.send.at[i], self.recv.at[i]
        if kind == "C":
            both = self.both(d)
            return remote(self.src.at[2 * self.ups[u] + 1 - c, both], self.core.at[u, both], *sems, device(z, x, y, 1 - c))
        if kind == "X":
            return remote(
                self.core.at[:, self.rows(d, 1 - x)], self.side.at[:, self.lane(d)], *sems, device(z, 1 - x, y, c)
            )
        if kind == "Z":
            return remote(self.side.at[:, self.lane(d)], self.line.at[d], *sems, device(self.row(d), x, y, c))
        return remote(self.line.at[0, 1 - y if n == 2 else 0], self.last, *sems, device(z, x, 1 - y, c))

    def far(self):
        return [*range(1, self.nz), 0]

    def begin(self):
        for d in self.far():
            for u in range(len(self.ups)):
                self.message("C", d, u).start()

    def chip(self, d):
        _, x, _, c = place()
        for u in range(len(self.ups)):
            self.message("C", d, u).wait_recv()
        for near in (False, True):
            rows = self.rows(d, x if near else 1 - x)
            for u, up in enumerate(self.ups):
                made = self.part[2 * up + c, rows].astype(F32) + self.core[u, rows].astype(F32)
                self.core[u, rows] = made.astype(BF16)
            if not near:
                self.message("X", d).start()

    def over(self, d):
        _, x, _, _ = place()
        self.message("X", d).wait_recv()
        rows, lane = self.rows(d, x), self.lane(d)
        for u in range(len(self.ups)):
            made = self.core[u, rows].astype(F32) + self.side[u, lane].astype(F32)
            self.side[u, lane] = made.astype(BF16)
        if d:
            self.message("Z", d).start()

    def along(self):
        _, _, y, _ = place()
        for d in range(1, self.nz):
            self.message("Z", d).wait_recv()
        lane = self.lane(0)
        for u in range(len(self.ups)):
            made = self.side[u, lane].astype(F32)
            for d in range(1, self.nz):
                made += self.line[d, u].astype(F32)
            self.line[0, u] = made.astype(BF16)
        if len(self.ups) == 2 or self.shared:
            self.message("Y", 0).start()
        else:
            pl.when(y != self.ups[0])(lambda: self.message("Y", 0).start())

    def end(self):
        _, _, y, _ = place()

        def receive():
            self.message("Y", 0).wait_recv()
            mine = self.line[0, y if len(self.ups) == 2 else 0]
            self.out[...] = mine.astype(F32) + self.last[...].astype(F32)

        if len(self.ups) == 2:
            receive()
            self.message("Y", 0).wait_send()
        elif self.shared:
            pl.when(y == self.ups[0])(receive)

            @pl.when(y != self.ups[0])
            def _():
                self.message("Y", 0).wait_recv()
                self.out[:, self.shared :] = self.line[0, 0, :, self.shared :].astype(F32) + self.last[
                    :, self.shared :
                ].astype(F32)

            self.message("Y", 0).wait_send()
        else:
            pl.when(y == self.ups[0])(receive)
            pl.when(y != self.ups[0])(lambda: self.message("Y", 0).wait_send())
        for d in range(self.nz):
            for u in range(len(self.ups)):
                self.message("C", d, u).wait_send()
            self.message("X", d).wait_send()
            if d:
                self.message("Z", d).wait_send()

    def order(self):
        return (
            [self.begin]
            + [functools.partial(self.chip, d) for d in self.far()]
            + [functools.partial(self.over, d) for d in self.far()]
            + [self.along, self.end]
        )


class Fold:
    def __init__(self, part, near, far, send, recv):
        self.part, self.near, self.far, self.send, self.recv = part, near, far, send, recv
        self.slots = part.shape[0]

    @staticmethod
    def scratch(n_mp, own, slots):
        dma = pltpu.SemaphoreType.DMA
        return [
            pltpu.VMEM((slots, n_mp, 2 * HDIM, own), BF16),
            pltpu.VMEM((slots, 2, 2 * HDIM, own), BF16),
            pltpu.VMEM((slots, 2 * HDIM, own), BF16),
            dma((slots, 3)),
            dma((slots, 3)),
        ]

    def message(self, kind, head):
        z, x, y, c = place()
        slot = lax.rem(head, self.slots)
        k = {"far": 0, "near": 1, "Y": 2}[kind]
        sems = self.send.at[slot, k], self.recv.at[slot, k]
        if kind == "Y":
            return remote(self.near.at[slot, 1 - y], self.far.at[slot], *sems, device(z, x, 1 - y, c))
        up = 1 - y if kind == "far" else y
        return remote(self.part.at[slot, 2 * up + 1 - c], self.near.at[slot, up], *sems, device(z, x, y, 1 - c))

    def begin(self, head):
        self.message("far", head).start()
        self.message("near", head).start()

    def chip(self, head):
        _, _, y, c = place()
        slot = lax.rem(head, self.slots)
        self.message("far", head).wait_recv()
        made = self.part[slot, 2 * (1 - y) + c].astype(F32) + self.near[slot, 1 - y].astype(F32)
        self.near[slot, 1 - y] = made.astype(BF16)
        self.message("Y", head).start()

    def end(self, head):
        _, _, y, c = place()
        slot = lax.rem(head, self.slots)
        self.message("near", head).wait_recv()
        self.message("Y", head).wait_recv()
        made = self.part[slot, 2 * y + c].astype(F32) + self.near[slot, y].astype(F32) + self.far[slot].astype(F32)
        for kind in ("far", "near", "Y"):
            self.message(kind, head).wait_send()
        return made.astype(BF16)


def project(w_ref, part, n1_ref, cos_ref, sin_ref, mine, q_ref, k_ref, v_ref):
    width, own = q_ref.shape
    heads = width // HDIM

    def some(i, carry):
        at = pl.ds(pl.multiple_of(i * own, own), own)
        made = dot(w_ref[part, :, width : 3 * width], n1_ref[:, at], TN)
        k_ref[:, at] = turn(made[:width], cos_ref[:, at], sin_ref[:, at], heads).astype(BF16)
        v_ref[:, at] = made[width:].astype(BF16)
        return carry

    lax.fori_loop(0, n1_ref.shape[1] // own, some, 0)
    made = dot(w_ref[part, :, :width], n1_ref[:, mine], TN) * (SCALE * LOG2E)
    q_ref[...] = turn(made, cos_ref[:, mine], sin_ref[:, mine], heads).astype(BF16)


def forward_kernel(nz, len_ref, tok_ref, *refs):
    linked = nz > 0
    given, refs = refs[: 6 if linked else 1], refs[6 if linked else 1 :]
    mine_ref, q_ref, k_ref, v_ref, cos_ref, sin_ref, o_ref, p_ref, inv_ref = refs[:9]
    full_refs, refs = refs[9 : 11 if linked else 9], refs[11 if linked else 9 :]
    w_ref, n1_ref, ka_ref, qa_ref, va_ref, load = refs[:6]
    refs = refs[6:]
    rows, features = tok_ref.shape
    own = q_ref.shape[1]
    docs = len_ref.shape[1]
    width = q_ref.shape[0]
    per = width // HDIM
    step = pl.program_id(0)
    me = lax.axis_index("mp")
    mine = pl.ds(pl.multiple_of(me * own, own), own)

    if linked:
        src_a, src_b = refs[:2]
        one = Gather(nz, src_a, w_ref, *refs[2:5])
        two = Gather(nz, src_b, full_refs[1], *refs[5:8])
        keep = pltpu.make_async_copy(w_ref, full_refs[0], load)

    @pl.when(step == 0)
    def _():
        if linked:
            wq_ref, wg_ref, wo_ref, wd_ref, one_ref, two_ref = given
            for i in range(3):
                src_a[:, i * width : (i + 1) * width] = wq_ref[i]
            src_a[:, 3 * width :] = one_ref[...].astype(F32).T.astype(BF16)
            greet(peers(nz))
            first = one.order()
            first[0]()
            units = wd_ref.shape[0]
            pair = 2 * units
            for i in range(2):
                src_b[:, i * units : (i + 1) * units] = wg_ref[i]
            src_b[:, pair : pair + width] = wo_ref[...].T
            src_b[:, pair + width : pair + width + units] = wd_ref[...].T
            src_b[:, pair + width + units :] = two_ref[...].astype(F32).T.astype(BF16)
        else:
            fetch = pltpu.make_async_copy(given[0], w_ref, load)
            fetch.start()

        _, position, _ = layout_rows(len_ref, docs, 0, rows)
        power = lax.broadcasted_iota(jnp.int32, (HALF, 1), 0).astype(F32) * (-2.0 / HDIM * math.log2(ROPE_BASE))
        angle = position.astype(F32) * jnp.exp2(power)
        cos_ref[...] = jnp.cos(angle)
        sin_ref[...] = jnp.sin(angle)
        keys, _, _ = layout_rows(len_ref, docs, 0, rows)
        queries, _, _ = layout_rows(len_ref, docs, me * own, own)
        kind = lax.broadcasted_iota(jnp.int32, (AUG - HDIM, 1), 0)
        ka_ref[HDIM:] = jnp.where(kind == keys, 1.0, 0.0).astype(BF16)
        qa_ref[HDIM:] = jnp.where(kind == queries, 0.0, FAR).astype(BF16)
        va_ref[HDIM:] = jnp.ones((AUG - HDIM, rows), BF16)
        if linked:
            for act in first[1:]:
                act()
            keep.start()
            two.begin()
        else:
            fetch.wait()
        gain = w_ref[0, :, 3 * width :].astype(F32)

        def norm(i, carry):
            at = pl.ds(pl.multiple_of(i * own, own), own)
            hat, _ = normalize(tok_ref[at, :].T.astype(F32))
            n1_ref[:, at] = (hat * gain).astype(BF16)
            return carry

        lax.fori_loop(0, rows // own, norm, 0)
        mine_ref[...] = n1_ref[:, mine]

    if linked:
        acts = two.order()[1:]
        heads = pl.num_programs(0)
        for at, act in zip(spread(len(acts), 12), acts):
            pl.when(step == at)(act)

    @pl.when(lax.rem(step, per) == 0)
    def _():
        project(w_ref, step // per, n1_ref, cos_ref, sin_ref, mine, q_ref, k_ref, v_ref)

    head = pl.ds(pl.multiple_of(lax.rem(step, per) * HDIM, HDIM), HDIM)
    ka_ref[:HDIM] = k_ref[head]
    qa_ref[:HDIM] = q_ref[head]
    va_ref[:HDIM] = v_ref[head]
    wide = 256
    for i in range(own // wide):
        at = slice(i * wide, (i + 1) * wide)
        scores = dot(ka_ref[...], qa_ref[:, at], TN)
        top = jnp.max(scores, axis=0, keepdims=True)
        probs = jnp.exp2(scores - top).astype(BF16)
        p_ref[0, :, at] = probs
        out = dot(va_ref[...], probs, NN)
        inv = 1.0 / out[HDIM : HDIM + 1]
        o_ref[:, at] = (out[:HDIM] * inv).astype(BF16)
        inv_ref[0, :, at] = inv
    if linked:

        @pl.when(step == pl.num_programs(0) - 1)
        def _():
            keep.wait()


def spread(count, steps):
    return [min(steps - 1, 1 + i * (steps - 1) // count) for i in range(count)]


def forward(nz, n_mp, lengths, tokens, weights, columns):
    rows, features = tokens.shape
    own, width, heads = rows // n_mp, features // n_mp, features // HDIM
    per = width // HDIM
    linked = nz > 0
    hbm = pl.BlockSpec(memory_space=pl.ANY)
    part = lambda h: (h // per, 0)
    vm = pl.BlockSpec(memory_space=pltpu.VMEM)
    n = Gather.count(nz) if linked else 0
    dma = pltpu.SemaphoreType.DMA
    depth = features // (2 * nz) if linked else 0
    full_shapes = [jax.ShapeDtypeStruct((n_mp, features, c), BF16) for c in columns] if linked else []
    return pl.pallas_call(
        functools.partial(forward_kernel, nz),
        grid=(heads,),
        in_specs=[pl.BlockSpec(memory_space=pltpu.SMEM), vm] + ([vm] * 6 if linked else [hbm]),
        out_specs=[
            whole(features, own),
            pl.BlockSpec((width, own), part),
            pl.BlockSpec((width, rows), part),
            pl.BlockSpec((width, rows), part),
            whole(HALF, rows),
            whole(HALF, rows),
            pl.BlockSpec((HDIM, own), lambda h: (h, 0)),
            pl.BlockSpec((1, rows, own), lambda h: (h, 0, 0)),
            pl.BlockSpec((1, 1, own), lambda h: (h, 0, 0)),
        ]
        + [hbm] * len(full_shapes),
        out_shape=[
            jax.ShapeDtypeStruct((features, own), BF16),
            jax.ShapeDtypeStruct((features, own), BF16),
            jax.ShapeDtypeStruct((features, rows), BF16),
            jax.ShapeDtypeStruct((features, rows), BF16),
            jax.ShapeDtypeStruct((HALF, rows), F32),
            jax.ShapeDtypeStruct((HALF, rows), F32),
            jax.ShapeDtypeStruct((features, own), BF16),
            jax.ShapeDtypeStruct((heads, rows, own), BF16),
            jax.ShapeDtypeStruct((heads, 1, own), F32),
        ]
        + full_shapes,
        scratch_shapes=[
            pltpu.VMEM((n_mp, features, columns[0]), BF16),
            pltpu.VMEM((features, rows), BF16),
            pltpu.VMEM((AUG, rows), BF16),
            pltpu.VMEM((AUG, own), BF16),
            pltpu.VMEM((AUG, rows), BF16),
            dma,
        ]
        + (
            [pltpu.VMEM((depth, c), BF16) for c in columns] + [dma((n,)), dma((n,)), dma] * 2
            if linked
            else []
        ),
        compiler_params=pltpu.CompilerParams(
            dimension_semantics=("arbitrary",),
            vmem_limit_bytes=VMEM_BYTES,
            **({"collective_id": 1, "has_side_effects": True} if linked else {}),
        ),
        name="forward",
    )(lengths, tokens, *weights)


def mid_kernel(
    linked, units, len_ref, tok_hbm, cot_hbm, heads_ref, inv_ref, w_hbm,
    out_ref, mcot_ref, do_ref, g_ref, tok_ref, cot_ref, w_ref, load, *share,
):
    own, features = tok_ref.shape
    me = lax.axis_index("mp")
    mine = pl.ds(pl.multiple_of(me * own, own), own)
    loads = [
        pltpu.make_async_copy(tok_hbm.at[mine], tok_ref, load.at[0]),
        pltpu.make_async_copy(cot_hbm.at[mine], cot_ref, load.at[1]),
        pltpu.make_async_copy(w_hbm, w_ref, load.at[2]),
    ]
    for copy in loads:
        copy.start()
    if linked:
        out_own = share[0]
        share = Share(out_own, out_ref, *share[1:])
        greet(peers(1))
    else:
        out_own = out_ref
    parts = w_ref.shape[0]
    width = features // parts
    heads = width // HDIM
    pair = 2 * units
    _, _, live = layout_rows(len_ref, len_ref.shape[1], me * own, own)
    for copy in loads:
        copy.wait()

    def w_gu(m):
        return w_ref[m, :, :pair]

    def w_out(m):
        return w_ref[m, :, pair : pair + width]

    def w_down(m):
        return w_ref[m, :, pair + width : pair + width + units]

    total = dot(w_out(0), heads_ref[:width], NN)
    for m in range(1, parts):
        total += dot(w_out(m), heads_ref[m * width : (m + 1) * width], NN)
    middle = tok_ref[...].T.astype(F32) + total
    gain = w_ref[0, :, pair + width + units :].astype(F32)
    hat, inv_sigma = normalize(middle)
    normed = (hat * gain).astype(BF16)
    branch = jnp.where(live, cot_ref[...].T.astype(F32), 0.0).astype(BF16)
    total = middle
    back = jnp.zeros((features, own), F32)
    kept = []
    for m in range(parts):
        gate_up = dot(w_gu(m), normed, TN)
        gate, up = gate_up[:units], gate_up[units:]
        phi, slope = gelu_parts(gate)
        act = gate * phi
        hidden = (act * up).astype(BF16)
        total += dot(w_down(m), hidden, NN)
        kept.append((hidden, up * (phi + slope), act))
    out_own[...] = total.astype(BF16).T
    if linked:
        share.begin(0)
    for m in range(parts):
        hidden, one, two = kept[m]
        hidden_cot = dot(w_down(m), branch, TN)
        g_ref[m, :, pair + width : pair + width + units] = dot(branch, hidden, NT).astype(BF16)
        cots = jnp.concatenate([hidden_cot * one, hidden_cot * two], axis=0).astype(BF16)
        g_ref[m, :, :pair] = dot(normed, cots, NT).astype(BF16)
        back += dot(w_gu(m), cots, NN)
    gain_cot = jnp.sum(back * hat, axis=1, keepdims=True).astype(BF16)
    d = back * gain
    middle_cot = branch.astype(F32) + inv_sigma * (
        d - jnp.mean(d, axis=0, keepdims=True) - hat * jnp.mean(d * hat, axis=0, keepdims=True)
    )
    mcot_ref[...] = middle_cot
    attn_cot = middle_cot.astype(BF16)
    for m in range(parts):
        g_ref[m, :, pair + width + units :] = gain_cot
        part = heads_ref[m * width : (m + 1) * width]
        g_ref[m, :, pair : pair + width] = dot(attn_cot, part, NT).astype(BF16)
        back_heads = dot(w_out(m), attn_cot, TN)
        for h in range(heads):
            head = m * heads + h
            rows = slice(h * HDIM, (h + 1) * HDIM)
            cot = back_heads[rows] * inv_ref[head]
            inner = jnp.sum(cot * part[rows].astype(F32), axis=0, keepdims=True)
            high = inner.astype(BF16).astype(F32)
            pad = jnp.zeros((AUG - HDIM - 2, own), F32)
            do_ref[head] = jnp.concatenate([cot, high, inner - high, pad], axis=0).astype(BF16)
    if linked:
        share.on(0)
        share.end()


def mid(linked, n_mp, lengths, tokens, out_grad, heads_out, inv, w_rest, units):
    features, own = heads_out.shape
    heads = inv.shape[0]
    vm = pl.BlockSpec(memory_space=pltpu.VMEM)
    hbm = pl.BlockSpec(memory_space=pl.ANY)
    return pl.pallas_call(
        functools.partial(mid_kernel, linked, units),
        in_specs=[pl.BlockSpec(memory_space=pltpu.SMEM), hbm, hbm, vm, vm, hbm],
        out_specs=[hbm if linked else vm] + [vm] * 3,
        out_shape=[
            jax.ShapeDtypeStruct((own * n_mp if linked else own, features), BF16),
            jax.ShapeDtypeStruct((features, own), F32),
            jax.ShapeDtypeStruct((heads, AUG, own), BF16),
            jax.ShapeDtypeStruct(w_rest.shape, BF16),
        ],
        scratch_shapes=[
            pltpu.VMEM((own, features), BF16),
            pltpu.VMEM((own, features), BF16),
            pltpu.VMEM(w_rest.shape, BF16),
            pltpu.SemaphoreType.DMA((3,)),
        ]
        + ([pltpu.VMEM((own, features), BF16)] + Share.sems(1) if linked else []),
        compiler_params=pltpu.CompilerParams(
            vmem_limit_bytes=VMEM_BYTES, **({"collective_id": 2, "has_side_effects": True} if linked else {})
        ),
        name="mid",
    )(lengths, tokens, out_grad, heads_out, inv, w_rest)


SLOTS = 4


def backward_kernel(nz, *refs):
    q_ref, k_ref, v_ref, do_ref, p_ref, cos_ref, sin_ref, n1_ref, mcot_ref, tok_hbm, w_hbm, gr_hbm = refs[:12]
    dq_ref, dr_ref, in_full = refs[12:15]
    w_ref, gr_ref, gq_ref, pc_ref, acc_ref, gc_ref, va_ref, tok_ref, in_own, load = refs[15:25]
    refs = refs[25:]
    rest = Scatter(nz, (0, 1), gr_hbm, gr_ref, dr_ref, *refs[:6])
    low = Scatter(nz, (0,), gq_ref, gq_ref, dq_ref, *refs[6:12])
    high = Scatter(nz, (1,), gq_ref, gq_ref, dq_ref, *refs[12:18], shared=gq_ref.shape[2] - 1)
    fold = Fold(*refs[18:23])
    share = Share(in_own, in_full, *refs[23:26])
    step, heads = pl.program_id(0), pl.num_programs(0)
    parts = w_ref.shape[0]
    features, own = n1_ref.shape
    rows = k_ref.shape[1]
    width = features // parts
    per = width // HDIM
    me = lax.axis_index("mp")
    mine = pl.ds(pl.multiple_of(me * own, own), own)
    loads = [
        pltpu.make_async_copy(w_hbm, w_ref, load.at[0]),
        pltpu.make_async_copy(gr_hbm, gr_ref, load.at[1]),
        pltpu.make_async_copy(tok_hbm.at[mine], tok_ref, load.at[2]),
    ]

    @pl.when(step == 0)
    def _():
        for copy in loads:
            copy.start()
        greet(peers(nz))
        rest.begin()
        va_ref[HDIM:] = jnp.full((AUG - HDIM, rows), -1.0, BF16)
        acc_ref[...] = jnp.zeros_like(acc_ref)
        gc_ref[...] = jnp.zeros_like(gc_ref)
        for m in range(2):
            gq_ref[m, :, 3 * width :] = jnp.zeros((features, 1), BF16)

    @pl.when(step == 1)
    def _():
        for copy in loads:
            copy.wait()

    def collect(head):
        made = fold.end(head)
        at = lax.rem(head, per) * HDIM
        pc_ref[pl.ds(pl.multiple_of(width + at, HDIM), HDIM)] = made[:HDIM]
        pc_ref[pl.ds(pl.multiple_of(2 * width + at, HDIM), HDIM)] = made[HDIM:]

    def close(part):
        for i in range(per):
            pc_ref[i * HDIM : (i + 1) * HDIM] = qc_ref[lax.rem(part, 2), i * HDIM : (i + 1) * HDIM]
        made = dot(n1_ref[...], pc_ref[...], NT)
        gq_ref[part, :, : 3 * width] = made.astype(BF16)
        weights = w_ref[part, :, : 3 * width]
        gc_ref[...] += jnp.sum(made * weights.astype(F32), axis=1, keepdims=True)
        acc_ref[...] += dot(weights, pc_ref[...], NN)

    qc_ref = refs[26]
    acts = rest.order()[1:]
    for at, act in zip(REST_STEPS, acts):
        pl.when(step == at)(act)

    va_ref[:HDIM] = v_ref[...]
    cot = dot(va_ref[...], do_ref[0], TN)
    probs = p_ref[0]
    score_cot = probs * cot.astype(BF16)
    dv = dot(do_ref[0, :HDIM], probs, NT).astype(BF16)
    dk = turn(dot(q_ref[...], score_cot, NT) * LN2, cos_ref[...], sin_ref[...], 1, True).astype(BF16)
    dq = turn(dot(k_ref[...], score_cot, NN) * SCALE, cos_ref[:, mine], sin_ref[:, mine], 1, True)
    slot = lax.rem(step, SLOTS)
    for m in range(parts):
        fold.part[slot, m, :HDIM] = dk[:, m * own : (m + 1) * own]
        fold.part[slot, m, HDIM:] = dv[:, m * own : (m + 1) * own]
    at = pl.ds(pl.multiple_of(lax.rem(step, per) * HDIM, HDIM), HDIM)
    qc_ref[lax.rem(step // per, 2), at] = dq.astype(BF16)

    @pl.when(step >= 2)
    def _():
        collect(step - 2)

    @pl.when(step >= 1)
    def _():
        fold.chip(step - 1)

    fold.begin(step)

    @pl.when((step >= per + 1) & (lax.rem(step - 2, per) == per - 1))
    def _():
        close((step - 2) // per)

    @pl.when(step == LOW_STEP)
    def _():
        low.begin()

    for at, act in zip(LOW_STEPS, low.order()[1:]):
        pl.when(step == at)(act)

    @pl.when(step == heads - 1)
    def _():
        collect(step - 1)
        fold.chip(step)
        for act in acts[len(REST_STEPS) :]:
            act()
        collect(step)
        close(parts - 1)
        gain = w_ref[0, :, 3 * width :].astype(F32)
        gain_cot = (gc_ref[...] / gain).astype(BF16)
        for m in range(2, parts):
            gq_ref[m, :, 3 * width :] = gain_cot
        high.begin()
        in_own[...] = finish(tok_ref[...], gain, acc_ref[...], mcot_ref[...])
        share.begin(0)
        acts_high = high.order()[1:]
        for act in low.order()[1 + len(LOW_STEPS) :]:
            act()
        for act in acts_high:
            act()
        share.on(0)
        share.end()


REST_STEPS = (1, 1, 2, 2, 5, 7, 9)
LOW_STEP = 8
LOW_STEPS = (9, 9, 10, 10)


def backward(nz, q, k, v, do, p, cos, sin, n1, mcot, tokens, w_qkv, g_rest):
    (features, own), rows = q.shape, k.shape[1]
    n_mp = w_qkv.shape[0]
    heads = features // HDIM
    width = features // n_mp
    depth = features // (2 * nz)
    columns = w_qkv.shape[2], g_rest.shape[2]
    hbm = pl.BlockSpec(memory_space=pl.ANY)
    vm = pl.BlockSpec(memory_space=pltpu.VMEM)
    row = lambda h: (h, 0)
    cube = lambda h: (h, 0, 0)
    return pl.pallas_call(
        functools.partial(backward_kernel, nz),
        grid=(heads,),
        in_specs=[
            pl.BlockSpec((HDIM, own), row),
            pl.BlockSpec((HDIM, rows), row),
            pl.BlockSpec((HDIM, rows), row),
            pl.BlockSpec((1, AUG, own), cube),
            pl.BlockSpec((1, rows, own), cube),
            vm,
            vm,
            vm,
            vm,
            hbm,
            hbm,
            hbm,
        ],
        out_specs=[vm, vm, hbm],
        out_shape=[
            jax.ShapeDtypeStruct((depth, columns[0]), F32),
            jax.ShapeDtypeStruct((depth, columns[1]), F32),
            jax.ShapeDtypeStruct((rows, features), BF16),
        ],
        scratch_shapes=[
            pltpu.VMEM(w_qkv.shape, BF16),
            pltpu.VMEM(g_rest.shape, BF16),
            pltpu.VMEM(w_qkv.shape, BF16),
            pltpu.VMEM((3 * width, own), BF16),
            pltpu.VMEM((features, own), F32),
            pltpu.VMEM((features, 1), F32),
            pltpu.VMEM((AUG, rows), BF16),
            pltpu.VMEM((own, features), BF16),
            pltpu.VMEM((own, features), BF16),
            pltpu.SemaphoreType.DMA((3,)),
        ]
        + Scatter.scratch(nz, (0, 1), depth, columns[1])
        + Scatter.scratch(nz, (0,), depth, columns[0])
        + Scatter.scratch(nz, (1,), depth, columns[0])
        + Fold.scratch(n_mp, own, SLOTS)
        + Share.sems(1)
        + [pltpu.VMEM((2, width, own), BF16)],
        compiler_params=pltpu.CompilerParams(
            dimension_semantics=("arbitrary",), collective_id=3, has_side_effects=True, vmem_limit_bytes=VMEM_BYTES
        ),
        name="backward",
    )(q, k, v, do, p, cos, sin, n1, mcot, tokens, w_qkv, g_rest)


def deliver_kernel(units, in_ref, dq_ref, dr_ref, grad_ref, gq_ref, go_ref, gg_ref, gd_ref, one_ref, two_ref):
    grad_ref[...] = in_ref[...].astype(F32)

    @pl.when(pl.program_id(0) == 0)
    def _():
        width = go_ref.shape[0]
        pair = 2 * units
        for i in range(3):
            gq_ref[i] = dq_ref[:, i * width : (i + 1) * width]
        one_ref[...] = dq_ref[:, 3 * width :].T
        for i in range(2):
            gg_ref[i] = dr_ref[:, i * units : (i + 1) * units]
        go_ref[...] = dr_ref[:, pair : pair + width].T
        gd_ref[...] = dr_ref[:, pair + width : pair + width + units].T
        two_ref[...] = dr_ref[:, pair + width + units :].T


def deliver(input_grad, d_qkv, d_rest, width, units):
    rows, features = input_grad.shape
    depth = d_qkv.shape[0]
    shape = lambda *s: jax.ShapeDtypeStruct(s, F32)
    shapes = [(3, depth, width), (width, depth), (2, depth, units), (units, depth), (1, depth), (1, depth)]
    steps = 4
    return pl.pallas_call(
        functools.partial(deliver_kernel, units),
        grid=(steps,),
        in_specs=[pl.BlockSpec((rows // steps, features), lambda i: (i, 0)), whole(*d_qkv.shape), whole(*d_rest.shape)],
        out_specs=[pl.BlockSpec((rows // steps, features), lambda i: (i, 0))] + [whole(*s) for s in shapes],
        out_shape=[shape(rows, features)] + [shape(*s) for s in shapes],
        compiler_params=params("arbitrary"),
        name="deliver",
    )(input_grad, d_qkv, d_rest)


def per_device(n_dp, n_mp, tokens, out_grad, w_qkv, w_out, w_gu, w_down, gain_attn, gain_mlp, lengths):
    rows, features = tokens.shape
    depth = w_qkv.shape[0]
    units, width = w_down.shape[0], w_out.shape[0]
    everyone = ("mp", "dp")
    linked = n_mp == 4 and n_dp % 2 == 0 and depth % 32 == 0 and features // HDIM == 12
    nz = n_dp // 2 if linked else 0
    columns = 3 * width + 1, 3 * units + width + 1
    wq, wg = w_qkv.transpose(1, 0, 2), w_gu.transpose(1, 0, 2)
    if linked:
        weights = wq, wg, w_out, w_down, gain_attn[None], gain_mlp[None]
        n1, q, k, v, cos, sin, heads_out, probs, inv, full_qkv, full_rest = forward(
            nz, n_mp, lengths, tokens, weights, columns
        )
    else:
        shards = [
            jnp.concatenate([*wq, gain_attn[:, None]], axis=1),
            jnp.concatenate([*wg, w_out.T, w_down.T, gain_mlp[:, None]], axis=1),
        ]
        full_qkv, full_rest = (
            lax.all_gather(s, everyone, axis=0, tiled=True).reshape(n_mp, features, s.shape[1]) for s in shards
        )
        n1, q, k, v, cos, sin, heads_out, probs, inv = forward(nz, n_mp, lengths, tokens, [full_qkv], columns)
    layer_out, middle_cot, do, g_rest = mid(linked, n_mp, lengths, tokens, out_grad, heads_out, inv, full_rest, units)
    if linked:
        d_qkv, d_rest, in_full = backward(nz, q, k, v, do, probs, cos, sin, n1, middle_cot, tokens, full_qkv, g_rest)
    else:
        own = middle_cot.shape[1]
        g_qkv, nc = last(q, k, v, do, probs, cos, sin, lax.all_gather(n1, "mp", axis=1, tiled=True), full_qkv)
        gain_one = full_qkv[0, :, 3 * width :].astype(F32)
        tok = lax.dynamic_slice_in_dim(tokens, lax.axis_index("mp") * own, own, 0)
        nc_own = lax.psum_scatter(nc, "mp", scatter_dimension=0, tiled=True)[0]
        in_own = finish(tok, gain_one, nc_own.astype(F32), middle_cot)
        layer_out, in_full = (lax.all_gather(v, "mp", axis=0, tiled=True) for v in (layer_out, in_own))
        d_qkv, d_rest = (
            lax.psum_scatter(
                g.reshape(n_mp * features, -1), everyone, scatter_dimension=0, tiled=True
            ).astype(F32)
            for g in (g_qkv, g_rest)
        )
    input_grad, g_q, g_o, g_g, g_d, one, two = deliver(in_full, d_qkv, d_rest, width, units)
    if not linked:
        one, two = (lax.all_gather(g, "mp")[0] for g in (one, two))
    return layer_out, input_grad, g_q.transpose(1, 0, 2), g_o, g_g.transpose(1, 0, 2), g_d, one[0], two[0]


def solution(mesh):
    n_dp, n_mp = mesh.shape["dp"], mesh.shape["mp"]
    return jax.shard_map(
        functools.partial(per_device, n_dp, n_mp),
        mesh=mesh,
        in_specs=(
            P("dp", None),
            P("dp", None),
            P("dp", None, "mp"),
            P("mp", "dp"),
            P("dp", None, "mp"),
            P("mp", "dp"),
            P("dp"),
            P("dp"),
            P("dp", None),
        ),
        out_specs=(
            P("dp", None),
            P("dp", None),
            P("dp", None, "mp"),
            P("mp", "dp"),
            P("dp", None, "mp"),
            P("mp", "dp"),
            P("dp"),
            P("dp"),
        ),
        check_vma=False,
    )
```

```python
import functools
import math

import jax
import jax.numpy as jnp
from jax import lax
from jax.experimental import pallas as pl
from jax.experimental.pallas import tpu as pltpu
from jax.sharding import PartitionSpec as P

HDIM = 64
HALF = HDIM // 2
AUG = HDIM + 16
EPS = 1e-05
ROPE_BASE = 160000.0
LOG2E = math.log2(math.e)
LN2 = math.log(2.0)
SCALE = HDIM ** (-0.5)
FAR = -1e30
BF16 = jnp.bfloat16
F32 = jnp.float32
VMEM_BYTES = 60 << 20
NN = (((1,), (0,)), ((), ()))
NT = (((1,), (1,)), ((), ()))
TN = (((0,), (0,)), ((), ()))


def dot(a, b, dims):
    return lax.dot_general(a, b, dims, preferred_element_type=F32)


def params(*semantics):
    return pltpu.CompilerParams(
        dimension_semantics=semantics or None, vmem_limit_bytes=VMEM_BYTES
    )


def whole(*shape):
    return pl.BlockSpec(shape, lambda *i: (0,) * len(shape))


def layout_rows(len_ref, docs, first, rows):
    index = first + lax.broadcasted_iota(jnp.int32, (1, rows), 1)
    segment = jnp.zeros((1, rows), jnp.int32)
    start = jnp.zeros((1, rows), jnp.int32)
    end = jnp.int32(0)
    for j in range(docs):
        end = end + len_ref[0, j]
        past = index >= end
        segment = segment + jnp.where(past, 1, 0)
        start = jnp.where(past, jnp.maximum(start, end), start)
    return segment, index - start, index < end


def moments(columns):
    mean = jnp.mean(columns, axis=0, keepdims=True)
    centered = columns - mean
    return mean, lax.rsqrt(jnp.mean(centered * centered, axis=0, keepdims=True) + EPS)


def normalize(columns):
    mean, inv = moments(columns)
    return (columns - mean) * inv, inv


def turn(block, cos, sin, heads, back=False):
    out = []
    for h in range(heads):
        one = block[h * HDIM : h * HDIM + HALF]
        two = block[h * HDIM + HALF : (h + 1) * HDIM]
        if back:
            out += [one * cos + two * sin, two * cos - one * sin]
        else:
            out += [one * cos - two * sin, two * cos + one * sin]
    return jnp.concatenate(out, axis=0)


def gelu_parts(gate):
    phi = 0.5 * (1.0 + lax.erf(gate * math.sqrt(0.5)))
    density = jnp.exp2(gate * gate * (-0.5 * LOG2E)) * (1.0 / math.sqrt(2.0 * math.pi))
    return phi, gate * density


def last_kernel(own_axis, q_ref, k_ref, v_ref, do_ref, p_ref, cos_ref, sin_ref, n1_ref, w_ref, gq_ref, nc_ref, gc_ref, dq_ref, pc_ref, acc_ref, va_ref):
    step, head = pl.program_id(0), pl.program_id(1)
    per = pl.num_programs(1)
    features, rows = n1_ref.shape
    own = q_ref.shape[1]
    width = per * HDIM
    mine = pl.ds(pl.multiple_of(lax.axis_index(own_axis) * own, own), own)

    @pl.when((step == 0) & (head == 0))
    def _():
        va_ref[HDIM:] = jnp.full((AUG - HDIM, rows), -1.0, BF16)
        acc_ref[...] = jnp.zeros_like(acc_ref)
        gc_ref[...] = jnp.zeros_like(gc_ref)

    va_ref[:HDIM] = v_ref[...]
    cot = dot(va_ref[...], do_ref[0], TN)
    probs = p_ref[0]
    score_cot = probs * cot.astype(BF16)
    at = pl.ds(pl.multiple_of(head * HDIM, HDIM), HDIM)
    dv = dot(do_ref[0, :HDIM], probs, NT)
    dk = dot(q_ref[...], score_cot, NT) * LN2
    dq = dot(k_ref[...], score_cot, NN) * SCALE
    pc_ref[pl.ds(pl.multiple_of(width + head * HDIM, HDIM), HDIM)] = dv.astype(BF16)
    pc_ref[at] = turn(dk, cos_ref[...], sin_ref[...], 1, True).astype(BF16)
    dq_ref[at] = turn(dq, cos_ref[:, mine], sin_ref[:, mine], 1, True).astype(BF16)

    @pl.when(head == per - 1)
    def _():
        kv = dot(n1_ref[...], pc_ref[...], NT)
        q = dot(n1_ref[:, mine], dq_ref[...], NT)
        gq_ref[step, :, :width] = q.astype(BF16)
        gq_ref[step, :, width : 3 * width] = kv.astype(BF16)
        gc_ref[...] += jnp.sum(q * w_ref[0, :, :width].astype(F32), axis=1, keepdims=True) + jnp.sum(
            kv * w_ref[0, :, width : 3 * width].astype(F32), axis=1, keepdims=True
        )

        def spread(i, carry):
            cols = pl.ds(pl.multiple_of(i * own, own), own)
            acc_ref[:, cols] += dot(w_ref[0, :, width : 3 * width], pc_ref[:, cols], NN)
            return carry

        lax.fori_loop(0, rows // own, spread, 0)
        acc_ref[:, mine] += dot(w_ref[0, :, :width], dq_ref[...], NN)

    @pl.when((step == pl.num_programs(0) - 1) & (head == per - 1))
    def _():
        gain_cot = (gc_ref[...] / w_ref[0, :, 3 * width :].astype(F32)).astype(BF16)
        for m in range(gq_ref.shape[0]):
            nc_ref[m] = acc_ref[:, m * own : (m + 1) * own].astype(BF16)
            gq_ref[m, :, 3 * width :] = gain_cot


def last(q, k, v, do, p, cos, sin, n1, w_qkv, own_axis="mp"):
    (features, own), rows = q.shape, k.shape[1]
    parts = w_qkv.shape[0]
    per = features // parts // HDIM
    width = per * HDIM
    head = lambda m, h: (m * per + h, 0)
    return pl.pallas_call(
        functools.partial(last_kernel, own_axis),
        grid=(parts, per),
        in_specs=[
            pl.BlockSpec((HDIM, own), head),
            pl.BlockSpec((HDIM, rows), head),
            pl.BlockSpec((HDIM, rows), head),
            pl.BlockSpec((1, AUG, own), lambda m, h: (m * per + h, 0, 0)),
            pl.BlockSpec((1, rows, own), lambda m, h: (m * per + h, 0, 0)),
            whole(HALF, rows),
            whole(HALF, rows),
            whole(features, rows),
            pl.BlockSpec((1,) + w_qkv.shape[1:], lambda m, h: (m, 0, 0)),
        ],
        out_specs=[
            whole(*w_qkv.shape),
            whole(parts, features, own),
        ],
        out_shape=[
            jax.ShapeDtypeStruct(w_qkv.shape, BF16),
            jax.ShapeDtypeStruct((parts, features, own), BF16),
        ],
        scratch_shapes=[
            pltpu.VMEM((features, 1), F32),
            pltpu.VMEM((width, own), BF16),
            pltpu.VMEM((2 * width, rows), BF16),
            pltpu.VMEM((features, rows), F32),
            pltpu.VMEM((AUG, rows), BF16),
        ],
        compiler_params=params("arbitrary", "arbitrary"),
        name="last",
    )(q, k, v, do, p, cos, sin, n1, w_qkv)


def place():
    dp, mp = lax.axis_index("dp"), lax.axis_index("mp")
    return dp // 2, lax.rem(dp, 2), mp // 2, lax.rem(mp, 2)


def device(z, x, y, c):
    return (2 * z + x, 2 * y + c)


def remote(src, dst, send, recv, target):
    return pltpu.make_async_remote_copy(
        src_ref=src, dst_ref=dst, send_sem=send, recv_sem=recv,
        device_id=target, device_id_type=pl.DeviceIdType.MESH,
    )


def greet(targets):
    barrier = pltpu.get_barrier_semaphore()
    for target in targets:
        pl.semaphore_signal(barrier, inc=1, device_id=target, device_id_type=pl.DeviceIdType.MESH)
    pl.semaphore_wait(barrier, len(targets))


def peers(nz):
    z, x, y, c = place()
    across = [device(z, 1 - x, y, c), device(z, x, 1 - y, c), device(z, x, y, 1 - c)]
    return across + [device(lax.bitwise_xor(z, d), x, y, c) for d in range(1, nz)]


class Gather:
    def __init__(self, nz, src, full, send, recv, local):
        self.nz, self.src, self.full, self.send, self.recv, self.local = nz, src, full, send, recv, local
        self.depth = src.shape[0]
        self.index = {}
        for kind in ("Z", "X", "Y", "S", "YA", "XB", "SX", "SY", "SA", "SB"):
            for d in range(1 if kind == "Z" else 0, nz):
                self.index[kind, d] = len(self.index)

    @staticmethod
    def count(nz):
        return nz - 1 + 9 * nz

    def block(self, z, x, y, c, half=None):
        first, size = (0, self.depth) if half is None else (half * self.depth // 2, self.depth // 2)
        return self.full.at[2 * y + c, pl.ds(pl.multiple_of((2 * z + x) * self.depth + first, 16), size)]

    def message(self, kind, d, sending):
        z, x, y, c = place()
        back = lax.bitwise_xor(z, d)
        sx, sy, sib = device(z, 1 - x, y, c), device(z, x, 1 - y, c), device(z, x, y, 1 - c)
        sent, got, half, target = {
            "Z": ((z, x, y, c), (back, x, y, c), None, device(back, x, y, c)),
            "X": ((back, x, y, c), (back, 1 - x, y, c), None, sx),
            "Y": ((back, x, y, c), (back, x, 1 - y, c), None, sy),
            "S": ((back, x, y, c), (back, x, y, 1 - c), None, sib),
            "YA": ((back, 1 - x, y, c), (back, 1 - x, 1 - y, c), 0, sy),
            "XB": ((back, x, 1 - y, c), (back, 1 - x, 1 - y, c), 1, sx),
            "SX": ((back, 1 - x, y, c), (back, 1 - x, y, 1 - c), None, sib),
            "SY": ((back, x, 1 - y, c), (back, x, 1 - y, 1 - c), None, sib),
            "SA": ((back, 1 - x, 1 - y, c), (back, 1 - x, 1 - y, 1 - c), 0, sib),
            "SB": ((back, 1 - x, 1 - y, c), (back, 1 - x, 1 - y, 1 - c), 1, sib),
        }[kind]
        i = self.index[kind, d]
        at = self.block(*(sent if sending else got), half)
        own = sending and (kind == "Z" or (d == 0 and kind in ("X", "Y", "S")))
        return remote(self.src if own else at, at, self.send.at[i], self.recv.at[i], target)

    def start(self, kind, d):
        self.message(kind, d, True).start()

    def arrived(self, kind, d):
        self.message(kind, d, False).wait_recv()

    def own(self):
        z, x, y, c = place()
        return pltpu.make_async_copy(self.src, self.block(z, x, y, c), self.local)

    def begin(self):
        self.start("Z", 1)
        for kind in ("X", "Y", "S"):
            self.start(kind, 0)
        self.own().start()

    def along(self, d):
        self.arrived("Z", d)
        if d + 1 < self.nz:
            self.start("Z", d + 1)
        for kind in ("X", "Y", "S"):
            self.start(kind, d)

    def over(self, d):
        self.arrived("X", d)
        self.start("YA", d)
        self.start("SX", d)
        self.arrived("Y", d)
        self.start("XB", d)
        self.start("SY", d)

    def corner(self, d):
        self.arrived("YA", d)
        self.start("SA", d)
        self.arrived("XB", d)
        self.start("SB", d)

    def end(self):
        self.own().wait()
        for d in range(self.nz):
            for kind in ("S", "SX", "SY", "SA", "SB"):
                self.arrived(kind, d)
        for kind, d in self.index:
            self.message(kind, d, True).wait_send()


class Share:
    def __init__(self, src, full, send, recv, local, pieces=1):
        self.src, self.full, self.send, self.recv, self.local, self.pieces = src, full, send, recv, local, pieces
        self.size = src.shape[0] // pieces

    @staticmethod
    def sems(pieces):
        dma = pltpu.SemaphoreType.DMA
        return [dma((3 * pieces,)), dma((3 * pieces,)), dma((pieces,))]

    def rows(self, y, c, i):
        own = self.size * self.pieces
        return pl.ds(pl.multiple_of((2 * y + c) * own + i * self.size, 16), self.size)

    def message(self, kind, i):
        z, x, y, c = place()
        n = self.pieces
        piece = self.src.at[pl.ds(i * self.size, self.size)]
        if kind == "own":
            return pltpu.make_async_copy(piece, self.full.at[self.rows(y, c, i)], self.local.at[i])
        k = {"Y": 0, "C": 1, "F": 2}[kind] * n + i
        sems = self.send.at[k], self.recv.at[k]
        sib = device(z, x, y, 1 - c)
        if kind == "Y":
            return remote(piece, self.full.at[self.rows(y, c, i)], *sems, device(z, x, 1 - y, c))
        if kind == "C":
            return remote(piece, self.full.at[self.rows(y, c, i)], *sems, sib)
        at = self.full.at[self.rows(1 - y, c, i)]
        return remote(at, at, *sems, sib)

    def begin(self, i):
        for kind in ("Y", "C", "own"):
            self.message(kind, i).start()

    def on(self, i):
        self.message("Y", i).wait_recv()
        self.message("F", i).start()

    def end(self):
        for i in range(self.pieces):
            self.message("own", i).wait()
            self.message("C", i).wait_recv()
            self.message("F", i).wait_recv()
            for kind in ("Y", "C", "F"):
                self.message(kind, i).wait_send()


def finish(tokens, gain, cot, middle_cot):
    hat, inv_sigma = normalize(tokens.T.astype(F32))
    d = cot * gain
    made = middle_cot + inv_sigma * (
        d - jnp.mean(d, axis=0, keepdims=True) - hat * jnp.mean(d * hat, axis=0, keepdims=True)
    )
    return made.T.astype(BF16)


class Scatter:
    def __init__(self, nz, ups, src, part, out, core, side, line, last, send, recv, shared=None):
        self.nz, self.ups, self.src, self.part, self.out, self.shared = nz, ups, src, part, out, shared
        self.core, self.side, self.line, self.last, self.send, self.recv = core, side, line, last, send, recv
        self.depth = out.shape[0]

    @staticmethod
    def scratch(nz, ups, depth, columns):
        count = len(ups) * nz + 2 * nz
        return [
            pltpu.VMEM((len(ups), 2 * nz * depth, columns), BF16),
            pltpu.VMEM((len(ups), nz * depth, columns), BF16),
            pltpu.VMEM((nz, len(ups), depth, columns), BF16),
            pltpu.VMEM((depth, columns), BF16),
            pltpu.SemaphoreType.DMA((count,)),
            pltpu.SemaphoreType.DMA((count,)),
        ]

    def row(self, d):
        z, _, _, _ = place()
        return lax.bitwise_xor(z, d)

    def rows(self, d, x):
        return pl.ds(pl.multiple_of((2 * self.row(d) + x) * self.depth, 16), self.depth)

    def both(self, d):
        return pl.ds(pl.multiple_of(2 * self.row(d) * self.depth, 16), 2 * self.depth)

    def lane(self, d):
        return pl.ds(pl.multiple_of(self.row(d) * self.depth, 16), self.depth)

    def message(self, kind, d, u=0):
        z, x, y, c = place()
        nz, n = self.nz, len(self.ups)
        i = {"C": u * nz + d, "X": n * nz + d, "Z": n * nz + nz + d, "Y": n * nz + nz}[kind]
        sems = self.send.at[i], self.recv.at[i]
        if kind == "C":
            both = self.both(d)
            return remote(self.src.at[2 * self.ups[u] + 1 - c, both], self.core.at[u, both], *sems, device(z, x, y, 1 - c))
        if kind == "X":
            return remote(
                self.core.at[:, self.rows(d, 1 - x)], self.side.at[:, self.lane(d)], *sems, device(z, 1 - x, y, c)
            )
        if kind == "Z":
            return remote(self.side.at[:, self.lane(d)], self.line.at[d], *sems, device(self.row(d), x, y, c))
        return remote(self.line.at[0, 1 - y if n == 2 else 0], self.last, *sems, device(z, x, 1 - y, c))

    def begin(self, *rows):
        for d in rows:
            for u in range(len(self.ups)):
                self.message("C", d, u).start()

    def cross(self, d):
        self.message("X", d).start()

    def chip(self, d):
        _, x, _, c = place()
        for u in range(len(self.ups)):
            self.message("C", d, u).wait_recv()
        for side in range(2):
            rows = self.rows(d, side)
            for u, up in enumerate(self.ups):
                made = self.part[2 * up + c, rows].astype(F32) + self.core[u, rows].astype(F32)
                self.core[u, rows] = made.astype(BF16)

    def over(self, d):
        _, x, _, _ = place()
        self.message("X", d).wait_recv()
        rows, lane = self.rows(d, x), self.lane(d)
        for u in range(len(self.ups)):
            made = self.core[u, rows].astype(F32) + self.side[u, lane].astype(F32)
            self.side[u, lane] = made.astype(BF16)
        if d:
            self.message("Z", d).start()

    def along(self):
        _, _, y, _ = place()
        for d in range(1, self.nz):
            self.message("Z", d).wait_recv()
        lane = self.lane(0)
        for u in range(len(self.ups)):
            made = self.side[u, lane].astype(F32)
            for d in range(1, self.nz):
                made += self.line[d, u].astype(F32)
            self.line[0, u] = made.astype(BF16)
        if len(self.ups) == 2 or self.shared:
            self.message("Y", 0).start()
        else:
            pl.when(y != self.ups[0])(lambda: self.message("Y", 0).start())

    def end(self):
        _, _, y, _ = place()

        def receive():
            self.message("Y", 0).wait_recv()
            mine = self.line[0, y if len(self.ups) == 2 else 0]
            self.out[...] = mine.astype(F32) + self.last[...].astype(F32)

        if len(self.ups) == 2:
            receive()
            self.message("Y", 0).wait_send()
        elif self.shared:
            pl.when(y == self.ups[0])(receive)

            @pl.when(y != self.ups[0])
            def _():
                self.message("Y", 0).wait_recv()
                self.out[:, self.shared :] = self.line[0, 0, :, self.shared :].astype(F32) + self.last[
                    :, self.shared :
                ].astype(F32)

            self.message("Y", 0).wait_send()
        else:
            pl.when(y == self.ups[0])(receive)
            pl.when(y != self.ups[0])(lambda: self.message("Y", 0).wait_send())
        for d in range(self.nz):
            for u in range(len(self.ups)):
                self.message("C", d, u).wait_send()
            self.message("X", d).wait_send()
            if d:
                self.message("Z", d).wait_send()


class Fold:
    def __init__(self, part, near, far, send, recv):
        self.part, self.near, self.far, self.send, self.recv = part, near, far, send, recv
        self.slots = part.shape[0]

    @staticmethod
    def scratch(n_mp, own, slots):
        dma = pltpu.SemaphoreType.DMA
        return [
            pltpu.VMEM((slots, n_mp, 2 * HDIM, own), BF16),
            pltpu.VMEM((slots, 2, 2 * HDIM, own), BF16),
            pltpu.VMEM((slots, 2 * HDIM, own), BF16),
            dma((slots, 3)),
            dma((slots, 3)),
        ]

    def message(self, kind, head):
        z, x, y, c = place()
        slot = lax.rem(head, self.slots)
        k = {"far": 0, "near": 1, "Y": 2}[kind]
        sems = self.send.at[slot, k], self.recv.at[slot, k]
        if kind == "Y":
            return remote(self.near.at[slot, 1 - y], self.far.at[slot], *sems, device(z, x, 1 - y, c))
        up = 1 - y if kind == "far" else y
        return remote(self.part.at[slot, 2 * up + 1 - c], self.near.at[slot, up], *sems, device(z, x, y, 1 - c))

    def begin(self, head):
        self.message("far", head).start()
        self.message("near", head).start()

    def chip(self, head):
        _, _, y, c = place()
        slot = lax.rem(head, self.slots)
        self.message("far", head).wait_recv()
        made = self.part[slot, 2 * (1 - y) + c].astype(F32) + self.near[slot, 1 - y].astype(F32)
        self.near[slot, 1 - y] = made.astype(BF16)
        self.message("Y", head).start()

    def end(self, head):
        _, _, y, c = place()
        slot = lax.rem(head, self.slots)
        self.message("near", head).wait_recv()
        self.message("Y", head).wait_recv()
        made = self.part[slot, 2 * y + c].astype(F32) + self.near[slot, y].astype(F32) + self.far[slot].astype(F32)
        for kind in ("far", "near", "Y"):
            self.message(kind, head).wait_send()
        return made.astype(BF16)


def project(w_ref, part, n1_ref, cos_ref, sin_ref, mine, q_ref, k_ref, v_ref):
    width, own = q_ref.shape
    heads = width // HDIM

    made = dot(w_ref[part, :, width : 3 * width], n1_ref[...], TN)
    k_ref[...] = turn(made[:width], cos_ref[...], sin_ref[...], heads).astype(BF16)
    v_ref[...] = made[width:].astype(BF16)
    made = dot(w_ref[part, :, :width], n1_ref[:, mine], TN) * (SCALE * LOG2E)
    q_ref[...] = turn(made, cos_ref[:, mine], sin_ref[:, mine], heads).astype(BF16)


def forward_kernel(nz, len_ref, tok_ref, *refs):
    linked = nz > 0
    given, refs = refs[: 6 if linked else 1], refs[6 if linked else 1 :]
    mine_ref, q_ref, k_ref, v_ref, cos_ref, sin_ref, o_ref, p_ref, inv_ref = refs[:9]
    full_refs, refs = refs[9 : 11 if linked else 9], refs[11 if linked else 9 :]
    w_ref, n1_ref, ka_ref, qa_ref, va_ref, stat_ref, load = refs[:7]
    refs = refs[7:]
    rows, features = tok_ref.shape
    own = q_ref.shape[1]
    docs = len_ref.shape[1]
    width = q_ref.shape[0]
    per = width // HDIM
    step = pl.program_id(0)
    me = lax.axis_index("mp")
    mine = pl.ds(pl.multiple_of(me * own, own), own)

    if linked:
        src_a, src_b = refs[:2]
        one = Gather(nz, src_a, w_ref, *refs[2:5])
        two = Gather(nz, src_b, full_refs[1], *refs[5:8])
        keep = pltpu.make_async_copy(w_ref, full_refs[0], load)

    @pl.when(step == 0)
    def _():
        if linked:
            wq_ref, wg_ref, wo_ref, wd_ref, one_ref, two_ref = given
            for i in range(3):
                src_a[:, i * width : (i + 1) * width] = wq_ref[i]
            src_a[:, 3 * width :] = one_ref[...].astype(F32).T.astype(BF16)
            greet(peers(nz))
            one.begin()
            units = wd_ref.shape[0]
            pair = 2 * units
            for i in range(2):
                src_b[:, i * units : (i + 1) * units] = wg_ref[i]
            src_b[:, pair : pair + width] = wo_ref[...].T
            src_b[:, pair + width : pair + width + units] = wd_ref[...].T
            src_b[:, pair + width + units :] = two_ref[...].astype(F32).T.astype(BF16)
        else:
            fetch = pltpu.make_async_copy(given[0], w_ref, load)
            fetch.start()

        _, position, _ = layout_rows(len_ref, docs, 0, rows)
        power = lax.broadcasted_iota(jnp.int32, (HALF, 1), 0).astype(F32) * (-2.0 / HDIM * math.log2(ROPE_BASE))
        angle = position.astype(F32) * jnp.exp2(power)
        cos_ref[...] = jnp.cos(angle)
        sin_ref[...] = jnp.sin(angle)
        keys, _, _ = layout_rows(len_ref, docs, 0, rows)
        queries, _, _ = layout_rows(len_ref, docs, me * own, own)
        kind = lax.broadcasted_iota(jnp.int32, (AUG - HDIM, 1), 0)
        ka_ref[HDIM:] = jnp.where(kind == keys, 1.0, 0.0).astype(BF16)
        qa_ref[HDIM:] = jnp.where(kind == queries, 0.0, FAR).astype(BF16)
        va_ref[HDIM:] = jnp.ones((AUG - HDIM, rows), BF16)

        def measure(i, carry):
            at = pl.ds(pl.multiple_of(i * own, own), own)
            turned = tok_ref[at, :].T
            n1_ref[:, at] = turned
            mean, inv = moments(turned.astype(F32))
            stat_ref[0:1, at] = mean
            stat_ref[1:2, at] = inv
            return carry

        lax.fori_loop(0, rows // own, measure, 0)
        if linked:
            for d in range(nz):
                if d:
                    one.along(d)
                one.over(d)
            two.begin()
            for d in range(nz):
                one.corner(d)
            one.end()
            keep.start()
        else:
            fetch.wait()
        gain = w_ref[0, :, 3 * width :].astype(F32)

        def norm(i, carry):
            at = pl.ds(pl.multiple_of(i * own, own), own)
            made = (n1_ref[:, at].astype(F32) - stat_ref[0:1, at]) * stat_ref[1:2, at] * gain
            n1_ref[:, at] = made.astype(BF16)
            return carry

        lax.fori_loop(0, rows // own, norm, 0)
        mine_ref[...] = n1_ref[:, mine]

    if linked:
        for at, name, d in GATHER_STEPS:
            pl.when(step == at)(functools.partial(getattr(two, name), d))

    @pl.when(lax.rem(step, per) == 0)
    def _():
        project(w_ref, step // per, n1_ref, cos_ref, sin_ref, mine, q_ref, k_ref, v_ref)

    head = pl.ds(pl.multiple_of(lax.rem(step, per) * HDIM, HDIM), HDIM)
    ka_ref[:HDIM] = k_ref[head]
    qa_ref[:HDIM] = q_ref[head]
    va_ref[:HDIM] = v_ref[head]
    wide = own
    for i in range(own // wide):
        at = slice(i * wide, (i + 1) * wide)
        scores = dot(ka_ref[...], qa_ref[:, at], TN)
        top = jnp.max(scores, axis=0, keepdims=True)
        probs = jnp.exp2(scores - top).astype(BF16)
        p_ref[0, :, at] = probs
        out = dot(va_ref[...], probs, NN)
        inv = 1.0 / out[HDIM : HDIM + 1]
        o_ref[:, at] = (out[:HDIM] * inv).astype(BF16)
        inv_ref[0, :, at] = inv
    if linked:

        @pl.when(step == pl.num_programs(0) - 1)
        def _():
            keep.wait()
            two.corner(nz - 1)
            two.end()


GATHER_STEPS = (
    (2, "along", 1),
    (2, "over", 0),
    (5, "over", 1),
    (5, "along", 2),
    (5, "corner", 0),
    (7, "over", 2),
    (8, "corner", 1),
    (9, "along", 3),
    (11, "over", 3),
    (11, "corner", 2),
)


def forward(nz, n_mp, lengths, tokens, weights, columns):
    rows, features = tokens.shape
    own, width, heads = rows // n_mp, features // n_mp, features // HDIM
    per = width // HDIM
    linked = nz > 0
    hbm = pl.BlockSpec(memory_space=pl.ANY)
    part = lambda h: (h // per, 0)
    vm = pl.BlockSpec(memory_space=pltpu.VMEM)
    n = Gather.count(nz) if linked else 0
    dma = pltpu.SemaphoreType.DMA
    depth = features // (2 * nz) if linked else 0
    full_shapes = [jax.ShapeDtypeStruct((n_mp, features, c), BF16) for c in columns] if linked else []
    return pl.pallas_call(
        functools.partial(forward_kernel, nz),
        grid=(heads,),
        in_specs=[pl.BlockSpec(memory_space=pltpu.SMEM), vm] + ([vm] * 6 if linked else [hbm]),
        out_specs=[
            whole(features, own),
            pl.BlockSpec((width, own), part),
            pl.BlockSpec((width, rows), part),
            pl.BlockSpec((width, rows), part),
            whole(HALF, rows),
            whole(HALF, rows),
            pl.BlockSpec((HDIM, own), lambda h: (h, 0)),
            pl.BlockSpec((1, rows, own), lambda h: (h, 0, 0)),
            pl.BlockSpec((1, 1, own), lambda h: (h, 0, 0)),
        ]
        + [hbm] * len(full_shapes),
        out_shape=[
            jax.ShapeDtypeStruct((features, own), BF16),
            jax.ShapeDtypeStruct((features, own), BF16),
            jax.ShapeDtypeStruct((features, rows), BF16),
            jax.ShapeDtypeStruct((features, rows), BF16),
            jax.ShapeDtypeStruct((HALF, rows), F32),
            jax.ShapeDtypeStruct((HALF, rows), F32),
            jax.ShapeDtypeStruct((features, own), BF16),
            jax.ShapeDtypeStruct((heads, rows, own), BF16),
            jax.ShapeDtypeStruct((heads, 1, own), F32),
        ]
        + full_shapes,
        scratch_shapes=[
            pltpu.VMEM((n_mp, features, columns[0]), BF16),
            pltpu.VMEM((features, rows), BF16),
            pltpu.VMEM((AUG, rows), BF16),
            pltpu.VMEM((AUG, own), BF16),
            pltpu.VMEM((AUG, rows), BF16),
            pltpu.VMEM((8, rows), F32),
            dma,
        ]
        + (
            [pltpu.VMEM((depth, c), BF16) for c in columns] + [dma((n,)), dma((n,)), dma] * 2
            if linked
            else []
        ),
        compiler_params=pltpu.CompilerParams(
            dimension_semantics=("arbitrary",),
            vmem_limit_bytes=VMEM_BYTES,
            **({"collective_id": 1, "has_side_effects": True} if linked else {}),
        ),
        name="forward",
    )(lengths, tokens, *weights)


def mid_kernel(
    linked, units, len_ref, tok_hbm, cot_hbm, heads_ref, inv_ref, w_hbm,
    out_ref, mcot_ref, do_ref, g_ref, tok_ref, cot_ref, w_ref, load, *share,
):
    own, features = tok_ref.shape
    me = lax.axis_index("mp")
    mine = pl.ds(pl.multiple_of(me * own, own), own)
    loads = [
        pltpu.make_async_copy(tok_hbm.at[mine], tok_ref, load.at[0]),
        pltpu.make_async_copy(cot_hbm.at[mine], cot_ref, load.at[1]),
        pltpu.make_async_copy(w_hbm, w_ref, load.at[2]),
    ]
    for copy in loads:
        copy.start()
    if linked:
        out_own = share[0]
        share = Share(out_own, out_ref, *share[1:])
        greet(peers(1))
    else:
        out_own = out_ref
    parts = w_ref.shape[0]
    width = features // parts
    heads = width // HDIM
    pair = 2 * units
    _, _, live = layout_rows(len_ref, len_ref.shape[1], me * own, own)
    for copy in loads:
        copy.wait()

    def w_gu(m):
        return w_ref[m, :, :pair]

    def w_out(m):
        return w_ref[m, :, pair : pair + width]

    def w_down(m):
        return w_ref[m, :, pair + width : pair + width + units]

    total = dot(w_out(0), heads_ref[:width], NN)
    for m in range(1, parts):
        total += dot(w_out(m), heads_ref[m * width : (m + 1) * width], NN)
    middle = tok_ref[...].T.astype(F32) + total
    gain = w_ref[0, :, pair + width + units :].astype(F32)
    hat, inv_sigma = normalize(middle)
    normed = (hat * gain).astype(BF16)
    branch = jnp.where(live, cot_ref[...].T.astype(F32), 0.0).astype(BF16)
    total = middle
    back = jnp.zeros((features, own), F32)
    kept = []
    for m in range(parts):
        gate_up = dot(w_gu(m), normed, TN)
        gate, up = gate_up[:units], gate_up[units:]
        phi, slope = gelu_parts(gate)
        act = gate * phi
        hidden = (act * up).astype(BF16)
        total += dot(w_down(m), hidden, NN)
        kept.append((hidden, up * (phi + slope), act))
    out_own[...] = total.astype(BF16).T
    if linked:
        share.begin(0)
    for m in range(parts):
        hidden, one, two = kept[m]
        hidden_cot = dot(w_down(m), branch, TN)
        g_ref[m, :, pair + width : pair + width + units] = dot(branch, hidden, NT).astype(BF16)
        cots = jnp.concatenate([hidden_cot * one, hidden_cot * two], axis=0).astype(BF16)
        g_ref[m, :, :pair] = dot(normed, cots, NT).astype(BF16)
        back += dot(w_gu(m), cots, NN)
    gain_cot = jnp.sum(back * hat, axis=1, keepdims=True).astype(BF16)
    d = back * gain
    middle_cot = branch.astype(F32) + inv_sigma * (
        d - jnp.mean(d, axis=0, keepdims=True) - hat * jnp.mean(d * hat, axis=0, keepdims=True)
    )
    mcot_ref[...] = middle_cot
    attn_cot = middle_cot.astype(BF16)
    for m in range(parts):
        g_ref[m, :, pair + width + units :] = gain_cot
        part = heads_ref[m * width : (m + 1) * width]
        g_ref[m, :, pair : pair + width] = dot(attn_cot, part, NT).astype(BF16)
        back_heads = dot(w_out(m), attn_cot, TN)
        for h in range(heads):
            head = m * heads + h
            rows = slice(h * HDIM, (h + 1) * HDIM)
            cot = back_heads[rows] * inv_ref[head]
            inner = jnp.sum(cot * part[rows].astype(F32), axis=0, keepdims=True)
            high = inner.astype(BF16).astype(F32)
            pad = jnp.zeros((AUG - HDIM - 2, own), F32)
            do_ref[head] = jnp.concatenate([cot, high, inner - high, pad], axis=0).astype(BF16)
    if linked:
        share.on(0)
        share.end()


def mid(linked, n_mp, lengths, tokens, out_grad, heads_out, inv, w_rest, units):
    features, own = heads_out.shape
    heads = inv.shape[0]
    vm = pl.BlockSpec(memory_space=pltpu.VMEM)
    hbm = pl.BlockSpec(memory_space=pl.ANY)
    return pl.pallas_call(
        functools.partial(mid_kernel, linked, units),
        in_specs=[pl.BlockSpec(memory_space=pltpu.SMEM), hbm, hbm, vm, vm, hbm],
        out_specs=[hbm if linked else vm] + [vm] * 3,
        out_shape=[
            jax.ShapeDtypeStruct((own * n_mp if linked else own, features), BF16),
            jax.ShapeDtypeStruct((features, own), F32),
            jax.ShapeDtypeStruct((heads, AUG, own), BF16),
            jax.ShapeDtypeStruct(w_rest.shape, BF16),
        ],
        scratch_shapes=[
            pltpu.VMEM((own, features), BF16),
            pltpu.VMEM((own, features), BF16),
            pltpu.VMEM(w_rest.shape, BF16),
            pltpu.SemaphoreType.DMA((3,)),
        ]
        + ([pltpu.VMEM((own, features), BF16)] + Share.sems(1) if linked else []),
        compiler_params=pltpu.CompilerParams(
            vmem_limit_bytes=VMEM_BYTES, **({"collective_id": 2, "has_side_effects": True} if linked else {})
        ),
        name="mid",
    )(lengths, tokens, out_grad, heads_out, inv, w_rest)


SLOTS = 7
LAG = 4


def backward_kernel(nz, *refs):
    q_ref, k_ref, v_ref, do_ref, p_ref, cos_ref, sin_ref, n1_ref, mcot_ref, tok_hbm, w_hbm, gr_hbm = refs[:12]
    dq_ref, dr_ref, in_full = refs[12:15]
    w_ref, gr_ref, gq_ref, pc_ref, acc_ref, gc_ref, va_ref, tok_ref, in_own, load = refs[15:25]
    refs = refs[25:]
    rest = Scatter(nz, (0, 1), gr_hbm, gr_ref, dr_ref, *refs[:6])
    low = Scatter(nz, (0,), gq_ref, gq_ref, dq_ref, *refs[6:12])
    high = Scatter(nz, (1,), gq_ref, gq_ref, dq_ref, *refs[12:18], shared=gq_ref.shape[2] - 1)
    fold = Fold(*refs[18:23])
    share = Share(in_own, in_full, *refs[23:26])
    qc_ref = refs[26]
    step, heads = pl.program_id(0), pl.num_programs(0)
    parts = w_ref.shape[0]
    features, own = n1_ref.shape
    rows = k_ref.shape[1]
    width = features // parts
    per = width // HDIM
    me = lax.axis_index("mp")
    mine = pl.ds(pl.multiple_of(me * own, own), own)
    loads = [
        pltpu.make_async_copy(w_hbm, w_ref, load.at[0]),
        pltpu.make_async_copy(gr_hbm, gr_ref, load.at[1]),
        pltpu.make_async_copy(tok_hbm.at[mine], tok_ref, load.at[2]),
    ]

    @pl.when(step == 0)
    def _():
        for copy in loads:
            copy.start()
        greet(peers(nz))
        rest.begin(2, 3)
        va_ref[HDIM:] = jnp.full((AUG - HDIM, rows), -1.0, BF16)
        acc_ref[...] = jnp.zeros_like(acc_ref)
        gc_ref[...] = jnp.zeros_like(gc_ref)
        for m in range(2):
            gq_ref[m, :, 3 * width :] = jnp.zeros((features, 1), BF16)

    @pl.when(step == 1)
    def _():
        for copy in loads:
            copy.wait()

    def collect(head):
        made = fold.end(head)
        at = lax.rem(head, per) * HDIM
        pc_ref[pl.ds(pl.multiple_of(width + at, HDIM), HDIM)] = made[:HDIM]
        pc_ref[pl.ds(pl.multiple_of(2 * width + at, HDIM), HDIM)] = made[HDIM:]

    def close(part):
        for i in range(per):
            pc_ref[i * HDIM : (i + 1) * HDIM] = qc_ref[lax.rem(part, 3), i * HDIM : (i + 1) * HDIM]
        made = dot(n1_ref[...], pc_ref[...], NT)
        gq_ref[part, :, : 3 * width] = made.astype(BF16)
        weights = w_ref[part, :, : 3 * width]
        gc_ref[...] += jnp.sum(made * weights.astype(F32), axis=1, keepdims=True)
        acc_ref[...] += dot(weights, pc_ref[...], NN)

    va_ref[:HDIM] = v_ref[...]
    cot = dot(va_ref[...], do_ref[0], TN)
    probs = p_ref[0]
    score_cot = probs * cot.astype(BF16)
    dv = dot(do_ref[0, :HDIM], probs, NT).astype(BF16)
    dk = turn(dot(q_ref[...], score_cot, NT) * LN2, cos_ref[...], sin_ref[...], 1, True).astype(BF16)
    dq = turn(dot(k_ref[...], score_cot, NN) * SCALE, cos_ref[:, mine], sin_ref[:, mine], 1, True)
    slot = lax.rem(step, SLOTS)
    for m in range(parts):
        fold.part[slot, m, :HDIM] = dk[:, m * own : (m + 1) * own]
        fold.part[slot, m, HDIM:] = dv[:, m * own : (m + 1) * own]
    at = pl.ds(pl.multiple_of(lax.rem(step, per) * HDIM, HDIM), HDIM)
    qc_ref[lax.rem(step // per, 3), at] = dq.astype(BF16)

    @pl.when(step >= LAG)
    def _():
        collect(step - LAG)

    @pl.when(step >= 1)
    def _():
        fold.chip(step - 1)

    fold.begin(step)

    @pl.when((step >= LAG) & (lax.rem(step - LAG, per) == per - 1))
    def _():
        close((step - LAG) // per)

    sums = {"rest": rest, "low": low, "high": high}
    for at, which, name, *d in SUM_STEPS:
        pl.when(step == at)(functools.partial(getattr(sums[which], name), *d))

    @pl.when(step == heads - 1)
    def _():
        fold.chip(step)
        for back in range(LAG - 1, -1, -1):
            collect(step - back)
            if (heads - 1 - back) % per == per - 1:
                close((step - back) // per)
        gain = w_ref[0, :, 3 * width :].astype(F32)
        gain_cot = (gc_ref[...] / gain).astype(BF16)
        for m in range(2, parts):
            gq_ref[m, :, 3 * width :] = gain_cot
        high.begin(2, 3, 1, 0)
        in_own[...] = finish(tok_ref[...], gain, acc_ref[...], mcot_ref[...])
        share.begin(0)
        for which, name, *d in LAST_STEPS:
            getattr(sums[which], name)(*d)
        share.on(0)
        for which in sums.values():
            which.along()
        for which in sums.values():
            which.end()
        share.end()


SUM_STEPS = (
    (1, "rest", "chip", 2),
    (1, "rest", "cross", 2),
    (1, "rest", "begin", 1, 0),
    (1, "rest", "chip", 3),
    (3, "rest", "chip", 1),
    (3, "rest", "chip", 0),
    (5, "rest", "over", 2),
    (5, "rest", "cross", 3),
    (9, "rest", "over", 3),
    (9, "rest", "cross", 1),
    (9, "low", "begin", 2, 3, 1, 0),
    (11, "low", "chip", 2),
    (11, "low", "chip", 3),
    (11, "low", "chip", 1),
    (11, "low", "chip", 0),
)
LAST_STEPS = (
    ("rest", "over", 1),
    ("rest", "cross", 0),
    ("low", "cross", 2),
    ("low", "cross", 3),
    ("high", "chip", 2),
    ("high", "chip", 3),
    ("high", "chip", 1),
    ("high", "chip", 0),
    ("rest", "over", 0),
    ("low", "cross", 1),
    ("low", "cross", 0),
    ("low", "over", 2),
    ("low", "over", 3),
    ("high", "cross", 2),
    ("high", "cross", 3),
    ("low", "over", 1),
    ("low", "over", 0),
    ("high", "cross", 1),
    ("high", "cross", 0),
    ("high", "over", 2),
    ("high", "over", 3),
    ("high", "over", 1),
    ("high", "over", 0),
)


def backward(nz, q, k, v, do, p, cos, sin, n1, mcot, tokens, w_qkv, g_rest):
    (features, own), rows = q.shape, k.shape[1]
    n_mp = w_qkv.shape[0]
    heads = features // HDIM
    width = features // n_mp
    depth = features // (2 * nz)
    columns = w_qkv.shape[2], g_rest.shape[2]
    hbm = pl.BlockSpec(memory_space=pl.ANY)
    vm = pl.BlockSpec(memory_space=pltpu.VMEM)
    row = lambda h: (h, 0)
    cube = lambda h: (h, 0, 0)
    return pl.pallas_call(
        functools.partial(backward_kernel, nz),
        grid=(heads,),
        in_specs=[
            pl.BlockSpec((HDIM, own), row),
            pl.BlockSpec((HDIM, rows), row),
            pl.BlockSpec((HDIM, rows), row),
            pl.BlockSpec((1, AUG, own), cube),
            pl.BlockSpec((1, rows, own), cube),
            vm,
            vm,
            vm,
            vm,
            hbm,
            hbm,
            hbm,
        ],
        out_specs=[vm, vm, hbm],
        out_shape=[
            jax.ShapeDtypeStruct((depth, columns[0]), F32),
            jax.ShapeDtypeStruct((depth, columns[1]), F32),
            jax.ShapeDtypeStruct((rows, features), BF16),
        ],
        scratch_shapes=[
            pltpu.VMEM(w_qkv.shape, BF16),
            pltpu.VMEM(g_rest.shape, BF16),
            pltpu.VMEM(w_qkv.shape, BF16),
            pltpu.VMEM((3 * width, own), BF16),
            pltpu.VMEM((features, own), F32),
            pltpu.VMEM((features, 1), F32),
            pltpu.VMEM((AUG, rows), BF16),
            pltpu.VMEM((own, features), BF16),
            pltpu.VMEM((own, features), BF16),
            pltpu.SemaphoreType.DMA((3,)),
        ]
        + Scatter.scratch(nz, (0, 1), depth, columns[1])
        + Scatter.scratch(nz, (0,), depth, columns[0])
        + Scatter.scratch(nz, (1,), depth, columns[0])
        + Fold.scratch(n_mp, own, SLOTS)
        + Share.sems(1)
        + [pltpu.VMEM((3, width, own), BF16)],
        compiler_params=pltpu.CompilerParams(
            dimension_semantics=("arbitrary",), collective_id=3, has_side_effects=True, vmem_limit_bytes=VMEM_BYTES
        ),
        name="backward",
    )(q, k, v, do, p, cos, sin, n1, mcot, tokens, w_qkv, g_rest)


def deliver_kernel(units, in_ref, dq_ref, dr_ref, grad_ref, gq_ref, go_ref, gg_ref, gd_ref, one_ref, two_ref):
    grad_ref[...] = in_ref[...].astype(F32)

    @pl.when(pl.program_id(0) == 0)
    def _():
        width = go_ref.shape[0]
        pair = 2 * units
        for i in range(3):
            gq_ref[i] = dq_ref[:, i * width : (i + 1) * width]
        one_ref[...] = dq_ref[:, 3 * width :].T
        for i in range(2):
            gg_ref[i] = dr_ref[:, i * units : (i + 1) * units]
        go_ref[...] = dr_ref[:, pair : pair + width].T
        gd_ref[...] = dr_ref[:, pair + width : pair + width + units].T
        two_ref[...] = dr_ref[:, pair + width + units :].T


def deliver(input_grad, d_qkv, d_rest, width, units):
    rows, features = input_grad.shape
    depth = d_qkv.shape[0]
    shape = lambda *s: jax.ShapeDtypeStruct(s, F32)
    shapes = [(3, depth, width), (width, depth), (2, depth, units), (units, depth), (1, depth), (1, depth)]
    steps = 4
    return pl.pallas_call(
        functools.partial(deliver_kernel, units),
        grid=(steps,),
        in_specs=[pl.BlockSpec((rows // steps, features), lambda i: (i, 0)), whole(*d_qkv.shape), whole(*d_rest.shape)],
        out_specs=[pl.BlockSpec((rows // steps, features), lambda i: (i, 0))] + [whole(*s) for s in shapes],
        out_shape=[shape(rows, features)] + [shape(*s) for s in shapes],
        compiler_params=params("arbitrary"),
        name="deliver",
    )(input_grad, d_qkv, d_rest)


def per_device(n_dp, n_mp, tokens, out_grad, w_qkv, w_out, w_gu, w_down, gain_attn, gain_mlp, lengths):
    rows, features = tokens.shape
    depth = w_qkv.shape[0]
    units, width = w_down.shape[0], w_out.shape[0]
    everyone = ("mp", "dp")
    linked = n_mp == 4 and n_dp == 8 and depth % 32 == 0 and features // HDIM == 12
    nz = n_dp // 2 if linked else 0
    columns = 3 * width + 1, 3 * units + width + 1
    wq, wg = w_qkv.transpose(1, 0, 2), w_gu.transpose(1, 0, 2)
    if linked:
        weights = wq, wg, w_out, w_down, gain_attn[None], gain_mlp[None]
        n1, q, k, v, cos, sin, heads_out, probs, inv, full_qkv, full_rest = forward(
            nz, n_mp, lengths, tokens, weights, columns
        )
    else:
        shards = [
            jnp.concatenate([*wq, gain_attn[:, None]], axis=1),
            jnp.concatenate([*wg, w_out.T, w_down.T, gain_mlp[:, None]], axis=1),
        ]
        full_qkv, full_rest = (
            lax.all_gather(s, everyone, axis=0, tiled=True).reshape(n_mp, features, s.shape[1]) for s in shards
        )
        n1, q, k, v, cos, sin, heads_out, probs, inv = forward(nz, n_mp, lengths, tokens, [full_qkv], columns)
    layer_out, middle_cot, do, g_rest = mid(linked, n_mp, lengths, tokens, out_grad, heads_out, inv, full_rest, units)
    if linked:
        d_qkv, d_rest, in_full = backward(nz, q, k, v, do, probs, cos, sin, n1, middle_cot, tokens, full_qkv, g_rest)
    else:
        own = middle_cot.shape[1]
        g_qkv, nc = last(q, k, v, do, probs, cos, sin, lax.all_gather(n1, "mp", axis=1, tiled=True), full_qkv)
        gain_one = full_qkv[0, :, 3 * width :].astype(F32)
        tok = lax.dynamic_slice_in_dim(tokens, lax.axis_index("mp") * own, own, 0)
        nc_own = lax.psum_scatter(nc, "mp", scatter_dimension=0, tiled=True)[0]
        in_own = finish(tok, gain_one, nc_own.astype(F32), middle_cot)
        layer_out, in_full = (lax.all_gather(v, "mp", axis=0, tiled=True) for v in (layer_out, in_own))
        d_qkv, d_rest = (
            lax.psum_scatter(
                g.reshape(n_mp * features, -1), everyone, scatter_dimension=0, tiled=True
            ).astype(F32)
            for g in (g_qkv, g_rest)
        )
    input_grad, g_q, g_o, g_g, g_d, one, two = deliver(in_full, d_qkv, d_rest, width, units)
    if not linked:
        one, two = (lax.all_gather(g, "mp")[0] for g in (one, two))
    return layer_out, input_grad, g_q.transpose(1, 0, 2), g_o, g_g.transpose(1, 0, 2), g_d, one[0], two[0]


def solution(mesh):
    n_dp, n_mp = mesh.shape["dp"], mesh.shape["mp"]
    return jax.shard_map(
        functools.partial(per_device, n_dp, n_mp),
        mesh=mesh,
        in_specs=(
            P("dp", None),
            P("dp", None),
            P("dp", None, "mp"),
            P("mp", "dp"),
            P("dp", None, "mp"),
            P("mp", "dp"),
            P("dp"),
            P("dp"),
            P("dp", None),
        ),
        out_specs=(
            P("dp", None),
            P("dp", None),
            P("dp", None, "mp"),
            P("mp", "dp"),
            P("dp", None, "mp"),
            P("mp", "dp"),
            P("dp"),
            P("dp"),
        ),
        check_vma=False,
    )
```

```python
import functools
import math

import jax
import jax.numpy as jnp
from jax import lax
from jax.experimental import pallas as pl
from jax.experimental.pallas import tpu as pltpu
from jax.sharding import PartitionSpec as P

HDIM = 64
HALF = HDIM // 2
AUG = HDIM + 16
EPS = 1e-05
ROPE_BASE = 160000.0
LOG2E = math.log2(math.e)
LN2 = math.log(2.0)
SCALE = HDIM ** (-0.5)
FAR = -1e30
BF16 = jnp.bfloat16
F32 = jnp.float32
VMEM_BYTES = 60 << 20
NN = (((1,), (0,)), ((), ()))
NT = (((1,), (1,)), ((), ()))
TN = (((0,), (0,)), ((), ()))


def dot(a, b, dims):
    return lax.dot_general(a, b, dims, preferred_element_type=F32)


def params(*semantics):
    return pltpu.CompilerParams(
        dimension_semantics=semantics or None, vmem_limit_bytes=VMEM_BYTES
    )


def whole(*shape):
    return pl.BlockSpec(shape, lambda *i: (0,) * len(shape))


def layout_rows(len_ref, docs, first, rows):
    index = first + lax.broadcasted_iota(jnp.int32, (1, rows), 1)
    segment = jnp.zeros((1, rows), jnp.int32)
    start = jnp.zeros((1, rows), jnp.int32)
    end = jnp.int32(0)
    for j in range(docs):
        end = end + len_ref[0, j]
        past = index >= end
        segment = segment + jnp.where(past, 1, 0)
        start = jnp.where(past, jnp.maximum(start, end), start)
    return segment, index - start, index < end


def moments(columns):
    mean = jnp.mean(columns, axis=0, keepdims=True)
    centered = columns - mean
    return mean, lax.rsqrt(jnp.mean(centered * centered, axis=0, keepdims=True) + EPS)


def normalize(columns):
    mean, inv = moments(columns)
    return (columns - mean) * inv, inv


def turn(block, cos, sin, heads, back=False):
    out = []
    for h in range(heads):
        one = block[h * HDIM : h * HDIM + HALF]
        two = block[h * HDIM + HALF : (h + 1) * HDIM]
        if back:
            out += [one * cos + two * sin, two * cos - one * sin]
        else:
            out += [one * cos - two * sin, two * cos + one * sin]
    return jnp.concatenate(out, axis=0)


def gelu_parts(gate):
    phi = 0.5 * (1.0 + lax.erf(gate * math.sqrt(0.5)))
    density = jnp.exp2(gate * gate * (-0.5 * LOG2E)) * (1.0 / math.sqrt(2.0 * math.pi))
    return phi, gate * density


def last_kernel(own_axis, q_ref, k_ref, v_ref, do_ref, p_ref, cos_ref, sin_ref, n1_ref, w_ref, gq_ref, nc_ref, gc_ref, dq_ref, pc_ref, acc_ref, va_ref):
    step, head = pl.program_id(0), pl.program_id(1)
    per = pl.num_programs(1)
    features, rows = n1_ref.shape
    own = q_ref.shape[1]
    width = per * HDIM
    mine = pl.ds(pl.multiple_of(lax.axis_index(own_axis) * own, own), own)

    @pl.when((step == 0) & (head == 0))
    def _():
        va_ref[HDIM:] = jnp.full((AUG - HDIM, rows), -1.0, BF16)
        acc_ref[...] = jnp.zeros_like(acc_ref)
        gc_ref[...] = jnp.zeros_like(gc_ref)

    va_ref[:HDIM] = v_ref[...]
    cot = dot(va_ref[...], do_ref[0], TN)
    probs = p_ref[0]
    score_cot = probs * cot.astype(BF16)
    at = pl.ds(pl.multiple_of(head * HDIM, HDIM), HDIM)
    dv = dot(do_ref[0, :HDIM], probs, NT)
    dk = dot(q_ref[...], score_cot, NT) * LN2
    dq = dot(k_ref[...], score_cot, NN) * SCALE
    pc_ref[pl.ds(pl.multiple_of(width + head * HDIM, HDIM), HDIM)] = dv.astype(BF16)
    pc_ref[at] = turn(dk, cos_ref[...], sin_ref[...], 1, True).astype(BF16)
    dq_ref[at] = turn(dq, cos_ref[:, mine], sin_ref[:, mine], 1, True).astype(BF16)

    @pl.when(head == per - 1)
    def _():
        kv = dot(n1_ref[...], pc_ref[...], NT)
        q = dot(n1_ref[:, mine], dq_ref[...], NT)
        gq_ref[step, :, :width] = q.astype(BF16)
        gq_ref[step, :, width : 3 * width] = kv.astype(BF16)
        gc_ref[...] += jnp.sum(q * w_ref[0, :, :width].astype(F32), axis=1, keepdims=True) + jnp.sum(
            kv * w_ref[0, :, width : 3 * width].astype(F32), axis=1, keepdims=True
        )

        def spread(i, carry):
            cols = pl.ds(pl.multiple_of(i * own, own), own)
            acc_ref[:, cols] += dot(w_ref[0, :, width : 3 * width], pc_ref[:, cols], NN)
            return carry

        lax.fori_loop(0, rows // own, spread, 0)
        acc_ref[:, mine] += dot(w_ref[0, :, :width], dq_ref[...], NN)

    @pl.when((step == pl.num_programs(0) - 1) & (head == per - 1))
    def _():
        gain_cot = (gc_ref[...] / w_ref[0, :, 3 * width :].astype(F32)).astype(BF16)
        for m in range(gq_ref.shape[0]):
            nc_ref[m] = acc_ref[:, m * own : (m + 1) * own].astype(BF16)
            gq_ref[m, :, 3 * width :] = gain_cot


def last(q, k, v, do, p, cos, sin, n1, w_qkv, own_axis="mp"):
    (features, own), rows = q.shape, k.shape[1]
    parts = w_qkv.shape[0]
    per = features // parts // HDIM
    width = per * HDIM
    head = lambda m, h: (m * per + h, 0)
    return pl.pallas_call(
        functools.partial(last_kernel, own_axis),
        grid=(parts, per),
        in_specs=[
            pl.BlockSpec((HDIM, own), head),
            pl.BlockSpec((HDIM, rows), head),
            pl.BlockSpec((HDIM, rows), head),
            pl.BlockSpec((1, AUG, own), lambda m, h: (m * per + h, 0, 0)),
            pl.BlockSpec((1, rows, own), lambda m, h: (m * per + h, 0, 0)),
            whole(HALF, rows),
            whole(HALF, rows),
            whole(features, rows),
            pl.BlockSpec((1,) + w_qkv.shape[1:], lambda m, h: (m, 0, 0)),
        ],
        out_specs=[
            whole(*w_qkv.shape),
            whole(parts, features, own),
        ],
        out_shape=[
            jax.ShapeDtypeStruct(w_qkv.shape, BF16),
            jax.ShapeDtypeStruct((parts, features, own), BF16),
        ],
        scratch_shapes=[
            pltpu.VMEM((features, 1), F32),
            pltpu.VMEM((width, own), BF16),
            pltpu.VMEM((2 * width, rows), BF16),
            pltpu.VMEM((features, rows), F32),
            pltpu.VMEM((AUG, rows), BF16),
        ],
        compiler_params=params("arbitrary", "arbitrary"),
        name="last",
    )(q, k, v, do, p, cos, sin, n1, w_qkv)


def place():
    dp, mp = lax.axis_index("dp"), lax.axis_index("mp")
    return dp // 2, lax.rem(dp, 2), mp // 2, lax.rem(mp, 2)


def device(z, x, y, c):
    return (2 * z + x, 2 * y + c)


def remote(src, dst, send, recv, target):
    return pltpu.make_async_remote_copy(
        src_ref=src, dst_ref=dst, send_sem=send, recv_sem=recv,
        device_id=target, device_id_type=pl.DeviceIdType.MESH,
    )


def greet(targets):
    barrier = pltpu.get_barrier_semaphore()
    for target in targets:
        pl.semaphore_signal(barrier, inc=1, device_id=target, device_id_type=pl.DeviceIdType.MESH)
    pl.semaphore_wait(barrier, len(targets))


def peers(nz):
    z, x, y, c = place()
    across = [device(z, 1 - x, y, c), device(z, x, 1 - y, c), device(z, x, y, 1 - c)]
    return across + [device(lax.bitwise_xor(z, d), x, y, c) for d in range(1, nz)]


class Gather:
    def __init__(self, nz, src, full, send, recv, local):
        self.nz, self.src, self.full, self.send, self.recv, self.local = nz, src, full, send, recv, local
        self.depth = src.shape[0]
        self.index = {}
        for kind in ("Z", "X", "Y", "S", "YA", "XB", "SX", "SY", "SA", "SB"):
            for d in range(1 if kind == "Z" else 0, nz):
                self.index[kind, d] = len(self.index)

    @staticmethod
    def count(nz):
        return nz - 1 + 9 * nz

    def block(self, z, x, y, c, half=None):
        first, size = (0, self.depth) if half is None else (half * self.depth // 2, self.depth // 2)
        return self.full.at[2 * y + c, pl.ds(pl.multiple_of((2 * z + x) * self.depth + first, 16), size)]

    def message(self, kind, d, sending):
        z, x, y, c = place()
        back = lax.bitwise_xor(z, d)
        sx, sy, sib = device(z, 1 - x, y, c), device(z, x, 1 - y, c), device(z, x, y, 1 - c)
        sent, got, half, target = {
            "Z": ((z, x, y, c), (back, x, y, c), None, device(back, x, y, c)),
            "X": ((back, x, y, c), (back, 1 - x, y, c), None, sx),
            "Y": ((back, x, y, c), (back, x, 1 - y, c), None, sy),
            "S": ((back, x, y, c), (back, x, y, 1 - c), None, sib),
            "YA": ((back, 1 - x, y, c), (back, 1 - x, 1 - y, c), 0, sy),
            "XB": ((back, x, 1 - y, c), (back, 1 - x, 1 - y, c), 1, sx),
            "SX": ((back, 1 - x, y, c), (back, 1 - x, y, 1 - c), None, sib),
            "SY": ((back, x, 1 - y, c), (back, x, 1 - y, 1 - c), None, sib),
            "SA": ((back, 1 - x, 1 - y, c), (back, 1 - x, 1 - y, 1 - c), 0, sib),
            "SB": ((back, 1 - x, 1 - y, c), (back, 1 - x, 1 - y, 1 - c), 1, sib),
        }[kind]
        i = self.index[kind, d]
        at = self.block(*(sent if sending else got), half)
        own = sending and (kind == "Z" or (d == 0 and kind in ("X", "Y", "S")))
        return remote(self.src if own else at, at, self.send.at[i], self.recv.at[i], target)

    def start(self, kind, d):
        self.message(kind, d, True).start()

    def arrived(self, kind, d):
        self.message(kind, d, False).wait_recv()

    def own(self):
        z, x, y, c = place()
        return pltpu.make_async_copy(self.src, self.block(z, x, y, c), self.local)

    def begin(self):
        self.start("Z", 1)
        for kind in ("X", "Y", "S"):
            self.start(kind, 0)
        self.own().start()

    def along(self, d):
        self.arrived("Z", d)
        if d + 1 < self.nz:
            self.start("Z", d + 1)
        for kind in ("X", "Y", "S"):
            self.start(kind, d)

    def over(self, d):
        self.arrived("X", d)
        self.start("YA", d)
        self.start("SX", d)
        self.arrived("Y", d)
        self.start("XB", d)
        self.start("SY", d)

    def corner(self, d):
        self.arrived("YA", d)
        self.start("SA", d)
        self.arrived("XB", d)
        self.start("SB", d)

    def end(self):
        self.own().wait()
        for d in range(self.nz):
            for kind in ("S", "SX", "SY", "SA", "SB"):
                self.arrived(kind, d)
        for kind, d in self.index:
            self.message(kind, d, True).wait_send()


class Share:
    def __init__(self, src, full, send, recv, local, pieces=1):
        self.src, self.full, self.send, self.recv, self.local, self.pieces = src, full, send, recv, local, pieces
        self.size = src.shape[0] // pieces

    @staticmethod
    def sems(pieces):
        dma = pltpu.SemaphoreType.DMA
        return [dma((3 * pieces,)), dma((3 * pieces,)), dma((pieces,))]

    def rows(self, y, c, i):
        own = self.size * self.pieces
        return pl.ds(pl.multiple_of((2 * y + c) * own + i * self.size, 16), self.size)

    def message(self, kind, i):
        z, x, y, c = place()
        n = self.pieces
        piece = self.src.at[pl.ds(i * self.size, self.size)]
        if kind == "own":
            return pltpu.make_async_copy(piece, self.full.at[self.rows(y, c, i)], self.local.at[i])
        k = {"Y": 0, "C": 1, "F": 2}[kind] * n + i
        sems = self.send.at[k], self.recv.at[k]
        sib = device(z, x, y, 1 - c)
        if kind == "Y":
            return remote(piece, self.full.at[self.rows(y, c, i)], *sems, device(z, x, 1 - y, c))
        if kind == "C":
            return remote(piece, self.full.at[self.rows(y, c, i)], *sems, sib)
        at = self.full.at[self.rows(1 - y, c, i)]
        return remote(at, at, *sems, sib)

    def begin(self, i):
        for kind in ("Y", "C", "own"):
            self.message(kind, i).start()

    def on(self, i):
        self.message("Y", i).wait_recv()
        self.message("F", i).start()

    def end(self):
        for i in range(self.pieces):
            self.message("own", i).wait()
            self.message("C", i).wait_recv()
            self.message("F", i).wait_recv()
            for kind in ("Y", "C", "F"):
                self.message(kind, i).wait_send()


def finish(tokens, gain, cot, middle_cot):
    hat, inv_sigma = normalize(tokens.T.astype(F32))
    d = cot * gain
    made = middle_cot + inv_sigma * (
        d - jnp.mean(d, axis=0, keepdims=True) - hat * jnp.mean(d * hat, axis=0, keepdims=True)
    )
    return made.T.astype(BF16)


class Scatter:
    def __init__(self, nz, ups, src, part, out, core, side, line, last, send, recv, shared=None):
        self.nz, self.ups, self.src, self.part, self.out, self.shared = nz, ups, src, part, out, shared
        self.core, self.side, self.line, self.last, self.send, self.recv = core, side, line, last, send, recv
        self.depth = out.shape[0]

    @staticmethod
    def scratch(nz, ups, depth, columns):
        count = len(ups) * nz + 2 * nz
        return [
            pltpu.VMEM((len(ups), 2 * nz * depth, columns), BF16),
            pltpu.VMEM((len(ups), nz * depth, columns), BF16),
            pltpu.VMEM((nz, len(ups), depth, columns), BF16),
            pltpu.VMEM((depth, columns), BF16),
            pltpu.SemaphoreType.DMA((count,)),
            pltpu.SemaphoreType.DMA((count,)),
        ]

    def row(self, d):
        z, _, _, _ = place()
        return lax.bitwise_xor(z, d)

    def rows(self, d, x):
        return pl.ds(pl.multiple_of((2 * self.row(d) + x) * self.depth, 16), self.depth)

    def both(self, d):
        return pl.ds(pl.multiple_of(2 * self.row(d) * self.depth, 16), 2 * self.depth)

    def lane(self, d):
        return pl.ds(pl.multiple_of(self.row(d) * self.depth, 16), self.depth)

    def message(self, kind, d, u=0):
        z, x, y, c = place()
        nz, n = self.nz, len(self.ups)
        i = {"C": u * nz + d, "X": n * nz + d, "Z": n * nz + nz + d, "Y": n * nz + nz}[kind]
        sems = self.send.at[i], self.recv.at[i]
        if kind == "C":
            both = self.both(d)
            return remote(self.src.at[2 * self.ups[u] + 1 - c, both], self.core.at[u, both], *sems, device(z, x, y, 1 - c))
        if kind == "X":
            return remote(
                self.core.at[:, self.rows(d, 1 - x)], self.side.at[:, self.lane(d)], *sems, device(z, 1 - x, y, c)
            )
        if kind == "Z":
            return remote(self.side.at[:, self.lane(d)], self.line.at[d], *sems, device(self.row(d), x, y, c))
        return remote(self.line.at[0, 1 - y if n == 2 else 0], self.last, *sems, device(z, x, 1 - y, c))

    def begin(self, *rows):
        for d in rows:
            for u in range(len(self.ups)):
                self.message("C", d, u).start()

    def cross(self, d):
        self.message("X", d).start()

    def chip(self, d):
        _, x, _, c = place()
        for u in range(len(self.ups)):
            self.message("C", d, u).wait_recv()
        for side in range(2):
            rows = self.rows(d, side)
            for u, up in enumerate(self.ups):
                made = self.part[2 * up + c, rows].astype(F32) + self.core[u, rows].astype(F32)
                self.core[u, rows] = made.astype(BF16)

    def over(self, d):
        _, x, _, _ = place()
        self.message("X", d).wait_recv()
        rows, lane = self.rows(d, x), self.lane(d)
        for u in range(len(self.ups)):
            made = self.core[u, rows].astype(F32) + self.side[u, lane].astype(F32)
            self.side[u, lane] = made.astype(BF16)
        if d:
            self.message("Z", d).start()

    def along(self):
        _, _, y, _ = place()
        for d in range(1, self.nz):
            self.message("Z", d).wait_recv()
        lane = self.lane(0)
        for u in range(len(self.ups)):
            made = self.side[u, lane].astype(F32)
            for d in range(1, self.nz):
                made += self.line[d, u].astype(F32)
            self.line[0, u] = made.astype(BF16)
        if len(self.ups) == 2 or self.shared:
            self.message("Y", 0).start()
        else:
            pl.when(y != self.ups[0])(lambda: self.message("Y", 0).start())

    def end(self):
        _, _, y, _ = place()

        def receive():
            self.message("Y", 0).wait_recv()
            mine = self.line[0, y if len(self.ups) == 2 else 0]
            self.out[...] = mine.astype(F32) + self.last[...].astype(F32)

        if len(self.ups) == 2:
            receive()
            self.message("Y", 0).wait_send()
        elif self.shared:
            pl.when(y == self.ups[0])(receive)

            @pl.when(y != self.ups[0])
            def _():
                self.message("Y", 0).wait_recv()
                self.out[:, self.shared :] = self.line[0, 0, :, self.shared :].astype(F32) + self.last[
                    :, self.shared :
                ].astype(F32)

            self.message("Y", 0).wait_send()
        else:
            pl.when(y == self.ups[0])(receive)
            pl.when(y != self.ups[0])(lambda: self.message("Y", 0).wait_send())
        for d in range(self.nz):
            for u in range(len(self.ups)):
                self.message("C", d, u).wait_send()
            self.message("X", d).wait_send()
            if d:
                self.message("Z", d).wait_send()


class Fold:
    def __init__(self, part, near, far, send, recv):
        self.part, self.near, self.far, self.send, self.recv = part, near, far, send, recv
        self.slots = part.shape[0]

    @staticmethod
    def scratch(n_mp, own, slots):
        dma = pltpu.SemaphoreType.DMA
        return [
            pltpu.VMEM((slots, n_mp, 2 * HDIM, own), BF16),
            pltpu.VMEM((slots, 2, 2 * HDIM, own), BF16),
            pltpu.VMEM((slots, 2 * HDIM, own), BF16),
            dma((slots, 3)),
            dma((slots, 3)),
        ]

    def message(self, kind, head):
        z, x, y, c = place()
        slot = lax.rem(head, self.slots)
        k = {"far": 0, "near": 1, "Y": 2}[kind]
        sems = self.send.at[slot, k], self.recv.at[slot, k]
        if kind == "Y":
            return remote(self.near.at[slot, 1 - y], self.far.at[slot], *sems, device(z, x, 1 - y, c))
        up = 1 - y if kind == "far" else y
        return remote(self.part.at[slot, 2 * up + 1 - c], self.near.at[slot, up], *sems, device(z, x, y, 1 - c))

    def begin(self, head):
        self.message("far", head).start()
        self.message("near", head).start()

    def chip(self, head):
        _, _, y, c = place()
        slot = lax.rem(head, self.slots)
        self.message("far", head).wait_recv()
        made = self.part[slot, 2 * (1 - y) + c].astype(F32) + self.near[slot, 1 - y].astype(F32)
        self.near[slot, 1 - y] = made.astype(BF16)
        self.message("Y", head).start()

    def end(self, head):
        _, _, y, c = place()
        slot = lax.rem(head, self.slots)
        self.message("near", head).wait_recv()
        self.message("Y", head).wait_recv()
        made = self.part[slot, 2 * y + c].astype(F32) + self.near[slot, y].astype(F32) + self.far[slot].astype(F32)
        for kind in ("far", "near", "Y"):
            self.message(kind, head).wait_send()
        return made.astype(BF16)


def project(w_ref, part, n1_ref, cos_ref, sin_ref, mine, q_ref, k_ref, v_ref):
    width, own = q_ref.shape
    heads = width // HDIM

    made = dot(w_ref[part, :, width : 3 * width], n1_ref[...], TN)
    k_ref[...] = turn(made[:width], cos_ref[...], sin_ref[...], heads).astype(BF16)
    v_ref[...] = made[width:].astype(BF16)
    made = dot(w_ref[part, :, :width], n1_ref[:, mine], TN) * (SCALE * LOG2E)
    q_ref[...] = turn(made, cos_ref[:, mine], sin_ref[:, mine], heads).astype(BF16)


def forward_kernel(nz, len_ref, tok_ref, *refs):
    linked = nz > 0
    given, refs = refs[: 6 if linked else 1], refs[6 if linked else 1 :]
    mine_ref, q_ref, k_ref, v_ref, cos_ref, sin_ref, o_ref, p_ref, inv_ref = refs[:9]
    full_refs, refs = refs[9 : 11 if linked else 9], refs[11 if linked else 9 :]
    w_ref, n1_ref, ka_ref, qa_ref, va_ref, stat_ref, load = refs[:7]
    refs = refs[7:]
    rows, features = tok_ref.shape
    own = q_ref.shape[1]
    docs = len_ref.shape[1]
    width = q_ref.shape[0]
    per = width // HDIM
    step = pl.program_id(0)
    me = lax.axis_index("mp")
    mine = pl.ds(pl.multiple_of(me * own, own), own)

    if linked:
        src_a, src_b = refs[:2]
        one = Gather(nz, src_a, w_ref, *refs[2:5])
        two = Gather(nz, src_b, full_refs[1], *refs[5:8])
        keep = pltpu.make_async_copy(w_ref, full_refs[0], load)

    @pl.when(step == 0)
    def _():
        if linked:
            wq_ref, wg_ref, wo_ref, wd_ref, one_ref, two_ref = given
            for i in range(3):
                src_a[:, i * width : (i + 1) * width] = wq_ref[i]
            src_a[:, 3 * width :] = one_ref[...].astype(F32).T.astype(BF16)
            greet(peers(nz))
            one.begin()
            units = wd_ref.shape[0]
            pair = 2 * units
            for i in range(2):
                src_b[:, i * units : (i + 1) * units] = wg_ref[:, i, :]
            src_b[:, pair : pair + width] = wo_ref[...].T
            src_b[:, pair + width : pair + width + units] = wd_ref[...].T
            src_b[:, pair + width + units :] = two_ref[...].astype(F32).T.astype(BF16)
        else:
            fetch = pltpu.make_async_copy(given[0], w_ref, load)
            fetch.start()

        _, position, _ = layout_rows(len_ref, docs, 0, rows)
        power = lax.broadcasted_iota(jnp.int32, (HALF, 1), 0).astype(F32) * (-2.0 / HDIM * math.log2(ROPE_BASE))
        angle = position.astype(F32) * jnp.exp2(power)
        cos_ref[...] = jnp.cos(angle)
        sin_ref[...] = jnp.sin(angle)
        keys, _, _ = layout_rows(len_ref, docs, 0, rows)
        queries, _, _ = layout_rows(len_ref, docs, me * own, own)
        kind = lax.broadcasted_iota(jnp.int32, (AUG - HDIM, 1), 0)
        ka_ref[HDIM:] = jnp.where(kind == keys, 1.0, 0.0).astype(BF16)
        qa_ref[HDIM:] = jnp.where(kind == queries, 0.0, FAR).astype(BF16)
        va_ref[HDIM:] = jnp.ones((AUG - HDIM, rows), BF16)

        def measure(i, carry):
            at = pl.ds(pl.multiple_of(i * own, own), own)
            turned = tok_ref[at, :].T
            n1_ref[:, at] = turned
            mean, inv = moments(turned.astype(F32))
            stat_ref[0:1, at] = mean
            stat_ref[1:2, at] = inv
            return carry

        lax.fori_loop(0, rows // own, measure, 0)
        if linked:
            for d in range(nz):
                if d:
                    one.along(d)
                one.over(d)
            two.begin()
            for d in range(nz):
                one.corner(d)
            one.end()
            keep.start()
        else:
            fetch.wait()
        gain = w_ref[0, :, 3 * width :].astype(F32)

        def norm(i, carry):
            at = pl.ds(pl.multiple_of(i * own, own), own)
            made = (n1_ref[:, at].astype(F32) - stat_ref[0:1, at]) * stat_ref[1:2, at] * gain
            n1_ref[:, at] = made.astype(BF16)
            return carry

        lax.fori_loop(0, rows // own, norm, 0)
        mine_ref[...] = n1_ref[:, mine]

    if linked:
        for at, name, d in GATHER_STEPS:
            pl.when(step == at)(functools.partial(getattr(two, name), d))

    @pl.when(lax.rem(step, per) == 0)
    def _():
        project(w_ref, step // per, n1_ref, cos_ref, sin_ref, mine, q_ref, k_ref, v_ref)

    head = pl.ds(pl.multiple_of(lax.rem(step, per) * HDIM, HDIM), HDIM)
    ka_ref[:HDIM] = k_ref[head]
    qa_ref[:HDIM] = q_ref[head]
    va_ref[:HDIM] = v_ref[head]
    wide = own
    for i in range(own // wide):
        at = slice(i * wide, (i + 1) * wide)
        scores = dot(ka_ref[...], qa_ref[:, at], TN)
        top = jnp.max(scores, axis=0, keepdims=True)
        probs = jnp.exp2(scores - top).astype(BF16)
        p_ref[0, :, at] = probs
        out = dot(va_ref[...], probs, NN)
        inv = 1.0 / out[HDIM : HDIM + 1]
        o_ref[:, at] = (out[:HDIM] * inv).astype(BF16)
        inv_ref[0, :, at] = inv
    if linked:

        @pl.when(step == pl.num_programs(0) - 1)
        def _():
            keep.wait()
            two.corner(nz - 1)
            two.end()


GATHER_STEPS = (
    (2, "along", 1),
    (2, "over", 0),
    (5, "over", 1),
    (5, "along", 2),
    (5, "corner", 0),
    (7, "over", 2),
    (8, "corner", 1),
    (9, "along", 3),
    (11, "over", 3),
    (11, "corner", 2),
)


def forward(nz, n_mp, lengths, tokens, weights, columns):
    rows, features = tokens.shape
    own, width, heads = rows // n_mp, features // n_mp, features // HDIM
    per = width // HDIM
    linked = nz > 0
    hbm = pl.BlockSpec(memory_space=pl.ANY)
    part = lambda h: (h // per, 0)
    vm = pl.BlockSpec(memory_space=pltpu.VMEM)
    n = Gather.count(nz) if linked else 0
    dma = pltpu.SemaphoreType.DMA
    depth = features // (2 * nz) if linked else 0
    full_shapes = [jax.ShapeDtypeStruct((n_mp, features, c), BF16) for c in columns] if linked else []
    return pl.pallas_call(
        functools.partial(forward_kernel, nz),
        grid=(heads,),
        in_specs=[pl.BlockSpec(memory_space=pltpu.SMEM), vm] + ([vm] * 6 if linked else [hbm]),
        out_specs=[
            whole(features, own),
            pl.BlockSpec((width, own), part),
            pl.BlockSpec((width, rows), part),
            pl.BlockSpec((width, rows), part),
            whole(HALF, rows),
            whole(HALF, rows),
            pl.BlockSpec((HDIM, own), lambda h: (h, 0)),
            pl.BlockSpec((1, rows, own), lambda h: (h, 0, 0)),
            pl.BlockSpec((1, 1, own), lambda h: (h, 0, 0)),
        ]
        + [hbm] * len(full_shapes),
        out_shape=[
            jax.ShapeDtypeStruct((features, own), BF16),
            jax.ShapeDtypeStruct((features, own), BF16),
            jax.ShapeDtypeStruct((features, rows), BF16),
            jax.ShapeDtypeStruct((features, rows), BF16),
            jax.ShapeDtypeStruct((HALF, rows), F32),
            jax.ShapeDtypeStruct((HALF, rows), F32),
            jax.ShapeDtypeStruct((features, own), BF16),
            jax.ShapeDtypeStruct((heads, rows, own), BF16),
            jax.ShapeDtypeStruct((heads, 1, own), F32),
        ]
        + full_shapes,
        scratch_shapes=[
            pltpu.VMEM((n_mp, features, columns[0]), BF16),
            pltpu.VMEM((features, rows), BF16),
            pltpu.VMEM((AUG, rows), BF16),
            pltpu.VMEM((AUG, own), BF16),
            pltpu.VMEM((AUG, rows), BF16),
            pltpu.VMEM((8, rows), F32),
            dma,
        ]
        + (
            [pltpu.VMEM((depth, c), BF16) for c in columns] + [dma((n,)), dma((n,)), dma] * 2
            if linked
            else []
        ),
        compiler_params=pltpu.CompilerParams(
            dimension_semantics=("arbitrary",),
            vmem_limit_bytes=VMEM_BYTES,
            **({"collective_id": 1, "has_side_effects": True} if linked else {}),
        ),
        name="forward",
    )(lengths, tokens, *weights)


def middle(len_ref, me, tok_ref, cot_ref, heads_ref, inv_ref, w_ref, units, out_ref, mcot_ref, do_ref, keep, sent, done):
    own, features = tok_ref.shape
    parts = w_ref.shape[0]
    width = features // parts
    heads = width // HDIM
    pair = 2 * units
    _, _, live = layout_rows(len_ref, len_ref.shape[1], me * own, own)

    def w_gu(m):
        return w_ref[m, :, :pair]

    def w_out(m):
        return w_ref[m, :, pair : pair + width]

    def w_down(m):
        return w_ref[m, :, pair + width : pair + width + units]

    total = dot(w_out(0), heads_ref[:width], NN)
    for m in range(1, parts):
        total += dot(w_out(m), heads_ref[m * width : (m + 1) * width], NN)
    middle = tok_ref[...].T.astype(F32) + total
    gain = w_ref[0, :, pair + width + units :].astype(F32)
    hat, inv_sigma = normalize(middle)
    normed = (hat * gain).astype(BF16)
    total = middle
    kept = []
    for m in range(parts):
        gate_up = dot(w_gu(m), normed, TN)
        gate, up = gate_up[:units], gate_up[units:]
        phi, slope = gelu_parts(gate)
        act = gate * phi
        hidden = (act * up).astype(BF16)
        total += dot(w_down(m), hidden, NN)
        kept.append((hidden, (up * (phi + slope)).astype(BF16), act.astype(BF16)))
    out_ref[...] = total.astype(BF16).T
    sent()
    branch = jnp.where(live, cot_ref[...].T.astype(F32), 0.0).astype(BF16)
    back = jnp.zeros((features, own), F32)
    for m in range(parts):
        hidden, one, two = kept[m]
        hidden_cot = dot(w_down(m), branch, TN)
        keep("down", m, dot(branch, hidden, NT).astype(BF16))
        cots = jnp.concatenate([hidden_cot * one.astype(F32), hidden_cot * two.astype(F32)], axis=0).astype(BF16)
        keep("gu", m, dot(normed, cots, NT).astype(BF16))
        back += dot(w_gu(m), cots, NN)
    done()
    gain_cot = jnp.sum(back * hat, axis=1, keepdims=True).astype(BF16)
    d = back * gain
    middle_cot = branch.astype(F32) + inv_sigma * (
        d - jnp.mean(d, axis=0, keepdims=True) - hat * jnp.mean(d * hat, axis=0, keepdims=True)
    )
    mcot_ref[...] = middle_cot
    attn_cot = middle_cot.astype(BF16)
    for m in range(parts):
        back_heads = dot(w_out(m), attn_cot, TN)
        for h in range(heads):
            head = m * heads + h
            rows = slice(h * HDIM, (h + 1) * HDIM)
            cot = back_heads[rows] * inv_ref[head]
            inner = jnp.sum(cot * heads_ref[head * HDIM : (head + 1) * HDIM].astype(F32), axis=0, keepdims=True)
            high = inner.astype(BF16).astype(F32)
            pad = jnp.zeros((AUG - HDIM - 2, own), F32)
            do_ref[head] = jnp.concatenate([cot, high, inner - high, pad], axis=0).astype(BF16)
    for m in range(parts):
        keep("out", m, dot(attn_cot, heads_ref[m * width : (m + 1) * width], NT).astype(BF16))
        keep("gain", m, gain_cot)


def mid_kernel(
    units, len_ref, tok_hbm, cot_hbm, heads_ref, inv_ref, w_hbm,
    out_ref, mcot_ref, do_ref, g_ref, o_ref, tok_ref, cot_ref, w_ref, load,
):
    own = tok_ref.shape[0]
    me = lax.axis_index("mp")
    mine = pl.ds(pl.multiple_of(me * own, own), own)
    loads = [
        pltpu.make_async_copy(tok_hbm.at[mine], tok_ref, load.at[0]),
        pltpu.make_async_copy(cot_hbm.at[mine], cot_ref, load.at[1]),
        pltpu.make_async_copy(w_hbm, w_ref, load.at[2]),
    ]
    for copy in loads:
        copy.start()
    for copy in loads:
        copy.wait()
    pair, width = 2 * units, o_ref.shape[2] - 1

    def keep(what, m, made):
        if what == "gu":
            g_ref[m, :, :pair] = made
        elif what == "down":
            g_ref[m, :, pair:] = made
        elif what == "out":
            o_ref[m, :, :width] = made
        else:
            o_ref[m, :, width:] = made

    nothing = lambda: None
    middle(
        len_ref, me, tok_ref, cot_ref, heads_ref, inv_ref, w_ref, units, out_ref, mcot_ref, do_ref, keep, nothing, nothing
    )


def mid(n_mp, lengths, tokens, out_grad, heads_out, inv, w_rest, units):
    features, own = heads_out.shape
    heads = inv.shape[0]
    vm = pl.BlockSpec(memory_space=pltpu.VMEM)
    hbm = pl.BlockSpec(memory_space=pl.ANY)
    return pl.pallas_call(
        functools.partial(mid_kernel, units),
        in_specs=[pl.BlockSpec(memory_space=pltpu.SMEM), hbm, hbm, vm, vm, hbm],
        out_specs=[vm] * 5,
        out_shape=[
            jax.ShapeDtypeStruct((own, features), BF16),
            jax.ShapeDtypeStruct((features, own), F32),
            jax.ShapeDtypeStruct((heads, AUG, own), BF16),
            jax.ShapeDtypeStruct((n_mp, features, 3 * units), BF16),
            jax.ShapeDtypeStruct((n_mp, features, features // n_mp + 1), BF16),
        ],
        scratch_shapes=[
            pltpu.VMEM((own, features), BF16),
            pltpu.VMEM((own, features), BF16),
            pltpu.VMEM(w_rest.shape, BF16),
            pltpu.SemaphoreType.DMA((3,)),
        ],
        compiler_params=pltpu.CompilerParams(vmem_limit_bytes=VMEM_BYTES),
        name="mid",
    )(lengths, tokens, out_grad, heads_out, inv, w_rest)


SLOTS = 7
LAG = 4


def backward_kernel(nz, units, *refs):
    len_ref, q_ref, k_ref, v_ref, p_ref, cos_ref, sin_ref, n1_ref, heads_ref, inv_ref, tok_hbm, cot_hbm, w_hbm, wr_hbm = refs[:14]
    dq_ref, dr_ref, in_full, out_full = refs[14:18]
    w_ref, wr_ref, gr_ref, do_ref, mcot_ref, pc_ref, qc_ref, acc_ref, gc_ref, va_ref, tok_ref, cot_ref, own_ref, load = refs[18:32]
    refs = refs[32:]
    gq_ref = wr_ref.at[:, :, pl.ds(0, dq_ref.shape[1])]
    rest = Scatter(nz, (0, 1), gr_ref, gr_ref, dr_ref, *refs[:6])
    low = Scatter(nz, (0,), gq_ref, gq_ref, dq_ref, *refs[6:12])
    high = Scatter(nz, (1,), gq_ref, gq_ref, dq_ref, *refs[12:18], shared=4 * (w_ref.shape[2] // 3))
    fold = Fold(*refs[18:23])
    in_share = Share(own_ref.at[0], in_full, *refs[23:26])
    out_share = Share(own_ref.at[1], out_full, *refs[26:29])
    step, heads = pl.program_id(0) - 1, pl.num_programs(0) - 1
    parts = w_ref.shape[0]
    features, own = n1_ref.shape
    rows = k_ref.shape[1]
    width = features // parts
    per = width // HDIM
    me = lax.axis_index("mp")
    mine = pl.ds(pl.multiple_of(me * own, own), own)
    late = pltpu.make_async_copy(w_hbm, w_ref, load.at[3])

    @pl.when(step < 0)
    def _():
        loads = [
            pltpu.make_async_copy(wr_hbm, wr_ref, load.at[0]),
            pltpu.make_async_copy(tok_hbm.at[mine], tok_ref, load.at[1]),
            pltpu.make_async_copy(cot_hbm.at[mine], cot_ref, load.at[2]),
        ]
        for copy in loads:
            copy.start()
        greet(peers(nz))
        for copy in loads:
            copy.wait()
        late.start()
        pair = 2 * units

        def keep(what, m, made):
            if what == "gu":
                gr_ref[m, :, :pair] = made
            elif what == "down":
                gr_ref[m, :, pair:] = made
            elif what == "out":
                wr_ref[m, :, 3 * width : 4 * width] = made
            else:
                wr_ref[m, :, 4 * width + 1 : 4 * width + 2] = made

        middle(
            len_ref, me, tok_ref, cot_ref, heads_ref, inv_ref, wr_ref, units, own_ref.at[1], mcot_ref, do_ref, keep,
            lambda: out_share.begin(0), lambda: rest.begin(2, 3),
        )
        va_ref[HDIM:] = jnp.full((AUG - HDIM, rows), -1.0, BF16)
        acc_ref[...] = jnp.zeros_like(acc_ref)
        gc_ref[...] = jnp.zeros_like(gc_ref)
        late.wait()

    def collect(head):
        made = fold.end(head)
        at = lax.rem(head, per) * HDIM
        pc_ref[pl.ds(pl.multiple_of(width + at, HDIM), HDIM)] = made[:HDIM]
        pc_ref[pl.ds(pl.multiple_of(2 * width + at, HDIM), HDIM)] = made[HDIM:]

    def close(part):
        for i in range(per):
            pc_ref[i * HDIM : (i + 1) * HDIM] = qc_ref[lax.rem(part, 3), i * HDIM : (i + 1) * HDIM]
        made = dot(n1_ref[...], pc_ref[...], NT)
        wr_ref[part, :, : 3 * width] = made.astype(BF16)
        weights = w_ref[part, :, : 3 * width]
        gc_ref[...] += jnp.sum(made * weights.astype(F32), axis=1, keepdims=True)
        acc_ref[...] += dot(weights, pc_ref[...], NN)

    @pl.when(step >= 0)
    def _():
        va_ref[:HDIM] = v_ref[...]
        cot = dot(va_ref[...], do_ref[step], TN)
        probs = p_ref[0]
        score_cot = probs * cot.astype(BF16)
        dv = dot(do_ref[step, :HDIM], probs, NT).astype(BF16)
        dk = turn(dot(q_ref[...], score_cot, NT) * LN2, cos_ref[...], sin_ref[...], 1, True).astype(BF16)
        dq = turn(dot(k_ref[...], score_cot, NN) * SCALE, cos_ref[:, mine], sin_ref[:, mine], 1, True)
        slot = lax.rem(step, SLOTS)
        for m in range(parts):
            fold.part[slot, m, :HDIM] = dk[:, m * own : (m + 1) * own]
            fold.part[slot, m, HDIM:] = dv[:, m * own : (m + 1) * own]
        at = pl.ds(pl.multiple_of(lax.rem(step, per) * HDIM, HDIM), HDIM)
        qc_ref[lax.rem(step // per, 3), at] = dq.astype(BF16)

        @pl.when(step >= LAG)
        def _():
            collect(step - LAG)

        @pl.when(step >= 1)
        def _():
            fold.chip(step - 1)

        fold.begin(step)

        @pl.when((step >= LAG) & (lax.rem(step - LAG, per) == per - 1))
        def _():
            close((step - LAG) // per)

    sums = {"rest": rest, "low": low, "high": high, "out": out_share}
    for at, which, name, *d in SUM_STEPS:
        pl.when(step == at)(functools.partial(getattr(sums[which], name), *d))

    @pl.when(step == heads - 1)
    def _():
        fold.chip(step)
        for back in range(LAG - 1, -1, -1):
            collect(step - back)
            if (heads - 1 - back) % per == per - 1:
                close((step - back) // per)
        gain = w_ref[0, :, 3 * width :].astype(F32)
        gain_cot = (gc_ref[...] / gain).astype(BF16)
        for m in range(2, parts):
            wr_ref[m, :, 4 * width : 4 * width + 1] = gain_cot
        high.begin(2, 3, 1, 0)
        own_ref[0] = finish(tok_ref[...], gain, acc_ref[...], mcot_ref[...])
        in_share.begin(0)
        for which, name, *d in LAST_STEPS:
            getattr(sums[which], name)(*d)
        in_share.on(0)
        for which in (rest, low, high):
            which.along()
        for which in (rest, low, high):
            which.end()
        out_share.end()
        in_share.end()


SUM_STEPS = (
    (-1, "rest", "chip", 2),
    (-1, "rest", "cross", 2),
    (-1, "rest", "begin", 1, 0),
    (-1, "rest", "chip", 3),
    (1, "rest", "chip", 1),
    (1, "rest", "chip", 0),
    (1, "out", "on", 0),
    (2, "rest", "over", 2),
    (2, "rest", "cross", 3),
    (5, "rest", "over", 3),
    (5, "rest", "cross", 1),
    (8, "rest", "over", 1),
    (8, "rest", "cross", 0),
    (9, "low", "begin", 2, 3, 1, 0),
    (10, "low", "chip", 2),
    (10, "low", "chip", 3),
    (10, "low", "chip", 1),
    (10, "low", "chip", 0),
    (11, "rest", "over", 0),
    (11, "low", "cross", 2),
    (11, "low", "cross", 3),
)
LAST_STEPS = (
    ("high", "chip", 2),
    ("high", "chip", 3),
    ("high", "chip", 1),
    ("high", "chip", 0),
    ("low", "over", 2),
    ("low", "cross", 1),
    ("low", "over", 3),
    ("low", "cross", 0),
    ("low", "over", 1),
    ("high", "cross", 2),
    ("high", "cross", 3),
    ("low", "over", 0),
    ("high", "over", 2),
    ("high", "cross", 1),
    ("high", "cross", 0),
    ("high", "over", 3),
    ("high", "over", 1),
    ("high", "over", 0),
)


def backward(nz, lengths, q, k, v, p, cos, sin, n1, heads_out, inv, tokens, out_grad, w_qkv, w_rest, units):
    (features, own), rows = q.shape, k.shape[1]
    n_mp = w_qkv.shape[0]
    heads = features // HDIM
    width = features // n_mp
    depth = features // (2 * nz)
    columns = lanes(4 * width + 2), 3 * units
    hbm = pl.BlockSpec(memory_space=pl.ANY)
    vm = pl.BlockSpec(memory_space=pltpu.VMEM)
    row = lambda h: (jnp.maximum(h - 1, 0), 0)
    cube = lambda h: (jnp.maximum(h - 1, 0), 0, 0)
    dma = pltpu.SemaphoreType.DMA
    return pl.pallas_call(
        functools.partial(backward_kernel, nz, units),
        grid=(heads + 1,),
        in_specs=[
            pl.BlockSpec(memory_space=pltpu.SMEM),
            pl.BlockSpec((HDIM, own), row),
            pl.BlockSpec((HDIM, rows), row),
            pl.BlockSpec((HDIM, rows), row),
            pl.BlockSpec((1, rows, own), cube),
        ]
        + [vm] * 5
        + [hbm] * 4,
        out_specs=[vm, vm, hbm, hbm],
        out_shape=[
            jax.ShapeDtypeStruct((depth, columns[0]), F32),
            jax.ShapeDtypeStruct((depth, columns[1]), F32),
            jax.ShapeDtypeStruct((rows, features), BF16),
            jax.ShapeDtypeStruct((rows, features), BF16),
        ],
        scratch_shapes=[
            pltpu.VMEM(w_qkv.shape, BF16),
            pltpu.VMEM(w_rest.shape, BF16),
            pltpu.VMEM((n_mp, features, 3 * units), BF16),
            pltpu.VMEM((heads, AUG, own), BF16),
            pltpu.VMEM((features, own), F32),
            pltpu.VMEM((3 * width, own), BF16),
            pltpu.VMEM((3, width, own), BF16),
            pltpu.VMEM((features, own), F32),
            pltpu.VMEM((features, 1), F32),
            pltpu.VMEM((AUG, rows), BF16),
            pltpu.VMEM((own, features), BF16),
            pltpu.VMEM((own, features), BF16),
            pltpu.VMEM((2, own, features), BF16),
            dma((4,)),
        ]
        + Scatter.scratch(nz, (0, 1), depth, columns[1])
        + Scatter.scratch(nz, (0,), depth, columns[0])
        + Scatter.scratch(nz, (1,), depth, columns[0])
        + Fold.scratch(n_mp, own, SLOTS)
        + Share.sems(1)
        + Share.sems(1),
        compiler_params=pltpu.CompilerParams(
            dimension_semantics=("arbitrary",), collective_id=3, has_side_effects=True, vmem_limit_bytes=VMEM_BYTES
        ),
        name="backward",
    )(lengths, q, k, v, p, cos, sin, n1, heads_out, inv, tokens, out_grad, w_qkv, w_rest)


def lanes(columns):
    return (columns + 127) // 128 * 128


def deliver_kernel(units, in_ref, out_ref, dq_ref, dr_ref, grad_ref, to_ref, gq_ref, go_ref, gg_ref, gd_ref, one_ref, two_ref):
    @pl.when(pl.program_id(0) == 0)
    def _():
        width = go_ref.shape[0]
        pair = 2 * units
        for i in range(3):
            gq_ref[i] = dq_ref[:, i * width : (i + 1) * width]
        go_ref[...] = dq_ref[:, 3 * width : 4 * width].T
        one_ref[...] = dq_ref[:, 4 * width : 4 * width + 1].T
        two_ref[...] = dq_ref[:, 4 * width + 1 : 4 * width + 2].T
        for i in range(2):
            gg_ref[:, i, :] = dr_ref[:, i * units : (i + 1) * units]
        gd_ref[...] = dr_ref[:, pair : pair + units].T

    grad_ref[...] = in_ref[...].astype(F32)
    to_ref[...] = out_ref[...]


def deliver(layer_out, input_grad, d_qkv, d_rest, width, units):
    rows, features = input_grad.shape
    depth = d_qkv.shape[0]
    shape = lambda *s: jax.ShapeDtypeStruct(s, F32)
    shapes = [(3, depth, width), (width, depth), (depth, 2, units), (units, depth), (1, depth), (1, depth)]
    steps = 4
    slab = pl.BlockSpec((rows // steps, features), lambda i: (i, 0))
    return pl.pallas_call(
        functools.partial(deliver_kernel, units),
        grid=(steps,),
        in_specs=[slab, slab, whole(*d_qkv.shape), whole(*d_rest.shape)],
        out_specs=[slab, slab] + [whole(*s) for s in shapes],
        out_shape=[shape(rows, features), jax.ShapeDtypeStruct((rows, features), BF16)] + [shape(*s) for s in shapes],
        compiler_params=params("arbitrary"),
        name="deliver",
    )(input_grad, layer_out, d_qkv, d_rest)


def per_device(n_dp, n_mp, tokens, out_grad, w_qkv, w_out, w_gu, w_down, gain_attn, gain_mlp, lengths):
    rows, features = tokens.shape
    depth = w_qkv.shape[0]
    units, width = w_down.shape[0], w_out.shape[0]
    everyone = ("mp", "dp")
    linked = n_mp == 4 and n_dp == 8 and depth % 32 == 0 and features // HDIM == 12
    nz = n_dp // 2 if linked else 0
    columns = 3 * width + 1, 3 * units + width + 1
    wq = w_qkv.transpose(1, 0, 2)
    if linked:
        weights = wq, w_gu, w_out, w_down, gain_attn[None], gain_mlp[None]
        n1, q, k, v, cos, sin, heads_out, probs, inv, full_qkv, full_rest = forward(
            nz, n_mp, lengths, tokens, weights, columns
        )
        d_qkv, d_rest, in_full, layer_out = backward(
            nz, lengths, q, k, v, probs, cos, sin, n1, heads_out, inv, tokens, out_grad, full_qkv, full_rest, units
        )
    else:
        shards = [
            jnp.concatenate([*wq, gain_attn[:, None]], axis=1),
            jnp.concatenate([w_gu.reshape(depth, -1), w_out.T, w_down.T, gain_mlp[:, None]], axis=1),
        ]
        full_qkv, full_rest = (
            lax.all_gather(s, everyone, axis=0, tiled=True).reshape(n_mp, features, s.shape[1]) for s in shards
        )
        n1, q, k, v, cos, sin, heads_out, probs, inv = forward(nz, n_mp, lengths, tokens, [full_qkv], columns)
        layer_out, middle_cot, do, g_rest, g_out = mid(
            n_mp, lengths, tokens, out_grad, heads_out, inv, full_rest, units
        )
        own = middle_cot.shape[1]
        g_qkv, nc = last(q, k, v, do, probs, cos, sin, lax.all_gather(n1, "mp", axis=1, tiled=True), full_qkv)
        gain_one = full_qkv[0, :, 3 * width :].astype(F32)
        tok = lax.dynamic_slice_in_dim(tokens, lax.axis_index("mp") * own, own, 0)
        nc_own = lax.psum_scatter(nc, "mp", scatter_dimension=0, tiled=True)[0]
        in_own = finish(tok, gain_one, nc_own.astype(F32), middle_cot)
        layer_out, in_full = (lax.all_gather(v, "mp", axis=0, tiled=True) for v in (layer_out, in_own))
        g_qkv = jnp.concatenate(
            [g_qkv[..., : 3 * width], g_out[..., :width], g_qkv[..., 3 * width :], g_out[..., width:]], axis=2
        )
        d_qkv, d_rest = (
            lax.psum_scatter(
                g.reshape(n_mp * features, -1), everyone, scatter_dimension=0, tiled=True
            ).astype(F32)
            for g in (g_qkv, g_rest)
        )
    input_grad, layer_out, g_q, g_o, g_g, g_d, one, two = deliver(layer_out, in_full, d_qkv, d_rest, width, units)
    if not linked:
        one, two = (lax.all_gather(g, "mp")[0] for g in (one, two))
    return layer_out, input_grad, g_q.transpose(1, 0, 2), g_o, g_g, g_d, one[0], two[0]


def solution(mesh):
    n_dp, n_mp = mesh.shape["dp"], mesh.shape["mp"]
    return jax.shard_map(
        functools.partial(per_device, n_dp, n_mp),
        mesh=mesh,
        in_specs=(
            P("dp", None),
            P("dp", None),
            P("dp", None, "mp"),
            P("mp", "dp"),
            P("dp", None, "mp"),
            P("mp", "dp"),
            P("dp"),
            P("dp"),
            P("dp", None),
        ),
        out_specs=(
            P("dp", None),
            P("dp", None),
            P("dp", None, "mp"),
            P("mp", "dp"),
            P("dp", None, "mp"),
            P("mp", "dp"),
            P("dp"),
            P("dp"),
        ),
        check_vma=False,
    )
```

```python
import functools
import math

import jax
import jax.numpy as jnp
from jax import lax
from jax.experimental import pallas as pl
from jax.experimental.pallas import tpu as pltpu
from jax.sharding import PartitionSpec as P

HDIM = 64
HALF = HDIM // 2
AUG = HDIM + 16
EPS = 1e-05
ROPE_BASE = 160000.0
LOG2E = math.log2(math.e)
LN2 = math.log(2.0)
SCALE = HDIM ** (-0.5)
FAR = -1e30
BF16 = jnp.bfloat16
F32 = jnp.float32
VMEM_BYTES = 60 << 20
NN = (((1,), (0,)), ((), ()))
NT = (((1,), (1,)), ((), ()))
TN = (((0,), (0,)), ((), ()))


def dot(a, b, dims):
    return lax.dot_general(a, b, dims, preferred_element_type=F32)


def params(*semantics):
    return pltpu.CompilerParams(
        dimension_semantics=semantics or None, vmem_limit_bytes=VMEM_BYTES
    )


def whole(*shape):
    return pl.BlockSpec(shape, lambda *i: (0,) * len(shape))


def layout_rows(len_ref, docs, first, rows):
    index = first + lax.broadcasted_iota(jnp.int32, (1, rows), 1)
    segment = jnp.zeros((1, rows), jnp.int32)
    start = jnp.zeros((1, rows), jnp.int32)
    end = jnp.int32(0)
    for j in range(docs):
        end = end + len_ref[0, j]
        past = index >= end
        segment = segment + jnp.where(past, 1, 0)
        start = jnp.where(past, jnp.maximum(start, end), start)
    return segment, index - start, index < end


def moments(columns):
    mean = jnp.mean(columns, axis=0, keepdims=True)
    centered = columns - mean
    return mean, lax.rsqrt(jnp.mean(centered * centered, axis=0, keepdims=True) + EPS)


def normalize(columns):
    mean, inv = moments(columns)
    return (columns - mean) * inv, inv


def turn(block, cos, sin, heads, back=False):
    out = []
    for h in range(heads):
        one = block[h * HDIM : h * HDIM + HALF]
        two = block[h * HDIM + HALF : (h + 1) * HDIM]
        if back:
            out += [one * cos + two * sin, two * cos - one * sin]
        else:
            out += [one * cos - two * sin, two * cos + one * sin]
    return jnp.concatenate(out, axis=0)


def gelu_parts(gate):
    phi = 0.5 * (1.0 + lax.erf(gate * math.sqrt(0.5)))
    density = jnp.exp2(gate * gate * (-0.5 * LOG2E)) * (1.0 / math.sqrt(2.0 * math.pi))
    return phi, gate * density


def last_kernel(own_axis, q_ref, k_ref, v_ref, do_ref, p_ref, cos_ref, sin_ref, n1_ref, w_ref, gq_ref, nc_ref, gc_ref, dq_ref, pc_ref, acc_ref, va_ref):
    step, head = pl.program_id(0), pl.program_id(1)
    per = pl.num_programs(1)
    features, rows = n1_ref.shape
    own = q_ref.shape[1]
    width = per * HDIM
    mine = pl.ds(pl.multiple_of(lax.axis_index(own_axis) * own, own), own)

    @pl.when((step == 0) & (head == 0))
    def _():
        va_ref[HDIM:] = jnp.full((AUG - HDIM, rows), -1.0, BF16)
        acc_ref[...] = jnp.zeros_like(acc_ref)
        gc_ref[...] = jnp.zeros_like(gc_ref)

    va_ref[:HDIM] = v_ref[...]
    cot = dot(va_ref[...], do_ref[0], TN)
    probs = p_ref[0]
    score_cot = probs * cot.astype(BF16)
    at = pl.ds(pl.multiple_of(head * HDIM, HDIM), HDIM)
    dv = dot(do_ref[0, :HDIM], probs, NT)
    dk = dot(q_ref[...], score_cot, NT) * LN2
    dq = dot(k_ref[...], score_cot, NN) * SCALE
    pc_ref[pl.ds(pl.multiple_of(width + head * HDIM, HDIM), HDIM)] = dv.astype(BF16)
    pc_ref[at] = turn(dk, cos_ref[...], sin_ref[...], 1, True).astype(BF16)
    dq_ref[at] = turn(dq, cos_ref[:, mine], sin_ref[:, mine], 1, True).astype(BF16)

    @pl.when(head == per - 1)
    def _():
        kv = dot(n1_ref[...], pc_ref[...], NT)
        q = dot(n1_ref[:, mine], dq_ref[...], NT)
        gq_ref[step, :, :width] = q.astype(BF16)
        gq_ref[step, :, width : 3 * width] = kv.astype(BF16)
        gc_ref[...] += jnp.sum(q * w_ref[0, :, :width].astype(F32), axis=1, keepdims=True) + jnp.sum(
            kv * w_ref[0, :, width : 3 * width].astype(F32), axis=1, keepdims=True
        )

        def spread(i, carry):
            cols = pl.ds(pl.multiple_of(i * own, own), own)
            acc_ref[:, cols] += dot(w_ref[0, :, width : 3 * width], pc_ref[:, cols], NN)
            return carry

        lax.fori_loop(0, rows // own, spread, 0)
        acc_ref[:, mine] += dot(w_ref[0, :, :width], dq_ref[...], NN)

    @pl.when((step == pl.num_programs(0) - 1) & (head == per - 1))
    def _():
        gain_cot = (gc_ref[...] / w_ref[0, :, 3 * width :].astype(F32)).astype(BF16)
        for m in range(gq_ref.shape[0]):
            nc_ref[m] = acc_ref[:, m * own : (m + 1) * own].astype(BF16)
            gq_ref[m, :, 3 * width :] = gain_cot


def last(q, k, v, do, p, cos, sin, n1, w_qkv, own_axis="mp"):
    (features, own), rows = q.shape, k.shape[1]
    parts = w_qkv.shape[0]
    per = features // parts // HDIM
    width = per * HDIM
    head = lambda m, h: (m * per + h, 0)
    return pl.pallas_call(
        functools.partial(last_kernel, own_axis),
        grid=(parts, per),
        in_specs=[
            pl.BlockSpec((HDIM, own), head),
            pl.BlockSpec((HDIM, rows), head),
            pl.BlockSpec((HDIM, rows), head),
            pl.BlockSpec((1, AUG, own), lambda m, h: (m * per + h, 0, 0)),
            pl.BlockSpec((1, rows, own), lambda m, h: (m * per + h, 0, 0)),
            whole(HALF, rows),
            whole(HALF, rows),
            whole(features, rows),
            pl.BlockSpec((1,) + w_qkv.shape[1:], lambda m, h: (m, 0, 0)),
        ],
        out_specs=[
            whole(*w_qkv.shape),
            whole(parts, features, own),
        ],
        out_shape=[
            jax.ShapeDtypeStruct(w_qkv.shape, BF16),
            jax.ShapeDtypeStruct((parts, features, own), BF16),
        ],
        scratch_shapes=[
            pltpu.VMEM((features, 1), F32),
            pltpu.VMEM((width, own), BF16),
            pltpu.VMEM((2 * width, rows), BF16),
            pltpu.VMEM((features, rows), F32),
            pltpu.VMEM((AUG, rows), BF16),
        ],
        compiler_params=params("arbitrary", "arbitrary"),
        name="last",
    )(q, k, v, do, p, cos, sin, n1, w_qkv)


def place():
    dp, mp = lax.axis_index("dp"), lax.axis_index("mp")
    return dp // 2, lax.rem(dp, 2), mp // 2, lax.rem(mp, 2)


def device(z, x, y, c):
    return (2 * z + x, 2 * y + c)


def remote(src, dst, send, recv, target):
    return pltpu.make_async_remote_copy(
        src_ref=src, dst_ref=dst, send_sem=send, recv_sem=recv,
        device_id=target, device_id_type=pl.DeviceIdType.MESH,
    )


def greet(targets):
    barrier = pltpu.get_barrier_semaphore()
    for target in targets:
        pl.semaphore_signal(barrier, inc=1, device_id=target, device_id_type=pl.DeviceIdType.MESH)
    pl.semaphore_wait(barrier, len(targets))


def peers(nz):
    z, x, y, c = place()
    across = [device(z, 1 - x, y, c), device(z, x, 1 - y, c), device(z, x, y, 1 - c)]
    return across + [device(lax.bitwise_xor(z, d), x, y, c) for d in range(1, nz)]


class Gather:
    def __init__(self, nz, src, full, send, recv, local, eager=False):
        self.nz, self.src, self.full, self.send, self.recv, self.local = nz, src, full, send, recv, local
        self.eager = eager
        self.depth = src.shape[0]
        self.index = {}
        for kind in ("Z", "X", "Y", "S", "YA", "XB", "SX", "SY", "SA", "SB"):
            for d in range(1 if kind == "Z" else 0, nz):
                self.index[kind, d] = len(self.index)

    @staticmethod
    def count(nz):
        return nz - 1 + 9 * nz

    def block(self, z, x, y, c, half=None):
        first, size = (0, self.depth) if half is None else (half * self.depth // 2, self.depth // 2)
        return self.full.at[2 * y + c, pl.ds(pl.multiple_of((2 * z + x) * self.depth + first, 16), size)]

    def message(self, kind, d, sending):
        z, x, y, c = place()
        back = lax.bitwise_xor(z, d)
        sx, sy, sib = device(z, 1 - x, y, c), device(z, x, 1 - y, c), device(z, x, y, 1 - c)
        sent, got, half, target = {
            "Z": ((z, x, y, c), (back, x, y, c), None, device(back, x, y, c)),
            "X": ((back, x, y, c), (back, 1 - x, y, c), None, sx),
            "Y": ((back, x, y, c), (back, x, 1 - y, c), None, sy),
            "S": ((back, x, y, c), (back, x, y, 1 - c), None, sib),
            "YA": ((back, 1 - x, y, c), (back, 1 - x, 1 - y, c), 0, sy),
            "XB": ((back, x, 1 - y, c), (back, 1 - x, 1 - y, c), 1, sx),
            "SX": ((back, 1 - x, y, c), (back, 1 - x, y, 1 - c), None, sib),
            "SY": ((back, x, 1 - y, c), (back, x, 1 - y, 1 - c), None, sib),
            "SA": ((back, 1 - x, 1 - y, c), (back, 1 - x, 1 - y, 1 - c), 0, sib),
            "SB": ((back, 1 - x, 1 - y, c), (back, 1 - x, 1 - y, 1 - c), 1, sib),
        }[kind]
        i = self.index[kind, d]
        at = self.block(*(sent if sending else got), half)
        own = sending and (kind == "Z" or (d == 0 and kind in ("X", "Y", "S")))
        return remote(self.src if own else at, at, self.send.at[i], self.recv.at[i], target)

    def start(self, kind, d):
        self.message(kind, d, True).start()

    def arrived(self, kind, d):
        self.message(kind, d, False).wait_recv()

    def own(self):
        z, x, y, c = place()
        return pltpu.make_async_copy(self.src, self.block(z, x, y, c), self.local)

    def begin(self):
        for d in range(1, self.nz if self.eager else 2):
            self.start("Z", d)
        for kind in ("X", "Y", "S"):
            self.start(kind, 0)
        self.own().start()

    def all_along(self):
        for d in range(1, self.nz):
            self.along(d)

    def all_over(self):
        for d in range(self.nz):
            self.over(d)

    def rest(self):
        for d in range(self.nz):
            self.corner(d)
        self.end()

    def along(self, d):
        self.arrived("Z", d)
        if d + 1 < self.nz and not self.eager:
            self.start("Z", d + 1)
        for kind in ("X", "Y", "S"):
            self.start(kind, d)

    def over(self, d):
        self.arrived("X", d)
        self.start("YA", d)
        self.start("SX", d)
        self.arrived("Y", d)
        self.start("XB", d)
        self.start("SY", d)

    def corner(self, d):
        self.arrived("YA", d)
        self.start("SA", d)
        self.arrived("XB", d)
        self.start("SB", d)

    def end(self):
        self.own().wait()
        for d in range(self.nz):
            for kind in ("S", "SX", "SY", "SA", "SB"):
                self.arrived(kind, d)
        for kind, d in self.index:
            self.message(kind, d, True).wait_send()


class Share:
    def __init__(self, src, full, send, recv, local, pieces=1):
        self.src, self.full, self.send, self.recv, self.local, self.pieces = src, full, send, recv, local, pieces
        self.size = src.shape[0] // pieces

    @staticmethod
    def sems(pieces):
        dma = pltpu.SemaphoreType.DMA
        return [dma((3 * pieces,)), dma((3 * pieces,)), dma((pieces,))]

    def rows(self, y, c, i):
        own = self.size * self.pieces
        return pl.ds(pl.multiple_of((2 * y + c) * own + i * self.size, 16), self.size)

    def message(self, kind, i):
        z, x, y, c = place()
        n = self.pieces
        piece = self.src.at[pl.ds(i * self.size, self.size)]
        if kind == "own":
            return pltpu.make_async_copy(piece, self.full.at[self.rows(y, c, i)], self.local.at[i])
        k = {"Y": 0, "C": 1, "F": 2}[kind] * n + i
        sems = self.send.at[k], self.recv.at[k]
        sib = device(z, x, y, 1 - c)
        if kind == "Y":
            return remote(piece, self.full.at[self.rows(y, c, i)], *sems, device(z, x, 1 - y, c))
        if kind == "C":
            return remote(piece, self.full.at[self.rows(y, c, i)], *sems, sib)
        at = self.full.at[self.rows(1 - y, c, i)]
        return remote(at, at, *sems, sib)

    def begin(self, i):
        for kind in ("Y", "C", "own"):
            self.message(kind, i).start()

    def on(self, i):
        self.message("Y", i).wait_recv()
        self.message("F", i).start()

    def end(self):
        for i in range(self.pieces):
            self.message("own", i).wait()
            self.message("C", i).wait_recv()
            self.message("F", i).wait_recv()
            for kind in ("Y", "C", "F"):
                self.message(kind, i).wait_send()


def finish(tokens, gain, cot, middle_cot):
    hat, inv_sigma = normalize(tokens.T.astype(F32))
    d = cot * gain
    made = middle_cot + inv_sigma * (
        d - jnp.mean(d, axis=0, keepdims=True) - hat * jnp.mean(d * hat, axis=0, keepdims=True)
    )
    return made.T.astype(BF16)


class Scatter:
    def __init__(self, nz, ups, src, part, out, core, side, line, last, send, recv):
        self.nz, self.ups, self.src, self.part, self.out = nz, ups, src, part, out
        self.core, self.side, self.line, self.last, self.send, self.recv = core, side, line, last, send, recv
        self.depth = out.shape[0]

    @staticmethod
    def scratch(nz, ups, depth, columns):
        count = len(ups) * nz + 2 * nz
        return [
            pltpu.VMEM((len(ups), 2 * nz * depth, columns), BF16),
            pltpu.VMEM((len(ups), nz * depth, columns), BF16),
            pltpu.VMEM((nz, len(ups), depth, columns), BF16),
            pltpu.VMEM((depth, columns), BF16),
            pltpu.SemaphoreType.DMA((count,)),
            pltpu.SemaphoreType.DMA((count,)),
        ]

    def row(self, d):
        z, _, _, _ = place()
        return lax.bitwise_xor(z, d)

    def rows(self, d, x):
        return pl.ds(pl.multiple_of((2 * self.row(d) + x) * self.depth, 16), self.depth)

    def both(self, d):
        return pl.ds(pl.multiple_of(2 * self.row(d) * self.depth, 16), 2 * self.depth)

    def lane(self, d):
        return pl.ds(pl.multiple_of(self.row(d) * self.depth, 16), self.depth)

    def message(self, kind, d, u=0):
        z, x, y, c = place()
        nz, n = self.nz, len(self.ups)
        i = {"C": u * nz + d, "X": n * nz + d, "Z": n * nz + nz + d, "Y": n * nz + nz}[kind]
        sems = self.send.at[i], self.recv.at[i]
        if kind == "C":
            both = self.both(d)
            return remote(self.src.at[2 * self.ups[u] + 1 - c, both], self.core.at[u, both], *sems, device(z, x, y, 1 - c))
        if kind == "X":
            return remote(
                self.core.at[:, self.rows(d, 1 - x)], self.side.at[:, self.lane(d)], *sems, device(z, 1 - x, y, c)
            )
        if kind == "Z":
            return remote(self.side.at[:, self.lane(d)], self.line.at[d], *sems, device(self.row(d), x, y, c))
        return remote(self.line.at[0, 1 - y if n == 2 else 0], self.last, *sems, device(z, x, 1 - y, c))

    def begin(self, *rows):
        for d in rows:
            for u in range(len(self.ups)):
                self.message("C", d, u).start()

    def cross(self, d):
        self.message("X", d).start()

    def chip(self, d):
        _, x, _, c = place()
        for u in range(len(self.ups)):
            self.message("C", d, u).wait_recv()
        for side in range(2):
            rows = self.rows(d, side)
            for u, up in enumerate(self.ups):
                made = self.part[2 * up + c, rows].astype(F32) + self.core[u, rows].astype(F32)
                self.core[u, rows] = made.astype(BF16)

    def over(self, d):
        _, x, _, _ = place()
        self.message("X", d).wait_recv()
        rows, lane = self.rows(d, x), self.lane(d)
        for u in range(len(self.ups)):
            made = self.core[u, rows].astype(F32) + self.side[u, lane].astype(F32)
            self.side[u, lane] = made.astype(BF16)
        if d:
            self.message("Z", d).start()

    def along(self):
        _, _, y, _ = place()
        for d in range(1, self.nz):
            self.message("Z", d).wait_recv()
        lane = self.lane(0)
        for u in range(len(self.ups)):
            made = self.side[u, lane].astype(F32)
            for d in range(1, self.nz):
                made += self.line[d, u].astype(F32)
            self.line[0, u] = made.astype(BF16)
        if len(self.ups) == 2:
            self.message("Y", 0).start()
        else:
            pl.when(y != self.ups[0])(lambda: self.message("Y", 0).start())

    def end(self):
        _, _, y, _ = place()

        def receive():
            self.message("Y", 0).wait_recv()
            mine = self.line[0, y if len(self.ups) == 2 else 0]
            self.out[...] = mine.astype(F32) + self.last[...].astype(F32)

        if len(self.ups) == 2:
            receive()
            self.message("Y", 0).wait_send()
        else:
            pl.when(y == self.ups[0])(receive)
            pl.when(y != self.ups[0])(lambda: self.message("Y", 0).wait_send())
        for d in range(self.nz):
            for u in range(len(self.ups)):
                self.message("C", d, u).wait_send()
            self.message("X", d).wait_send()
            if d:
                self.message("Z", d).wait_send()


class Everyone:
    def __init__(self, held, got, send, recv):
        self.held, self.got, self.send, self.recv = held, got, send, recv
        self.hops = got.shape[0]

    @staticmethod
    def scratch(nz, rows):
        hops = 3 + nz.bit_length() - 1
        dma = pltpu.SemaphoreType.DMA
        return [pltpu.VMEM((hops + 1, rows, 128), F32), pltpu.VMEM((hops, rows, 128), F32), dma((hops,)), dma((hops,))]

    def message(self, i):
        z, x, y, c = place()
        target = (
            device(z, x, y, 1 - c) if i == 0
            else device(z, x, 1 - y, c) if i == 1
            else device(z, 1 - x, y, c) if i == 2
            else device(lax.bitwise_xor(z, 1 << (i - 3)), x, y, c)
        )
        return remote(self.held.at[i], self.got.at[i], self.send.at[i], self.recv.at[i], target)

    def begin(self):
        self.message(0).start()

    def hop(self, i):
        self.message(i).wait_recv()
        self.held[i + 1] = self.held[i] + self.got[i]
        if i + 1 < self.hops:
            self.message(i + 1).start()

    def end(self):
        for i in range(self.hops):
            self.message(i).wait_send()
        return self.held[self.hops]


class Fold:
    def __init__(self, part, near, far, send, recv):
        self.part, self.near, self.far, self.send, self.recv = part, near, far, send, recv
        self.slots = part.shape[0]

    @staticmethod
    def scratch(n_mp, own, slots):
        dma = pltpu.SemaphoreType.DMA
        return [
            pltpu.VMEM((slots, n_mp, 2 * HDIM, own), BF16),
            pltpu.VMEM((slots, 2, 2 * HDIM, own), BF16),
            pltpu.VMEM((slots, 2 * HDIM, own), BF16),
            dma((slots, 3)),
            dma((slots, 3)),
        ]

    def message(self, kind, head):
        z, x, y, c = place()
        slot = lax.rem(head, self.slots)
        k = {"far": 0, "near": 1, "Y": 2}[kind]
        sems = self.send.at[slot, k], self.recv.at[slot, k]
        if kind == "Y":
            return remote(self.near.at[slot, 1 - y], self.far.at[slot], *sems, device(z, x, 1 - y, c))
        up = 1 - y if kind == "far" else y
        return remote(self.part.at[slot, 2 * up + 1 - c], self.near.at[slot, up], *sems, device(z, x, y, 1 - c))

    def begin(self, head):
        self.message("far", head).start()
        self.message("near", head).start()

    def chip(self, head):
        _, _, y, c = place()
        slot = lax.rem(head, self.slots)
        self.message("far", head).wait_recv()
        made = self.part[slot, 2 * (1 - y) + c].astype(F32) + self.near[slot, 1 - y].astype(F32)
        self.near[slot, 1 - y] = made.astype(BF16)
        self.message("Y", head).start()

    def end(self, head):
        _, _, y, c = place()
        slot = lax.rem(head, self.slots)
        self.message("near", head).wait_recv()
        self.message("Y", head).wait_recv()
        made = self.part[slot, 2 * y + c].astype(F32) + self.near[slot, y].astype(F32) + self.far[slot].astype(F32)
        for kind in ("far", "near", "Y"):
            self.message(kind, head).wait_send()
        return made.astype(BF16)


def forward_kernel(nz, units, len_ref, tok_ref, *refs):
    linked = nz > 0
    given, refs = refs[: 6 if linked else 2], refs[6 if linked else 2 :]
    mine_ref, q_ref, k_ref, v_ref, cos_ref, sin_ref, o_ref, p_ref, inv_ref = refs[:9]
    full_refs, refs = refs[9 : 12 if linked else 9], refs[12 if linked else 9 :]
    wa_ref, wb_ref, w_ref, n1_ref, ka_ref, qa_ref, va_ref, stat_ref, load = refs[:9]
    refs = refs[9:]
    rows, features = tok_ref.shape
    own = q_ref.shape[1]
    docs = len_ref.shape[1]
    step = pl.program_id(0)
    parts = wa_ref.shape[0]
    part, turn_at = lax.rem(step, parts), step // parts
    me = lax.axis_index("mp")
    mine = pl.ds(pl.multiple_of(me * own, own), own)
    three = 3 * HDIM

    if linked:
        srcs = refs[:3]
        one = Gather(nz, srcs[0], wa_ref, *refs[3:6], eager=True)
        two = Gather(nz, srcs[1], wb_ref, *refs[6:9], eager=True)
        last = Gather(nz, srcs[2], full_refs[2], *refs[9:12])
        keeps = [
            pltpu.make_async_copy(wa_ref, full_refs[0], load.at[0]),
            pltpu.make_async_copy(wb_ref, full_refs[1], load.at[1]),
        ]

    @pl.when(step == 0)
    def _():
        if linked:
            wq_ref, wg_ref, wo_ref, wd_ref, one_ref, two_ref = given
            for i in range(3):
                srcs[0][:, i * HDIM : (i + 1) * HDIM] = wq_ref[i, :, :HDIM]
            srcs[0][:, three : three + 1] = one_ref[...].astype(F32).T.astype(BF16)
            srcs[0][:, three + 1 : three + 2] = two_ref[...].astype(F32).T.astype(BF16)
            down = wd_ref[...].T
            srcs[0][:, 256 - units % 128 :] = down[:, units - units % 128 :]
            greet(peers(nz))
            one.begin()
            for r in range(1, wq_ref.shape[2] // HDIM):
                for i in range(3):
                    at = (r - 1) * three + i * HDIM
                    srcs[1][:, at : at + HDIM] = wq_ref[i, :, r * HDIM : (r + 1) * HDIM]
            two.begin()
            pair, width = 2 * units, wo_ref.shape[0]
            for i in range(2):
                srcs[2][:, i * units : (i + 1) * units] = wg_ref[:, i, :]
            srcs[2][:, pair : pair + width] = wo_ref[...].T
            srcs[2][:, pair + width :] = down[:, : units - units % 128]
        else:
            fetches = [pltpu.make_async_copy(g, w, load.at[i]) for i, (g, w) in enumerate(zip(given, (wa_ref, wb_ref)))]
            for fetch in fetches:
                fetch.start()
        _, position, _ = layout_rows(len_ref, docs, 0, rows)
        power = lax.broadcasted_iota(jnp.int32, (HALF, 1), 0).astype(F32) * (-2.0 / HDIM * math.log2(ROPE_BASE))
        angle = position.astype(F32) * jnp.exp2(power)
        cos_ref[...] = jnp.cos(angle)
        sin_ref[...] = jnp.sin(angle)
        keys, _, _ = layout_rows(len_ref, docs, 0, rows)
        queries, _, _ = layout_rows(len_ref, docs, me * own, own)
        kind = lax.broadcasted_iota(jnp.int32, (AUG - HDIM, 1), 0)
        ka_ref[HDIM:] = jnp.where(kind == keys, 1.0, 0.0).astype(BF16)
        qa_ref[HDIM:] = jnp.where(kind == queries, 0.0, FAR).astype(BF16)
        va_ref[HDIM:] = jnp.ones((AUG - HDIM, rows), BF16)

        def measure(i, carry):
            at = pl.ds(pl.multiple_of(i * own, own), own)
            turned = tok_ref[at, :].T
            n1_ref[:, at] = turned
            mean, inv = moments(turned.astype(F32))
            stat_ref[0:1, at] = mean
            stat_ref[1:2, at] = inv
            return carry

        if linked:
            one.all_along()
        lax.fori_loop(0, rows // own, measure, 0)
        if linked:
            one.all_over()
            last.begin()
            one.rest()
            keeps[0].start()
        else:
            for fetch in fetches:
                fetch.wait()
        gain = wa_ref[0, :, three : three + 1].astype(F32)

        def norm(i, carry):
            at = pl.ds(pl.multiple_of(i * own, own), own)
            made = (n1_ref[:, at].astype(F32) - stat_ref[0:1, at]) * stat_ref[1:2, at] * gain
            n1_ref[:, at] = made.astype(BF16)
            return carry

        lax.fori_loop(0, rows // own, norm, 0)
        mine_ref[...] = n1_ref[:, mine]

    if linked:
        gathers = {"two": two, "last": last}
        for at, which, name, *d in GATHER_STEPS:
            pl.when(step == at)(functools.partial(getattr(gathers[which], name), *d))

        @pl.when(step == parts)
        def _():
            two.rest()
            keeps[1].start()

    @pl.when(turn_at == 0)
    def _():
        w_ref[...] = wa_ref[part, :, :three]

    for r in range(1, 1 + wb_ref.shape[2] // three):

        @pl.when(turn_at == r)
        def _():
            w_ref[...] = wb_ref[part, :, (r - 1) * three : r * three]

    made = dot(w_ref[:, HDIM:], n1_ref[...], TN)
    keys = turn(made[:HDIM], cos_ref[...], sin_ref[...], 1).astype(BF16)
    k_ref[...] = keys
    ka_ref[:HDIM] = keys
    values = made[HDIM:].astype(BF16)
    v_ref[...] = values
    va_ref[:HDIM] = values
    made = dot(w_ref[:, :HDIM], n1_ref[:, mine], TN) * (SCALE * LOG2E)
    queries = turn(made, cos_ref[:, mine], sin_ref[:, mine], 1).astype(BF16)
    q_ref[...] = queries
    qa_ref[:HDIM] = queries
    scores = dot(ka_ref[...], qa_ref[...], TN)
    top = jnp.max(scores, axis=0, keepdims=True)
    probs = jnp.exp2(scores - top).astype(BF16)
    p_ref[0] = probs
    out = dot(va_ref[...], probs, NN)
    inv = 1.0 / out[HDIM : HDIM + 1]
    o_ref[...] = (out[:HDIM] * inv).astype(BF16)
    inv_ref[0] = inv
    if linked:

        @pl.when(step == pl.num_programs(0) - 1)
        def _():
            for keep in keeps:
                keep.wait()
            last.corner(3)
            last.end()


GATHER_STEPS = (
    (0, "two", "along", 1),
    (0, "two", "along", 2),
    (0, "two", "along", 3),
    (1, "two", "over", 0),
    (1, "two", "over", 1),
    (2, "two", "over", 2),
    (2, "two", "over", 3),
    (3, "last", "along", 1),
    (3, "last", "over", 0),
    (5, "last", "over", 1),
    (5, "last", "along", 2),
    (6, "last", "corner", 0),
    (7, "last", "over", 2),
    (8, "last", "corner", 1),
    (8, "last", "along", 3),
    (10, "last", "corner", 2),
    (10, "last", "over", 3),
)


def forward(nz, n_mp, units, lengths, tokens, weights, columns):
    rows, features = tokens.shape
    own, width, heads = rows // n_mp, features // n_mp, features // HDIM
    per = width // HDIM
    linked = nz > 0
    hbm = pl.BlockSpec(memory_space=pl.ANY)
    head = lambda h: lax.rem(h, n_mp) * per + h // n_mp
    row = lambda h: (head(h), 0)
    cube = lambda h: (head(h), 0, 0)
    vm = pl.BlockSpec(memory_space=pltpu.VMEM)
    n = Gather.count(nz) if linked else 0
    dma = pltpu.SemaphoreType.DMA
    depth = features // (2 * nz) if linked else 0
    full_shapes = [jax.ShapeDtypeStruct((n_mp, features, c), BF16) for c in columns] if linked else []
    return pl.pallas_call(
        functools.partial(forward_kernel, nz, units),
        grid=(heads,),
        in_specs=[pl.BlockSpec(memory_space=pltpu.SMEM), vm] + ([vm] * 6 if linked else [hbm] * 2),
        out_specs=[
            whole(features, own),
            pl.BlockSpec((HDIM, own), row),
            pl.BlockSpec((HDIM, rows), row),
            pl.BlockSpec((HDIM, rows), row),
            whole(HALF, rows),
            whole(HALF, rows),
            pl.BlockSpec((HDIM, own), row),
            pl.BlockSpec((1, rows, own), cube),
            pl.BlockSpec((1, 1, own), cube),
        ]
        + [hbm] * len(full_shapes),
        out_shape=[
            jax.ShapeDtypeStruct((features, own), BF16),
            jax.ShapeDtypeStruct((features, own), BF16),
            jax.ShapeDtypeStruct((features, rows), BF16),
            jax.ShapeDtypeStruct((features, rows), BF16),
            jax.ShapeDtypeStruct((HALF, rows), F32),
            jax.ShapeDtypeStruct((HALF, rows), F32),
            jax.ShapeDtypeStruct((features, own), BF16),
            jax.ShapeDtypeStruct((heads, rows, own), BF16),
            jax.ShapeDtypeStruct((heads, 1, own), F32),
        ]
        + full_shapes,
        scratch_shapes=[
            pltpu.VMEM((n_mp, features, columns[0]), BF16),
            pltpu.VMEM((n_mp, features, columns[1]), BF16),
            pltpu.VMEM((features, 3 * HDIM), BF16),
            pltpu.VMEM((features, rows), BF16),
            pltpu.VMEM((AUG, rows), BF16),
            pltpu.VMEM((AUG, own), BF16),
            pltpu.VMEM((AUG, rows), BF16),
            pltpu.VMEM((8, rows), F32),
            dma((2,)),
        ]
        + (
            [pltpu.VMEM((depth, c), BF16) for c in columns] + [dma((n,)), dma((n,)), dma] * 3
            if linked
            else []
        ),
        compiler_params=pltpu.CompilerParams(
            dimension_semantics=("arbitrary",),
            vmem_limit_bytes=VMEM_BYTES,
            **({"collective_id": 1, "has_side_effects": True} if linked else {}),
        ),
        name="forward",
    )(lengths, tokens, *weights)


def middle(len_ref, me, tok_ref, cot_ref, heads_ref, inv_ref, w_ref, gain, units, out_ref, mcot_ref, do_ref, keep, sent, done):
    own, features = tok_ref.shape
    parts = w_ref.shape[0]
    width = features // parts
    heads = width // HDIM
    pair = 2 * units
    _, _, live = layout_rows(len_ref, len_ref.shape[1], me * own, own)

    def w_gu(m):
        return w_ref[m, :, :pair]

    def w_out(m):
        return w_ref[m, :, pair : pair + width]

    def w_down(m):
        return w_ref[m, :, pair + width : pair + width + units]

    total = dot(w_out(0), heads_ref[:width], NN)
    for m in range(1, parts):
        total += dot(w_out(m), heads_ref[m * width : (m + 1) * width], NN)
    middle = tok_ref[...].T.astype(F32) + total
    hat, inv_sigma = normalize(middle)
    normed = (hat * gain).astype(BF16)
    total = middle
    kept = []
    for m in range(parts):
        gate_up = dot(w_gu(m), normed, TN)
        gate, up = gate_up[:units], gate_up[units:]
        phi, slope = gelu_parts(gate)
        act = gate * phi
        hidden = (act * up).astype(BF16)
        total += dot(w_down(m), hidden, NN)
        kept.append((hidden, (up * (phi + slope)).astype(BF16), act.astype(BF16)))
    out_ref[...] = total.astype(BF16).T
    sent()
    branch = jnp.where(live, cot_ref[...].T.astype(F32), 0.0).astype(BF16)
    back = jnp.zeros((features, own), F32)
    for m in range(parts):
        hidden, one, two = kept[m]
        hidden_cot = dot(w_down(m), branch, TN)
        keep("down", m, dot(branch, hidden, NT).astype(BF16))
        cots = jnp.concatenate([hidden_cot * one.astype(F32), hidden_cot * two.astype(F32)], axis=0).astype(BF16)
        keep("gu", m, dot(normed, cots, NT).astype(BF16))
        back += dot(w_gu(m), cots, NN)
    done()
    keep("gain", 0, jnp.sum(back * hat, axis=1, keepdims=True))
    d = back * gain
    middle_cot = branch.astype(F32) + inv_sigma * (
        d - jnp.mean(d, axis=0, keepdims=True) - hat * jnp.mean(d * hat, axis=0, keepdims=True)
    )
    mcot_ref[...] = middle_cot
    attn_cot = middle_cot.astype(BF16)
    for m in range(parts):
        back_heads = dot(w_out(m), attn_cot, TN)
        for h in range(heads):
            head = m * heads + h
            rows = slice(h * HDIM, (h + 1) * HDIM)
            cot = back_heads[rows] * inv_ref[head]
            inner = jnp.sum(cot * heads_ref[head * HDIM : (head + 1) * HDIM].astype(F32), axis=0, keepdims=True)
            high = inner.astype(BF16).astype(F32)
            pad = jnp.zeros((AUG - HDIM - 2, own), F32)
            do_ref[head] = jnp.concatenate([cot, high, inner - high, pad], axis=0).astype(BF16)
    for m in range(parts):
        keep("out", m, dot(attn_cot, heads_ref[m * width : (m + 1) * width], NT).astype(BF16))


def mid_kernel(
    units, len_ref, tok_hbm, cot_hbm, heads_ref, inv_ref, two_ref, w_hbm,
    out_ref, mcot_ref, do_ref, g_ref, o_ref, gain_ref, tok_ref, cot_ref, w_ref, load,
):
    own = tok_ref.shape[0]
    me = lax.axis_index("mp")
    mine = pl.ds(pl.multiple_of(me * own, own), own)
    loads = [
        pltpu.make_async_copy(tok_hbm.at[mine], tok_ref, load.at[0]),
        pltpu.make_async_copy(cot_hbm.at[mine], cot_ref, load.at[1]),
        pltpu.make_async_copy(w_hbm, w_ref, load.at[2]),
    ]
    for copy in loads:
        copy.start()
    for copy in loads:
        copy.wait()
    pair = 2 * units

    def keep(what, m, made):
        if what == "gu":
            g_ref[m, :, :pair] = made
        elif what == "down":
            g_ref[m, :, pair:] = made
        elif what == "out":
            o_ref[m] = made
        else:
            gain_ref[...] = made

    nothing = lambda: None
    middle(
        len_ref, me, tok_ref, cot_ref, heads_ref, inv_ref, w_ref, two_ref[...].astype(F32), units, out_ref, mcot_ref, do_ref,
        keep, nothing, nothing,
    )


def mid(n_mp, lengths, tokens, out_grad, heads_out, inv, gain, w_rest, units):
    features, own = heads_out.shape
    heads = inv.shape[0]
    vm = pl.BlockSpec(memory_space=pltpu.VMEM)
    hbm = pl.BlockSpec(memory_space=pl.ANY)
    return pl.pallas_call(
        functools.partial(mid_kernel, units),
        in_specs=[pl.BlockSpec(memory_space=pltpu.SMEM), hbm, hbm, vm, vm, vm, hbm],
        out_specs=[vm] * 6,
        out_shape=[
            jax.ShapeDtypeStruct((own, features), BF16),
            jax.ShapeDtypeStruct((features, own), F32),
            jax.ShapeDtypeStruct((heads, AUG, own), BF16),
            jax.ShapeDtypeStruct((n_mp, features, 3 * units), BF16),
            jax.ShapeDtypeStruct((n_mp, features, features // n_mp), BF16),
            jax.ShapeDtypeStruct((features, 1), F32),
        ],
        scratch_shapes=[
            pltpu.VMEM((own, features), BF16),
            pltpu.VMEM((own, features), BF16),
            pltpu.VMEM(w_rest.shape, BF16),
            pltpu.SemaphoreType.DMA((3,)),
        ],
        compiler_params=pltpu.CompilerParams(vmem_limit_bytes=VMEM_BYTES),
        name="mid",
    )(lengths, tokens, out_grad, heads_out, inv, gain, w_rest)


SLOTS = 7
LAG = 4


def backward_kernel(nz, units, *refs):
    len_ref, q_ref, k_ref, v_ref, p_ref, cos_ref, sin_ref, n1_ref, heads_ref, inv_ref, wa_ref, tok_hbm, cot_hbm, wb_hbm, wr_hbm = refs[:15]
    dq_ref, dr_ref, gains_ref, in_full, out_full = refs[15:20]
    wb_ref, wr_ref, gr_ref, do_ref, mcot_ref, pc_ref, qc_ref, acc_ref, gc_ref, va_ref, tok_ref, cot_ref, own_ref, load = refs[20:34]
    refs = refs[34:]
    gq_ref = wr_ref.at[:, :, pl.ds(0, dq_ref.shape[1])]
    rest = Scatter(nz, (0, 1), gr_ref, gr_ref, dr_ref, *refs[:6])
    low = Scatter(nz, (0,), gq_ref, gq_ref, dq_ref, *refs[6:12])
    high = Scatter(nz, (1,), gq_ref, gq_ref, dq_ref, *refs[12:18])
    fold = Fold(*refs[18:23])
    in_share = Share(own_ref.at[0], in_full, *refs[23:26])
    out_share = Share(own_ref.at[1], out_full, *refs[26:29])
    gains = Everyone(*refs[29:33])
    step, heads = pl.program_id(0) - 1, pl.num_programs(0) - 1
    parts = wa_ref.shape[0]
    features, own = n1_ref.shape
    rows = k_ref.shape[1]
    width = features // parts
    per = width // HDIM
    me = lax.axis_index("mp")
    mine = pl.ds(pl.multiple_of(me * own, own), own)
    late = pltpu.make_async_copy(wb_hbm, wb_ref, load.at[3])
    three = 3 * HDIM
    shards = features // gains_ref.shape[1]

    def put(row, column):
        for i in range(shards):
            at = row * shards + i
            gains.held[0, at : at + 1, : features // shards] = column[i * (features // shards) : (i + 1) * (features // shards)].T

    @pl.when(step < 0)
    def _():
        gains.held[0] = jnp.zeros(gains.held.shape[1:], F32)
        loads = [
            pltpu.make_async_copy(wr_hbm, wr_ref.at[:, :, pl.ds(0, wr_hbm.shape[2])], load.at[0]),
            pltpu.make_async_copy(tok_hbm.at[mine], tok_ref, load.at[1]),
            pltpu.make_async_copy(cot_hbm.at[mine], cot_ref, load.at[2]),
        ]
        for copy in loads:
            copy.start()
        greet(peers(nz))
        for copy in loads:
            copy.wait()
        late.start()
        pair = 2 * units
        for m in range(parts):
            wr_ref[m, :, wr_hbm.shape[2] :] = wa_ref[m, :, 256 - units % 128 :]

        def keep(what, m, made):
            if what == "gu":
                gr_ref[m, :, :pair] = made
            elif what == "down":
                gr_ref[m, :, pair:] = made
            elif what == "out":
                wr_ref[m, :, 3 * width : 4 * width] = made
            else:
                put(1, made)

        middle(
            len_ref, me, tok_ref, cot_ref, heads_ref, inv_ref, wr_ref, wa_ref[0, :, three + 1 : three + 2].astype(F32), units,
            own_ref.at[1], mcot_ref, do_ref, keep,
            lambda: out_share.begin(0), lambda: rest.begin(2, 3),
        )
        va_ref[HDIM:] = jnp.full((AUG - HDIM, rows), -1.0, BF16)
        acc_ref[...] = jnp.zeros_like(acc_ref)
        gc_ref[...] = jnp.zeros_like(gc_ref)
        late.wait()

    def collect(head):
        at = lax.rem(head, per) * three
        pc_ref[pl.ds(pl.multiple_of(at + HDIM, HDIM), 2 * HDIM)] = fold.end(head)

    def close(part):
        for i in range(per):
            pc_ref[i * three : i * three + HDIM] = qc_ref[lax.rem(part, 3), i * HDIM : (i + 1) * HDIM]
        made = dot(n1_ref[...], pc_ref[...], NT)
        wr_ref[part, :, : 3 * width] = made.astype(BF16)
        weights = jnp.concatenate([wa_ref[part, :, :three], wb_ref[part]], axis=1)
        gc_ref[...] += jnp.sum(made * weights.astype(F32), axis=1, keepdims=True)
        acc_ref[...] += dot(weights, pc_ref[...], NN)

    @pl.when(step >= 0)
    def _():
        va_ref[:HDIM] = v_ref[...]
        cot = dot(va_ref[...], do_ref[step], TN)
        probs = p_ref[0]
        score_cot = probs * cot.astype(BF16)
        dv = dot(do_ref[step, :HDIM], probs, NT).astype(BF16)
        dk = turn(dot(q_ref[...], score_cot, NT) * LN2, cos_ref[...], sin_ref[...], 1, True).astype(BF16)
        dq = turn(dot(k_ref[...], score_cot, NN) * SCALE, cos_ref[:, mine], sin_ref[:, mine], 1, True)
        slot = lax.rem(step, SLOTS)
        for m in range(parts):
            fold.part[slot, m, :HDIM] = dk[:, m * own : (m + 1) * own]
            fold.part[slot, m, HDIM:] = dv[:, m * own : (m + 1) * own]
        at = pl.ds(pl.multiple_of(lax.rem(step, per) * HDIM, HDIM), HDIM)
        qc_ref[lax.rem(step // per, 3), at] = dq.astype(BF16)

        @pl.when(step >= LAG)
        def _():
            collect(step - LAG)

        @pl.when(step >= 1)
        def _():
            fold.chip(step - 1)

        fold.begin(step)

        @pl.when((step >= LAG) & (lax.rem(step - LAG, per) == per - 1))
        def _():
            close((step - LAG) // per)

    sums = {"rest": rest, "low": low, "high": high, "out": out_share, "gains": gains}
    for at, which, name, *d in SUM_STEPS:
        pl.when(step == at)(functools.partial(getattr(sums[which], name), *d))

    @pl.when(step == heads - 1)
    def _():
        fold.chip(step)
        for back in range(LAG - 1, -1, -1):
            collect(step - back)
            if (heads - 1 - back) % per == per - 1:
                close((step - back) // per)
        high.begin(2, 3, 1, 0)
        gain = wa_ref[0, :, three : three + 1].astype(F32)
        put(0, gc_ref[...] / gain)
        gains.begin()
        own_ref[0] = finish(tok_ref[...], gain, acc_ref[...], mcot_ref[...])
        in_share.begin(0)
        for which, name, *d in LAST_STEPS:
            getattr(sums[which], name)(*d)
        in_share.on(0)
        for which in (rest, low, high):
            which.along()
        gains.hop(4)
        for which in (rest, low, high):
            which.end()
        out_share.end()
        in_share.end()
        made = gains.end()
        dp = lax.axis_index("dp")
        for row in range(2):
            for i in range(shards):

                @pl.when(dp == i)
                def _():
                    gains_ref[row : row + 1] = made[row * shards + i : row * shards + i + 1, : features // shards]


SUM_STEPS = (
    (-1, "rest", "chip", 2),
    (-1, "rest", "cross", 2),
    (-1, "rest", "begin", 1, 0),
    (-1, "rest", "chip", 3),
    (1, "rest", "chip", 1),
    (1, "rest", "chip", 0),
    (1, "out", "on", 0),
    (2, "rest", "over", 2),
    (2, "rest", "cross", 3),
    (5, "rest", "over", 3),
    (5, "rest", "cross", 1),
    (8, "rest", "over", 1),
    (8, "rest", "cross", 0),
    (9, "low", "begin", 2, 3, 1, 0),
    (10, "low", "chip", 2),
    (10, "low", "chip", 3),
    (10, "low", "chip", 1),
    (10, "low", "chip", 0),
    (11, "rest", "over", 0),
    (11, "low", "cross", 2),
    (11, "low", "cross", 3),
)
LAST_STEPS = (
    ("high", "chip", 2),
    ("high", "chip", 3),
    ("high", "chip", 1),
    ("high", "chip", 0),
    ("low", "over", 2),
    ("low", "cross", 1),
    ("low", "over", 3),
    ("low", "cross", 0),
    ("low", "over", 1),
    ("high", "cross", 2),
    ("high", "cross", 3),
    ("low", "over", 0),
    ("gains", "hop", 0),
    ("high", "over", 2),
    ("high", "cross", 1),
    ("high", "cross", 0),
    ("gains", "hop", 1),
    ("high", "over", 3),
    ("gains", "hop", 2),
    ("high", "over", 1),
    ("gains", "hop", 3),
    ("high", "over", 0),
)


def backward(nz, lengths, q, k, v, p, cos, sin, n1, heads_out, inv, tokens, out_grad, w_a, w_b, w_rest, units):
    (features, own), rows = q.shape, k.shape[1]
    n_mp = w_a.shape[0]
    heads = features // HDIM
    width = features // n_mp
    depth = features // (2 * nz)
    columns = 4 * width, 3 * units
    hbm = pl.BlockSpec(memory_space=pl.ANY)
    vm = pl.BlockSpec(memory_space=pltpu.VMEM)
    row = lambda h: (jnp.maximum(h - 1, 0), 0)
    cube = lambda h: (jnp.maximum(h - 1, 0), 0, 0)
    dma = pltpu.SemaphoreType.DMA
    return pl.pallas_call(
        functools.partial(backward_kernel, nz, units),
        grid=(heads + 1,),
        in_specs=[
            pl.BlockSpec(memory_space=pltpu.SMEM),
            pl.BlockSpec((HDIM, own), row),
            pl.BlockSpec((HDIM, rows), row),
            pl.BlockSpec((HDIM, rows), row),
            pl.BlockSpec((1, rows, own), cube),
        ]
        + [vm] * 6
        + [hbm] * 4,
        out_specs=[vm, vm, vm, hbm, hbm],
        out_shape=[
            jax.ShapeDtypeStruct((depth, columns[0]), F32),
            jax.ShapeDtypeStruct((depth, columns[1]), F32),
            jax.ShapeDtypeStruct((2, depth), F32),
            jax.ShapeDtypeStruct((rows, features), BF16),
            jax.ShapeDtypeStruct((rows, features), BF16),
        ],
        scratch_shapes=[
            pltpu.VMEM(w_b.shape, BF16),
            pltpu.VMEM((n_mp, features, width + 3 * units), BF16),
            pltpu.VMEM((n_mp, features, 3 * units), BF16),
            pltpu.VMEM((heads, AUG, own), BF16),
            pltpu.VMEM((features, own), F32),
            pltpu.VMEM((3 * width, own), BF16),
            pltpu.VMEM((3, width, own), BF16),
            pltpu.VMEM((features, own), F32),
            pltpu.VMEM((features, 1), F32),
            pltpu.VMEM((AUG, rows), BF16),
            pltpu.VMEM((own, features), BF16),
            pltpu.VMEM((own, features), BF16),
            pltpu.VMEM((2, own, features), BF16),
            dma((4,)),
        ]
        + Scatter.scratch(nz, (0, 1), depth, columns[1])
        + Scatter.scratch(nz, (0,), depth, columns[0])
        + Scatter.scratch(nz, (1,), depth, columns[0])
        + Fold.scratch(n_mp, own, SLOTS)
        + Share.sems(1)
        + Share.sems(1)
        + Everyone.scratch(nz, 4 * nz),
        compiler_params=pltpu.CompilerParams(
            dimension_semantics=("arbitrary",), collective_id=3, has_side_effects=True, vmem_limit_bytes=VMEM_BYTES
        ),
        name="backward",
    )(lengths, q, k, v, p, cos, sin, n1, heads_out, inv, w_a, tokens, out_grad, w_b, w_rest)


def deliver_kernel(units, in_ref, out_ref, dq_ref, dr_ref, gains_ref, grad_ref, to_ref, gq_ref, go_ref, gg_ref, gd_ref, one_ref, two_ref):
    @pl.when(pl.program_id(0) == 0)
    def _():
        width = go_ref.shape[0]
        pair = 2 * units
        for r in range(width // HDIM):
            for i in range(3):
                at = (3 * r + i) * HDIM
                gq_ref[i, :, r * HDIM : (r + 1) * HDIM] = dq_ref[:, at : at + HDIM]
        go_ref[...] = dq_ref[:, 3 * width : 4 * width].T
        one_ref[...] = gains_ref[0:1]
        two_ref[...] = gains_ref[1:2]
        for i in range(2):
            gg_ref[:, i, :] = dr_ref[:, i * units : (i + 1) * units]
        gd_ref[...] = dr_ref[:, pair : pair + units].T

    grad_ref[...] = in_ref[...].astype(F32)
    to_ref[...] = out_ref[...]


def deliver(layer_out, input_grad, d_qkv, d_rest, gains, width, units):
    rows, features = input_grad.shape
    depth = d_qkv.shape[0]
    shape = lambda *s: jax.ShapeDtypeStruct(s, F32)
    shapes = [(3, depth, width), (width, depth), (depth, 2, units), (units, depth), (1, depth), (1, depth)]
    steps = 4
    slab = pl.BlockSpec((rows // steps, features), lambda i: (i, 0))
    return pl.pallas_call(
        functools.partial(deliver_kernel, units),
        grid=(steps,),
        in_specs=[slab, slab, whole(*d_qkv.shape), whole(*d_rest.shape), whole(*gains.shape)],
        out_specs=[slab, slab] + [whole(*s) for s in shapes],
        out_shape=[shape(rows, features), jax.ShapeDtypeStruct((rows, features), BF16)] + [shape(*s) for s in shapes],
        compiler_params=params("arbitrary"),
        name="deliver",
    )(input_grad, layer_out, d_qkv, d_rest, gains)


def per_device(n_dp, n_mp, tokens, out_grad, w_qkv, w_out, w_gu, w_down, gain_attn, gain_mlp, lengths):
    rows, features = tokens.shape
    depth = w_qkv.shape[0]
    units, width = w_down.shape[0], w_out.shape[0]
    everyone = ("mp", "dp")
    linked = n_mp == 4 and n_dp == 8 and depth % 32 == 0 and features // HDIM == 12
    nz = n_dp // 2 if linked else 0
    three = 3 * HDIM
    loose = units % 128
    columns = 256, 3 * width - three, 3 * units + width - loose
    wq = w_qkv.transpose(1, 0, 2)
    if linked:
        weights = wq, w_gu, w_out, w_down, gain_attn[None], gain_mlp[None]
        n1, q, k, v, cos, sin, heads_out, probs, inv, w_a, w_b, w_c = forward(
            nz, n_mp, units, lengths, tokens, weights, columns
        )
        d_qkv, d_rest, gains, in_full, layer_out = backward(
            nz, lengths, q, k, v, probs, cos, sin, n1, heads_out, inv, tokens, out_grad, w_a, w_b, w_c, units
        )
    else:
        by_head = w_qkv.reshape(depth, 3, width // HDIM, HDIM).transpose(0, 2, 1, 3).reshape(depth, 3 * width)
        blank = jnp.zeros((depth, columns[0] - three - 2), BF16)
        shards = [
            jnp.concatenate([by_head[:, :three], gain_attn[:, None], gain_mlp[:, None], blank], axis=1),
            by_head[:, three:],
            jnp.concatenate([w_gu.reshape(depth, -1), w_out.T, w_down.T], axis=1),
        ]
        w_a, w_b, w_c = (
            lax.all_gather(s, everyone, axis=0, tiled=True).reshape(n_mp, features, s.shape[1]) for s in shards
        )
        n1, q, k, v, cos, sin, heads_out, probs, inv = forward(nz, n_mp, units, lengths, tokens, [w_a, w_b], columns)
        layer_out, middle_cot, do, g_rest, g_out, gain_two = mid(
            n_mp, lengths, tokens, out_grad, heads_out, inv, w_a[0, :, three + 1 : three + 2], w_c, units
        )
        own = middle_cot.shape[1]
        swap = lambda g, a, b: g.reshape(n_mp, features, a, b, HDIM).swapaxes(2, 3).reshape(n_mp, features, 3 * width)
        natural = jnp.concatenate([w_a[..., :three], w_b], axis=2)
        natural = jnp.concatenate([swap(natural, width // HDIM, 3), w_a[..., three : three + 1]], axis=2)
        g_qkv, nc = last(q, k, v, do, probs, cos, sin, lax.all_gather(n1, "mp", axis=1, tiled=True), natural)
        gain_one = w_a[0, :, three : three + 1].astype(F32)
        tok = lax.dynamic_slice_in_dim(tokens, lax.axis_index("mp") * own, own, 0)
        nc_own = lax.psum_scatter(nc, "mp", scatter_dimension=0, tiled=True)[0]
        in_own = finish(tok, gain_one, nc_own.astype(F32), middle_cot)
        layer_out, in_full = (lax.all_gather(v, "mp", axis=0, tiled=True) for v in (layer_out, in_own))
        both = jnp.stack([g_qkv[0, :, -1].astype(F32), gain_two[:, 0]])
        both = lax.psum(both, everyone)
        gains = lax.dynamic_slice_in_dim(both, lax.axis_index("dp") * depth, depth, 1)
        g_qkv = jnp.concatenate([swap(g_qkv[..., : 3 * width], 3, width // HDIM), g_out], axis=2)
        d_qkv, d_rest = (
            lax.psum_scatter(
                g.reshape(n_mp * features, -1), everyone, scatter_dimension=0, tiled=True
            ).astype(F32)
            for g in (g_qkv, g_rest)
        )
    input_grad, layer_out, g_q, g_o, g_g, g_d, one, two = deliver(
        layer_out, in_full, d_qkv, d_rest, gains, width, units
    )
    return layer_out, input_grad, g_q.transpose(1, 0, 2), g_o, g_g, g_d, one[0], two[0]


def solution(mesh):
    n_dp, n_mp = mesh.shape["dp"], mesh.shape["mp"]
    return jax.shard_map(
        functools.partial(per_device, n_dp, n_mp),
        mesh=mesh,
        in_specs=(
            P("dp", None),
            P("dp", None),
            P("dp", None, "mp"),
            P("mp", "dp"),
            P("dp", None, "mp"),
            P("mp", "dp"),
            P("dp"),
            P("dp"),
            P("dp", None),
        ),
        out_specs=(
            P("dp", None),
            P("dp", None),
            P("dp", None, "mp"),
            P("mp", "dp"),
            P("dp", None, "mp"),
            P("mp", "dp"),
            P("dp"),
            P("dp"),
        ),
        check_vma=False,
    )
```

```python
import functools
import math

import jax
import jax.numpy as jnp
from jax import lax
from jax.experimental import pallas as pl
from jax.experimental.pallas import tpu as pltpu
from jax.sharding import PartitionSpec as P

HDIM = 64
HALF = HDIM // 2
AUG = HDIM + 16
EPS = 1e-05
ROPE_BASE = 160000.0
LOG2E = math.log2(math.e)
LN2 = math.log(2.0)
SCALE = HDIM ** (-0.5)
FAR = -1e30
BF16 = jnp.bfloat16
F32 = jnp.float32
VMEM_BYTES = 60 << 20
NN = (((1,), (0,)), ((), ()))
NT = (((1,), (1,)), ((), ()))
TN = (((0,), (0,)), ((), ()))


def dot(a, b, dims):
    return lax.dot_general(a, b, dims, preferred_element_type=F32)


def params(*semantics):
    return pltpu.CompilerParams(
        dimension_semantics=semantics or None, vmem_limit_bytes=VMEM_BYTES
    )


def whole(*shape):
    return pl.BlockSpec(shape, lambda *i: (0,) * len(shape))


def layout_rows(len_ref, docs, first, rows):
    index = first + lax.broadcasted_iota(jnp.int32, (1, rows), 1)
    segment = jnp.zeros((1, rows), jnp.int32)
    start = jnp.zeros((1, rows), jnp.int32)
    end = jnp.int32(0)
    for j in range(docs):
        end = end + len_ref[0, j]
        past = index >= end
        segment = segment + jnp.where(past, 1, 0)
        start = jnp.where(past, jnp.maximum(start, end), start)
    return segment, index - start, index < end


def moments(columns):
    mean = jnp.mean(columns, axis=0, keepdims=True)
    centered = columns - mean
    return mean, lax.rsqrt(jnp.mean(centered * centered, axis=0, keepdims=True) + EPS)


def normalize(columns):
    mean, inv = moments(columns)
    return (columns - mean) * inv, inv


def turn(block, cos, sin, heads, back=False):
    out = []
    for h in range(heads):
        one = block[h * HDIM : h * HDIM + HALF]
        two = block[h * HDIM + HALF : (h + 1) * HDIM]
        if back:
            out += [one * cos + two * sin, two * cos - one * sin]
        else:
            out += [one * cos - two * sin, two * cos + one * sin]
    return jnp.concatenate(out, axis=0)


def gelu_parts(gate):
    phi = 0.5 * (1.0 + lax.erf(gate * math.sqrt(0.5)))
    density = jnp.exp2(gate * gate * (-0.5 * LOG2E)) * (1.0 / math.sqrt(2.0 * math.pi))
    return phi, gate * density


def last_kernel(own_axis, q_ref, k_ref, v_ref, do_ref, p_ref, cos_ref, sin_ref, n1_ref, w_ref, gq_ref, nc_ref, gc_ref, dq_ref, pc_ref, acc_ref, va_ref):
    step, head = pl.program_id(0), pl.program_id(1)
    per = pl.num_programs(1)
    features, rows = n1_ref.shape
    own = q_ref.shape[1]
    width = per * HDIM
    mine = pl.ds(pl.multiple_of(lax.axis_index(own_axis) * own, own), own)

    @pl.when((step == 0) & (head == 0))
    def _():
        va_ref[HDIM:] = jnp.full((AUG - HDIM, rows), -1.0, BF16)
        acc_ref[...] = jnp.zeros_like(acc_ref)
        gc_ref[...] = jnp.zeros_like(gc_ref)

    va_ref[:HDIM] = v_ref[...]
    cot = dot(va_ref[...], do_ref[0], TN)
    probs = p_ref[0]
    score_cot = probs * cot.astype(BF16)
    at = pl.ds(pl.multiple_of(head * HDIM, HDIM), HDIM)
    dv = dot(do_ref[0, :HDIM], probs, NT)
    dk = dot(q_ref[...], score_cot, NT) * LN2
    dq = dot(k_ref[...], score_cot, NN) * SCALE
    pc_ref[pl.ds(pl.multiple_of(width + head * HDIM, HDIM), HDIM)] = dv.astype(BF16)
    pc_ref[at] = turn(dk, cos_ref[...], sin_ref[...], 1, True).astype(BF16)
    dq_ref[at] = turn(dq, cos_ref[:, mine], sin_ref[:, mine], 1, True).astype(BF16)

    @pl.when(head == per - 1)
    def _():
        kv = dot(n1_ref[...], pc_ref[...], NT)
        q = dot(n1_ref[:, mine], dq_ref[...], NT)
        gq_ref[step, :, :width] = q.astype(BF16)
        gq_ref[step, :, width : 3 * width] = kv.astype(BF16)
        gc_ref[...] += jnp.sum(q * w_ref[0, :, :width].astype(F32), axis=1, keepdims=True) + jnp.sum(
            kv * w_ref[0, :, width : 3 * width].astype(F32), axis=1, keepdims=True
        )

        def spread(i, carry):
            cols = pl.ds(pl.multiple_of(i * own, own), own)
            acc_ref[:, cols] += dot(w_ref[0, :, width : 3 * width], pc_ref[:, cols], NN)
            return carry

        lax.fori_loop(0, rows // own, spread, 0)
        acc_ref[:, mine] += dot(w_ref[0, :, :width], dq_ref[...], NN)

    @pl.when((step == pl.num_programs(0) - 1) & (head == per - 1))
    def _():
        gain_cot = (gc_ref[...] / w_ref[0, :, 3 * width :].astype(F32)).astype(BF16)
        for m in range(gq_ref.shape[0]):
            nc_ref[m] = acc_ref[:, m * own : (m + 1) * own].astype(BF16)
            gq_ref[m, :, 3 * width :] = gain_cot


def last(q, k, v, do, p, cos, sin, n1, w_qkv, own_axis="mp"):
    (features, own), rows = q.shape, k.shape[1]
    parts = w_qkv.shape[0]
    per = features // parts // HDIM
    width = per * HDIM
    head = lambda m, h: (m * per + h, 0)
    return pl.pallas_call(
        functools.partial(last_kernel, own_axis),
        grid=(parts, per),
        in_specs=[
            pl.BlockSpec((HDIM, own), head),
            pl.BlockSpec((HDIM, rows), head),
            pl.BlockSpec((HDIM, rows), head),
            pl.BlockSpec((1, AUG, own), lambda m, h: (m * per + h, 0, 0)),
            pl.BlockSpec((1, rows, own), lambda m, h: (m * per + h, 0, 0)),
            whole(HALF, rows),
            whole(HALF, rows),
            whole(features, rows),
            pl.BlockSpec((1,) + w_qkv.shape[1:], lambda m, h: (m, 0, 0)),
        ],
        out_specs=[
            whole(*w_qkv.shape),
            whole(parts, features, own),
        ],
        out_shape=[
            jax.ShapeDtypeStruct(w_qkv.shape, BF16),
            jax.ShapeDtypeStruct((parts, features, own), BF16),
        ],
        scratch_shapes=[
            pltpu.VMEM((features, 1), F32),
            pltpu.VMEM((width, own), BF16),
            pltpu.VMEM((2 * width, rows), BF16),
            pltpu.VMEM((features, rows), F32),
            pltpu.VMEM((AUG, rows), BF16),
        ],
        compiler_params=params("arbitrary", "arbitrary"),
        name="last",
    )(q, k, v, do, p, cos, sin, n1, w_qkv)


def place():
    dp, mp = lax.axis_index("dp"), lax.axis_index("mp")
    return dp // 2, lax.rem(dp, 2), mp // 2, lax.rem(mp, 2)


def device(z, x, y, c):
    return (2 * z + x, 2 * y + c)


def remote(src, dst, send, recv, target):
    return pltpu.make_async_remote_copy(
        src_ref=src, dst_ref=dst, send_sem=send, recv_sem=recv,
        device_id=target, device_id_type=pl.DeviceIdType.MESH,
    )


def greet(targets):
    barrier = pltpu.get_barrier_semaphore()
    for target in targets:
        pl.semaphore_signal(barrier, inc=1, device_id=target, device_id_type=pl.DeviceIdType.MESH)
    pl.semaphore_wait(barrier, len(targets))


def peers(nz):
    z, x, y, c = place()
    across = [device(z, 1 - x, y, c), device(z, x, 1 - y, c), device(z, x, y, 1 - c)]
    return across + [device(lax.bitwise_xor(z, d), x, y, c) for d in range(1, nz)]


class Gather:
    def __init__(self, nz, src, full, send, recv, local, eager=False):
        self.nz, self.src, self.full, self.send, self.recv, self.local = nz, src, full, send, recv, local
        self.eager = eager
        self.depth = src.shape[0]
        self.index = {}
        for kind in ("Z", "X", "Y", "S", "YA", "XB", "SX", "SY", "SA", "SB"):
            for d in range(1 if kind == "Z" else 0, nz):
                self.index[kind, d] = len(self.index)

    @staticmethod
    def count(nz):
        return nz - 1 + 9 * nz

    def block(self, z, x, y, c, half=None):
        first, size = (0, self.depth) if half is None else (half * self.depth // 2, self.depth // 2)
        return self.full.at[2 * y + c, pl.ds(pl.multiple_of((2 * z + x) * self.depth + first, 16), size)]

    def message(self, kind, d, sending):
        z, x, y, c = place()
        back = lax.bitwise_xor(z, d)
        sx, sy, sib = device(z, 1 - x, y, c), device(z, x, 1 - y, c), device(z, x, y, 1 - c)
        sent, got, half, target = {
            "Z": ((z, x, y, c), (back, x, y, c), None, device(back, x, y, c)),
            "X": ((back, x, y, c), (back, 1 - x, y, c), None, sx),
            "Y": ((back, x, y, c), (back, x, 1 - y, c), None, sy),
            "S": ((back, x, y, c), (back, x, y, 1 - c), None, sib),
            "YA": ((back, 1 - x, y, c), (back, 1 - x, 1 - y, c), 0, sy),
            "XB": ((back, x, 1 - y, c), (back, 1 - x, 1 - y, c), 1, sx),
            "SX": ((back, 1 - x, y, c), (back, 1 - x, y, 1 - c), None, sib),
            "SY": ((back, x, 1 - y, c), (back, x, 1 - y, 1 - c), None, sib),
            "SA": ((back, 1 - x, 1 - y, c), (back, 1 - x, 1 - y, 1 - c), 0, sib),
            "SB": ((back, 1 - x, 1 - y, c), (back, 1 - x, 1 - y, 1 - c), 1, sib),
        }[kind]
        i = self.index[kind, d]
        at = self.block(*(sent if sending else got), half)
        own = sending and (kind == "Z" or (d == 0 and kind in ("X", "Y", "S")))
        return remote(self.src if own else at, at, self.send.at[i], self.recv.at[i], target)

    def start(self, kind, d):
        self.message(kind, d, True).start()

    def arrived(self, kind, d):
        self.message(kind, d, False).wait_recv()

    def own(self):
        z, x, y, c = place()
        return pltpu.make_async_copy(self.src, self.block(z, x, y, c), self.local)

    def begin(self):
        for d in range(1, self.nz if self.eager else 2):
            self.start("Z", d)
        for kind in ("X", "Y", "S"):
            self.start(kind, 0)
        self.own().start()

    def push(self, d):
        self.start("Z", d)

    def all_along(self):
        for d in range(1, self.nz):
            self.along(d)

    def all_over(self):
        for d in range(self.nz):
            self.over(d)

    def rest(self):
        for d in range(self.nz):
            self.corner(d)
        self.end()

    def along(self, d):
        self.arrived("Z", d)
        for kind in ("X", "Y", "S"):
            self.start(kind, d)

    def over(self, d):
        self.arrived("X", d)
        self.start("YA", d)
        self.start("SX", d)
        self.arrived("Y", d)
        self.start("XB", d)
        self.start("SY", d)

    def corner(self, d):
        self.arrived("YA", d)
        self.start("SA", d)
        self.arrived("XB", d)
        self.start("SB", d)

    def end(self):
        self.own().wait()
        for d in range(self.nz):
            for kind in ("S", "SX", "SY", "SA", "SB"):
                self.arrived(kind, d)
        for kind, d in self.index:
            self.message(kind, d, True).wait_send()


class Share:
    def __init__(self, src, full, send, recv, local, pieces=1):
        self.src, self.full, self.send, self.recv, self.local, self.pieces = src, full, send, recv, local, pieces
        self.size = src.shape[0] // pieces

    @staticmethod
    def sems(pieces):
        dma = pltpu.SemaphoreType.DMA
        return [dma((3 * pieces,)), dma((3 * pieces,)), dma((pieces,))]

    def rows(self, y, c, i):
        own = self.size * self.pieces
        return pl.ds(pl.multiple_of((2 * y + c) * own + i * self.size, 16), self.size)

    def message(self, kind, i):
        z, x, y, c = place()
        n = self.pieces
        piece = self.src.at[pl.ds(i * self.size, self.size)]
        if kind == "own":
            return pltpu.make_async_copy(piece, self.full.at[self.rows(y, c, i)], self.local.at[i])
        k = {"Y": 0, "C": 1, "F": 2}[kind] * n + i
        sems = self.send.at[k], self.recv.at[k]
        sib = device(z, x, y, 1 - c)
        if kind == "Y":
            return remote(piece, self.full.at[self.rows(y, c, i)], *sems, device(z, x, 1 - y, c))
        if kind == "C":
            return remote(piece, self.full.at[self.rows(y, c, i)], *sems, sib)
        at = self.full.at[self.rows(1 - y, c, i)]
        return remote(at, at, *sems, sib)

    def begin(self, i):
        for kind in ("Y", "C", "own"):
            self.message(kind, i).start()

    def on(self, i):
        self.message("Y", i).wait_recv()
        self.message("F", i).start()

    def end(self):
        for i in range(self.pieces):
            self.message("own", i).wait()
            self.message("C", i).wait_recv()
            self.message("F", i).wait_recv()
            for kind in ("Y", "C", "F"):
                self.message(kind, i).wait_send()


def finish(tokens, gain, cot, middle_cot):
    hat, inv_sigma = normalize(tokens.T.astype(F32))
    d = cot * gain
    made = middle_cot + inv_sigma * (
        d - jnp.mean(d, axis=0, keepdims=True) - hat * jnp.mean(d * hat, axis=0, keepdims=True)
    )
    return made.T.astype(BF16)


class Scatter:
    def __init__(self, nz, ups, src, part, out, core, side, line, last, send, recv):
        self.nz, self.ups, self.src, self.part, self.out = nz, ups, src, part, out
        self.core, self.side, self.line, self.last, self.send, self.recv = core, side, line, last, send, recv
        self.depth = out.shape[0]

    @staticmethod
    def scratch(nz, ups, depth, columns):
        count = len(ups) * nz + 2 * nz
        return [
            pltpu.VMEM((len(ups), 2 * nz * depth, columns), BF16),
            pltpu.VMEM((len(ups), nz * depth, columns), BF16),
            pltpu.VMEM((nz, len(ups), depth, columns), BF16),
            pltpu.VMEM((depth, columns), BF16),
            pltpu.SemaphoreType.DMA((count,)),
            pltpu.SemaphoreType.DMA((count,)),
        ]

    def row(self, d):
        z, _, _, _ = place()
        return lax.bitwise_xor(z, d)

    def rows(self, d, x):
        return pl.ds(pl.multiple_of((2 * self.row(d) + x) * self.depth, 16), self.depth)

    def both(self, d):
        return pl.ds(pl.multiple_of(2 * self.row(d) * self.depth, 16), 2 * self.depth)

    def lane(self, d):
        return pl.ds(pl.multiple_of(self.row(d) * self.depth, 16), self.depth)

    def message(self, kind, d, u=0):
        z, x, y, c = place()
        nz, n = self.nz, len(self.ups)
        i = {"C": u * nz + d, "X": n * nz + d, "Z": n * nz + nz + d, "Y": n * nz + nz}[kind]
        sems = self.send.at[i], self.recv.at[i]
        if kind == "C":
            both = self.both(d)
            return remote(self.src.at[2 * self.ups[u] + 1 - c, both], self.core.at[u, both], *sems, device(z, x, y, 1 - c))
        if kind == "X":
            return remote(
                self.core.at[:, self.rows(d, 1 - x)], self.side.at[:, self.lane(d)], *sems, device(z, 1 - x, y, c)
            )
        if kind == "Z":
            return remote(self.side.at[:, self.lane(d)], self.line.at[d], *sems, device(self.row(d), x, y, c))
        return remote(self.line.at[0, 1 - y if n == 2 else 0], self.last, *sems, device(z, x, 1 - y, c))

    def begin(self, *rows):
        for d in rows:
            for u in range(len(self.ups)):
                self.message("C", d, u).start()

    def cross(self, d):
        self.message("X", d).start()

    def chip(self, d):
        _, x, _, c = place()
        for u in range(len(self.ups)):
            self.message("C", d, u).wait_recv()
        for side in range(2):
            rows = self.rows(d, side)
            for u, up in enumerate(self.ups):
                self.core[u, rows] = self.part[2 * up + c, rows] + self.core[u, rows]

    def over(self, d):
        _, x, _, _ = place()
        self.message("X", d).wait_recv()
        rows, lane = self.rows(d, x), self.lane(d)
        for u in range(len(self.ups)):
            self.side[u, lane] = self.core[u, rows] + self.side[u, lane]
        if d:
            self.message("Z", d).start()

    def along(self):
        _, _, y, _ = place()
        for d in range(1, self.nz):
            self.message("Z", d).wait_recv()
        lane = self.lane(0)
        for u in range(len(self.ups)):
            made = self.side[u, lane].astype(F32)
            for d in range(1, self.nz):
                made += self.line[d, u].astype(F32)
            self.line[0, u] = made.astype(BF16)
        if len(self.ups) == 2:
            self.message("Y", 0).start()
        else:
            pl.when(y != self.ups[0])(lambda: self.message("Y", 0).start())

    def end(self):
        _, _, y, _ = place()

        def receive():
            self.message("Y", 0).wait_recv()
            mine = self.line[0, y if len(self.ups) == 2 else 0]
            self.out[...] = mine.astype(F32) + self.last[...].astype(F32)

        if len(self.ups) == 2:
            receive()
            self.message("Y", 0).wait_send()
        else:
            pl.when(y == self.ups[0])(receive)
            pl.when(y != self.ups[0])(lambda: self.message("Y", 0).wait_send())
        for d in range(self.nz):
            for u in range(len(self.ups)):
                self.message("C", d, u).wait_send()
            self.message("X", d).wait_send()
            if d:
                self.message("Z", d).wait_send()


class Everyone:
    def __init__(self, held, got, send, recv):
        self.held, self.got, self.send, self.recv = held, got, send, recv
        self.hops = got.shape[0]

    @staticmethod
    def scratch(nz, rows):
        hops = 3 + nz.bit_length() - 1
        dma = pltpu.SemaphoreType.DMA
        return [pltpu.VMEM((hops + 1, rows, 128), F32), pltpu.VMEM((hops, rows, 128), F32), dma((hops,)), dma((hops,))]

    def message(self, i):
        z, x, y, c = place()
        target = (
            device(z, x, y, 1 - c) if i == 0
            else device(z, x, 1 - y, c) if i == 1
            else device(z, 1 - x, y, c) if i == 2
            else device(lax.bitwise_xor(z, 1 << (i - 3)), x, y, c)
        )
        return remote(self.held.at[i], self.got.at[i], self.send.at[i], self.recv.at[i], target)

    def begin(self):
        self.message(0).start()

    def hop(self, i):
        self.message(i).wait_recv()
        self.held[i + 1] = self.held[i] + self.got[i]
        if i + 1 < self.hops:
            self.message(i + 1).start()

    def end(self):
        for i in range(self.hops):
            self.message(i).wait_send()
        return self.held[self.hops]


class Fold:
    def __init__(self, part, near, far, send, recv):
        self.part, self.near, self.far, self.send, self.recv = part, near, far, send, recv
        self.slots = part.shape[0]

    @staticmethod
    def scratch(n_mp, own, slots):
        dma = pltpu.SemaphoreType.DMA
        return [
            pltpu.VMEM((slots, n_mp, 2 * HDIM, own), BF16),
            pltpu.VMEM((slots, 2, 2 * HDIM, own), BF16),
            pltpu.VMEM((slots, 2 * HDIM, own), BF16),
            dma((slots, 3)),
            dma((slots, 3)),
        ]

    def message(self, kind, head):
        z, x, y, c = place()
        slot = lax.rem(head, self.slots)
        k = {"far": 0, "near": 1, "Y": 2}[kind]
        sems = self.send.at[slot, k], self.recv.at[slot, k]
        if kind == "Y":
            return remote(self.near.at[slot, 1 - y], self.far.at[slot], *sems, device(z, x, 1 - y, c))
        up = 1 - y if kind == "far" else y
        return remote(self.part.at[slot, 2 * up + 1 - c], self.near.at[slot, up], *sems, device(z, x, y, 1 - c))

    def begin(self, head):
        self.message("far", head).start()
        self.message("near", head).start()

    def chip(self, head):
        _, _, y, c = place()
        slot = lax.rem(head, self.slots)
        self.message("far", head).wait_recv()
        self.near[slot, 1 - y] = self.part[slot, 2 * (1 - y) + c] + self.near[slot, 1 - y]
        self.message("Y", head).start()

    def end(self, head):
        _, _, y, c = place()
        slot = lax.rem(head, self.slots)
        self.message("near", head).wait_recv()
        self.message("Y", head).wait_recv()
        made = self.part[slot, 2 * y + c].astype(F32) + self.near[slot, y].astype(F32) + self.far[slot].astype(F32)
        for kind in ("far", "near", "Y"):
            self.message(kind, head).wait_send()
        return made.astype(BF16)


def forward_kernel(nz, units, len_ref, tok_ref, *refs):
    linked = nz > 0
    given, refs = refs[: 6 if linked else 2], refs[6 if linked else 2 :]
    mine_ref, q_ref, k_ref, v_ref, cos_ref, sin_ref, o_ref, p_ref, inv_ref = refs[:9]
    full_refs, refs = refs[9 : 12 if linked else 9], refs[12 if linked else 9 :]
    wa_ref, wb_ref, w_ref, n1_ref, ka_ref, qa_ref, va_ref, stat_ref, load = refs[:9]
    refs = refs[9:]
    rows, features = tok_ref.shape
    own = q_ref.shape[1]
    docs = len_ref.shape[1]
    step = pl.program_id(0)
    parts = wa_ref.shape[0]
    part, turn_at = lax.rem(step, parts), step // parts
    me = lax.axis_index("mp")
    mine = pl.ds(pl.multiple_of(me * own, own), own)
    three = 3 * HDIM

    if linked:
        srcs = refs[:3]
        one = Gather(nz, srcs[0], wa_ref, *refs[3:6], eager=True)
        two = Gather(nz, srcs[1], wb_ref, *refs[6:9], eager=True)
        last = Gather(nz, srcs[2], full_refs[2], *refs[9:12])
        keeps = [
            pltpu.make_async_copy(wa_ref, full_refs[0], load.at[0]),
            pltpu.make_async_copy(wb_ref, full_refs[1], load.at[1]),
        ]

    @pl.when(step == 0)
    def _():
        if linked:
            wq_ref, wg_ref, wo_ref, wd_ref, one_ref, two_ref = given
            for i in range(3):
                srcs[0][:, i * HDIM : (i + 1) * HDIM] = wq_ref[i, :, :HDIM]
            srcs[0][:, three : three + 1] = one_ref[...].astype(F32).T.astype(BF16)
            srcs[0][:, three + 1 : three + 2] = two_ref[...].astype(F32).T.astype(BF16)
            down = wd_ref[...].T
            srcs[0][:, 256 - units % 128 :] = down[:, units - units % 128 :]
            greet(peers(nz))
            one.begin()
            for r in range(1, wq_ref.shape[2] // HDIM):
                for i in range(3):
                    at = (r - 1) * three + i * HDIM
                    srcs[1][:, at : at + HDIM] = wq_ref[i, :, r * HDIM : (r + 1) * HDIM]
            two.begin()
            pair, width = 2 * units, wo_ref.shape[0]
            for i in range(2):
                srcs[2][:, i * units : (i + 1) * units] = wg_ref[:, i, :]
            srcs[2][:, pair : pair + width] = wo_ref[...].T
            srcs[2][:, pair + width :] = down[:, : units - units % 128]
        else:
            fetches = [pltpu.make_async_copy(g, w, load.at[i]) for i, (g, w) in enumerate(zip(given, (wa_ref, wb_ref)))]
            for fetch in fetches:
                fetch.start()
        _, position, _ = layout_rows(len_ref, docs, 0, rows)
        power = lax.broadcasted_iota(jnp.int32, (HALF, 1), 0).astype(F32) * (-2.0 / HDIM * math.log2(ROPE_BASE))
        angle = position.astype(F32) * jnp.exp2(power)
        cos_ref[...] = jnp.cos(angle)
        sin_ref[...] = jnp.sin(angle)
        keys, _, _ = layout_rows(len_ref, docs, 0, rows)
        queries, _, _ = layout_rows(len_ref, docs, me * own, own)
        kind = lax.broadcasted_iota(jnp.int32, (AUG - HDIM, 1), 0)
        ka_ref[HDIM:] = jnp.where(kind == keys, 1.0, 0.0).astype(BF16)
        qa_ref[HDIM:] = jnp.where(kind == queries, 0.0, FAR).astype(BF16)
        va_ref[HDIM:] = jnp.ones((AUG - HDIM, rows), BF16)

        def measure(i, carry):
            at = pl.ds(pl.multiple_of(i * own, own), own)
            turned = tok_ref[at, :].T
            n1_ref[:, at] = turned
            mean, inv = moments(turned.astype(F32))
            stat_ref[0:1, at] = mean
            stat_ref[1:2, at] = inv
            return carry

        if linked:
            one.all_along()
        lax.fori_loop(0, rows // own, measure, 0)
        if linked:
            one.all_over()
            last.begin()
            one.rest()
            keeps[0].start()
        else:
            for fetch in fetches:
                fetch.wait()
        gain = wa_ref[0, :, three : three + 1].astype(F32)

        def norm(i, carry):
            at = pl.ds(pl.multiple_of(i * own, own), own)
            made = (n1_ref[:, at].astype(F32) - stat_ref[0:1, at]) * stat_ref[1:2, at] * gain
            n1_ref[:, at] = made.astype(BF16)
            return carry

        lax.fori_loop(0, rows // own, norm, 0)
        mine_ref[...] = n1_ref[:, mine]

    if linked:
        gathers = {"two": two, "last": last}
        for at, which, name, *d in GATHER_STEPS:
            pl.when(step == at)(functools.partial(getattr(gathers[which], name), *d))

        @pl.when(step == parts)
        def _():
            two.rest()
            keeps[1].start()

    @pl.when(turn_at == 0)
    def _():
        w_ref[...] = wa_ref[part, :, :three]

    for r in range(1, 1 + wb_ref.shape[2] // three):

        @pl.when(turn_at == r)
        def _():
            w_ref[...] = wb_ref[part, :, (r - 1) * three : r * three]

    made = dot(w_ref[:, HDIM:], n1_ref[...], TN)
    keys = turn(made[:HDIM], cos_ref[...], sin_ref[...], 1).astype(BF16)
    k_ref[...] = keys
    ka_ref[:HDIM] = keys
    values = made[HDIM:].astype(BF16)
    v_ref[...] = values
    va_ref[:HDIM] = values
    made = dot(w_ref[:, :HDIM], n1_ref[:, mine], TN) * (SCALE * LOG2E)
    queries = turn(made, cos_ref[:, mine], sin_ref[:, mine], 1).astype(BF16)
    q_ref[...] = queries
    qa_ref[:HDIM] = queries
    scores = dot(ka_ref[...], qa_ref[...], TN)
    top = jnp.max(scores, axis=0, keepdims=True)
    probs = jnp.exp2(scores - top).astype(BF16)
    p_ref[0] = probs
    out = dot(va_ref[...], probs, NN)
    inv = 1.0 / out[HDIM : HDIM + 1]
    o_ref[...] = (out[:HDIM] * inv).astype(BF16)
    inv_ref[0] = inv
    if linked:

        @pl.when(step == pl.num_programs(0) - 1)
        def _():
            for keep in keeps:
                keep.wait()
            last.corner(3)
            last.end()


GATHER_STEPS = (
    (0, "two", "along", 1),
    (0, "two", "along", 2),
    (0, "two", "along", 3),
    (0, "last", "push", 2),
    (1, "two", "over", 0),
    (1, "two", "over", 1),
    (2, "two", "over", 2),
    (2, "two", "over", 3),
    (2, "last", "push", 3),
    (3, "last", "along", 1),
    (3, "last", "over", 0),
    (4, "last", "along", 2),
    (5, "last", "over", 1),
    (6, "last", "corner", 0),
    (6, "last", "along", 3),
    (7, "last", "over", 2),
    (8, "last", "corner", 1),
    (9, "last", "over", 3),
    (11, "last", "corner", 2),
)


def forward(nz, n_mp, units, lengths, tokens, weights, columns):
    rows, features = tokens.shape
    own, width, heads = rows // n_mp, features // n_mp, features // HDIM
    per = width // HDIM
    linked = nz > 0
    hbm = pl.BlockSpec(memory_space=pl.ANY)
    head = lambda h: lax.rem(h, n_mp) * per + h // n_mp
    row = lambda h: (head(h), 0)
    cube = lambda h: (head(h), 0, 0)
    vm = pl.BlockSpec(memory_space=pltpu.VMEM)
    n = Gather.count(nz) if linked else 0
    dma = pltpu.SemaphoreType.DMA
    depth = features // (2 * nz) if linked else 0
    full_shapes = [jax.ShapeDtypeStruct((n_mp, features, c), BF16) for c in columns] if linked else []
    return pl.pallas_call(
        functools.partial(forward_kernel, nz, units),
        grid=(heads,),
        in_specs=[pl.BlockSpec(memory_space=pltpu.SMEM), vm] + ([vm] * 6 if linked else [hbm] * 2),
        out_specs=[
            whole(features, own),
            pl.BlockSpec((HDIM, own), row),
            pl.BlockSpec((HDIM, rows), row),
            pl.BlockSpec((HDIM, rows), row),
            whole(HALF, rows),
            whole(HALF, rows),
            pl.BlockSpec((HDIM, own), row),
            pl.BlockSpec((1, rows, own), cube),
            pl.BlockSpec((1, 1, own), cube),
        ]
        + [hbm] * len(full_shapes),
        out_shape=[
            jax.ShapeDtypeStruct((features, own), BF16),
            jax.ShapeDtypeStruct((features, own), BF16),
            jax.ShapeDtypeStruct((features, rows), BF16),
            jax.ShapeDtypeStruct((features, rows), BF16),
            jax.ShapeDtypeStruct((HALF, rows), F32),
            jax.ShapeDtypeStruct((HALF, rows), F32),
            jax.ShapeDtypeStruct((features, own), BF16),
            jax.ShapeDtypeStruct((heads, rows, own), BF16),
            jax.ShapeDtypeStruct((heads, 1, own), F32),
        ]
        + full_shapes,
        scratch_shapes=[
            pltpu.VMEM((n_mp, features, columns[0]), BF16),
            pltpu.VMEM((n_mp, features, columns[1]), BF16),
            pltpu.VMEM((features, 3 * HDIM), BF16),
            pltpu.VMEM((features, rows), BF16),
            pltpu.VMEM((AUG, rows), BF16),
            pltpu.VMEM((AUG, own), BF16),
            pltpu.VMEM((AUG, rows), BF16),
            pltpu.VMEM((8, rows), F32),
            dma((2,)),
        ]
        + (
            [pltpu.VMEM((depth, c), BF16) for c in columns] + [dma((n,)), dma((n,)), dma] * 3
            if linked
            else []
        ),
        compiler_params=pltpu.CompilerParams(
            dimension_semantics=("arbitrary",),
            vmem_limit_bytes=VMEM_BYTES,
            **({"collective_id": 1, "has_side_effects": True} if linked else {}),
        ),
        name="forward",
    )(lengths, tokens, *weights)


def middle(len_ref, me, tok_ref, cot_ref, heads_ref, inv_ref, w_ref, gain, units, out_ref, mcot_ref, do_ref, keep, sent, done, later):
    own, features = tok_ref.shape
    parts = w_ref.shape[0]
    width = features // parts
    heads = width // HDIM
    pair = 2 * units
    _, _, live = layout_rows(len_ref, len_ref.shape[1], me * own, own)

    def w_gu(m):
        return w_ref[m, :, :pair]

    def w_out(m):
        return w_ref[m, :, pair : pair + width]

    def w_down(m):
        return w_ref[m, :, pair + width : pair + width + units]

    total = dot(w_out(0), heads_ref[:width], NN)
    for m in range(1, parts):
        total += dot(w_out(m), heads_ref[m * width : (m + 1) * width], NN)
    middle = tok_ref[...].T.astype(F32) + total
    hat, inv_sigma = normalize(middle)
    normed = (hat * gain).astype(BF16)
    total = middle
    kept = []
    for m in range(parts):
        gate_up = dot(w_gu(m), normed, TN)
        gate, up = gate_up[:units], gate_up[units:]
        phi, slope = gelu_parts(gate)
        act = gate * phi
        hidden = (act * up).astype(BF16)
        total += dot(w_down(m), hidden, NN)
        kept.append((hidden, (up * (phi + slope)).astype(BF16), act.astype(BF16)))
    out_ref[...] = total.astype(BF16).T
    sent()
    branch = jnp.where(live, cot_ref[...].T.astype(F32), 0.0).astype(BF16)
    back = jnp.zeros((features, own), F32)
    for m in range(parts):
        hidden, one, two = kept[m]
        hidden_cot = dot(w_down(m), branch, TN)
        keep("down", m, dot(branch, hidden, NT).astype(BF16))
        cots = jnp.concatenate([hidden_cot * one.astype(F32), hidden_cot * two.astype(F32)], axis=0).astype(BF16)
        keep("gu", m, dot(normed, cots, NT).astype(BF16))
        back += dot(w_gu(m), cots, NN)
    done()
    keep("gain", 0, jnp.sum(back * hat, axis=1, keepdims=True))
    d = back * gain
    middle_cot = branch.astype(F32) + inv_sigma * (
        d - jnp.mean(d, axis=0, keepdims=True) - hat * jnp.mean(d * hat, axis=0, keepdims=True)
    )
    mcot_ref[...] = middle_cot
    attn_cot = middle_cot.astype(BF16)
    for m in range(parts):
        back_heads = dot(w_out(m), attn_cot, TN)
        for h in range(heads):
            head = m * heads + h
            rows = slice(h * HDIM, (h + 1) * HDIM)
            cot = back_heads[rows] * inv_ref[head]
            inner = jnp.sum(cot * heads_ref[head * HDIM : (head + 1) * HDIM].astype(F32), axis=0, keepdims=True)
            high = inner.astype(BF16).astype(F32)
            pad = jnp.zeros((AUG - HDIM - 2, own), F32)
            do_ref[head] = jnp.concatenate([cot, high, inner - high, pad], axis=0).astype(BF16)
    later()
    for m in range(parts):
        keep("out", m, dot(attn_cot, heads_ref[m * width : (m + 1) * width], NT).astype(BF16))


def mid_kernel(
    units, len_ref, tok_hbm, cot_hbm, heads_ref, inv_ref, two_ref, w_hbm,
    out_ref, mcot_ref, do_ref, g_ref, o_ref, gain_ref, tok_ref, cot_ref, w_ref, load,
):
    own = tok_ref.shape[0]
    me = lax.axis_index("mp")
    mine = pl.ds(pl.multiple_of(me * own, own), own)
    loads = [
        pltpu.make_async_copy(tok_hbm.at[mine], tok_ref, load.at[0]),
        pltpu.make_async_copy(cot_hbm.at[mine], cot_ref, load.at[1]),
        pltpu.make_async_copy(w_hbm, w_ref, load.at[2]),
    ]
    for copy in loads:
        copy.start()
    for copy in loads:
        copy.wait()
    pair = 2 * units

    def keep(what, m, made):
        if what == "gu":
            g_ref[m, :, :pair] = made
        elif what == "down":
            g_ref[m, :, pair:] = made
        elif what == "out":
            o_ref[m] = made
        else:
            gain_ref[...] = made

    nothing = lambda: None
    middle(
        len_ref, me, tok_ref, cot_ref, heads_ref, inv_ref, w_ref, two_ref[...].astype(F32), units, out_ref, mcot_ref, do_ref,
        keep, nothing, nothing, nothing,
    )


def mid(n_mp, lengths, tokens, out_grad, heads_out, inv, gain, w_rest, units):
    features, own = heads_out.shape
    heads = inv.shape[0]
    vm = pl.BlockSpec(memory_space=pltpu.VMEM)
    hbm = pl.BlockSpec(memory_space=pl.ANY)
    return pl.pallas_call(
        functools.partial(mid_kernel, units),
        in_specs=[pl.BlockSpec(memory_space=pltpu.SMEM), hbm, hbm, vm, vm, vm, hbm],
        out_specs=[vm] * 6,
        out_shape=[
            jax.ShapeDtypeStruct((own, features), BF16),
            jax.ShapeDtypeStruct((features, own), F32),
            jax.ShapeDtypeStruct((heads, AUG, own), BF16),
            jax.ShapeDtypeStruct((n_mp, features, 3 * units), BF16),
            jax.ShapeDtypeStruct((n_mp, features, features // n_mp), BF16),
            jax.ShapeDtypeStruct((features, 1), F32),
        ],
        scratch_shapes=[
            pltpu.VMEM((own, features), BF16),
            pltpu.VMEM((own, features), BF16),
            pltpu.VMEM(w_rest.shape, BF16),
            pltpu.SemaphoreType.DMA((3,)),
        ],
        compiler_params=pltpu.CompilerParams(vmem_limit_bytes=VMEM_BYTES),
        name="mid",
    )(lengths, tokens, out_grad, heads_out, inv, gain, w_rest)


SLOTS = 7
LAG = 4
PIECES = 4


def backward_kernel(nz, units, *refs):
    len_ref, q_ref, k_ref, v_ref, p_ref, cos_ref, sin_ref, n1_ref, heads_ref, inv_ref, wa_ref, tok_hbm, cot_hbm, wb_hbm, wr_hbm = refs[:15]
    dq_ref, dr_ref, gains_ref, in_full, out_full = refs[15:20]
    wb_ref, wr_ref, gr_ref, do_ref, mcot_ref, pc_ref, qc_ref, acc_ref, gc_ref, va_ref, tok_ref, cot_ref, own_ref, load = refs[20:34]
    refs = refs[34:]
    gq_ref = wr_ref.at[:, :, pl.ds(0, dq_ref.shape[1])]
    rest = Scatter(nz, (0, 1), gr_ref, gr_ref, dr_ref, *refs[:6])
    low = Scatter(nz, (0,), gq_ref, gq_ref, dq_ref, *refs[6:12])
    high = Scatter(nz, (1,), gq_ref, gq_ref, dq_ref, *refs[12:18])
    fold = Fold(*refs[18:23])
    in_share = Share(own_ref.at[0], in_full, *refs[23:26], PIECES)
    out_share = Share(own_ref.at[1], out_full, *refs[26:29])
    gains = Everyone(*refs[29:33])
    step, heads = pl.program_id(0) - 1, pl.num_programs(0) - 1
    parts = wa_ref.shape[0]
    features, own = n1_ref.shape
    rows = k_ref.shape[1]
    width = features // parts
    per = width // HDIM
    me = lax.axis_index("mp")
    mine = pl.ds(pl.multiple_of(me * own, own), own)
    late = pltpu.make_async_copy(wb_hbm, wb_ref, load.at[3])
    three = 3 * HDIM
    shards = features // gains_ref.shape[1]

    def put(row, column):
        for i in range(shards):
            at = row * shards + i
            gains.held[0, at : at + 1, : features // shards] = column[i * (features // shards) : (i + 1) * (features // shards)].T

    @pl.when(step < 0)
    def _():
        gains.held[0] = jnp.zeros(gains.held.shape[1:], F32)
        loads = [
            pltpu.make_async_copy(wr_hbm, wr_ref.at[:, :, pl.ds(0, wr_hbm.shape[2])], load.at[0]),
            pltpu.make_async_copy(tok_hbm.at[mine], tok_ref, load.at[1]),
            pltpu.make_async_copy(cot_hbm.at[mine], cot_ref, load.at[2]),
        ]
        for copy in loads:
            copy.start()
        greet(peers(nz))
        for copy in loads:
            copy.wait()
        late.start()
        pair = 2 * units

        def first():
            rest.chip(2)
            rest.cross(2)

        for m in range(parts):
            wr_ref[m, :, wr_hbm.shape[2] :] = wa_ref[m, :, 256 - units % 128 :]

        def keep(what, m, made):
            if what == "gu":
                gr_ref[m, :, :pair] = made
            elif what == "down":
                gr_ref[m, :, pair:] = made
            elif what == "out":
                wr_ref[m, :, 3 * width : 4 * width] = made
            else:
                put(1, made)

        middle(
            len_ref, me, tok_ref, cot_ref, heads_ref, inv_ref, wr_ref, wa_ref[0, :, three + 1 : three + 2].astype(F32), units,
            own_ref.at[1], mcot_ref, do_ref, keep,
            lambda: out_share.begin(0), lambda: rest.begin(2, 3), first,
        )
        va_ref[HDIM:] = jnp.full((AUG - HDIM, rows), -1.0, BF16)
        acc_ref[...] = jnp.zeros_like(acc_ref)
        gc_ref[...] = jnp.zeros_like(gc_ref)
        late.wait()

    def collect(head):
        at = lax.rem(head, per) * three
        pc_ref[pl.ds(pl.multiple_of(at + HDIM, HDIM), 2 * HDIM)] = fold.end(head)

    def close(part):
        for i in range(per):
            pc_ref[i * three : i * three + HDIM] = qc_ref[lax.rem(part, 3), i * HDIM : (i + 1) * HDIM]
        made = dot(n1_ref[...], pc_ref[...], NT)
        wr_ref[part, :, : 3 * width] = made.astype(BF16)
        weights = jnp.concatenate([wa_ref[part, :, :three], wb_ref[part]], axis=1)
        gc_ref[...] += jnp.sum(made * weights.astype(F32), axis=1, keepdims=True)
        acc_ref[...] += dot(weights, pc_ref[...], NN)

    @pl.when(step >= 0)
    def _():
        va_ref[:HDIM] = v_ref[...]
        cot = dot(va_ref[...], do_ref[step], TN)
        probs = p_ref[0]
        score_cot = probs * cot.astype(BF16)
        dv = dot(do_ref[step, :HDIM], probs, NT).astype(BF16)
        dk = turn(dot(q_ref[...], score_cot, NT) * LN2, cos_ref[...], sin_ref[...], 1, True).astype(BF16)
        dq = turn(dot(k_ref[...], score_cot, NN) * SCALE, cos_ref[:, mine], sin_ref[:, mine], 1, True)
        slot = lax.rem(step, SLOTS)
        for m in range(parts):
            fold.part[slot, m, :HDIM] = dk[:, m * own : (m + 1) * own]
            fold.part[slot, m, HDIM:] = dv[:, m * own : (m + 1) * own]
        at = pl.ds(pl.multiple_of(lax.rem(step, per) * HDIM, HDIM), HDIM)
        qc_ref[lax.rem(step // per, 3), at] = dq.astype(BF16)

        @pl.when(step >= LAG)
        def _():
            collect(step - LAG)

        @pl.when(step >= 1)
        def _():
            fold.chip(step - 1)

        fold.begin(step)

        @pl.when((step >= LAG) & (lax.rem(step - LAG, per) == per - 1))
        def _():
            close((step - LAG) // per)

    sums = {"rest": rest, "low": low, "high": high, "out": out_share, "in": in_share, "gains": gains}
    for at, which, name, *d in SUM_STEPS:
        pl.when(step == at)(functools.partial(getattr(sums[which], name), *d))

    @pl.when(step == heads - 1)
    def _():
        fold.chip(step)
        for which, name, *d in FLUSH_STEPS:
            getattr(sums[which], name)(*d)
        for back in range(LAG - 1, -1, -1):
            collect(step - back)
            if (features // HDIM - 1 - back) % per == per - 1:
                close((step - back) // per)
        high.begin(2, 3, 1, 0)
        gain = wa_ref[0, :, three : three + 1].astype(F32)
        size = own // PIECES
        for i in range(PIECES):
            at = slice(i * size, (i + 1) * size)
            own_ref[0, at] = finish(tok_ref[at], gain, acc_ref[:, at], mcot_ref[:, at])
            in_share.begin(i)
        put(0, gc_ref[...] / gain)
        gains.begin()
        for which, name, *d in LAST_STEPS:
            getattr(sums[which], name)(*d)
        high.along()
        gains.hop(4)
        for which in (rest, low, high):
            which.end()
        out_share.end()
        in_share.end()
        made = gains.end()
        dp = lax.axis_index("dp")
        for row in range(2):
            for i in range(shards):

                @pl.when(dp == i)
                def _():
                    gains_ref[row : row + 1] = made[row * shards + i : row * shards + i + 1, : features // shards]


SUM_STEPS = (
    (-1, "rest", "begin", 1, 0),
    (-1, "rest", "chip", 3),
    (0, "rest", "cross", 3),
    (0, "rest", "chip", 1),
    (0, "rest", "chip", 0),
    (1, "rest", "over", 2),
    (1, "out", "on", 0),
    (3, "rest", "cross", 1),
    (4, "rest", "over", 3),
    (6, "rest", "cross", 0),
    (7, "rest", "over", 1),
    (9, "low", "begin", 2, 3, 1, 0),
    (10, "low", "chip", 2),
    (10, "low", "chip", 3),
    (10, "low", "chip", 1),
    (10, "low", "chip", 0),
    (10, "low", "cross", 2),
    (10, "low", "cross", 3),
    (10, "low", "cross", 1),
    (10, "low", "cross", 0),
    (9, "rest", "over", 0),
)
FLUSH_STEPS = (
    ("rest", "along"),
    ("low", "over", 2),
    ("low", "over", 3),
)
LAST_STEPS = (
    ("high", "chip", 2),
    ("high", "cross", 2),
    ("high", "chip", 3),
    ("high", "cross", 3),
    ("high", "chip", 1),
    ("high", "cross", 1),
    ("high", "chip", 0),
    ("high", "cross", 0),
    ("low", "over", 1),
    ("low", "over", 0),
    ("gains", "hop", 0),
    ("high", "over", 2),
    ("in", "on", 0),
    ("gains", "hop", 1),
    ("high", "over", 3),
    ("in", "on", 1),
    ("gains", "hop", 2),
    ("high", "over", 1),
    ("low", "along"),
    ("gains", "hop", 3),
    ("high", "over", 0),
    ("in", "on", 2),
    ("in", "on", 3),
)


def backward(nz, lengths, q, k, v, p, cos, sin, n1, heads_out, inv, tokens, out_grad, w_a, w_b, w_rest, units):
    (features, own), rows = q.shape, k.shape[1]
    n_mp = w_a.shape[0]
    heads = features // HDIM
    width = features // n_mp
    depth = features // (2 * nz)
    columns = 4 * width, 3 * units
    hbm = pl.BlockSpec(memory_space=pl.ANY)
    vm = pl.BlockSpec(memory_space=pltpu.VMEM)
    row = lambda h: (jnp.maximum(h - 1, 0), 0)
    cube = lambda h: (jnp.maximum(h - 1, 0), 0, 0)
    dma = pltpu.SemaphoreType.DMA
    return pl.pallas_call(
        functools.partial(backward_kernel, nz, units),
        grid=(heads + 1,),
        in_specs=[
            pl.BlockSpec(memory_space=pltpu.SMEM),
            pl.BlockSpec((HDIM, own), row),
            pl.BlockSpec((HDIM, rows), row),
            pl.BlockSpec((HDIM, rows), row),
            pl.BlockSpec((1, rows, own), cube),
        ]
        + [vm] * 6
        + [hbm] * 4,
        out_specs=[vm, vm, vm, hbm, hbm],
        out_shape=[
            jax.ShapeDtypeStruct((depth, columns[0]), F32),
            jax.ShapeDtypeStruct((depth, columns[1]), F32),
            jax.ShapeDtypeStruct((2, depth), F32),
            jax.ShapeDtypeStruct((rows, features), BF16),
            jax.ShapeDtypeStruct((rows, features), BF16),
        ],
        scratch_shapes=[
            pltpu.VMEM(w_b.shape, BF16),
            pltpu.VMEM((n_mp, features, width + 3 * units), BF16),
            pltpu.VMEM((n_mp, features, 3 * units), BF16),
            pltpu.VMEM((heads, AUG, own), BF16),
            pltpu.VMEM((features, own), F32),
            pltpu.VMEM((3 * width, own), BF16),
            pltpu.VMEM((3, width, own), BF16),
            pltpu.VMEM((features, own), F32),
            pltpu.VMEM((features, 1), F32),
            pltpu.VMEM((AUG, rows), BF16),
            pltpu.VMEM((own, features), BF16),
            pltpu.VMEM((own, features), BF16),
            pltpu.VMEM((2, own, features), BF16),
            dma((4,)),
        ]
        + Scatter.scratch(nz, (0, 1), depth, columns[1])
        + Scatter.scratch(nz, (0,), depth, columns[0])
        + Scatter.scratch(nz, (1,), depth, columns[0])
        + Fold.scratch(n_mp, own, SLOTS)
        + Share.sems(PIECES)
        + Share.sems(1)
        + Everyone.scratch(nz, 4 * nz),
        compiler_params=pltpu.CompilerParams(
            dimension_semantics=("arbitrary",), collective_id=3, has_side_effects=True, vmem_limit_bytes=VMEM_BYTES
        ),
        name="backward",
    )(lengths, q, k, v, p, cos, sin, n1, heads_out, inv, w_a, tokens, out_grad, w_b, w_rest)


def deliver_kernel(units, in_ref, out_ref, dq_ref, dr_ref, gains_ref, grad_ref, to_ref, gq_ref, go_ref, gg_ref, gd_ref, one_ref, two_ref):
    @pl.when(pl.program_id(0) == 0)
    def _():
        width = go_ref.shape[0]
        pair = 2 * units
        for r in range(width // HDIM):
            for i in range(3):
                at = (3 * r + i) * HDIM
                gq_ref[i, :, r * HDIM : (r + 1) * HDIM] = dq_ref[:, at : at + HDIM]
        go_ref[...] = dq_ref[:, 3 * width : 4 * width].T
        one_ref[...] = gains_ref[0:1]
        two_ref[...] = gains_ref[1:2]
        for i in range(2):
            gg_ref[:, i, :] = dr_ref[:, i * units : (i + 1) * units]
        gd_ref[...] = dr_ref[:, pair : pair + units].T

    grad_ref[...] = in_ref[...].astype(F32)
    to_ref[...] = out_ref[...]


def deliver(layer_out, input_grad, d_qkv, d_rest, gains, width, units):
    rows, features = input_grad.shape
    depth = d_qkv.shape[0]
    shape = lambda *s: jax.ShapeDtypeStruct(s, F32)
    shapes = [(3, depth, width), (width, depth), (depth, 2, units), (units, depth), (1, depth), (1, depth)]
    steps = 2
    slab = pl.BlockSpec((rows // steps, features), lambda i: (i, 0))
    return pl.pallas_call(
        functools.partial(deliver_kernel, units),
        grid=(steps,),
        in_specs=[slab, slab, whole(*d_qkv.shape), whole(*d_rest.shape), whole(*gains.shape)],
        out_specs=[slab, slab] + [whole(*s) for s in shapes],
        out_shape=[shape(rows, features), jax.ShapeDtypeStruct((rows, features), BF16)] + [shape(*s) for s in shapes],
        compiler_params=params("arbitrary"),
        name="deliver",
    )(input_grad, layer_out, d_qkv, d_rest, gains)


def per_device(n_dp, n_mp, tokens, out_grad, w_qkv, w_out, w_gu, w_down, gain_attn, gain_mlp, lengths):
    rows, features = tokens.shape
    depth = w_qkv.shape[0]
    units, width = w_down.shape[0], w_out.shape[0]
    everyone = ("mp", "dp")
    linked = n_mp == 4 and n_dp == 8 and depth % 32 == 0 and features // HDIM == 12
    nz = n_dp // 2 if linked else 0
    three = 3 * HDIM
    loose = units % 128
    columns = 256, 3 * width - three, 3 * units + width - loose
    wq = w_qkv.transpose(1, 0, 2)
    if linked:
        weights = wq, w_gu, w_out, w_down, gain_attn[None], gain_mlp[None]
        n1, q, k, v, cos, sin, heads_out, probs, inv, w_a, w_b, w_c = forward(
            nz, n_mp, units, lengths, tokens, weights, columns
        )
        d_qkv, d_rest, gains, in_full, layer_out = backward(
            nz, lengths, q, k, v, probs, cos, sin, n1, heads_out, inv, tokens, out_grad, w_a, w_b, w_c, units
        )
    else:
        by_head = w_qkv.reshape(depth, 3, width // HDIM, HDIM).transpose(0, 2, 1, 3).reshape(depth, 3 * width)
        blank = jnp.zeros((depth, columns[0] - three - 2), BF16)
        shards = [
            jnp.concatenate([by_head[:, :three], gain_attn[:, None], gain_mlp[:, None], blank], axis=1),
            by_head[:, three:],
            jnp.concatenate([w_gu.reshape(depth, -1), w_out.T, w_down.T], axis=1),
        ]
        w_a, w_b, w_c = (
            lax.all_gather(s, everyone, axis=0, tiled=True).reshape(n_mp, features, s.shape[1]) for s in shards
        )
        n1, q, k, v, cos, sin, heads_out, probs, inv = forward(nz, n_mp, units, lengths, tokens, [w_a, w_b], columns)
        layer_out, middle_cot, do, g_rest, g_out, gain_two = mid(
            n_mp, lengths, tokens, out_grad, heads_out, inv, w_a[0, :, three + 1 : three + 2], w_c, units
        )
        own = middle_cot.shape[1]
        swap = lambda g, a, b: g.reshape(n_mp, features, a, b, HDIM).swapaxes(2, 3).reshape(n_mp, features, 3 * width)
        natural = jnp.concatenate([w_a[..., :three], w_b], axis=2)
        natural = jnp.concatenate([swap(natural, width // HDIM, 3), w_a[..., three : three + 1]], axis=2)
        g_qkv, nc = last(q, k, v, do, probs, cos, sin, lax.all_gather(n1, "mp", axis=1, tiled=True), natural)
        gain_one = w_a[0, :, three : three + 1].astype(F32)
        tok = lax.dynamic_slice_in_dim(tokens, lax.axis_index("mp") * own, own, 0)
        nc_own = lax.psum_scatter(nc, "mp", scatter_dimension=0, tiled=True)[0]
        in_own = finish(tok, gain_one, nc_own.astype(F32), middle_cot)
        layer_out, in_full = (lax.all_gather(v, "mp", axis=0, tiled=True) for v in (layer_out, in_own))
        both = jnp.stack([g_qkv[0, :, -1].astype(F32), gain_two[:, 0]])
        both = lax.psum(both, everyone)
        gains = lax.dynamic_slice_in_dim(both, lax.axis_index("dp") * depth, depth, 1)
        g_qkv = jnp.concatenate([swap(g_qkv[..., : 3 * width], 3, width // HDIM), g_out], axis=2)
        d_qkv, d_rest = (
            lax.psum_scatter(
                g.reshape(n_mp * features, -1), everyone, scatter_dimension=0, tiled=True
            ).astype(F32)
            for g in (g_qkv, g_rest)
        )
    input_grad, layer_out, g_q, g_o, g_g, g_d, one, two = deliver(
        layer_out, in_full, d_qkv, d_rest, gains, width, units
    )
    return layer_out, input_grad, g_q.transpose(1, 0, 2), g_o, g_g, g_d, one[0], two[0]


def solution(mesh):
    n_dp, n_mp = mesh.shape["dp"], mesh.shape["mp"]
    return jax.shard_map(
        functools.partial(per_device, n_dp, n_mp),
        mesh=mesh,
        in_specs=(
            P("dp", None),
            P("dp", None),
            P("dp", None, "mp"),
            P("mp", "dp"),
            P("dp", None, "mp"),
            P("mp", "dp"),
            P("dp"),
            P("dp"),
            P("dp", None),
        ),
        out_specs=(
            P("dp", None),
            P("dp", None),
            P("dp", None, "mp"),
            P("mp", "dp"),
            P("dp", None, "mp"),
            P("mp", "dp"),
            P("dp"),
            P("dp"),
        ),
        check_vma=False,
    )
```

```python
import functools
import math

import jax
import jax.numpy as jnp
from jax import lax
from jax.experimental import pallas as pl
from jax.experimental.pallas import tpu as pltpu
from jax.sharding import PartitionSpec as P

HDIM = 64
HALF = HDIM // 2
AUG = HDIM + 16
EPS = 1e-05
ROPE_BASE = 160000.0
LOG2E = math.log2(math.e)
LN2 = math.log(2.0)
SCALE = HDIM ** (-0.5)
FAR = -1e30
BF16 = jnp.bfloat16
F32 = jnp.float32
VMEM_BYTES = 60 << 20
NN = (((1,), (0,)), ((), ()))
NT = (((1,), (1,)), ((), ()))
TN = (((0,), (0,)), ((), ()))


def dot(a, b, dims):
    return lax.dot_general(a, b, dims, preferred_element_type=F32)


def params(*semantics):
    return pltpu.CompilerParams(
        dimension_semantics=semantics or None, vmem_limit_bytes=VMEM_BYTES
    )


def whole(*shape):
    return pl.BlockSpec(shape, lambda *i: (0,) * len(shape))


def layout_rows(len_ref, docs, first, rows):
    index = first + lax.broadcasted_iota(jnp.int32, (1, rows), 1)
    segment = jnp.zeros((1, rows), jnp.int32)
    start = jnp.zeros((1, rows), jnp.int32)
    end = jnp.int32(0)
    for j in range(docs):
        end = end + len_ref[0, j]
        past = index >= end
        segment = segment + jnp.where(past, 1, 0)
        start = jnp.where(past, jnp.maximum(start, end), start)
    return segment, index - start, index < end


def moments(columns):
    mean = jnp.mean(columns, axis=0, keepdims=True)
    centered = columns - mean
    return mean, lax.rsqrt(jnp.mean(centered * centered, axis=0, keepdims=True) + EPS)


def normalize(columns):
    mean, inv = moments(columns)
    return (columns - mean) * inv, inv


def turn(block, cos, sin, heads, back=False):
    out = []
    for h in range(heads):
        one = block[h * HDIM : h * HDIM + HALF]
        two = block[h * HDIM + HALF : (h + 1) * HDIM]
        if back:
            out += [one * cos + two * sin, two * cos - one * sin]
        else:
            out += [one * cos - two * sin, two * cos + one * sin]
    return jnp.concatenate(out, axis=0)


def gelu_parts(gate):
    phi = 0.5 * (1.0 + lax.erf(gate * math.sqrt(0.5)))
    density = jnp.exp2(gate * gate * (-0.5 * LOG2E)) * (1.0 / math.sqrt(2.0 * math.pi))
    return phi, gate * density


def last_kernel(own_axis, q_ref, k_ref, v_ref, do_ref, p_ref, cos_ref, sin_ref, n1_ref, w_ref, gq_ref, nc_ref, gc_ref, dq_ref, pc_ref, acc_ref, va_ref):
    step, head = pl.program_id(0), pl.program_id(1)
    per = pl.num_programs(1)
    features, rows = n1_ref.shape
    own = q_ref.shape[1]
    width = per * HDIM
    mine = pl.ds(pl.multiple_of(lax.axis_index(own_axis) * own, own), own)

    @pl.when((step == 0) & (head == 0))
    def _():
        va_ref[HDIM:] = jnp.full((AUG - HDIM, rows), -1.0, BF16)
        acc_ref[...] = jnp.zeros_like(acc_ref)
        gc_ref[...] = jnp.zeros_like(gc_ref)

    va_ref[:HDIM] = v_ref[...]
    cot = dot(va_ref[...], do_ref[0], TN)
    probs = p_ref[0]
    score_cot = probs * cot.astype(BF16)
    at = pl.ds(pl.multiple_of(head * HDIM, HDIM), HDIM)
    dv = dot(do_ref[0, :HDIM], probs, NT)
    dk = dot(q_ref[...], score_cot, NT) * LN2
    dq = dot(k_ref[...], score_cot, NN) * SCALE
    pc_ref[pl.ds(pl.multiple_of(width + head * HDIM, HDIM), HDIM)] = dv.astype(BF16)
    pc_ref[at] = turn(dk, cos_ref[...], sin_ref[...], 1, True).astype(BF16)
    dq_ref[at] = turn(dq, cos_ref[:, mine], sin_ref[:, mine], 1, True).astype(BF16)

    @pl.when(head == per - 1)
    def _():
        kv = dot(n1_ref[...], pc_ref[...], NT)
        q = dot(n1_ref[:, mine], dq_ref[...], NT)
        gq_ref[step, :, :width] = q.astype(BF16)
        gq_ref[step, :, width : 3 * width] = kv.astype(BF16)
        gc_ref[...] += jnp.sum(q * w_ref[0, :, :width].astype(F32), axis=1, keepdims=True) + jnp.sum(
            kv * w_ref[0, :, width : 3 * width].astype(F32), axis=1, keepdims=True
        )

        def spread(i, carry):
            cols = pl.ds(pl.multiple_of(i * own, own), own)
            acc_ref[:, cols] += dot(w_ref[0, :, width : 3 * width], pc_ref[:, cols], NN)
            return carry

        lax.fori_loop(0, rows // own, spread, 0)
        acc_ref[:, mine] += dot(w_ref[0, :, :width], dq_ref[...], NN)

    @pl.when((step == pl.num_programs(0) - 1) & (head == per - 1))
    def _():
        gain_cot = (gc_ref[...] / w_ref[0, :, 3 * width :].astype(F32)).astype(BF16)
        for m in range(gq_ref.shape[0]):
            nc_ref[m] = acc_ref[:, m * own : (m + 1) * own].astype(BF16)
            gq_ref[m, :, 3 * width :] = gain_cot


def last(q, k, v, do, p, cos, sin, n1, w_qkv, own_axis="mp"):
    (features, own), rows = q.shape, k.shape[1]
    parts = w_qkv.shape[0]
    per = features // parts // HDIM
    width = per * HDIM
    head = lambda m, h: (m * per + h, 0)
    return pl.pallas_call(
        functools.partial(last_kernel, own_axis),
        grid=(parts, per),
        in_specs=[
            pl.BlockSpec((HDIM, own), head),
            pl.BlockSpec((HDIM, rows), head),
            pl.BlockSpec((HDIM, rows), head),
            pl.BlockSpec((1, AUG, own), lambda m, h: (m * per + h, 0, 0)),
            pl.BlockSpec((1, rows, own), lambda m, h: (m * per + h, 0, 0)),
            whole(HALF, rows),
            whole(HALF, rows),
            whole(features, rows),
            pl.BlockSpec((1,) + w_qkv.shape[1:], lambda m, h: (m, 0, 0)),
        ],
        out_specs=[
            whole(*w_qkv.shape),
            whole(parts, features, own),
        ],
        out_shape=[
            jax.ShapeDtypeStruct(w_qkv.shape, BF16),
            jax.ShapeDtypeStruct((parts, features, own), BF16),
        ],
        scratch_shapes=[
            pltpu.VMEM((features, 1), F32),
            pltpu.VMEM((width, own), BF16),
            pltpu.VMEM((2 * width, rows), BF16),
            pltpu.VMEM((features, rows), F32),
            pltpu.VMEM((AUG, rows), BF16),
        ],
        compiler_params=params("arbitrary", "arbitrary"),
        name="last",
    )(q, k, v, do, p, cos, sin, n1, w_qkv)


def place():
    dp, mp = lax.axis_index("dp"), lax.axis_index("mp")
    return dp // 2, lax.rem(dp, 2), mp // 2, lax.rem(mp, 2)


def device(z, x, y, c):
    return (2 * z + x, 2 * y + c)


def remote(src, dst, send, recv, target):
    return pltpu.make_async_remote_copy(
        src_ref=src, dst_ref=dst, send_sem=send, recv_sem=recv,
        device_id=target, device_id_type=pl.DeviceIdType.MESH,
    )


def greet(targets):
    barrier = pltpu.get_barrier_semaphore()
    for target in targets:
        pl.semaphore_signal(barrier, inc=1, device_id=target, device_id_type=pl.DeviceIdType.MESH)
    pl.semaphore_wait(barrier, len(targets))


def peers(nz):
    z, x, y, c = place()
    across = [device(z, 1 - x, y, c), device(z, x, 1 - y, c), device(z, x, y, 1 - c)]
    return across + [device(lax.bitwise_xor(z, d), x, y, c) for d in range(1, nz)]


class Gather:
    def __init__(self, nz, src, full, send, recv, local, eager=False):
        self.nz, self.src, self.full, self.send, self.recv, self.local = nz, src, full, send, recv, local
        self.eager = eager
        self.depth = src.shape[0]
        self.index = {}
        for kind in ("Z", "X", "Y", "S", "YA", "XB", "SX", "SY", "SA", "SB"):
            for d in range(1 if kind == "Z" else 0, nz):
                self.index[kind, d] = len(self.index)

    @staticmethod
    def count(nz):
        return nz - 1 + 9 * nz

    def block(self, z, x, y, c, half=None):
        first, size = (0, self.depth) if half is None else (half * self.depth // 2, self.depth // 2)
        return self.full.at[2 * y + c, pl.ds(pl.multiple_of((2 * z + x) * self.depth + first, 16), size)]

    def message(self, kind, d, sending):
        z, x, y, c = place()
        back = lax.bitwise_xor(z, d)
        sx, sy, sib = device(z, 1 - x, y, c), device(z, x, 1 - y, c), device(z, x, y, 1 - c)
        sent, got, half, target = {
            "Z": ((z, x, y, c), (back, x, y, c), None, device(back, x, y, c)),
            "X": ((back, x, y, c), (back, 1 - x, y, c), None, sx),
            "Y": ((back, x, y, c), (back, x, 1 - y, c), None, sy),
            "S": ((back, x, y, c), (back, x, y, 1 - c), None, sib),
            "YA": ((back, 1 - x, y, c), (back, 1 - x, 1 - y, c), 0, sy),
            "XB": ((back, x, 1 - y, c), (back, 1 - x, 1 - y, c), 1, sx),
            "SX": ((back, 1 - x, y, c), (back, 1 - x, y, 1 - c), None, sib),
            "SY": ((back, x, 1 - y, c), (back, x, 1 - y, 1 - c), None, sib),
            "SA": ((back, 1 - x, 1 - y, c), (back, 1 - x, 1 - y, 1 - c), 0, sib),
            "SB": ((back, 1 - x, 1 - y, c), (back, 1 - x, 1 - y, 1 - c), 1, sib),
        }[kind]
        i = self.index[kind, d]
        at = self.block(*(sent if sending else got), half)
        own = sending and (kind == "Z" or (d == 0 and kind in ("X", "Y", "S")))
        return remote(self.src if own else at, at, self.send.at[i], self.recv.at[i], target)

    def start(self, kind, d):
        self.message(kind, d, True).start()

    def arrived(self, kind, d):
        self.message(kind, d, False).wait_recv()

    def own(self):
        z, x, y, c = place()
        return pltpu.make_async_copy(self.src, self.block(z, x, y, c), self.local)

    def begin(self):
        for d in range(1, self.nz if self.eager else 2):
            self.start("Z", d)
        for kind in ("X", "Y", "S"):
            self.start(kind, 0)
        self.own().start()

    def push(self, d):
        self.start("Z", d)

    def all_along(self):
        for d in range(1, self.nz):
            self.along(d)

    def all_over(self):
        for d in range(self.nz):
            self.over(d)

    def rest(self):
        for d in range(self.nz):
            self.corner(d)
        self.end()

    def along(self, d):
        self.arrived("Z", d)
        for kind in ("X", "Y", "S"):
            self.start(kind, d)

    def over(self, d):
        self.arrived("X", d)
        self.start("YA", d)
        self.start("SX", d)
        self.arrived("Y", d)
        self.start("XB", d)
        self.start("SY", d)

    def corner(self, d):
        self.arrived("YA", d)
        self.start("SA", d)
        self.arrived("XB", d)
        self.start("SB", d)

    def end(self):
        self.own().wait()
        for d in range(self.nz):
            for kind in ("S", "SX", "SY", "SA", "SB"):
                self.arrived(kind, d)
        for kind, d in self.index:
            self.message(kind, d, True).wait_send()


class Share:
    def __init__(self, src, full, send, recv, local, pieces=1):
        self.src, self.full, self.send, self.recv, self.local, self.pieces = src, full, send, recv, local, pieces
        self.size = src.shape[0] // pieces

    @staticmethod
    def sems(pieces):
        dma = pltpu.SemaphoreType.DMA
        return [dma((3 * pieces,)), dma((3 * pieces,)), dma((pieces,))]

    def rows(self, y, c, i):
        own = self.size * self.pieces
        return pl.ds(pl.multiple_of((2 * y + c) * own + i * self.size, 16), self.size)

    def message(self, kind, i):
        z, x, y, c = place()
        n = self.pieces
        piece = self.src.at[pl.ds(i * self.size, self.size)]
        if kind == "own":
            return pltpu.make_async_copy(piece, self.full.at[self.rows(y, c, i)], self.local.at[i])
        k = {"Y": 0, "C": 1, "F": 2}[kind] * n + i
        sems = self.send.at[k], self.recv.at[k]
        sib = device(z, x, y, 1 - c)
        if kind == "Y":
            return remote(piece, self.full.at[self.rows(y, c, i)], *sems, device(z, x, 1 - y, c))
        if kind == "C":
            return remote(piece, self.full.at[self.rows(y, c, i)], *sems, sib)
        at = self.full.at[self.rows(1 - y, c, i)]
        return remote(at, at, *sems, sib)

    def begin(self, i):
        for kind in ("Y", "C", "own"):
            self.message(kind, i).start()

    def on(self, i):
        self.message("Y", i).wait_recv()
        self.message("F", i).start()

    def end(self):
        for i in range(self.pieces):
            self.message("own", i).wait()
            self.message("C", i).wait_recv()
            self.message("F", i).wait_recv()
            for kind in ("Y", "C", "F"):
                self.message(kind, i).wait_send()


def finish(tokens, gain, cot, middle_cot):
    hat, inv_sigma = normalize(tokens.T.astype(F32))
    d = cot * gain
    made = middle_cot + inv_sigma * (
        d - jnp.mean(d, axis=0, keepdims=True) - hat * jnp.mean(d * hat, axis=0, keepdims=True)
    )
    return made.T.astype(BF16)


class Scatter:
    def __init__(self, nz, ups, src, part, out, core, side, line, last, send, recv):
        self.nz, self.ups, self.src, self.part, self.out = nz, ups, src, part, out
        self.core, self.side, self.line, self.last, self.send, self.recv = core, side, line, last, send, recv
        self.depth = out.shape[0]

    @staticmethod
    def scratch(nz, ups, depth, columns):
        count = len(ups) * nz + 2 * nz
        return [
            pltpu.VMEM((len(ups), 2 * nz * depth, columns), BF16),
            pltpu.VMEM((len(ups), nz * depth, columns), BF16),
            pltpu.VMEM((nz, len(ups), depth, columns), BF16),
            pltpu.VMEM((depth, columns), BF16),
            pltpu.SemaphoreType.DMA((count,)),
            pltpu.SemaphoreType.DMA((count,)),
        ]

    def row(self, d):
        z, _, _, _ = place()
        return lax.bitwise_xor(z, d)

    def rows(self, d, x):
        return pl.ds(pl.multiple_of((2 * self.row(d) + x) * self.depth, 16), self.depth)

    def both(self, d):
        return pl.ds(pl.multiple_of(2 * self.row(d) * self.depth, 16), 2 * self.depth)

    def lane(self, d):
        return pl.ds(pl.multiple_of(self.row(d) * self.depth, 16), self.depth)

    def message(self, kind, d, u=0):
        z, x, y, c = place()
        nz, n = self.nz, len(self.ups)
        i = {"C": u * nz + d, "X": n * nz + d, "Z": n * nz + nz + d, "Y": n * nz + nz}[kind]
        sems = self.send.at[i], self.recv.at[i]
        if kind == "C":
            both = self.both(d)
            return remote(self.src.at[2 * self.ups[u] + 1 - c, both], self.core.at[u, both], *sems, device(z, x, y, 1 - c))
        if kind == "X":
            return remote(
                self.core.at[:, self.rows(d, 1 - x)], self.side.at[:, self.lane(d)], *sems, device(z, 1 - x, y, c)
            )
        if kind == "Z":
            return remote(self.side.at[:, self.lane(d)], self.line.at[d], *sems, device(self.row(d), x, y, c))
        return remote(self.line.at[0, 1 - y if n == 2 else 0], self.last, *sems, device(z, x, 1 - y, c))

    def begin(self, *rows):
        for d in rows:
            for u in range(len(self.ups)):
                self.message("C", d, u).start()

    def cross(self, d):
        self.message("X", d).start()

    def chip(self, d):
        _, x, _, c = place()
        for u in range(len(self.ups)):
            self.message("C", d, u).wait_recv()
        for side in range(2):
            rows = self.rows(d, side)
            for u, up in enumerate(self.ups):
                self.core[u, rows] = self.part[2 * up + c, rows] + self.core[u, rows]

    def over(self, d):
        _, x, _, _ = place()
        self.message("X", d).wait_recv()
        rows, lane = self.rows(d, x), self.lane(d)
        for u in range(len(self.ups)):
            self.side[u, lane] = self.core[u, rows] + self.side[u, lane]
        if d:
            self.message("Z", d).start()

    def along(self):
        _, _, y, _ = place()
        for d in range(1, self.nz):
            self.message("Z", d).wait_recv()
        lane = self.lane(0)
        for u in range(len(self.ups)):
            made = self.side[u, lane].astype(F32)
            for d in range(1, self.nz):
                made += self.line[d, u].astype(F32)
            self.line[0, u] = made.astype(BF16)
        if len(self.ups) == 2:
            self.message("Y", 0).start()
        else:
            pl.when(y != self.ups[0])(lambda: self.message("Y", 0).start())

    def end(self):
        _, _, y, _ = place()

        def receive():
            self.message("Y", 0).wait_recv()
            mine = self.line[0, y if len(self.ups) == 2 else 0]
            self.out[...] = mine.astype(F32) + self.last[...].astype(F32)

        if len(self.ups) == 2:
            receive()
            self.message("Y", 0).wait_send()
        else:
            pl.when(y == self.ups[0])(receive)
            pl.when(y != self.ups[0])(lambda: self.message("Y", 0).wait_send())
        for d in range(self.nz):
            for u in range(len(self.ups)):
                self.message("C", d, u).wait_send()
            self.message("X", d).wait_send()
            if d:
                self.message("Z", d).wait_send()


class Everyone:
    def __init__(self, held, near, full, far, send, recv):
        self.held, self.near, self.full, self.far, self.send, self.recv = held, near, full, far, send, recv
        self.group, self.owners = near.shape[0], far.shape[0]

    @staticmethod
    def scratch(n_mp, n_dp):
        dma = pltpu.SemaphoreType.DMA
        blocks = pltpu.VMEM((n_dp, 8, 128), F32)
        count = n_mp + n_dp
        return [blocks, pltpu.VMEM((n_mp, n_dp, 8, 128), F32), blocks, blocks, dma((count,)), dma((count,))]

    @staticmethod
    def peers(n_mp, n_dp):
        dp, mp = lax.axis_index("dp"), lax.axis_index("mp")
        return [(dp, lax.bitwise_xor(mp, k)) for k in range(1, n_mp)] + [
            (lax.bitwise_xor(dp, k), mp) for k in range(1, n_dp)
        ]

    def within(self, k):
        dp, mp = lax.axis_index("dp"), lax.axis_index("mp")
        sems = self.send.at[k], self.recv.at[k]
        return remote(self.held, self.near.at[mp], *sems, (dp, lax.bitwise_xor(mp, k)))

    def owner(self, k):
        dp, mp = lax.axis_index("dp"), lax.axis_index("mp")
        other = lax.bitwise_xor(dp, k)
        sems = self.send.at[self.group + k], self.recv.at[self.group + k]
        return remote(self.full.at[other], self.far.at[dp], *sems, (other, mp))

    def begin(self):
        for k in range(1, self.group):
            self.within(k).start()
        self.near[lax.axis_index("mp")] = self.held[...]

    def pass_on(self):
        for k in range(1, self.group):
            self.within(k).wait_recv()
        made = self.near[0]
        for i in range(1, self.group):
            made += self.near[i]
        self.full[...] = made
        for k in range(1, self.owners):
            self.owner(k).start()
        dp = lax.axis_index("dp")
        self.far[dp] = self.full[dp]

    def end(self):
        for k in range(1, self.owners):
            self.owner(k).wait_recv()
        made = self.far[0]
        for i in range(1, self.owners):
            made += self.far[i]
        for k in range(1, self.group):
            self.within(k).wait_send()
        for k in range(1, self.owners):
            self.owner(k).wait_send()
        return made


class Fold:
    def __init__(self, part, near, far, send, recv):
        self.part, self.near, self.far, self.send, self.recv = part, near, far, send, recv
        self.slots = part.shape[0]

    @staticmethod
    def scratch(n_mp, own, slots):
        dma = pltpu.SemaphoreType.DMA
        return [
            pltpu.VMEM((slots, n_mp, 2 * HDIM, own), BF16),
            pltpu.VMEM((slots, 2, 2 * HDIM, own), BF16),
            pltpu.VMEM((slots, 2 * HDIM, own), BF16),
            dma((slots, 3)),
            dma((slots, 3)),
        ]

    def message(self, kind, head):
        z, x, y, c = place()
        slot = lax.rem(head, self.slots)
        k = {"far": 0, "near": 1, "Y": 2}[kind]
        sems = self.send.at[slot, k], self.recv.at[slot, k]
        if kind == "Y":
            return remote(self.near.at[slot, 1 - y], self.far.at[slot], *sems, device(z, x, 1 - y, c))
        up = 1 - y if kind == "far" else y
        return remote(self.part.at[slot, 2 * up + 1 - c], self.near.at[slot, up], *sems, device(z, x, y, 1 - c))

    def begin(self, head):
        self.message("far", head).start()
        self.message("near", head).start()

    def chip(self, head):
        _, _, y, c = place()
        slot = lax.rem(head, self.slots)
        self.message("far", head).wait_recv()
        self.near[slot, 1 - y] = self.part[slot, 2 * (1 - y) + c] + self.near[slot, 1 - y]
        self.message("Y", head).start()

    def end(self, head):
        _, _, y, c = place()
        slot = lax.rem(head, self.slots)
        self.message("near", head).wait_recv()
        self.message("Y", head).wait_recv()
        made = self.part[slot, 2 * y + c].astype(F32) + self.near[slot, y].astype(F32) + self.far[slot].astype(F32)
        for kind in ("far", "near", "Y"):
            self.message(kind, head).wait_send()
        return made.astype(BF16)


def forward_kernel(nz, units, len_ref, tok_ref, *refs):
    linked = nz > 0
    given, refs = refs[: 6 if linked else 2], refs[6 if linked else 2 :]
    mine_ref, q_ref, k_ref, v_ref, cos_ref, sin_ref, o_ref, p_ref, inv_ref = refs[:9]
    full_refs, refs = refs[9 : 12 if linked else 9], refs[12 if linked else 9 :]
    wa_ref, wb_ref, w_ref, n1_ref, ka_ref, qa_ref, va_ref, stat_ref, load = refs[:9]
    refs = refs[9:]
    rows, features = tok_ref.shape
    own = q_ref.shape[1]
    docs = len_ref.shape[1]
    step = pl.program_id(0)
    parts = wa_ref.shape[0]
    part, turn_at = lax.rem(step, parts), step // parts
    me = lax.axis_index("mp")
    mine = pl.ds(pl.multiple_of(me * own, own), own)
    three = 3 * HDIM

    if linked:
        srcs = refs[:3]
        one = Gather(nz, srcs[0], wa_ref, *refs[3:6], eager=True)
        two = Gather(nz, srcs[1], wb_ref, *refs[6:9], eager=True)
        last = Gather(nz, srcs[2], full_refs[2], *refs[9:12])
        keeps = [
            pltpu.make_async_copy(wa_ref, full_refs[0], load.at[0]),
            pltpu.make_async_copy(wb_ref, full_refs[1], load.at[1]),
        ]

    @pl.when(step == 0)
    def _():
        if linked:
            wq_ref, wg_ref, wo_ref, wd_ref, one_ref, two_ref = given
            for i in range(3):
                srcs[0][:, i * HDIM : (i + 1) * HDIM] = wq_ref[i, :, :HDIM]
            srcs[0][:, three : three + 1] = one_ref[...].astype(F32).T.astype(BF16)
            srcs[0][:, three + 1 : three + 2] = two_ref[...].astype(F32).T.astype(BF16)
            down = wd_ref[...].T
            srcs[0][:, 256 - units % 128 :] = down[:, units - units % 128 :]
            greet(peers(nz))
            one.begin()
            for r in range(1, wq_ref.shape[2] // HDIM):
                for i in range(3):
                    at = (r - 1) * three + i * HDIM
                    srcs[1][:, at : at + HDIM] = wq_ref[i, :, r * HDIM : (r + 1) * HDIM]
            two.begin()
            pair, width = 2 * units, wo_ref.shape[0]
            for i in range(2):
                srcs[2][:, i * units : (i + 1) * units] = wg_ref[:, i, :]
            srcs[2][:, pair : pair + width] = wo_ref[...].T
            srcs[2][:, pair + width :] = down[:, : units - units % 128]
        else:
            fetches = [pltpu.make_async_copy(g, w, load.at[i]) for i, (g, w) in enumerate(zip(given, (wa_ref, wb_ref)))]
            for fetch in fetches:
                fetch.start()
        _, position, _ = layout_rows(len_ref, docs, 0, rows)
        power = lax.broadcasted_iota(jnp.int32, (HALF, 1), 0).astype(F32) * (-2.0 / HDIM * math.log2(ROPE_BASE))
        angle = position.astype(F32) * jnp.exp2(power)
        cos_ref[...] = jnp.cos(angle)
        sin_ref[...] = jnp.sin(angle)
        keys, _, _ = layout_rows(len_ref, docs, 0, rows)
        queries, _, _ = layout_rows(len_ref, docs, me * own, own)
        kind = lax.broadcasted_iota(jnp.int32, (AUG - HDIM, 1), 0)
        ka_ref[HDIM:] = jnp.where(kind == keys, 1.0, 0.0).astype(BF16)
        qa_ref[HDIM:] = jnp.where(kind == queries, 0.0, FAR).astype(BF16)
        va_ref[HDIM:] = jnp.ones((AUG - HDIM, rows), BF16)

        def measure(i, carry):
            at = pl.ds(pl.multiple_of(i * own, own), own)
            turned = tok_ref[at, :].T
            n1_ref[:, at] = turned
            mean, inv = moments(turned.astype(F32))
            stat_ref[0:1, at] = mean
            stat_ref[1:2, at] = inv
            return carry

        if linked:
            one.all_along()
        lax.fori_loop(0, rows // own, measure, 0)
        if linked:
            one.all_over()
            last.begin()
            one.rest()
            keeps[0].start()
        else:
            for fetch in fetches:
                fetch.wait()
        gain = wa_ref[0, :, three : three + 1].astype(F32)

        def norm(i, carry):
            at = pl.ds(pl.multiple_of(i * own, own), own)
            made = (n1_ref[:, at].astype(F32) - stat_ref[0:1, at]) * stat_ref[1:2, at] * gain
            n1_ref[:, at] = made.astype(BF16)
            return carry

        lax.fori_loop(0, rows // own, norm, 0)
        mine_ref[...] = n1_ref[:, mine]

    if linked:
        gathers = {"two": two, "last": last}
        for at, which, name, *d in GATHER_STEPS:
            pl.when(step == at)(functools.partial(getattr(gathers[which], name), *d))

        @pl.when(step == parts)
        def _():
            two.rest()
            keeps[1].start()

    @pl.when(turn_at == 0)
    def _():
        w_ref[...] = wa_ref[part, :, :three]

    for r in range(1, 1 + wb_ref.shape[2] // three):

        @pl.when(turn_at == r)
        def _():
            w_ref[...] = wb_ref[part, :, (r - 1) * three : r * three]

    made = dot(w_ref[:, HDIM:], n1_ref[...], TN)
    keys = turn(made[:HDIM], cos_ref[...], sin_ref[...], 1).astype(BF16)
    k_ref[...] = keys
    ka_ref[:HDIM] = keys
    values = made[HDIM:].astype(BF16)
    v_ref[...] = values
    va_ref[:HDIM] = values
    made = dot(w_ref[:, :HDIM], n1_ref[:, mine], TN) * (SCALE * LOG2E)
    queries = turn(made, cos_ref[:, mine], sin_ref[:, mine], 1).astype(BF16)
    q_ref[...] = queries
    qa_ref[:HDIM] = queries
    scores = dot(ka_ref[...], qa_ref[...], TN)
    top = jnp.max(scores, axis=0, keepdims=True)
    probs = jnp.exp2(scores - top).astype(BF16)
    p_ref[0] = probs
    out = dot(va_ref[...], probs, NN)
    inv = 1.0 / out[HDIM : HDIM + 1]
    o_ref[...] = (out[:HDIM] * inv).astype(BF16)
    inv_ref[0] = inv
    if linked:

        @pl.when(step == pl.num_programs(0) - 1)
        def _():
            for keep in keeps:
                keep.wait()
            last.corner(3)
            last.end()


GATHER_STEPS = (
    (0, "two", "along", 1),
    (0, "two", "along", 2),
    (0, "two", "along", 3),
    (0, "last", "push", 2),
    (1, "two", "over", 0),
    (1, "two", "over", 1),
    (2, "two", "over", 2),
    (2, "two", "over", 3),
    (2, "last", "push", 3),
    (3, "last", "along", 1),
    (3, "last", "over", 0),
    (4, "last", "along", 2),
    (5, "last", "over", 1),
    (6, "last", "corner", 0),
    (6, "last", "along", 3),
    (7, "last", "over", 2),
    (8, "last", "corner", 1),
    (9, "last", "over", 3),
    (11, "last", "corner", 2),
)


def forward(nz, n_mp, units, lengths, tokens, weights, columns):
    rows, features = tokens.shape
    own, width, heads = rows // n_mp, features // n_mp, features // HDIM
    per = width // HDIM
    linked = nz > 0
    hbm = pl.BlockSpec(memory_space=pl.ANY)
    head = lambda h: lax.rem(h, n_mp) * per + h // n_mp
    row = lambda h: (head(h), 0)
    cube = lambda h: (head(h), 0, 0)
    vm = pl.BlockSpec(memory_space=pltpu.VMEM)
    n = Gather.count(nz) if linked else 0
    dma = pltpu.SemaphoreType.DMA
    depth = features // (2 * nz) if linked else 0
    full_shapes = [jax.ShapeDtypeStruct((n_mp, features, c), BF16) for c in columns] if linked else []
    return pl.pallas_call(
        functools.partial(forward_kernel, nz, units),
        grid=(heads,),
        in_specs=[pl.BlockSpec(memory_space=pltpu.SMEM), vm] + ([vm] * 6 if linked else [hbm] * 2),
        out_specs=[
            whole(features, own),
            pl.BlockSpec((HDIM, own), row),
            pl.BlockSpec((HDIM, rows), row),
            pl.BlockSpec((HDIM, rows), row),
            whole(HALF, rows),
            whole(HALF, rows),
            pl.BlockSpec((HDIM, own), row),
            pl.BlockSpec((1, rows, own), cube),
            pl.BlockSpec((1, 1, own), cube),
        ]
        + [hbm] * len(full_shapes),
        out_shape=[
            jax.ShapeDtypeStruct((features, own), BF16),
            jax.ShapeDtypeStruct((features, own), BF16),
            jax.ShapeDtypeStruct((features, rows), BF16),
            jax.ShapeDtypeStruct((features, rows), BF16),
            jax.ShapeDtypeStruct((HALF, rows), F32),
            jax.ShapeDtypeStruct((HALF, rows), F32),
            jax.ShapeDtypeStruct((features, own), BF16),
            jax.ShapeDtypeStruct((heads, rows, own), BF16),
            jax.ShapeDtypeStruct((heads, 1, own), F32),
        ]
        + full_shapes,
        scratch_shapes=[
            pltpu.VMEM((n_mp, features, columns[0]), BF16),
            pltpu.VMEM((n_mp, features, columns[1]), BF16),
            pltpu.VMEM((features, 3 * HDIM), BF16),
            pltpu.VMEM((features, rows), BF16),
            pltpu.VMEM((AUG, rows), BF16),
            pltpu.VMEM((AUG, own), BF16),
            pltpu.VMEM((AUG, rows), BF16),
            pltpu.VMEM((8, rows), F32),
            dma((2,)),
        ]
        + (
            [pltpu.VMEM((depth, c), BF16) for c in columns] + [dma((n,)), dma((n,)), dma] * 3
            if linked
            else []
        ),
        compiler_params=pltpu.CompilerParams(
            dimension_semantics=("arbitrary",),
            vmem_limit_bytes=VMEM_BYTES,
            **({"collective_id": 1, "has_side_effects": True} if linked else {}),
        ),
        name="forward",
    )(lengths, tokens, *weights)


def middle(len_ref, me, tok_ref, cot_ref, heads_ref, inv_ref, w_ref, gain, units, out_ref, mcot_ref, do_ref, keep, sent, done, later):
    own, features = tok_ref.shape
    parts = w_ref.shape[0]
    width = features // parts
    heads = width // HDIM
    pair = 2 * units
    _, _, live = layout_rows(len_ref, len_ref.shape[1], me * own, own)

    def w_gu(m):
        return w_ref[m, :, :pair]

    def w_out(m):
        return w_ref[m, :, pair : pair + width]

    def w_down(m):
        return w_ref[m, :, pair + width : pair + width + units]

    total = dot(w_out(0), heads_ref[:width], NN)
    for m in range(1, parts):
        total += dot(w_out(m), heads_ref[m * width : (m + 1) * width], NN)
    middle = tok_ref[...].T.astype(F32) + total
    hat, inv_sigma = normalize(middle)
    normed = (hat * gain).astype(BF16)
    total = middle
    kept = []
    for m in range(parts):
        gate_up = dot(w_gu(m), normed, TN)
        gate, up = gate_up[:units], gate_up[units:]
        phi, slope = gelu_parts(gate)
        act = gate * phi
        hidden = (act * up).astype(BF16)
        total += dot(w_down(m), hidden, NN)
        kept.append((hidden, (up * (phi + slope)).astype(BF16), act.astype(BF16)))
    out_ref[...] = total.astype(BF16).T
    sent()
    branch = jnp.where(live, cot_ref[...].T.astype(F32), 0.0).astype(BF16)
    back = jnp.zeros((features, own), F32)
    for m in range(parts):
        hidden, one, two = kept[m]
        hidden_cot = dot(w_down(m), branch, TN)
        keep("down", m, dot(branch, hidden, NT).astype(BF16))
        cots = jnp.concatenate([hidden_cot * one.astype(F32), hidden_cot * two.astype(F32)], axis=0).astype(BF16)
        keep("gu", m, dot(normed, cots, NT).astype(BF16))
        back += dot(w_gu(m), cots, NN)
    done()
    keep("gain", 0, jnp.sum(back * hat, axis=1, keepdims=True))
    d = back * gain
    middle_cot = branch.astype(F32) + inv_sigma * (
        d - jnp.mean(d, axis=0, keepdims=True) - hat * jnp.mean(d * hat, axis=0, keepdims=True)
    )
    mcot_ref[...] = middle_cot
    attn_cot = middle_cot.astype(BF16)
    for m in range(parts):
        back_heads = dot(w_out(m), attn_cot, TN)
        for h in range(heads):
            head = m * heads + h
            rows = slice(h * HDIM, (h + 1) * HDIM)
            cot = back_heads[rows] * inv_ref[head]
            inner = jnp.sum(cot * heads_ref[head * HDIM : (head + 1) * HDIM].astype(F32), axis=0, keepdims=True)
            high = inner.astype(BF16).astype(F32)
            pad = jnp.zeros((AUG - HDIM - 2, own), F32)
            do_ref[head] = jnp.concatenate([cot, high, inner - high, pad], axis=0).astype(BF16)
    later()
    for m in range(parts):
        keep("out", m, dot(attn_cot, heads_ref[m * width : (m + 1) * width], NT).astype(BF16))


def mid_kernel(
    units, len_ref, tok_hbm, cot_hbm, heads_ref, inv_ref, two_ref, w_hbm,
    out_ref, mcot_ref, do_ref, g_ref, o_ref, gain_ref, tok_ref, cot_ref, w_ref, load,
):
    own = tok_ref.shape[0]
    me = lax.axis_index("mp")
    mine = pl.ds(pl.multiple_of(me * own, own), own)
    loads = [
        pltpu.make_async_copy(tok_hbm.at[mine], tok_ref, load.at[0]),
        pltpu.make_async_copy(cot_hbm.at[mine], cot_ref, load.at[1]),
        pltpu.make_async_copy(w_hbm, w_ref, load.at[2]),
    ]
    for copy in loads:
        copy.start()
    for copy in loads:
        copy.wait()
    pair = 2 * units

    def keep(what, m, made):
        if what == "gu":
            g_ref[m, :, :pair] = made
        elif what == "down":
            g_ref[m, :, pair:] = made
        elif what == "out":
            o_ref[m] = made
        else:
            gain_ref[...] = made

    nothing = lambda: None
    middle(
        len_ref, me, tok_ref, cot_ref, heads_ref, inv_ref, w_ref, two_ref[...].astype(F32), units, out_ref, mcot_ref, do_ref,
        keep, nothing, nothing, nothing,
    )


def mid(n_mp, lengths, tokens, out_grad, heads_out, inv, gain, w_rest, units):
    features, own = heads_out.shape
    heads = inv.shape[0]
    vm = pl.BlockSpec(memory_space=pltpu.VMEM)
    hbm = pl.BlockSpec(memory_space=pl.ANY)
    return pl.pallas_call(
        functools.partial(mid_kernel, units),
        in_specs=[pl.BlockSpec(memory_space=pltpu.SMEM), hbm, hbm, vm, vm, vm, hbm],
        out_specs=[vm] * 6,
        out_shape=[
            jax.ShapeDtypeStruct((own, features), BF16),
            jax.ShapeDtypeStruct((features, own), F32),
            jax.ShapeDtypeStruct((heads, AUG, own), BF16),
            jax.ShapeDtypeStruct((n_mp, features, 3 * units), BF16),
            jax.ShapeDtypeStruct((n_mp, features, features // n_mp), BF16),
            jax.ShapeDtypeStruct((features, 1), F32),
        ],
        scratch_shapes=[
            pltpu.VMEM((own, features), BF16),
            pltpu.VMEM((own, features), BF16),
            pltpu.VMEM(w_rest.shape, BF16),
            pltpu.SemaphoreType.DMA((3,)),
        ],
        compiler_params=pltpu.CompilerParams(vmem_limit_bytes=VMEM_BYTES),
        name="mid",
    )(lengths, tokens, out_grad, heads_out, inv, gain, w_rest)


SLOTS = 7
LAG = 4
PIECES = 4


def backward_kernel(nz, units, *refs):
    len_ref, q_ref, k_ref, v_ref, p_ref, cos_ref, sin_ref, n1_ref, heads_ref, inv_ref, wa_ref, tok_hbm, cot_hbm, wb_hbm, wr_hbm = refs[:15]
    dq_ref, dr_ref, gains_ref, in_full, out_full = refs[15:20]
    wb_ref, wr_ref, gr_ref, do_ref, mcot_ref, pc_ref, qc_ref, acc_ref, gc_ref, va_ref, tok_ref, cot_ref, own_ref, load = refs[20:34]
    refs = refs[34:]
    gq_ref = wr_ref.at[:, :, pl.ds(0, dq_ref.shape[1])]
    rest = Scatter(nz, (0, 1), gr_ref, gr_ref, dr_ref, *refs[:6])
    low = Scatter(nz, (0,), gq_ref, gq_ref, dq_ref, *refs[6:12])
    high = Scatter(nz, (1,), gq_ref, gq_ref, dq_ref, *refs[12:18])
    fold = Fold(*refs[18:23])
    in_share = Share(own_ref.at[0], in_full, *refs[23:26], PIECES)
    out_share = Share(own_ref.at[1], out_full, *refs[26:29])
    gains = Everyone(*refs[29:35])
    step, heads = pl.program_id(0) - 1, pl.num_programs(0) - 1
    parts = wa_ref.shape[0]
    features, own = n1_ref.shape
    rows = k_ref.shape[1]
    width = features // parts
    per = width // HDIM
    me = lax.axis_index("mp")
    mine = pl.ds(pl.multiple_of(me * own, own), own)
    late = pltpu.make_async_copy(wb_hbm, wb_ref, load.at[3])
    three = 3 * HDIM
    depth = gains_ref.shape[1]
    shards = features // depth

    def put(row, column):
        for i in range(shards):
            gains.held[i, row : row + 1, :depth] = column[i * depth : (i + 1) * depth].T

    @pl.when(step < 0)
    def _():
        gains.held[0] = jnp.zeros(gains.held.shape[1:], F32)
        loads = [
            pltpu.make_async_copy(wr_hbm, wr_ref.at[:, :, pl.ds(0, wr_hbm.shape[2])], load.at[0]),
            pltpu.make_async_copy(tok_hbm.at[mine], tok_ref, load.at[1]),
            pltpu.make_async_copy(cot_hbm.at[mine], cot_ref, load.at[2]),
        ]
        for copy in loads:
            copy.start()
        greet(Everyone.peers(parts, 2 * nz))
        for copy in loads:
            copy.wait()
        late.start()
        pair = 2 * units

        def first():
            rest.chip(2)
            rest.cross(2)

        for m in range(parts):
            wr_ref[m, :, wr_hbm.shape[2] :] = wa_ref[m, :, 256 - units % 128 :]

        def keep(what, m, made):
            if what == "gu":
                gr_ref[m, :, :pair] = made
            elif what == "down":
                gr_ref[m, :, pair:] = made
            elif what == "out":
                wr_ref[m, :, 3 * width : 4 * width] = made
            else:
                put(1, made)

        middle(
            len_ref, me, tok_ref, cot_ref, heads_ref, inv_ref, wr_ref, wa_ref[0, :, three + 1 : three + 2].astype(F32), units,
            own_ref.at[1], mcot_ref, do_ref, keep,
            lambda: out_share.begin(0), lambda: rest.begin(2, 3), first,
        )
        va_ref[HDIM:] = jnp.full((AUG - HDIM, rows), -1.0, BF16)
        acc_ref[...] = jnp.zeros_like(acc_ref)
        gc_ref[...] = jnp.zeros_like(gc_ref)
        late.wait()

    def collect(head):
        at = lax.rem(head, per) * three
        pc_ref[pl.ds(pl.multiple_of(at + HDIM, HDIM), 2 * HDIM)] = fold.end(head)

    def close(part):
        for i in range(per):
            pc_ref[i * three : i * three + HDIM] = qc_ref[lax.rem(part, 3), i * HDIM : (i + 1) * HDIM]
        made = dot(n1_ref[...], pc_ref[...], NT)
        wr_ref[part, :, : 3 * width] = made.astype(BF16)
        weights = jnp.concatenate([wa_ref[part, :, :three], wb_ref[part]], axis=1)
        gc_ref[...] += jnp.sum(made * weights.astype(F32), axis=1, keepdims=True)
        acc_ref[...] += dot(weights, pc_ref[...], NN)

    @pl.when(step >= 0)
    def _():
        va_ref[:HDIM] = v_ref[...]
        cot = dot(va_ref[...], do_ref[step], TN)
        probs = p_ref[0]
        score_cot = probs * cot.astype(BF16)
        dv = dot(do_ref[step, :HDIM], probs, NT).astype(BF16)
        dk = turn(dot(q_ref[...], score_cot, NT) * LN2, cos_ref[...], sin_ref[...], 1, True).astype(BF16)
        dq = turn(dot(k_ref[...], score_cot, NN) * SCALE, cos_ref[:, mine], sin_ref[:, mine], 1, True)
        slot = lax.rem(step, SLOTS)
        for m in range(parts):
            fold.part[slot, m, :HDIM] = dk[:, m * own : (m + 1) * own]
            fold.part[slot, m, HDIM:] = dv[:, m * own : (m + 1) * own]
        at = pl.ds(pl.multiple_of(lax.rem(step, per) * HDIM, HDIM), HDIM)
        qc_ref[lax.rem(step // per, 3), at] = dq.astype(BF16)

        @pl.when(step >= LAG)
        def _():
            collect(step - LAG)

        @pl.when(step >= 1)
        def _():
            fold.chip(step - 1)

        fold.begin(step)

        @pl.when((step >= LAG) & (lax.rem(step - LAG, per) == per - 1))
        def _():
            close((step - LAG) // per)

    sums = {"rest": rest, "low": low, "high": high, "out": out_share, "in": in_share, "gains": gains}
    for at, which, name, *d in SUM_STEPS:
        pl.when(step == at)(functools.partial(getattr(sums[which], name), *d))

    @pl.when(step == heads - 1)
    def _():
        fold.chip(step)
        for which, name, *d in FLUSH_STEPS:
            getattr(sums[which], name)(*d)
        for back in range(LAG - 1, -1, -1):
            collect(step - back)
            if (features // HDIM - 1 - back) % per == per - 1:
                close((step - back) // per)
        high.begin(2, 3, 1, 0)
        gain = wa_ref[0, :, three : three + 1].astype(F32)
        put(0, gc_ref[...] / gain)
        gains.begin()
        size = own // PIECES
        for i in range(PIECES):
            at = slice(i * size, (i + 1) * size)
            own_ref[0, at] = finish(tok_ref[at], gain, acc_ref[:, at], mcot_ref[:, at])
            in_share.begin(i)
        for which, name, *d in LAST_STEPS:
            getattr(sums[which], name)(*d)
        high.along()
        for which in (rest, low, high):
            which.end()
        out_share.end()
        in_share.end()
        gains_ref[...] = gains.end()[:2, :depth]


SUM_STEPS = (
    (-1, "rest", "begin", 1, 0),
    (-1, "rest", "chip", 3),
    (0, "rest", "cross", 3),
    (0, "rest", "chip", 1),
    (0, "rest", "chip", 0),
    (1, "rest", "over", 2),
    (1, "out", "on", 0),
    (3, "rest", "cross", 1),
    (4, "rest", "over", 3),
    (6, "rest", "cross", 0),
    (7, "rest", "over", 1),
    (9, "low", "begin", 2, 3, 1, 0),
    (10, "low", "chip", 2),
    (10, "low", "chip", 3),
    (10, "low", "chip", 1),
    (10, "low", "chip", 0),
    (10, "low", "cross", 2),
    (10, "low", "cross", 3),
    (10, "low", "cross", 1),
    (10, "low", "cross", 0),
    (9, "rest", "over", 0),
)
FLUSH_STEPS = (
    ("rest", "along"),
    ("low", "over", 2),
    ("low", "over", 3),
)
LAST_STEPS = (
    ("high", "chip", 2),
    ("high", "cross", 2),
    ("high", "chip", 3),
    ("high", "cross", 3),
    ("high", "chip", 1),
    ("high", "cross", 1),
    ("high", "chip", 0),
    ("high", "cross", 0),
    ("low", "over", 1),
    ("low", "over", 0),
    ("gains", "pass_on"),
    ("high", "over", 2),
    ("in", "on", 0),
    ("high", "over", 3),
    ("in", "on", 1),
    ("high", "over", 1),
    ("low", "along"),
    ("high", "over", 0),
    ("in", "on", 2),
    ("in", "on", 3),
)


def backward(nz, lengths, q, k, v, p, cos, sin, n1, heads_out, inv, tokens, out_grad, w_a, w_b, w_rest, units):
    (features, own), rows = q.shape, k.shape[1]
    n_mp = w_a.shape[0]
    heads = features // HDIM
    width = features // n_mp
    depth = features // (2 * nz)
    columns = 4 * width, 3 * units
    hbm = pl.BlockSpec(memory_space=pl.ANY)
    vm = pl.BlockSpec(memory_space=pltpu.VMEM)
    row = lambda h: (jnp.maximum(h - 1, 0), 0)
    cube = lambda h: (jnp.maximum(h - 1, 0), 0, 0)
    dma = pltpu.SemaphoreType.DMA
    return pl.pallas_call(
        functools.partial(backward_kernel, nz, units),
        grid=(heads + 1,),
        in_specs=[
            pl.BlockSpec(memory_space=pltpu.SMEM),
            pl.BlockSpec((HDIM, own), row),
            pl.BlockSpec((HDIM, rows), row),
            pl.BlockSpec((HDIM, rows), row),
            pl.BlockSpec((1, rows, own), cube),
        ]
        + [vm] * 6
        + [hbm] * 4,
        out_specs=[vm, vm, vm, hbm, hbm],
        out_shape=[
            jax.ShapeDtypeStruct((depth, columns[0]), F32),
            jax.ShapeDtypeStruct((depth, columns[1]), F32),
            jax.ShapeDtypeStruct((2, depth), F32),
            jax.ShapeDtypeStruct((rows, features), BF16),
            jax.ShapeDtypeStruct((rows, features), BF16),
        ],
        scratch_shapes=[
            pltpu.VMEM(w_b.shape, BF16),
            pltpu.VMEM((n_mp, features, width + 3 * units), BF16),
            pltpu.VMEM((n_mp, features, 3 * units), BF16),
            pltpu.VMEM((heads, AUG, own), BF16),
            pltpu.VMEM((features, own), F32),
            pltpu.VMEM((3 * width, own), BF16),
            pltpu.VMEM((3, width, own), BF16),
            pltpu.VMEM((features, own), F32),
            pltpu.VMEM((features, 1), F32),
            pltpu.VMEM((AUG, rows), BF16),
            pltpu.VMEM((own, features), BF16),
            pltpu.VMEM((own, features), BF16),
            pltpu.VMEM((2, own, features), BF16),
            dma((4,)),
        ]
        + Scatter.scratch(nz, (0, 1), depth, columns[1])
        + Scatter.scratch(nz, (0,), depth, columns[0])
        + Scatter.scratch(nz, (1,), depth, columns[0])
        + Fold.scratch(n_mp, own, SLOTS)
        + Share.sems(PIECES)
        + Share.sems(1)
        + Everyone.scratch(n_mp, 2 * nz),
        compiler_params=pltpu.CompilerParams(
            dimension_semantics=("arbitrary",), collective_id=3, has_side_effects=True, vmem_limit_bytes=VMEM_BYTES
        ),
        name="backward",
    )(lengths, q, k, v, p, cos, sin, n1, heads_out, inv, w_a, tokens, out_grad, w_b, w_rest)


def deliver_kernel(units, in_ref, out_ref, dq_ref, dr_ref, gains_ref, grad_ref, to_ref, gq_ref, go_ref, gg_ref, gd_ref, one_ref, two_ref):
    @pl.when(pl.program_id(0) == 0)
    def _():
        width = go_ref.shape[0]
        pair = 2 * units
        for r in range(width // HDIM):
            for i in range(3):
                at = (3 * r + i) * HDIM
                gq_ref[i, :, r * HDIM : (r + 1) * HDIM] = dq_ref[:, at : at + HDIM]
        go_ref[...] = dq_ref[:, 3 * width : 4 * width].T
        one_ref[...] = gains_ref[0:1]
        two_ref[...] = gains_ref[1:2]
        for i in range(2):
            gg_ref[:, i, :] = dr_ref[:, i * units : (i + 1) * units]
        gd_ref[...] = dr_ref[:, pair : pair + units].T

    grad_ref[...] = in_ref[...].astype(F32)
    to_ref[...] = out_ref[...]


def deliver(layer_out, input_grad, d_qkv, d_rest, gains, width, units):
    rows, features = input_grad.shape
    depth = d_qkv.shape[0]
    shape = lambda *s: jax.ShapeDtypeStruct(s, F32)
    shapes = [(3, depth, width), (width, depth), (depth, 2, units), (units, depth), (1, depth), (1, depth)]
    steps = 2
    slab = pl.BlockSpec((rows // steps, features), lambda i: (i, 0))
    return pl.pallas_call(
        functools.partial(deliver_kernel, units),
        grid=(steps,),
        in_specs=[slab, slab, whole(*d_qkv.shape), whole(*d_rest.shape), whole(*gains.shape)],
        out_specs=[slab, slab] + [whole(*s) for s in shapes],
        out_shape=[shape(rows, features), jax.ShapeDtypeStruct((rows, features), BF16)] + [shape(*s) for s in shapes],
        compiler_params=params("arbitrary"),
        name="deliver",
    )(input_grad, layer_out, d_qkv, d_rest, gains)


def per_device(n_dp, n_mp, tokens, out_grad, w_qkv, w_out, w_gu, w_down, gain_attn, gain_mlp, lengths):
    rows, features = tokens.shape
    depth = w_qkv.shape[0]
    units, width = w_down.shape[0], w_out.shape[0]
    everyone = ("mp", "dp")
    linked = n_mp == 4 and n_dp == 8 and depth % 32 == 0 and features // HDIM == 12
    nz = n_dp // 2 if linked else 0
    three = 3 * HDIM
    loose = units % 128
    columns = 256, 3 * width - three, 3 * units + width - loose
    wq = w_qkv.transpose(1, 0, 2)
    if linked:
        weights = wq, w_gu, w_out, w_down, gain_attn[None], gain_mlp[None]
        n1, q, k, v, cos, sin, heads_out, probs, inv, w_a, w_b, w_c = forward(
            nz, n_mp, units, lengths, tokens, weights, columns
        )
        d_qkv, d_rest, gains, in_full, layer_out = backward(
            nz, lengths, q, k, v, probs, cos, sin, n1, heads_out, inv, tokens, out_grad, w_a, w_b, w_c, units
        )
    else:
        by_head = w_qkv.reshape(depth, 3, width // HDIM, HDIM).transpose(0, 2, 1, 3).reshape(depth, 3 * width)
        blank = jnp.zeros((depth, columns[0] - three - 2), BF16)
        shards = [
            jnp.concatenate([by_head[:, :three], gain_attn[:, None], gain_mlp[:, None], blank], axis=1),
            by_head[:, three:],
            jnp.concatenate([w_gu.reshape(depth, -1), w_out.T, w_down.T], axis=1),
        ]
        w_a, w_b, w_c = (
            lax.all_gather(s, everyone, axis=0, tiled=True).reshape(n_mp, features, s.shape[1]) for s in shards
        )
        n1, q, k, v, cos, sin, heads_out, probs, inv = forward(nz, n_mp, units, lengths, tokens, [w_a, w_b], columns)
        layer_out, middle_cot, do, g_rest, g_out, gain_two = mid(
            n_mp, lengths, tokens, out_grad, heads_out, inv, w_a[0, :, three + 1 : three + 2], w_c, units
        )
        own = middle_cot.shape[1]
        swap = lambda g, a, b: g.reshape(n_mp, features, a, b, HDIM).swapaxes(2, 3).reshape(n_mp, features, 3 * width)
        natural = jnp.concatenate([w_a[..., :three], w_b], axis=2)
        natural = jnp.concatenate([swap(natural, width // HDIM, 3), w_a[..., three : three + 1]], axis=2)
        g_qkv, nc = last(q, k, v, do, probs, cos, sin, lax.all_gather(n1, "mp", axis=1, tiled=True), natural)
        gain_one = w_a[0, :, three : three + 1].astype(F32)
        tok = lax.dynamic_slice_in_dim(tokens, lax.axis_index("mp") * own, own, 0)
        nc_own = lax.psum_scatter(nc, "mp", scatter_dimension=0, tiled=True)[0]
        in_own = finish(tok, gain_one, nc_own.astype(F32), middle_cot)
        layer_out, in_full = (lax.all_gather(v, "mp", axis=0, tiled=True) for v in (layer_out, in_own))
        both = jnp.stack([g_qkv[0, :, -1].astype(F32), gain_two[:, 0]])
        both = lax.psum(both, everyone)
        gains = lax.dynamic_slice_in_dim(both, lax.axis_index("dp") * depth, depth, 1)
        g_qkv = jnp.concatenate([swap(g_qkv[..., : 3 * width], 3, width // HDIM), g_out], axis=2)
        d_qkv, d_rest = (
            lax.psum_scatter(
                g.reshape(n_mp * features, -1), everyone, scatter_dimension=0, tiled=True
            ).astype(F32)
            for g in (g_qkv, g_rest)
        )
    input_grad, layer_out, g_q, g_o, g_g, g_d, one, two = deliver(
        layer_out, in_full, d_qkv, d_rest, gains, width, units
    )
    return layer_out, input_grad, g_q.transpose(1, 0, 2), g_o, g_g, g_d, one[0], two[0]


def solution(mesh):
    n_dp, n_mp = mesh.shape["dp"], mesh.shape["mp"]
    return jax.shard_map(
        functools.partial(per_device, n_dp, n_mp),
        mesh=mesh,
        in_specs=(
            P("dp", None),
            P("dp", None),
            P("dp", None, "mp"),
            P("mp", "dp"),
            P("dp", None, "mp"),
            P("mp", "dp"),
            P("dp"),
            P("dp"),
            P("dp", None),
        ),
        out_specs=(
            P("dp", None),
            P("dp", None),
            P("dp", None, "mp"),
            P("mp", "dp"),
            P("dp", None, "mp"),
            P("mp", "dp"),
            P("dp"),
            P("dp"),
        ),
        check_vma=False,
    )
```

```python
import functools
import math

import jax
import jax.numpy as jnp
from jax import lax
from jax.experimental import pallas as pl
from jax.experimental.pallas import tpu as pltpu
from jax.sharding import PartitionSpec as P

HDIM = 64
HALF = HDIM // 2
AUG = HDIM + 16
EPS = 1e-05
ROPE_BASE = 160000.0
LOG2E = math.log2(math.e)
LN2 = math.log(2.0)
SCALE = HDIM ** (-0.5)
FAR = -1e30
BF16 = jnp.bfloat16
F32 = jnp.float32
VMEM_BYTES = 60 << 20
NN = (((1,), (0,)), ((), ()))
NT = (((1,), (1,)), ((), ()))
TN = (((0,), (0,)), ((), ()))


def dot(a, b, dims):
    return lax.dot_general(a, b, dims, preferred_element_type=F32)


def params(*semantics):
    return pltpu.CompilerParams(
        dimension_semantics=semantics or None, vmem_limit_bytes=VMEM_BYTES
    )


def whole(*shape):
    return pl.BlockSpec(shape, lambda *i: (0,) * len(shape))


def layout_rows(len_ref, docs, first, rows):
    index = first + lax.broadcasted_iota(jnp.int32, (1, rows), 1)
    segment = jnp.zeros((1, rows), jnp.int32)
    start = jnp.zeros((1, rows), jnp.int32)
    end = jnp.int32(0)
    for j in range(docs):
        end = end + len_ref[0, j]
        past = index >= end
        segment = segment + jnp.where(past, 1, 0)
        start = jnp.where(past, jnp.maximum(start, end), start)
    return segment, index - start, index < end


def moments(columns):
    mean = jnp.mean(columns, axis=0, keepdims=True)
    centered = columns - mean
    return mean, lax.rsqrt(jnp.mean(centered * centered, axis=0, keepdims=True) + EPS)


def normalize(columns):
    mean, inv = moments(columns)
    return (columns - mean) * inv, inv


def turn(block, cos, sin, heads, back=False):
    out = []
    for h in range(heads):
        one = block[h * HDIM : h * HDIM + HALF]
        two = block[h * HDIM + HALF : (h + 1) * HDIM]
        if back:
            out += [one * cos + two * sin, two * cos - one * sin]
        else:
            out += [one * cos - two * sin, two * cos + one * sin]
    return jnp.concatenate(out, axis=0)


def gelu_parts(gate):
    phi = 0.5 * (1.0 + lax.erf(gate * math.sqrt(0.5)))
    density = jnp.exp2(gate * gate * (-0.5 * LOG2E)) * (1.0 / math.sqrt(2.0 * math.pi))
    return phi, gate * density


def last_kernel(own_axis, q_ref, k_ref, v_ref, do_ref, p_ref, cos_ref, sin_ref, n1_ref, w_ref, gq_ref, nc_ref, gc_ref, dq_ref, pc_ref, acc_ref, va_ref):
    step, head = pl.program_id(0), pl.program_id(1)
    per = pl.num_programs(1)
    features, rows = n1_ref.shape
    own = q_ref.shape[1]
    width = per * HDIM
    mine = pl.ds(pl.multiple_of(lax.axis_index(own_axis) * own, own), own)

    @pl.when((step == 0) & (head == 0))
    def _():
        va_ref[HDIM:] = jnp.full((AUG - HDIM, rows), -1.0, BF16)
        acc_ref[...] = jnp.zeros_like(acc_ref)
        gc_ref[...] = jnp.zeros_like(gc_ref)

    va_ref[:HDIM] = v_ref[...]
    cot = dot(va_ref[...], do_ref[0], TN)
    probs = p_ref[0]
    score_cot = probs * cot.astype(BF16)
    at = pl.ds(pl.multiple_of(head * HDIM, HDIM), HDIM)
    dv = dot(do_ref[0, :HDIM], probs, NT)
    dk = dot(q_ref[...], score_cot, NT) * LN2
    dq = dot(k_ref[...], score_cot, NN) * SCALE
    pc_ref[pl.ds(pl.multiple_of(width + head * HDIM, HDIM), HDIM)] = dv.astype(BF16)
    pc_ref[at] = turn(dk, cos_ref[...], sin_ref[...], 1, True).astype(BF16)
    dq_ref[at] = turn(dq, cos_ref[:, mine], sin_ref[:, mine], 1, True).astype(BF16)

    @pl.when(head == per - 1)
    def _():
        kv = dot(n1_ref[...], pc_ref[...], NT)
        q = dot(n1_ref[:, mine], dq_ref[...], NT)
        gq_ref[step, :, :width] = q.astype(BF16)
        gq_ref[step, :, width : 3 * width] = kv.astype(BF16)
        gc_ref[...] += jnp.sum(q * w_ref[0, :, :width].astype(F32), axis=1, keepdims=True) + jnp.sum(
            kv * w_ref[0, :, width : 3 * width].astype(F32), axis=1, keepdims=True
        )

        def spread(i, carry):
            cols = pl.ds(pl.multiple_of(i * own, own), own)
            acc_ref[:, cols] += dot(w_ref[0, :, width : 3 * width], pc_ref[:, cols], NN)
            return carry

        lax.fori_loop(0, rows // own, spread, 0)
        acc_ref[:, mine] += dot(w_ref[0, :, :width], dq_ref[...], NN)

    @pl.when((step == pl.num_programs(0) - 1) & (head == per - 1))
    def _():
        gain_cot = (gc_ref[...] / w_ref[0, :, 3 * width :].astype(F32)).astype(BF16)
        for m in range(gq_ref.shape[0]):
            nc_ref[m] = acc_ref[:, m * own : (m + 1) * own].astype(BF16)
            gq_ref[m, :, 3 * width :] = gain_cot


def last(q, k, v, do, p, cos, sin, n1, w_qkv, own_axis="mp"):
    (features, own), rows = q.shape, k.shape[1]
    parts = w_qkv.shape[0]
    per = features // parts // HDIM
    width = per * HDIM
    head = lambda m, h: (m * per + h, 0)
    return pl.pallas_call(
        functools.partial(last_kernel, own_axis),
        grid=(parts, per),
        in_specs=[
            pl.BlockSpec((HDIM, own), head),
            pl.BlockSpec((HDIM, rows), head),
            pl.BlockSpec((HDIM, rows), head),
            pl.BlockSpec((1, AUG, own), lambda m, h: (m * per + h, 0, 0)),
            pl.BlockSpec((1, rows, own), lambda m, h: (m * per + h, 0, 0)),
            whole(HALF, rows),
            whole(HALF, rows),
            whole(features, rows),
            pl.BlockSpec((1,) + w_qkv.shape[1:], lambda m, h: (m, 0, 0)),
        ],
        out_specs=[
            whole(*w_qkv.shape),
            whole(parts, features, own),
        ],
        out_shape=[
            jax.ShapeDtypeStruct(w_qkv.shape, BF16),
            jax.ShapeDtypeStruct((parts, features, own), BF16),
        ],
        scratch_shapes=[
            pltpu.VMEM((features, 1), F32),
            pltpu.VMEM((width, own), BF16),
            pltpu.VMEM((2 * width, rows), BF16),
            pltpu.VMEM((features, rows), F32),
            pltpu.VMEM((AUG, rows), BF16),
        ],
        compiler_params=params("arbitrary", "arbitrary"),
        name="last",
    )(q, k, v, do, p, cos, sin, n1, w_qkv)


def place():
    dp, mp = lax.axis_index("dp"), lax.axis_index("mp")
    return dp // 2, lax.rem(dp, 2), mp // 2, lax.rem(mp, 2)


def device(z, x, y, c):
    return (2 * z + x, 2 * y + c)


def remote(src, dst, send, recv, target):
    return pltpu.make_async_remote_copy(
        src_ref=src, dst_ref=dst, send_sem=send, recv_sem=recv,
        device_id=target, device_id_type=pl.DeviceIdType.MESH,
    )


def greet(targets):
    barrier = pltpu.get_barrier_semaphore()
    for target in targets:
        pl.semaphore_signal(barrier, inc=1, device_id=target, device_id_type=pl.DeviceIdType.MESH)
    pl.semaphore_wait(barrier, len(targets))


def peers(nz):
    z, x, y, c = place()
    across = [device(z, 1 - x, y, c), device(z, x, 1 - y, c), device(z, x, y, 1 - c)]
    return across + [device(lax.bitwise_xor(z, d), x, y, c) for d in range(1, nz)]


class Gather:
    def __init__(self, nz, src, full, send, recv, local, eager=False):
        self.nz, self.src, self.full, self.send, self.recv, self.local = nz, src, full, send, recv, local
        self.eager = eager
        self.depth = src.shape[0]
        self.index = {}
        for kind in ("Z", "X", "Y", "S", "YA", "XB", "SX", "SY", "SA", "SB"):
            for d in range(1 if kind == "Z" else 0, nz):
                self.index[kind, d] = len(self.index)

    @staticmethod
    def count(nz):
        return nz - 1 + 9 * nz

    def block(self, z, x, y, c, half=None):
        first, size = (0, self.depth) if half is None else (half * self.depth // 2, self.depth // 2)
        return self.full.at[2 * y + c, pl.ds(pl.multiple_of((2 * z + x) * self.depth + first, 16), size)]

    def message(self, kind, d, sending):
        z, x, y, c = place()
        back = lax.bitwise_xor(z, d)
        sx, sy, sib = device(z, 1 - x, y, c), device(z, x, 1 - y, c), device(z, x, y, 1 - c)
        sent, got, half, target = {
            "Z": ((z, x, y, c), (back, x, y, c), None, device(back, x, y, c)),
            "X": ((back, x, y, c), (back, 1 - x, y, c), None, sx),
            "Y": ((back, x, y, c), (back, x, 1 - y, c), None, sy),
            "S": ((back, x, y, c), (back, x, y, 1 - c), None, sib),
            "YA": ((back, 1 - x, y, c), (back, 1 - x, 1 - y, c), 0, sy),
            "XB": ((back, x, 1 - y, c), (back, 1 - x, 1 - y, c), 1, sx),
            "SX": ((back, 1 - x, y, c), (back, 1 - x, y, 1 - c), None, sib),
            "SY": ((back, x, 1 - y, c), (back, x, 1 - y, 1 - c), None, sib),
            "SA": ((back, 1 - x, 1 - y, c), (back, 1 - x, 1 - y, 1 - c), 0, sib),
            "SB": ((back, 1 - x, 1 - y, c), (back, 1 - x, 1 - y, 1 - c), 1, sib),
        }[kind]
        i = self.index[kind, d]
        at = self.block(*(sent if sending else got), half)
        own = sending and (kind == "Z" or (d == 0 and kind in ("X", "Y", "S")))
        return remote(self.src if own else at, at, self.send.at[i], self.recv.at[i], target)

    def start(self, kind, d):
        self.message(kind, d, True).start()

    def arrived(self, kind, d):
        self.message(kind, d, False).wait_recv()

    def own(self):
        z, x, y, c = place()
        return pltpu.make_async_copy(self.src, self.block(z, x, y, c), self.local)

    def begin(self):
        for d in range(1, self.nz if self.eager else 2):
            self.start("Z", d)
        for kind in ("X", "Y", "S"):
            self.start(kind, 0)
        self.own().start()

    def push(self, d):
        self.start("Z", d)

    def all_along(self):
        for d in range(1, self.nz):
            self.along(d)

    def all_over(self):
        for d in range(self.nz):
            self.over(d)

    def rest(self):
        for d in range(self.nz):
            self.corner(d)
        self.end()

    def along(self, d):
        self.arrived("Z", d)
        for kind in ("X", "Y", "S"):
            self.start(kind, d)

    def over(self, d):
        self.arrived("X", d)
        self.start("YA", d)
        self.start("SX", d)
        self.arrived("Y", d)
        self.start("XB", d)
        self.start("SY", d)

    def corner(self, d):
        self.arrived("YA", d)
        self.start("SA", d)
        self.arrived("XB", d)
        self.start("SB", d)

    def end(self):
        self.own().wait()
        for d in range(self.nz):
            for kind in ("S", "SX", "SY", "SA", "SB"):
                self.arrived(kind, d)
        for kind, d in self.index:
            self.message(kind, d, True).wait_send()


class Share:
    def __init__(self, src, full, send, recv, local, pieces=1):
        self.src, self.full, self.send, self.recv, self.local, self.pieces = src, full, send, recv, local, pieces
        self.size = src.shape[0] // pieces

    @staticmethod
    def sems(pieces):
        dma = pltpu.SemaphoreType.DMA
        return [dma((3 * pieces,)), dma((3 * pieces,)), dma((pieces,))]

    def rows(self, y, c, i):
        own = self.size * self.pieces
        return pl.ds(pl.multiple_of((2 * y + c) * own + i * self.size, 16), self.size)

    def message(self, kind, i):
        z, x, y, c = place()
        n = self.pieces
        piece = self.src.at[pl.ds(i * self.size, self.size)]
        if kind == "own":
            return pltpu.make_async_copy(piece, self.full.at[self.rows(y, c, i)], self.local.at[i])
        k = {"Y": 0, "C": 1, "F": 2}[kind] * n + i
        sems = self.send.at[k], self.recv.at[k]
        sib = device(z, x, y, 1 - c)
        if kind == "Y":
            return remote(piece, self.full.at[self.rows(y, c, i)], *sems, device(z, x, 1 - y, c))
        if kind == "C":
            return remote(piece, self.full.at[self.rows(y, c, i)], *sems, sib)
        at = self.full.at[self.rows(1 - y, c, i)]
        return remote(at, at, *sems, sib)

    def begin(self, i):
        for kind in ("Y", "C", "own"):
            self.message(kind, i).start()

    def on(self, i):
        self.message("Y", i).wait_recv()
        self.message("F", i).start()

    def end(self):
        for i in range(self.pieces):
            self.message("own", i).wait()
            self.message("C", i).wait_recv()
            self.message("F", i).wait_recv()
            for kind in ("Y", "C", "F"):
                self.message(kind, i).wait_send()


def finish(tokens, gain, cot, middle_cot):
    hat, inv_sigma = normalize(tokens.T.astype(F32))
    d = cot * gain
    made = middle_cot + inv_sigma * (
        d - jnp.mean(d, axis=0, keepdims=True) - hat * jnp.mean(d * hat, axis=0, keepdims=True)
    )
    return made.T.astype(BF16)


class Scatter:
    def __init__(self, nz, ups, src, part, out, core, side, line, last, send, recv):
        self.nz, self.ups, self.src, self.part, self.out = nz, ups, src, part, out
        self.core, self.side, self.line, self.last, self.send, self.recv = core, side, line, last, send, recv
        self.depth = out.shape[0]

    @staticmethod
    def scratch(nz, ups, depth, columns):
        count = len(ups) * nz + 2 * nz
        return [
            pltpu.VMEM((len(ups), 2 * nz * depth, columns), BF16),
            pltpu.VMEM((len(ups), nz * depth, columns), BF16),
            pltpu.VMEM((nz, len(ups), depth, columns), BF16),
            pltpu.VMEM((depth, columns), BF16),
            pltpu.SemaphoreType.DMA((count,)),
            pltpu.SemaphoreType.DMA((count,)),
        ]

    def row(self, d):
        z, _, _, _ = place()
        return lax.bitwise_xor(z, d)

    def rows(self, d, x):
        return pl.ds(pl.multiple_of((2 * self.row(d) + x) * self.depth, 16), self.depth)

    def both(self, d):
        return pl.ds(pl.multiple_of(2 * self.row(d) * self.depth, 16), 2 * self.depth)

    def lane(self, d):
        return pl.ds(pl.multiple_of(self.row(d) * self.depth, 16), self.depth)

    def message(self, kind, d, u=0):
        z, x, y, c = place()
        nz, n = self.nz, len(self.ups)
        i = {"C": u * nz + d, "X": n * nz + d, "Z": n * nz + nz + d, "Y": n * nz + nz}[kind]
        sems = self.send.at[i], self.recv.at[i]
        if kind == "C":
            both = self.both(d)
            return remote(self.src.at[2 * self.ups[u] + 1 - c, both], self.core.at[u, both], *sems, device(z, x, y, 1 - c))
        if kind == "X":
            return remote(
                self.core.at[:, self.rows(d, 1 - x)], self.side.at[:, self.lane(d)], *sems, device(z, 1 - x, y, c)
            )
        if kind == "Z":
            return remote(self.side.at[:, self.lane(d)], self.line.at[d], *sems, device(self.row(d), x, y, c))
        return remote(self.line.at[0, 1 - y if n == 2 else 0], self.last, *sems, device(z, x, 1 - y, c))

    def begin(self, *rows):
        for d in rows:
            for u in range(len(self.ups)):
                self.message("C", d, u).start()

    def cross(self, d):
        self.message("X", d).start()

    def chip(self, d):
        _, x, _, c = place()
        for u in range(len(self.ups)):
            self.message("C", d, u).wait_recv()
        for side in range(2):
            rows = self.rows(d, side)
            for u, up in enumerate(self.ups):
                self.core[u, rows] = self.part[2 * up + c, rows] + self.core[u, rows]

    def over(self, d):
        _, x, _, _ = place()
        self.message("X", d).wait_recv()
        rows, lane = self.rows(d, x), self.lane(d)
        for u in range(len(self.ups)):
            self.side[u, lane] = self.core[u, rows] + self.side[u, lane]
        if d:
            self.message("Z", d).start()

    def along(self):
        _, _, y, _ = place()
        for d in range(1, self.nz):
            self.message("Z", d).wait_recv()
        lane = self.lane(0)
        for u in range(len(self.ups)):
            made = self.side[u, lane].astype(F32)
            for d in range(1, self.nz):
                made += self.line[d, u].astype(F32)
            self.line[0, u] = made.astype(BF16)
        if len(self.ups) == 2:
            self.message("Y", 0).start()
        else:
            pl.when(y != self.ups[0])(lambda: self.message("Y", 0).start())

    def end(self):
        _, _, y, _ = place()

        def receive():
            self.message("Y", 0).wait_recv()
            mine = self.line[0, y if len(self.ups) == 2 else 0]
            self.out[...] = mine.astype(F32) + self.last[...].astype(F32)

        if len(self.ups) == 2:
            receive()
            self.message("Y", 0).wait_send()
        else:
            pl.when(y == self.ups[0])(receive)
            pl.when(y != self.ups[0])(lambda: self.message("Y", 0).wait_send())
        for d in range(self.nz):
            for u in range(len(self.ups)):
                self.message("C", d, u).wait_send()
            self.message("X", d).wait_send()
            if d:
                self.message("Z", d).wait_send()


class Everyone:
    def __init__(self, held, near, full, far, send, recv):
        self.held, self.near, self.full, self.far, self.send, self.recv = held, near, full, far, send, recv
        self.group, self.owners = near.shape[0], far.shape[0]

    @staticmethod
    def scratch(n_mp, n_dp):
        dma = pltpu.SemaphoreType.DMA
        blocks = pltpu.VMEM((n_dp, 8, 128), F32)
        count = n_mp + n_dp
        return [blocks, pltpu.VMEM((n_mp, n_dp, 8, 128), F32), blocks, blocks, dma((count,)), dma((count,))]

    @staticmethod
    def peers(n_mp, n_dp):
        dp, mp = lax.axis_index("dp"), lax.axis_index("mp")
        return [(dp, lax.bitwise_xor(mp, k)) for k in range(1, n_mp)] + [
            (lax.bitwise_xor(dp, k), mp) for k in range(1, n_dp)
        ]

    def within(self, k):
        dp, mp = lax.axis_index("dp"), lax.axis_index("mp")
        sems = self.send.at[k], self.recv.at[k]
        return remote(self.held, self.near.at[mp], *sems, (dp, lax.bitwise_xor(mp, k)))

    def owner(self, k):
        dp, mp = lax.axis_index("dp"), lax.axis_index("mp")
        other = lax.bitwise_xor(dp, k)
        sems = self.send.at[self.group + k], self.recv.at[self.group + k]
        return remote(self.full.at[other], self.far.at[dp], *sems, (other, mp))

    def begin(self):
        for k in range(1, self.group):
            self.within(k).start()
        self.near[lax.axis_index("mp")] = self.held[...]

    def pass_on(self):
        for k in range(1, self.group):
            self.within(k).wait_recv()
        made = self.near[0]
        for i in range(1, self.group):
            made += self.near[i]
        self.full[...] = made
        for k in range(1, self.owners):
            self.owner(k).start()
        dp = lax.axis_index("dp")
        self.far[dp] = self.full[dp]

    def end(self):
        for k in range(1, self.owners):
            self.owner(k).wait_recv()
        made = self.far[0]
        for i in range(1, self.owners):
            made += self.far[i]
        for k in range(1, self.group):
            self.within(k).wait_send()
        for k in range(1, self.owners):
            self.owner(k).wait_send()
        return made


class Fold:
    def __init__(self, part, near, far, send, recv):
        self.part, self.near, self.far, self.send, self.recv = part, near, far, send, recv
        self.slots = part.shape[0]

    @staticmethod
    def scratch(n_mp, own, slots):
        dma = pltpu.SemaphoreType.DMA
        return [
            pltpu.VMEM((slots, n_mp, 2 * HDIM, own), BF16),
            pltpu.VMEM((slots, 2, 2 * HDIM, own), BF16),
            pltpu.VMEM((slots, 2 * HDIM, own), BF16),
            dma((slots, 3)),
            dma((slots, 3)),
        ]

    def message(self, kind, head):
        z, x, y, c = place()
        slot = lax.rem(head, self.slots)
        k = {"far": 0, "near": 1, "Y": 2}[kind]
        sems = self.send.at[slot, k], self.recv.at[slot, k]
        if kind == "Y":
            return remote(self.near.at[slot, 1 - y], self.far.at[slot], *sems, device(z, x, 1 - y, c))
        up = 1 - y if kind == "far" else y
        return remote(self.part.at[slot, 2 * up + 1 - c], self.near.at[slot, up], *sems, device(z, x, y, 1 - c))

    def begin(self, head):
        self.message("far", head).start()
        self.message("near", head).start()

    def chip(self, head):
        _, _, y, c = place()
        slot = lax.rem(head, self.slots)
        self.message("far", head).wait_recv()
        self.near[slot, 1 - y] = self.part[slot, 2 * (1 - y) + c] + self.near[slot, 1 - y]
        self.message("Y", head).start()

    def end(self, head):
        _, _, y, c = place()
        slot = lax.rem(head, self.slots)
        self.message("near", head).wait_recv()
        self.message("Y", head).wait_recv()
        made = self.part[slot, 2 * y + c].astype(F32) + self.near[slot, y].astype(F32) + self.far[slot].astype(F32)
        for kind in ("far", "near", "Y"):
            self.message(kind, head).wait_send()
        return made.astype(BF16)


def forward_kernel(nz, units, len_ref, tok_hbm, *refs):
    linked = nz > 0
    given, refs = refs[: 6 if linked else 2], refs[6 if linked else 2 :]
    mine_ref, q_ref, k_ref, v_ref, cos_ref, sin_ref, o_ref, p_ref, inv_ref = refs[:9]
    full_refs, refs = refs[9 : 12 if linked else 9], refs[12 if linked else 9 :]
    wa_ref, wb_ref, w_ref, n1_ref, ka_ref, qa_ref, va_ref, stat_ref, tok_ref, load = refs[:10]
    refs = refs[10:]
    rows, features = tok_ref.shape
    own = q_ref.shape[1]
    docs = len_ref.shape[1]
    step = pl.program_id(0)
    parts = wa_ref.shape[0]
    part, turn_at = lax.rem(step, parts), step // parts
    me = lax.axis_index("mp")
    mine = pl.ds(pl.multiple_of(me * own, own), own)
    three = 3 * HDIM

    if linked:
        srcs = refs[:3]
        one = Gather(nz, srcs[0], wa_ref, *refs[3:6], eager=True)
        two = Gather(nz, srcs[1], wb_ref, *refs[6:9], eager=True)
        last = Gather(nz, srcs[2], full_refs[2], *refs[9:12])
        keeps = [
            pltpu.make_async_copy(wa_ref, full_refs[0], load.at[0]),
            pltpu.make_async_copy(wb_ref, full_refs[1], load.at[1]),
        ]

    @pl.when(step == 0)
    def _():
        bring = pltpu.make_async_copy(tok_hbm, tok_ref, load.at[2])
        bring.start()
        if linked:
            wq_ref, wg_ref, wo_ref, wd_ref, one_ref, two_ref = given
            for i in range(3):
                srcs[0][:, i * HDIM : (i + 1) * HDIM] = wq_ref[i, :, :HDIM]
            srcs[0][:, three : three + 1] = one_ref[...].astype(F32).T.astype(BF16)
            srcs[0][:, three + 1 : three + 2] = two_ref[...].astype(F32).T.astype(BF16)
            down = wd_ref[...].T
            srcs[0][:, 256 - units % 128 :] = down[:, units - units % 128 :]
            greet(peers(nz))
            one.begin()
            for r in range(1, wq_ref.shape[2] // HDIM):
                for i in range(3):
                    at = (r - 1) * three + i * HDIM
                    srcs[1][:, at : at + HDIM] = wq_ref[i, :, r * HDIM : (r + 1) * HDIM]
            two.begin()
            pair, width = 2 * units, wo_ref.shape[0]
            for i in range(2):
                srcs[2][:, i * units : (i + 1) * units] = wg_ref[:, i, :]
            srcs[2][:, pair : pair + width] = wo_ref[...].T
            srcs[2][:, pair + width :] = down[:, : units - units % 128]
        else:
            fetches = [pltpu.make_async_copy(g, w, load.at[i]) for i, (g, w) in enumerate(zip(given, (wa_ref, wb_ref)))]
            for fetch in fetches:
                fetch.start()
        _, position, _ = layout_rows(len_ref, docs, 0, rows)
        power = lax.broadcasted_iota(jnp.int32, (HALF, 1), 0).astype(F32) * (-2.0 / HDIM * math.log2(ROPE_BASE))
        angle = position.astype(F32) * jnp.exp2(power)
        cos_ref[...] = jnp.cos(angle)
        sin_ref[...] = jnp.sin(angle)
        keys, _, _ = layout_rows(len_ref, docs, 0, rows)
        queries, _, _ = layout_rows(len_ref, docs, me * own, own)
        kind = lax.broadcasted_iota(jnp.int32, (AUG - HDIM, 1), 0)
        ka_ref[HDIM:] = jnp.where(kind == keys, 1.0, 0.0).astype(BF16)
        qa_ref[HDIM:] = jnp.where(kind == queries, 0.0, FAR).astype(BF16)
        va_ref[HDIM:] = jnp.ones((AUG - HDIM, rows), BF16)

        def measure(i, carry):
            at = pl.ds(pl.multiple_of(i * own, own), own)
            turned = tok_ref[at, :].T
            n1_ref[:, at] = turned
            mean, inv = moments(turned.astype(F32))
            stat_ref[0:1, at] = mean
            stat_ref[1:2, at] = inv
            return carry

        if linked:
            one.all_along()
        bring.wait()
        lax.fori_loop(0, rows // own, measure, 0)
        if linked:
            one.all_over()
            last.begin()
            one.rest()
            keeps[0].start()
        else:
            for fetch in fetches:
                fetch.wait()
        gain = wa_ref[0, :, three : three + 1].astype(F32)

        def norm(i, carry):
            at = pl.ds(pl.multiple_of(i * own, own), own)
            made = (n1_ref[:, at].astype(F32) - stat_ref[0:1, at]) * stat_ref[1:2, at] * gain
            n1_ref[:, at] = made.astype(BF16)
            return carry

        lax.fori_loop(0, rows // own, norm, 0)
        mine_ref[...] = n1_ref[:, mine]

    if linked:
        gathers = {"two": two, "last": last}
        for at, which, name, *d in GATHER_STEPS:
            pl.when(step == at)(functools.partial(getattr(gathers[which], name), *d))

        @pl.when(step == parts)
        def _():
            two.rest()
            keeps[1].start()

    @pl.when(turn_at == 0)
    def _():
        w_ref[...] = wa_ref[part, :, :three]

    for r in range(1, 1 + wb_ref.shape[2] // three):

        @pl.when(turn_at == r)
        def _():
            w_ref[...] = wb_ref[part, :, (r - 1) * three : r * three]

    made = dot(w_ref[:, HDIM:], n1_ref[...], TN)
    keys = turn(made[:HDIM], cos_ref[...], sin_ref[...], 1).astype(BF16)
    k_ref[...] = keys
    ka_ref[:HDIM] = keys
    values = made[HDIM:].astype(BF16)
    v_ref[...] = values
    va_ref[:HDIM] = values
    made = dot(w_ref[:, :HDIM], n1_ref[:, mine], TN) * (SCALE * LOG2E)
    queries = turn(made, cos_ref[:, mine], sin_ref[:, mine], 1).astype(BF16)
    q_ref[...] = queries
    qa_ref[:HDIM] = queries
    scores = dot(ka_ref[...], qa_ref[...], TN)
    top = jnp.max(scores, axis=0, keepdims=True)
    probs = jnp.exp2(scores - top).astype(BF16)
    p_ref[0] = probs
    out = dot(va_ref[...], probs, NN)
    inv = 1.0 / out[HDIM : HDIM + 1]
    o_ref[...] = (out[:HDIM] * inv).astype(BF16)
    inv_ref[0] = inv
    if linked:

        @pl.when(step == pl.num_programs(0) - 1)
        def _():
            for keep in keeps:
                keep.wait()
            last.corner(3)
            last.end()


GATHER_STEPS = (
    (0, "two", "along", 1),
    (0, "two", "along", 2),
    (0, "two", "along", 3),
    (0, "last", "push", 2),
    (1, "two", "over", 0),
    (1, "two", "over", 1),
    (2, "two", "over", 2),
    (2, "two", "over", 3),
    (2, "last", "push", 3),
    (3, "last", "along", 1),
    (3, "last", "over", 0),
    (4, "last", "along", 2),
    (5, "last", "over", 1),
    (6, "last", "corner", 0),
    (6, "last", "along", 3),
    (7, "last", "over", 2),
    (8, "last", "corner", 1),
    (9, "last", "over", 3),
    (11, "last", "corner", 2),
)


def forward(nz, n_mp, units, lengths, tokens, weights, columns):
    rows, features = tokens.shape
    own, width, heads = rows // n_mp, features // n_mp, features // HDIM
    per = width // HDIM
    linked = nz > 0
    hbm = pl.BlockSpec(memory_space=pl.ANY)
    head = lambda h: lax.rem(h, n_mp) * per + h // n_mp
    row = lambda h: (head(h), 0)
    cube = lambda h: (head(h), 0, 0)
    vm = pl.BlockSpec(memory_space=pltpu.VMEM)
    n = Gather.count(nz) if linked else 0
    dma = pltpu.SemaphoreType.DMA
    depth = features // (2 * nz) if linked else 0
    full_shapes = [jax.ShapeDtypeStruct((n_mp, features, c), BF16) for c in columns] if linked else []
    return pl.pallas_call(
        functools.partial(forward_kernel, nz, units),
        grid=(heads,),
        in_specs=[pl.BlockSpec(memory_space=pltpu.SMEM), hbm] + ([vm] * 6 if linked else [hbm] * 2),
        out_specs=[
            whole(features, own),
            pl.BlockSpec((HDIM, own), row),
            pl.BlockSpec((HDIM, rows), row),
            pl.BlockSpec((HDIM, rows), row),
            whole(HALF, rows),
            whole(HALF, rows),
            pl.BlockSpec((HDIM, own), row),
            pl.BlockSpec((1, rows, own), cube),
            pl.BlockSpec((1, 1, own), cube),
        ]
        + [hbm] * len(full_shapes),
        out_shape=[
            jax.ShapeDtypeStruct((features, own), BF16),
            jax.ShapeDtypeStruct((features, own), BF16),
            jax.ShapeDtypeStruct((features, rows), BF16),
            jax.ShapeDtypeStruct((features, rows), BF16),
            jax.ShapeDtypeStruct((HALF, rows), F32),
            jax.ShapeDtypeStruct((HALF, rows), F32),
            jax.ShapeDtypeStruct((features, own), BF16),
            jax.ShapeDtypeStruct((heads, rows, own), BF16),
            jax.ShapeDtypeStruct((heads, 1, own), F32),
        ]
        + full_shapes,
        scratch_shapes=[
            pltpu.VMEM((n_mp, features, columns[0]), BF16),
            pltpu.VMEM((n_mp, features, columns[1]), BF16),
            pltpu.VMEM((features, 3 * HDIM), BF16),
            pltpu.VMEM((features, rows), BF16),
            pltpu.VMEM((AUG, rows), BF16),
            pltpu.VMEM((AUG, own), BF16),
            pltpu.VMEM((AUG, rows), BF16),
            pltpu.VMEM((8, rows), F32),
            pltpu.VMEM((rows, features), BF16),
            dma((3,)),
        ]
        + (
            [pltpu.VMEM((depth, c), BF16) for c in columns] + [dma((n,)), dma((n,)), dma] * 3
            if linked
            else []
        ),
        compiler_params=pltpu.CompilerParams(
            dimension_semantics=("arbitrary",),
            vmem_limit_bytes=VMEM_BYTES,
            **({"collective_id": 1, "has_side_effects": True} if linked else {}),
        ),
        name="forward",
    )(lengths, tokens, *weights)


def middle(len_ref, me, tok_ref, cot_ref, heads_ref, inv_ref, w_ref, gain, units, out_ref, mcot_ref, do_ref, keep, sent, done, later):
    own, features = tok_ref.shape
    parts = w_ref.shape[0]
    width = features // parts
    heads = width // HDIM
    pair = 2 * units
    _, _, live = layout_rows(len_ref, len_ref.shape[1], me * own, own)

    def w_gu(m):
        return w_ref[m, :, :pair]

    def w_out(m):
        return w_ref[m, :, pair : pair + width]

    def w_down(m):
        return w_ref[m, :, pair + width : pair + width + units]

    total = dot(w_out(0), heads_ref[:width], NN)
    for m in range(1, parts):
        total += dot(w_out(m), heads_ref[m * width : (m + 1) * width], NN)
    middle = tok_ref[...].T.astype(F32) + total
    hat, inv_sigma = normalize(middle)
    normed = (hat * gain).astype(BF16)
    total = middle
    kept = []
    for m in range(parts):
        gate_up = dot(w_gu(m), normed, TN)
        gate, up = gate_up[:units], gate_up[units:]
        phi, slope = gelu_parts(gate)
        act = gate * phi
        hidden = (act * up).astype(BF16)
        total += dot(w_down(m), hidden, NN)
        kept.append((hidden, (up * (phi + slope)).astype(BF16), act.astype(BF16)))
    out_ref[...] = total.astype(BF16).T
    sent()
    branch = jnp.where(live, cot_ref[...].T.astype(F32), 0.0).astype(BF16)
    back = jnp.zeros((features, own), F32)
    for m in range(parts):
        hidden, one, two = kept[m]
        hidden_cot = dot(w_down(m), branch, TN)
        keep("down", m, dot(branch, hidden, NT).astype(BF16))
        cots = jnp.concatenate([hidden_cot * one.astype(F32), hidden_cot * two.astype(F32)], axis=0).astype(BF16)
        keep("gu", m, dot(normed, cots, NT).astype(BF16))
        back += dot(w_gu(m), cots, NN)
    done()
    keep("gain", 0, jnp.sum(back * hat, axis=1, keepdims=True))
    d = back * gain
    middle_cot = branch.astype(F32) + inv_sigma * (
        d - jnp.mean(d, axis=0, keepdims=True) - hat * jnp.mean(d * hat, axis=0, keepdims=True)
    )
    mcot_ref[...] = middle_cot
    attn_cot = middle_cot.astype(BF16)
    for m in range(parts):
        back_heads = dot(w_out(m), attn_cot, TN)
        for h in range(heads):
            head = m * heads + h
            rows = slice(h * HDIM, (h + 1) * HDIM)
            cot = back_heads[rows] * inv_ref[head]
            inner = jnp.sum(cot * heads_ref[head * HDIM : (head + 1) * HDIM].astype(F32), axis=0, keepdims=True)
            high = inner.astype(BF16).astype(F32)
            pad = jnp.zeros((AUG - HDIM - 2, own), F32)
            do_ref[head] = jnp.concatenate([cot, high, inner - high, pad], axis=0).astype(BF16)
    later()
    for m in range(parts):
        keep("out", m, dot(attn_cot, heads_ref[m * width : (m + 1) * width], NT).astype(BF16))


def mid_kernel(
    units, len_ref, tok_hbm, cot_hbm, heads_ref, inv_ref, two_ref, w_hbm,
    out_ref, mcot_ref, do_ref, g_ref, o_ref, gain_ref, tok_ref, cot_ref, w_ref, load,
):
    own = tok_ref.shape[0]
    me = lax.axis_index("mp")
    mine = pl.ds(pl.multiple_of(me * own, own), own)
    loads = [
        pltpu.make_async_copy(tok_hbm.at[mine], tok_ref, load.at[0]),
        pltpu.make_async_copy(cot_hbm.at[mine], cot_ref, load.at[1]),
        pltpu.make_async_copy(w_hbm, w_ref, load.at[2]),
    ]
    for copy in loads:
        copy.start()
    for copy in loads:
        copy.wait()
    pair = 2 * units

    def keep(what, m, made):
        if what == "gu":
            g_ref[m, :, :pair] = made
        elif what == "down":
            g_ref[m, :, pair:] = made
        elif what == "out":
            o_ref[m] = made
        else:
            gain_ref[...] = made

    nothing = lambda: None
    middle(
        len_ref, me, tok_ref, cot_ref, heads_ref, inv_ref, w_ref, two_ref[...].astype(F32), units, out_ref, mcot_ref, do_ref,
        keep, nothing, nothing, nothing,
    )


def mid(n_mp, lengths, tokens, out_grad, heads_out, inv, gain, w_rest, units):
    features, own = heads_out.shape
    heads = inv.shape[0]
    vm = pl.BlockSpec(memory_space=pltpu.VMEM)
    hbm = pl.BlockSpec(memory_space=pl.ANY)
    return pl.pallas_call(
        functools.partial(mid_kernel, units),
        in_specs=[pl.BlockSpec(memory_space=pltpu.SMEM), hbm, hbm, vm, vm, vm, hbm],
        out_specs=[vm] * 6,
        out_shape=[
            jax.ShapeDtypeStruct((own, features), BF16),
            jax.ShapeDtypeStruct((features, own), F32),
            jax.ShapeDtypeStruct((heads, AUG, own), BF16),
            jax.ShapeDtypeStruct((n_mp, features, 3 * units), BF16),
            jax.ShapeDtypeStruct((n_mp, features, features // n_mp), BF16),
            jax.ShapeDtypeStruct((features, 1), F32),
        ],
        scratch_shapes=[
            pltpu.VMEM((own, features), BF16),
            pltpu.VMEM((own, features), BF16),
            pltpu.VMEM(w_rest.shape, BF16),
            pltpu.SemaphoreType.DMA((3,)),
        ],
        compiler_params=pltpu.CompilerParams(vmem_limit_bytes=VMEM_BYTES),
        name="mid",
    )(lengths, tokens, out_grad, heads_out, inv, gain, w_rest)


SLOTS = 7
LAG = 4
PIECES = 4


def backward_kernel(nz, units, *refs):
    len_ref, q_ref, k_ref, v_ref, p_ref, cos_ref, sin_ref, n1_ref, heads_ref, inv_ref, wa_ref, tok_hbm, cot_hbm, wb_hbm, wr_hbm = refs[:15]
    dq_ref, dr_ref, gains_ref, in_full, out_full = refs[15:20]
    wb_ref, wr_ref, gr_ref, do_ref, mcot_ref, pc_ref, qc_ref, acc_ref, gc_ref, va_ref, tok_ref, cot_ref, own_ref, load = refs[20:34]
    refs = refs[34:]
    gq_ref = wr_ref.at[:, :, pl.ds(0, dq_ref.shape[1])]
    rest = Scatter(nz, (0, 1), gr_ref, gr_ref, dr_ref, *refs[:6])
    low = Scatter(nz, (0,), gq_ref, gq_ref, dq_ref, *refs[6:12])
    high = Scatter(nz, (1,), gq_ref, gq_ref, dq_ref, *refs[12:18])
    fold = Fold(*refs[18:23])
    in_share = Share(own_ref.at[0], in_full, *refs[23:26], PIECES)
    out_share = Share(own_ref.at[1], out_full, *refs[26:29])
    gains = Everyone(*refs[29:35])
    step, heads = pl.program_id(0) - 1, pl.num_programs(0) - 1
    parts = wa_ref.shape[0]
    features, own = n1_ref.shape
    rows = k_ref.shape[1]
    width = features // parts
    per = width // HDIM
    me = lax.axis_index("mp")
    mine = pl.ds(pl.multiple_of(me * own, own), own)
    late = pltpu.make_async_copy(wb_hbm, wb_ref, load.at[3])
    three = 3 * HDIM
    depth = gains_ref.shape[1]
    shards = features // depth

    def put(row, column):
        for i in range(shards):
            gains.held[i, row : row + 1, :depth] = column[i * depth : (i + 1) * depth].T

    @pl.when(step < 0)
    def _():
        gains.held[0] = jnp.zeros(gains.held.shape[1:], F32)
        loads = [
            pltpu.make_async_copy(wr_hbm, wr_ref.at[:, :, pl.ds(0, wr_hbm.shape[2])], load.at[0]),
            pltpu.make_async_copy(tok_hbm.at[mine], tok_ref, load.at[1]),
            pltpu.make_async_copy(cot_hbm.at[mine], cot_ref, load.at[2]),
        ]
        for copy in loads:
            copy.start()
        greet(Everyone.peers(parts, 2 * nz))
        for copy in loads:
            copy.wait()
        late.start()
        pair = 2 * units

        def first():
            rest.chip(2)
            rest.cross(2)

        for m in range(parts):
            wr_ref[m, :, wr_hbm.shape[2] :] = wa_ref[m, :, 256 - units % 128 :]

        def keep(what, m, made):
            if what == "gu":
                gr_ref[m, :, :pair] = made
            elif what == "down":
                gr_ref[m, :, pair:] = made
            elif what == "out":
                wr_ref[m, :, 3 * width : 4 * width] = made
            else:
                put(1, made)

        middle(
            len_ref, me, tok_ref, cot_ref, heads_ref, inv_ref, wr_ref, wa_ref[0, :, three + 1 : three + 2].astype(F32), units,
            own_ref.at[1], mcot_ref, do_ref, keep,
            lambda: out_share.begin(0), lambda: rest.begin(2, 3), first,
        )
        va_ref[HDIM:] = jnp.full((AUG - HDIM, rows), -1.0, BF16)
        acc_ref[...] = jnp.zeros_like(acc_ref)
        gc_ref[...] = jnp.zeros_like(gc_ref)
        late.wait()

    def collect(head):
        at = lax.rem(head, per) * three
        pc_ref[pl.ds(pl.multiple_of(at + HDIM, HDIM), 2 * HDIM)] = fold.end(head)

    def close(part):
        for i in range(per):
            pc_ref[i * three : i * three + HDIM] = qc_ref[lax.rem(part, 3), i * HDIM : (i + 1) * HDIM]
        made = dot(n1_ref[...], pc_ref[...], NT)
        wr_ref[part, :, : 3 * width] = made.astype(BF16)
        weights = jnp.concatenate([wa_ref[part, :, :three], wb_ref[part]], axis=1)
        gc_ref[...] += jnp.sum(made * weights.astype(F32), axis=1, keepdims=True)
        acc_ref[...] += dot(weights, pc_ref[...], NN)

    @pl.when(step >= 0)
    def _():
        va_ref[:HDIM] = v_ref[...]
        cot = dot(va_ref[...], do_ref[step], TN)
        probs = p_ref[0]
        score_cot = probs * cot.astype(BF16)
        dv = dot(do_ref[step, :HDIM], probs, NT).astype(BF16)
        dk = turn(dot(q_ref[...], score_cot, NT) * LN2, cos_ref[...], sin_ref[...], 1, True).astype(BF16)
        dq = turn(dot(k_ref[...], score_cot, NN) * SCALE, cos_ref[:, mine], sin_ref[:, mine], 1, True)
        slot = lax.rem(step, SLOTS)
        for m in range(parts):
            fold.part[slot, m, :HDIM] = dk[:, m * own : (m + 1) * own]
            fold.part[slot, m, HDIM:] = dv[:, m * own : (m + 1) * own]
        at = pl.ds(pl.multiple_of(lax.rem(step, per) * HDIM, HDIM), HDIM)
        qc_ref[lax.rem(step // per, 3), at] = dq.astype(BF16)

        @pl.when(step >= LAG)
        def _():
            collect(step - LAG)

        @pl.when(step >= 1)
        def _():
            fold.chip(step - 1)

        fold.begin(step)

        @pl.when((step >= LAG) & (lax.rem(step - LAG, per) == per - 1))
        def _():
            close((step - LAG) // per)

    sums = {"rest": rest, "low": low, "high": high, "out": out_share, "in": in_share, "gains": gains}
    for at, which, name, *d in SUM_STEPS:
        pl.when(step == at)(functools.partial(getattr(sums[which], name), *d))

    @pl.when(step == heads - 1)
    def _():
        fold.chip(step)
        for which, name, *d in FLUSH_STEPS:
            getattr(sums[which], name)(*d)
        for back in range(LAG - 1, -1, -1):
            collect(step - back)
            if (features // HDIM - 1 - back) % per == per - 1:
                close((step - back) // per)
        high.begin(2, 3, 1, 0)
        gain = wa_ref[0, :, three : three + 1].astype(F32)
        put(0, gc_ref[...] / gain)
        gains.begin()
        size = own // PIECES
        for i in range(PIECES):
            at = slice(i * size, (i + 1) * size)
            own_ref[0, at] = finish(tok_ref[at], gain, acc_ref[:, at], mcot_ref[:, at])
            in_share.begin(i)
        for which, name, *d in LAST_STEPS:
            getattr(sums[which], name)(*d)
        high.along()
        for which in (rest, low, high):
            which.end()
        out_share.end()
        in_share.end()
        gains_ref[...] = gains.end()[:2, :depth]


SUM_STEPS = (
    (-1, "rest", "begin", 1, 0),
    (-1, "rest", "chip", 3),
    (0, "rest", "cross", 3),
    (0, "rest", "chip", 1),
    (0, "rest", "chip", 0),
    (1, "rest", "over", 2),
    (1, "out", "on", 0),
    (3, "rest", "cross", 1),
    (4, "rest", "over", 3),
    (6, "rest", "cross", 0),
    (7, "rest", "over", 1),
    (9, "low", "begin", 2, 3, 1, 0),
    (10, "low", "chip", 2),
    (10, "low", "chip", 3),
    (10, "low", "chip", 1),
    (10, "low", "chip", 0),
    (10, "low", "cross", 2),
    (10, "low", "cross", 3),
    (10, "low", "cross", 1),
    (10, "low", "cross", 0),
    (9, "rest", "over", 0),
)
FLUSH_STEPS = (
    ("rest", "along"),
    ("low", "over", 2),
    ("low", "over", 3),
)
LAST_STEPS = (
    ("high", "chip", 2),
    ("high", "cross", 2),
    ("high", "chip", 3),
    ("high", "cross", 3),
    ("high", "chip", 1),
    ("high", "cross", 1),
    ("high", "chip", 0),
    ("high", "cross", 0),
    ("low", "over", 1),
    ("low", "over", 0),
    ("gains", "pass_on"),
    ("high", "over", 2),
    ("in", "on", 0),
    ("high", "over", 3),
    ("in", "on", 1),
    ("high", "over", 1),
    ("low", "along"),
    ("high", "over", 0),
    ("in", "on", 2),
    ("in", "on", 3),
)


def backward(nz, lengths, q, k, v, p, cos, sin, n1, heads_out, inv, tokens, out_grad, w_a, w_b, w_rest, units):
    (features, own), rows = q.shape, k.shape[1]
    n_mp = w_a.shape[0]
    heads = features // HDIM
    width = features // n_mp
    depth = features // (2 * nz)
    columns = 4 * width, 3 * units
    hbm = pl.BlockSpec(memory_space=pl.ANY)
    vm = pl.BlockSpec(memory_space=pltpu.VMEM)
    row = lambda h: (jnp.maximum(h - 1, 0), 0)
    cube = lambda h: (jnp.maximum(h - 1, 0), 0, 0)
    dma = pltpu.SemaphoreType.DMA
    return pl.pallas_call(
        functools.partial(backward_kernel, nz, units),
        grid=(heads + 1,),
        in_specs=[
            pl.BlockSpec(memory_space=pltpu.SMEM),
            pl.BlockSpec((HDIM, own), row),
            pl.BlockSpec((HDIM, rows), row),
            pl.BlockSpec((HDIM, rows), row),
            pl.BlockSpec((1, rows, own), cube),
        ]
        + [vm] * 6
        + [hbm] * 4,
        out_specs=[vm, vm, vm, hbm, hbm],
        out_shape=[
            jax.ShapeDtypeStruct((depth, columns[0]), F32),
            jax.ShapeDtypeStruct((depth, columns[1]), F32),
            jax.ShapeDtypeStruct((2, depth), F32),
            jax.ShapeDtypeStruct((rows, features), BF16),
            jax.ShapeDtypeStruct((rows, features), BF16),
        ],
        scratch_shapes=[
            pltpu.VMEM(w_b.shape, BF16),
            pltpu.VMEM((n_mp, features, width + 3 * units), BF16),
            pltpu.VMEM((n_mp, features, 3 * units), BF16),
            pltpu.VMEM((heads, AUG, own), BF16),
            pltpu.VMEM((features, own), F32),
            pltpu.VMEM((3 * width, own), BF16),
            pltpu.VMEM((3, width, own), BF16),
            pltpu.VMEM((features, own), F32),
            pltpu.VMEM((features, 1), F32),
            pltpu.VMEM((AUG, rows), BF16),
            pltpu.VMEM((own, features), BF16),
            pltpu.VMEM((own, features), BF16),
            pltpu.VMEM((2, own, features), BF16),
            dma((4,)),
        ]
        + Scatter.scratch(nz, (0, 1), depth, columns[1])
        + Scatter.scratch(nz, (0,), depth, columns[0])
        + Scatter.scratch(nz, (1,), depth, columns[0])
        + Fold.scratch(n_mp, own, SLOTS)
        + Share.sems(PIECES)
        + Share.sems(1)
        + Everyone.scratch(n_mp, 2 * nz),
        compiler_params=pltpu.CompilerParams(
            dimension_semantics=("arbitrary",), collective_id=3, has_side_effects=True, vmem_limit_bytes=VMEM_BYTES
        ),
        name="backward",
    )(lengths, q, k, v, p, cos, sin, n1, heads_out, inv, w_a, tokens, out_grad, w_b, w_rest)


def deliver_kernel(units, in_ref, out_ref, dq_ref, dr_ref, gains_ref, grad_ref, to_ref, gq_ref, go_ref, gg_ref, gd_ref, one_ref, two_ref):
    @pl.when(pl.program_id(0) == 0)
    def _():
        width = go_ref.shape[0]
        pair = 2 * units
        for r in range(width // HDIM):
            for i in range(3):
                at = (3 * r + i) * HDIM
                gq_ref[i, :, r * HDIM : (r + 1) * HDIM] = dq_ref[:, at : at + HDIM]
        go_ref[...] = dq_ref[:, 3 * width : 4 * width].T
        one_ref[...] = gains_ref[0:1]
        two_ref[...] = gains_ref[1:2]
        for i in range(2):
            gg_ref[:, i, :] = dr_ref[:, i * units : (i + 1) * units]
        gd_ref[...] = dr_ref[:, pair : pair + units].T

    grad_ref[...] = in_ref[...].astype(F32)
    to_ref[...] = out_ref[...]


def deliver(layer_out, input_grad, d_qkv, d_rest, gains, width, units):
    rows, features = input_grad.shape
    depth = d_qkv.shape[0]
    shape = lambda *s: jax.ShapeDtypeStruct(s, F32)
    shapes = [(3, depth, width), (width, depth), (depth, 2, units), (units, depth), (1, depth), (1, depth)]
    steps = 2
    slab = pl.BlockSpec((rows // steps, features), lambda i: (i, 0))
    return pl.pallas_call(
        functools.partial(deliver_kernel, units),
        grid=(steps,),
        in_specs=[slab, slab, whole(*d_qkv.shape), whole(*d_rest.shape), whole(*gains.shape)],
        out_specs=[slab, slab] + [whole(*s) for s in shapes],
        out_shape=[shape(rows, features), jax.ShapeDtypeStruct((rows, features), BF16)] + [shape(*s) for s in shapes],
        compiler_params=params("arbitrary"),
        name="deliver",
    )(input_grad, layer_out, d_qkv, d_rest, gains)


def per_device(n_dp, n_mp, tokens, out_grad, w_qkv, w_out, w_gu, w_down, gain_attn, gain_mlp, lengths):
    rows, features = tokens.shape
    depth = w_qkv.shape[0]
    units, width = w_down.shape[0], w_out.shape[0]
    everyone = ("mp", "dp")
    linked = n_mp == 4 and n_dp == 8 and depth % 32 == 0 and features // HDIM == 12
    nz = n_dp // 2 if linked else 0
    three = 3 * HDIM
    loose = units % 128
    columns = 256, 3 * width - three, 3 * units + width - loose
    wq = w_qkv.transpose(1, 0, 2)
    if linked:
        weights = wq, w_gu, w_out, w_down, gain_attn[None], gain_mlp[None]
        n1, q, k, v, cos, sin, heads_out, probs, inv, w_a, w_b, w_c = forward(
            nz, n_mp, units, lengths, tokens, weights, columns
        )
        d_qkv, d_rest, gains, in_full, layer_out = backward(
            nz, lengths, q, k, v, probs, cos, sin, n1, heads_out, inv, tokens, out_grad, w_a, w_b, w_c, units
        )
    else:
        by_head = w_qkv.reshape(depth, 3, width // HDIM, HDIM).transpose(0, 2, 1, 3).reshape(depth, 3 * width)
        blank = jnp.zeros((depth, columns[0] - three - 2), BF16)
        shards = [
            jnp.concatenate([by_head[:, :three], gain_attn[:, None], gain_mlp[:, None], blank], axis=1),
            by_head[:, three:],
            jnp.concatenate([w_gu.reshape(depth, -1), w_out.T, w_down.T], axis=1),
        ]
        w_a, w_b, w_c = (
            lax.all_gather(s, everyone, axis=0, tiled=True).reshape(n_mp, features, s.shape[1]) for s in shards
        )
        n1, q, k, v, cos, sin, heads_out, probs, inv = forward(nz, n_mp, units, lengths, tokens, [w_a, w_b], columns)
        layer_out, middle_cot, do, g_rest, g_out, gain_two = mid(
            n_mp, lengths, tokens, out_grad, heads_out, inv, w_a[0, :, three + 1 : three + 2], w_c, units
        )
        own = middle_cot.shape[1]
        swap = lambda g, a, b: g.reshape(n_mp, features, a, b, HDIM).swapaxes(2, 3).reshape(n_mp, features, 3 * width)
        natural = jnp.concatenate([w_a[..., :three], w_b], axis=2)
        natural = jnp.concatenate([swap(natural, width // HDIM, 3), w_a[..., three : three + 1]], axis=2)
        g_qkv, nc = last(q, k, v, do, probs, cos, sin, lax.all_gather(n1, "mp", axis=1, tiled=True), natural)
        gain_one = w_a[0, :, three : three + 1].astype(F32)
        tok = lax.dynamic_slice_in_dim(tokens, lax.axis_index("mp") * own, own, 0)
        nc_own = lax.psum_scatter(nc, "mp", scatter_dimension=0, tiled=True)[0]
        in_own = finish(tok, gain_one, nc_own.astype(F32), middle_cot)
        layer_out, in_full = (lax.all_gather(v, "mp", axis=0, tiled=True) for v in (layer_out, in_own))
        both = jnp.stack([g_qkv[0, :, -1].astype(F32), gain_two[:, 0]])
        both = lax.psum(both, everyone)
        gains = lax.dynamic_slice_in_dim(both, lax.axis_index("dp") * depth, depth, 1)
        g_qkv = jnp.concatenate([swap(g_qkv[..., : 3 * width], 3, width // HDIM), g_out], axis=2)
        d_qkv, d_rest = (
            lax.psum_scatter(
                g.reshape(n_mp * features, -1), everyone, scatter_dimension=0, tiled=True
            ).astype(F32)
            for g in (g_qkv, g_rest)
        )
    input_grad, layer_out, g_q, g_o, g_g, g_d, one, two = deliver(
        layer_out, in_full, d_qkv, d_rest, gains, width, units
    )
    return layer_out, input_grad, g_q.transpose(1, 0, 2), g_o, g_g, g_d, one[0], two[0]


def solution(mesh):
    n_dp, n_mp = mesh.shape["dp"], mesh.shape["mp"]
    return jax.shard_map(
        functools.partial(per_device, n_dp, n_mp),
        mesh=mesh,
        in_specs=(
            P("dp", None),
            P("dp", None),
            P("dp", None, "mp"),
            P("mp", "dp"),
            P("dp", None, "mp"),
            P("mp", "dp"),
            P("dp"),
            P("dp"),
            P("dp", None),
        ),
        out_specs=(
            P("dp", None),
            P("dp", None),
            P("dp", None, "mp"),
            P("mp", "dp"),
            P("dp", None, "mp"),
            P("mp", "dp"),
            P("dp"),
            P("dp"),
        ),
        check_vma=False,
    )
```

```python
import functools
import math

import jax
import jax.numpy as jnp
from jax import lax
from jax.experimental import pallas as pl
from jax.experimental.pallas import tpu as pltpu
from jax.sharding import PartitionSpec as P

HDIM = 64
HALF = HDIM // 2
AUG = HDIM + 16
EPS = 1e-05
ROPE_BASE = 160000.0
LOG2E = math.log2(math.e)
LN2 = math.log(2.0)
SCALE = HDIM ** (-0.5)
FAR = -1e30
BF16 = jnp.bfloat16
F32 = jnp.float32
VMEM_BYTES = 60 << 20
NN = (((1,), (0,)), ((), ()))
NT = (((1,), (1,)), ((), ()))
TN = (((0,), (0,)), ((), ()))


def dot(a, b, dims):
    return lax.dot_general(a, b, dims, preferred_element_type=F32)


def params(*semantics):
    return pltpu.CompilerParams(
        dimension_semantics=semantics or None, vmem_limit_bytes=VMEM_BYTES
    )


def whole(*shape):
    return pl.BlockSpec(shape, lambda *i: (0,) * len(shape))


def layout_rows(len_ref, docs, first, rows):
    index = first + lax.broadcasted_iota(jnp.int32, (1, rows), 1)
    segment = jnp.zeros((1, rows), jnp.int32)
    start = jnp.zeros((1, rows), jnp.int32)
    end = jnp.int32(0)
    for j in range(docs):
        end = end + len_ref[0, j]
        past = index >= end
        segment = segment + jnp.where(past, 1, 0)
        start = jnp.where(past, jnp.maximum(start, end), start)
    return segment, index - start, index < end


def moments(columns):
    mean = jnp.mean(columns, axis=0, keepdims=True)
    centered = columns - mean
    return mean, lax.rsqrt(jnp.mean(centered * centered, axis=0, keepdims=True) + EPS)


def normalize(columns):
    mean, inv = moments(columns)
    return (columns - mean) * inv, inv


def turn(block, cos, sin, heads, back=False):
    out = []
    for h in range(heads):
        one = block[h * HDIM : h * HDIM + HALF]
        two = block[h * HDIM + HALF : (h + 1) * HDIM]
        if back:
            out += [one * cos + two * sin, two * cos - one * sin]
        else:
            out += [one * cos - two * sin, two * cos + one * sin]
    return jnp.concatenate(out, axis=0)


def gelu_parts(gate):
    phi = 0.5 * (1.0 + lax.erf(gate * math.sqrt(0.5)))
    density = jnp.exp2(gate * gate * (-0.5 * LOG2E)) * (1.0 / math.sqrt(2.0 * math.pi))
    return phi, gate * density


def last_kernel(own_axis, q_ref, k_ref, v_ref, do_ref, p_ref, cos_ref, sin_ref, n1_ref, w_ref, gq_ref, nc_ref, gc_ref, dq_ref, pc_ref, acc_ref, va_ref):
    step, head = pl.program_id(0), pl.program_id(1)
    per = pl.num_programs(1)
    features, rows = n1_ref.shape
    own = q_ref.shape[1]
    width = per * HDIM
    mine = pl.ds(pl.multiple_of(lax.axis_index(own_axis) * own, own), own)

    @pl.when((step == 0) & (head == 0))
    def _():
        va_ref[HDIM:] = jnp.full((AUG - HDIM, rows), -1.0, BF16)
        acc_ref[...] = jnp.zeros_like(acc_ref)
        gc_ref[...] = jnp.zeros_like(gc_ref)

    va_ref[:HDIM] = v_ref[...]
    cot = dot(va_ref[...], do_ref[0], TN)
    probs = p_ref[0]
    score_cot = probs * cot.astype(BF16)
    at = pl.ds(pl.multiple_of(head * HDIM, HDIM), HDIM)
    dv = dot(do_ref[0, :HDIM], probs, NT)
    dk = dot(q_ref[...], score_cot, NT) * LN2
    dq = dot(k_ref[...], score_cot, NN) * SCALE
    pc_ref[pl.ds(pl.multiple_of(width + head * HDIM, HDIM), HDIM)] = dv.astype(BF16)
    pc_ref[at] = turn(dk, cos_ref[...], sin_ref[...], 1, True).astype(BF16)
    dq_ref[at] = turn(dq, cos_ref[:, mine], sin_ref[:, mine], 1, True).astype(BF16)

    @pl.when(head == per - 1)
    def _():
        kv = dot(n1_ref[...], pc_ref[...], NT)
        q = dot(n1_ref[:, mine], dq_ref[...], NT)
        gq_ref[step, :, :width] = q.astype(BF16)
        gq_ref[step, :, width : 3 * width] = kv.astype(BF16)
        gc_ref[...] += jnp.sum(q * w_ref[0, :, :width].astype(F32), axis=1, keepdims=True) + jnp.sum(
            kv * w_ref[0, :, width : 3 * width].astype(F32), axis=1, keepdims=True
        )

        def spread(i, carry):
            cols = pl.ds(pl.multiple_of(i * own, own), own)
            acc_ref[:, cols] += dot(w_ref[0, :, width : 3 * width], pc_ref[:, cols], NN)
            return carry

        lax.fori_loop(0, rows // own, spread, 0)
        acc_ref[:, mine] += dot(w_ref[0, :, :width], dq_ref[...], NN)

    @pl.when((step == pl.num_programs(0) - 1) & (head == per - 1))
    def _():
        gain_cot = (gc_ref[...] / w_ref[0, :, 3 * width :].astype(F32)).astype(BF16)
        for m in range(gq_ref.shape[0]):
            nc_ref[m] = acc_ref[:, m * own : (m + 1) * own].astype(BF16)
            gq_ref[m, :, 3 * width :] = gain_cot


def last(q, k, v, do, p, cos, sin, n1, w_qkv, own_axis="mp"):
    (features, own), rows = q.shape, k.shape[1]
    parts = w_qkv.shape[0]
    per = features // parts // HDIM
    width = per * HDIM
    head = lambda m, h: (m * per + h, 0)
    return pl.pallas_call(
        functools.partial(last_kernel, own_axis),
        grid=(parts, per),
        in_specs=[
            pl.BlockSpec((HDIM, own), head),
            pl.BlockSpec((HDIM, rows), head),
            pl.BlockSpec((HDIM, rows), head),
            pl.BlockSpec((1, AUG, own), lambda m, h: (m * per + h, 0, 0)),
            pl.BlockSpec((1, rows, own), lambda m, h: (m * per + h, 0, 0)),
            whole(HALF, rows),
            whole(HALF, rows),
            whole(features, rows),
            pl.BlockSpec((1,) + w_qkv.shape[1:], lambda m, h: (m, 0, 0)),
        ],
        out_specs=[
            whole(*w_qkv.shape),
            whole(parts, features, own),
        ],
        out_shape=[
            jax.ShapeDtypeStruct(w_qkv.shape, BF16),
            jax.ShapeDtypeStruct((parts, features, own), BF16),
        ],
        scratch_shapes=[
            pltpu.VMEM((features, 1), F32),
            pltpu.VMEM((width, own), BF16),
            pltpu.VMEM((2 * width, rows), BF16),
            pltpu.VMEM((features, rows), F32),
            pltpu.VMEM((AUG, rows), BF16),
        ],
        compiler_params=params("arbitrary", "arbitrary"),
        name="last",
    )(q, k, v, do, p, cos, sin, n1, w_qkv)


def place():
    dp, mp = lax.axis_index("dp"), lax.axis_index("mp")
    return dp // 2, lax.rem(dp, 2), mp // 2, lax.rem(mp, 2)


def device(z, x, y, c):
    return (2 * z + x, 2 * y + c)


def remote(src, dst, send, recv, target):
    return pltpu.make_async_remote_copy(
        src_ref=src, dst_ref=dst, send_sem=send, recv_sem=recv,
        device_id=target, device_id_type=pl.DeviceIdType.MESH,
    )


def hail(targets):
    barrier = pltpu.get_barrier_semaphore()
    for target in targets:
        pl.semaphore_signal(barrier, inc=1, device_id=target, device_id_type=pl.DeviceIdType.MESH)


def greet(targets):
    hail(targets)
    pl.semaphore_wait(pltpu.get_barrier_semaphore(), len(targets))


def peers(nz):
    z, x, y, c = place()
    across = [device(z, 1 - x, y, c), device(z, x, 1 - y, c), device(z, x, y, 1 - c)]
    return across + [device(lax.bitwise_xor(z, d), x, y, c) for d in range(1, nz)]


class Gather:
    def __init__(self, nz, src, full, send, recv, local, eager=False):
        self.nz, self.src, self.full, self.send, self.recv, self.local = nz, src, full, send, recv, local
        self.eager = eager
        self.depth = src.shape[0]
        self.index = {}
        for kind in ("Z", "X", "Y", "S", "YA", "XB", "SX", "SY", "SA", "SB"):
            for d in range(1 if kind == "Z" else 0, nz):
                self.index[kind, d] = len(self.index)

    @staticmethod
    def count(nz):
        return nz - 1 + 9 * nz

    def block(self, z, x, y, c, half=None):
        first, size = (0, self.depth) if half is None else (half * self.depth // 2, self.depth // 2)
        return self.full.at[2 * y + c, pl.ds(pl.multiple_of((2 * z + x) * self.depth + first, 16), size)]

    def message(self, kind, d, sending):
        z, x, y, c = place()
        back = lax.bitwise_xor(z, d)
        sx, sy, sib = device(z, 1 - x, y, c), device(z, x, 1 - y, c), device(z, x, y, 1 - c)
        sent, got, half, target = {
            "Z": ((z, x, y, c), (back, x, y, c), None, device(back, x, y, c)),
            "X": ((back, x, y, c), (back, 1 - x, y, c), None, sx),
            "Y": ((back, x, y, c), (back, x, 1 - y, c), None, sy),
            "S": ((back, x, y, c), (back, x, y, 1 - c), None, sib),
            "YA": ((back, 1 - x, y, c), (back, 1 - x, 1 - y, c), 0, sy),
            "XB": ((back, x, 1 - y, c), (back, 1 - x, 1 - y, c), 1, sx),
            "SX": ((back, 1 - x, y, c), (back, 1 - x, y, 1 - c), None, sib),
            "SY": ((back, x, 1 - y, c), (back, x, 1 - y, 1 - c), None, sib),
            "SA": ((back, 1 - x, 1 - y, c), (back, 1 - x, 1 - y, 1 - c), 0, sib),
            "SB": ((back, 1 - x, 1 - y, c), (back, 1 - x, 1 - y, 1 - c), 1, sib),
        }[kind]
        i = self.index[kind, d]
        at = self.block(*(sent if sending else got), half)
        own = sending and (kind == "Z" or (d == 0 and kind in ("X", "Y", "S")))
        return remote(self.src if own else at, at, self.send.at[i], self.recv.at[i], target)

    def start(self, kind, d):
        self.message(kind, d, True).start()

    def arrived(self, kind, d):
        self.message(kind, d, False).wait_recv()

    def own(self):
        z, x, y, c = place()
        return pltpu.make_async_copy(self.src, self.block(z, x, y, c), self.local)

    def begin(self):
        for d in range(1, self.nz if self.eager else 2):
            self.start("Z", d)
        for kind in ("X", "Y", "S"):
            self.start(kind, 0)
        self.own().start()

    def push(self, d):
        self.start("Z", d)

    def all_along(self):
        for d in range(1, self.nz):
            self.along(d)

    def all_over(self):
        for d in range(self.nz):
            self.over(d)

    def rest(self):
        for d in range(self.nz):
            self.corner(d)
        self.end()

    def along(self, d):
        self.arrived("Z", d)
        for kind in ("X", "Y", "S"):
            self.start(kind, d)

    def over(self, d):
        self.arrived("X", d)
        self.start("YA", d)
        self.start("SX", d)
        self.arrived("Y", d)
        self.start("XB", d)
        self.start("SY", d)

    def corner(self, d):
        self.arrived("YA", d)
        self.start("SA", d)
        self.arrived("XB", d)
        self.start("SB", d)

    def end(self):
        self.own().wait()
        for d in range(self.nz):
            for kind in ("S", "SX", "SY", "SA", "SB"):
                self.arrived(kind, d)
        for kind, d in self.index:
            self.message(kind, d, True).wait_send()


class Share:
    def __init__(self, src, full, send, recv, local, pieces=1):
        self.src, self.full, self.send, self.recv, self.local, self.pieces = src, full, send, recv, local, pieces
        self.size = src.shape[0] // pieces

    @staticmethod
    def sems(pieces):
        dma = pltpu.SemaphoreType.DMA
        return [dma((3 * pieces,)), dma((3 * pieces,)), dma((pieces,))]

    def rows(self, y, c, i):
        own = self.size * self.pieces
        return pl.ds(pl.multiple_of((2 * y + c) * own + i * self.size, 16), self.size)

    def message(self, kind, i):
        z, x, y, c = place()
        n = self.pieces
        piece = self.src.at[pl.ds(i * self.size, self.size)]
        if kind == "own":
            return pltpu.make_async_copy(piece, self.full.at[self.rows(y, c, i)], self.local.at[i])
        k = {"Y": 0, "C": 1, "F": 2}[kind] * n + i
        sems = self.send.at[k], self.recv.at[k]
        sib = device(z, x, y, 1 - c)
        if kind == "Y":
            return remote(piece, self.full.at[self.rows(y, c, i)], *sems, device(z, x, 1 - y, c))
        if kind == "C":
            return remote(piece, self.full.at[self.rows(y, c, i)], *sems, sib)
        at = self.full.at[self.rows(1 - y, c, i)]
        return remote(at, at, *sems, sib)

    def begin(self, i):
        for kind in ("Y", "C", "own"):
            self.message(kind, i).start()

    def on(self, i):
        self.message("Y", i).wait_recv()
        self.message("F", i).start()

    def end(self):
        for i in range(self.pieces):
            self.message("own", i).wait()
            self.message("C", i).wait_recv()
            self.message("F", i).wait_recv()
            for kind in ("Y", "C", "F"):
                self.message(kind, i).wait_send()


def finish(tokens, gain, cot, middle_cot):
    hat, inv_sigma = normalize(tokens.T.astype(F32))
    d = cot * gain
    made = middle_cot + inv_sigma * (
        d - jnp.mean(d, axis=0, keepdims=True) - hat * jnp.mean(d * hat, axis=0, keepdims=True)
    )
    return made.T.astype(BF16)


class Scatter:
    def __init__(self, nz, ups, src, part, out, core, side, line, last, send, recv):
        self.nz, self.ups, self.src, self.part, self.out = nz, ups, src, part, out
        self.core, self.side, self.line, self.last, self.send, self.recv = core, side, line, last, send, recv
        self.depth = out.shape[0]

    @staticmethod
    def scratch(nz, ups, depth, columns):
        count = len(ups) * nz + 2 * nz
        return [
            pltpu.VMEM((len(ups), 2 * nz * depth, columns), BF16),
            pltpu.VMEM((len(ups), nz * depth, columns), BF16),
            pltpu.VMEM((nz, len(ups), depth, columns), BF16),
            pltpu.VMEM((depth, columns), BF16),
            pltpu.SemaphoreType.DMA((count,)),
            pltpu.SemaphoreType.DMA((count,)),
        ]

    def row(self, d):
        z, _, _, _ = place()
        return lax.bitwise_xor(z, d)

    def rows(self, d, x):
        return pl.ds(pl.multiple_of((2 * self.row(d) + x) * self.depth, 16), self.depth)

    def both(self, d):
        return pl.ds(pl.multiple_of(2 * self.row(d) * self.depth, 16), 2 * self.depth)

    def lane(self, d):
        return pl.ds(pl.multiple_of(self.row(d) * self.depth, 16), self.depth)

    def message(self, kind, d, u=0):
        z, x, y, c = place()
        nz, n = self.nz, len(self.ups)
        i = {"C": u * nz + d, "X": n * nz + d, "Z": n * nz + nz + d, "Y": n * nz + nz}[kind]
        sems = self.send.at[i], self.recv.at[i]
        if kind == "C":
            both = self.both(d)
            return remote(self.src.at[2 * self.ups[u] + 1 - c, both], self.core.at[u, both], *sems, device(z, x, y, 1 - c))
        if kind == "X":
            return remote(
                self.core.at[:, self.rows(d, 1 - x)], self.side.at[:, self.lane(d)], *sems, device(z, 1 - x, y, c)
            )
        if kind == "Z":
            return remote(self.side.at[:, self.lane(d)], self.line.at[d], *sems, device(self.row(d), x, y, c))
        return remote(self.line.at[0, 1 - y if n == 2 else 0], self.last, *sems, device(z, x, 1 - y, c))

    def begin(self, *rows):
        for d in rows:
            for u in range(len(self.ups)):
                self.message("C", d, u).start()

    def cross(self, d):
        self.message("X", d).start()

    def chip(self, d):
        _, x, _, c = place()
        for u in range(len(self.ups)):
            self.message("C", d, u).wait_recv()
        for side in range(2):
            rows = self.rows(d, side)
            for u, up in enumerate(self.ups):
                self.core[u, rows] = self.part[2 * up + c, rows] + self.core[u, rows]

    def over(self, d):
        _, x, _, _ = place()
        self.message("X", d).wait_recv()
        rows, lane = self.rows(d, x), self.lane(d)
        for u in range(len(self.ups)):
            self.side[u, lane] = self.core[u, rows] + self.side[u, lane]
        if d:
            self.message("Z", d).start()

    def along(self):
        _, _, y, _ = place()
        for d in range(1, self.nz):
            self.message("Z", d).wait_recv()
        lane = self.lane(0)
        for u in range(len(self.ups)):
            made = self.side[u, lane].astype(F32)
            for d in range(1, self.nz):
                made += self.line[d, u].astype(F32)
            self.line[0, u] = made.astype(BF16)
        if len(self.ups) == 2:
            self.message("Y", 0).start()
        else:
            pl.when(y != self.ups[0])(lambda: self.message("Y", 0).start())

    def end(self):
        _, _, y, _ = place()

        def receive():
            self.message("Y", 0).wait_recv()
            mine = self.line[0, y if len(self.ups) == 2 else 0]
            self.out[...] = mine.astype(F32) + self.last[...].astype(F32)

        if len(self.ups) == 2:
            receive()
            self.message("Y", 0).wait_send()
        else:
            pl.when(y == self.ups[0])(receive)
            pl.when(y != self.ups[0])(lambda: self.message("Y", 0).wait_send())
        for d in range(self.nz):
            for u in range(len(self.ups)):
                self.message("C", d, u).wait_send()
            self.message("X", d).wait_send()
            if d:
                self.message("Z", d).wait_send()


class Everyone:
    def __init__(self, held, near, full, far, send, recv):
        self.held, self.near, self.full, self.far, self.send, self.recv = held, near, full, far, send, recv
        self.group, self.owners = near.shape[0], far.shape[0]

    @staticmethod
    def scratch(n_mp, n_dp):
        dma = pltpu.SemaphoreType.DMA
        blocks = pltpu.VMEM((n_dp, 8, 128), F32)
        count = n_mp + n_dp
        return [blocks, pltpu.VMEM((n_mp, n_dp, 8, 128), F32), blocks, blocks, dma((count,)), dma((count,))]

    @staticmethod
    def peers(n_mp, n_dp):
        dp, mp = lax.axis_index("dp"), lax.axis_index("mp")
        return [(dp, lax.bitwise_xor(mp, k)) for k in range(1, n_mp)] + [
            (lax.bitwise_xor(dp, k), mp) for k in range(1, n_dp)
        ]

    def within(self, k):
        dp, mp = lax.axis_index("dp"), lax.axis_index("mp")
        sems = self.send.at[k], self.recv.at[k]
        return remote(self.held, self.near.at[mp], *sems, (dp, lax.bitwise_xor(mp, k)))

    def owner(self, k):
        dp, mp = lax.axis_index("dp"), lax.axis_index("mp")
        other = lax.bitwise_xor(dp, k)
        sems = self.send.at[self.group + k], self.recv.at[self.group + k]
        return remote(self.full.at[other], self.far.at[dp], *sems, (other, mp))

    def begin(self):
        for k in range(1, self.group):
            self.within(k).start()
        self.near[lax.axis_index("mp")] = self.held[...]

    def pass_on(self):
        for k in range(1, self.group):
            self.within(k).wait_recv()
        made = self.near[0]
        for i in range(1, self.group):
            made += self.near[i]
        self.full[...] = made
        for k in range(1, self.owners):
            self.owner(k).start()
        dp = lax.axis_index("dp")
        self.far[dp] = self.full[dp]

    def end(self):
        for k in range(1, self.owners):
            self.owner(k).wait_recv()
        made = self.far[0]
        for i in range(1, self.owners):
            made += self.far[i]
        for k in range(1, self.group):
            self.within(k).wait_send()
        for k in range(1, self.owners):
            self.owner(k).wait_send()
        return made


class Fold:
    def __init__(self, part, near, far, send, recv):
        self.part, self.near, self.far, self.send, self.recv = part, near, far, send, recv
        self.slots = part.shape[0]

    @staticmethod
    def scratch(n_mp, own, slots):
        dma = pltpu.SemaphoreType.DMA
        return [
            pltpu.VMEM((slots, n_mp, 2 * HDIM, own), BF16),
            pltpu.VMEM((slots, 2, 2 * HDIM, own), BF16),
            pltpu.VMEM((slots, 2 * HDIM, own), BF16),
            dma((slots, 3)),
            dma((slots, 3)),
        ]

    def message(self, kind, head):
        z, x, y, c = place()
        slot = lax.rem(head, self.slots)
        k = {"far": 0, "near": 1, "Y": 2}[kind]
        sems = self.send.at[slot, k], self.recv.at[slot, k]
        if kind == "Y":
            return remote(self.near.at[slot, 1 - y], self.far.at[slot], *sems, device(z, x, 1 - y, c))
        up = 1 - y if kind == "far" else y
        return remote(self.part.at[slot, 2 * up + 1 - c], self.near.at[slot, up], *sems, device(z, x, y, 1 - c))

    def begin(self, head):
        self.message("far", head).start()
        self.message("near", head).start()

    def chip(self, head):
        _, _, y, c = place()
        slot = lax.rem(head, self.slots)
        self.message("far", head).wait_recv()
        self.near[slot, 1 - y] = self.part[slot, 2 * (1 - y) + c] + self.near[slot, 1 - y]
        self.message("Y", head).start()

    def end(self, head):
        _, _, y, c = place()
        slot = lax.rem(head, self.slots)
        self.message("near", head).wait_recv()
        self.message("Y", head).wait_recv()
        made = self.part[slot, 2 * y + c].astype(F32) + self.near[slot, y].astype(F32) + self.far[slot].astype(F32)
        for kind in ("far", "near", "Y"):
            self.message(kind, head).wait_send()
        return made.astype(BF16)


def forward_kernel(nz, units, len_ref, tok_hbm, *refs):
    linked = nz > 0
    given, refs = refs[: 6 if linked else 2], refs[6 if linked else 2 :]
    mine_ref, q_ref, k_ref, v_ref, cos_ref, sin_ref, o_ref, p_ref, inv_ref = refs[:9]
    full_refs, refs = refs[9 : 12 if linked else 9], refs[12 if linked else 9 :]
    wa_ref, wb_ref, w_ref, n1_ref, ka_ref, qa_ref, va_ref, stat_ref, tok_ref, load = refs[:10]
    refs = refs[10:]
    rows, features = tok_ref.shape
    own = q_ref.shape[1]
    docs = len_ref.shape[1]
    step = pl.program_id(0)
    parts = wa_ref.shape[0]
    part, turn_at = lax.rem(step, parts), step // parts
    me = lax.axis_index("mp")
    mine = pl.ds(pl.multiple_of(me * own, own), own)
    three = 3 * HDIM

    if linked:
        srcs = refs[:3]
        one = Gather(nz, srcs[0], wa_ref, *refs[3:6], eager=True)
        two = Gather(nz, srcs[1], wb_ref, *refs[6:9], eager=True)
        last = Gather(nz, srcs[2], full_refs[2], *refs[9:12])
        keeps = [
            pltpu.make_async_copy(wa_ref, full_refs[0], load.at[0]),
            pltpu.make_async_copy(wb_ref, full_refs[1], load.at[1]),
        ]

    @pl.when(step == 0)
    def _():
        bring = pltpu.make_async_copy(tok_hbm, tok_ref, load.at[2])
        bring.start()
        if linked:
            wq_ref, wg_ref, wo_ref, wd_ref, one_ref, two_ref = given
            hail(peers(nz))
            for i in range(3):
                srcs[0][:, i * HDIM : (i + 1) * HDIM] = wq_ref[i, :, :HDIM]
            srcs[0][:, three : three + 1] = one_ref[...].astype(F32).T.astype(BF16)
            srcs[0][:, three + 1 : three + 2] = two_ref[...].astype(F32).T.astype(BF16)
            down = wd_ref[...].T
            srcs[0][:, 256 - units % 128 :] = down[:, units - units % 128 :]
            pl.semaphore_wait(pltpu.get_barrier_semaphore(), len(peers(nz)))
            one.begin()
            for r in range(1, wq_ref.shape[2] // HDIM):
                for i in range(3):
                    at = (r - 1) * three + i * HDIM
                    srcs[1][:, at : at + HDIM] = wq_ref[i, :, r * HDIM : (r + 1) * HDIM]
            two.begin()
            pair, width = 2 * units, wo_ref.shape[0]
            for i in range(2):
                srcs[2][:, i * units : (i + 1) * units] = wg_ref[:, i, :]
            srcs[2][:, pair : pair + width] = wo_ref[...].T
            srcs[2][:, pair + width :] = down[:, : units - units % 128]
        else:
            fetches = [pltpu.make_async_copy(g, w, load.at[i]) for i, (g, w) in enumerate(zip(given, (wa_ref, wb_ref)))]
            for fetch in fetches:
                fetch.start()
        _, position, _ = layout_rows(len_ref, docs, 0, rows)
        power = lax.broadcasted_iota(jnp.int32, (HALF, 1), 0).astype(F32) * (-2.0 / HDIM * math.log2(ROPE_BASE))
        angle = position.astype(F32) * jnp.exp2(power)
        cos_ref[...] = jnp.cos(angle)
        sin_ref[...] = jnp.sin(angle)
        keys, _, _ = layout_rows(len_ref, docs, 0, rows)
        queries, _, _ = layout_rows(len_ref, docs, me * own, own)
        kind = lax.broadcasted_iota(jnp.int32, (AUG - HDIM, 1), 0)
        ka_ref[HDIM:] = jnp.where(kind == keys, 1.0, 0.0).astype(BF16)
        qa_ref[HDIM:] = jnp.where(kind == queries, 0.0, FAR).astype(BF16)
        va_ref[HDIM:] = jnp.ones((AUG - HDIM, rows), BF16)

        def measure(i, carry):
            at = pl.ds(pl.multiple_of(i * own, own), own)
            turned = tok_ref[at, :].T
            n1_ref[:, at] = turned
            mean, inv = moments(turned.astype(F32))
            stat_ref[0:1, at] = mean
            stat_ref[1:2, at] = inv
            return carry

        if linked:
            one.all_along()
        bring.wait()
        lax.fori_loop(0, rows // own, measure, 0)
        if linked:
            one.all_over()
            last.begin()
            one.rest()
            keeps[0].start()
        else:
            for fetch in fetches:
                fetch.wait()
        gain = wa_ref[0, :, three : three + 1].astype(F32)

        def norm(i, carry):
            at = pl.ds(pl.multiple_of(i * own, own), own)
            made = (n1_ref[:, at].astype(F32) - stat_ref[0:1, at]) * stat_ref[1:2, at] * gain
            n1_ref[:, at] = made.astype(BF16)
            return carry

        lax.fori_loop(0, rows // own, norm, 0)
        mine_ref[...] = n1_ref[:, mine]

    if linked:
        gathers = {"two": two, "last": last}
        for at, which, name, *d in GATHER_STEPS:
            pl.when(step == at)(functools.partial(getattr(gathers[which], name), *d))

        @pl.when(step == parts)
        def _():
            two.rest()
            keeps[1].start()

    @pl.when(turn_at == 0)
    def _():
        w_ref[...] = wa_ref[part, :, :three]

    for r in range(1, 1 + wb_ref.shape[2] // three):

        @pl.when(turn_at == r)
        def _():
            w_ref[...] = wb_ref[part, :, (r - 1) * three : r * three]

    made = dot(w_ref[:, HDIM:], n1_ref[...], TN)
    keys = turn(made[:HDIM], cos_ref[...], sin_ref[...], 1).astype(BF16)
    k_ref[...] = keys
    ka_ref[:HDIM] = keys
    values = made[HDIM:].astype(BF16)
    v_ref[...] = values
    va_ref[:HDIM] = values
    made = dot(w_ref[:, :HDIM], n1_ref[:, mine], TN) * (SCALE * LOG2E)
    queries = turn(made, cos_ref[:, mine], sin_ref[:, mine], 1).astype(BF16)
    q_ref[...] = queries
    qa_ref[:HDIM] = queries
    scores = dot(ka_ref[...], qa_ref[...], TN)
    top = jnp.max(scores, axis=0, keepdims=True)
    probs = jnp.exp2(scores - top).astype(BF16)
    p_ref[0] = probs
    out = dot(va_ref[...], probs, NN)
    inv = 1.0 / out[HDIM : HDIM + 1]
    o_ref[...] = (out[:HDIM] * inv).astype(BF16)
    inv_ref[0] = inv
    if linked:

        @pl.when(step == pl.num_programs(0) - 1)
        def _():
            for keep in keeps:
                keep.wait()
            last.corner(3)
            last.end()


GATHER_STEPS = (
    (0, "two", "along", 1),
    (0, "two", "along", 2),
    (0, "two", "along", 3),
    (0, "last", "push", 2),
    (1, "two", "over", 0),
    (1, "two", "over", 1),
    (2, "two", "over", 2),
    (2, "two", "over", 3),
    (2, "last", "push", 3),
    (3, "last", "along", 1),
    (3, "last", "over", 0),
    (4, "last", "along", 2),
    (5, "last", "over", 1),
    (6, "last", "corner", 0),
    (6, "last", "along", 3),
    (7, "last", "over", 2),
    (8, "last", "corner", 1),
    (9, "last", "over", 3),
    (11, "last", "corner", 2),
)


def forward(nz, n_mp, units, lengths, tokens, weights, columns):
    rows, features = tokens.shape
    own, width, heads = rows // n_mp, features // n_mp, features // HDIM
    per = width // HDIM
    linked = nz > 0
    hbm = pl.BlockSpec(memory_space=pl.ANY)
    head = lambda h: lax.rem(h, n_mp) * per + h // n_mp
    row = lambda h: (head(h), 0)
    cube = lambda h: (head(h), 0, 0)
    vm = pl.BlockSpec(memory_space=pltpu.VMEM)
    n = Gather.count(nz) if linked else 0
    dma = pltpu.SemaphoreType.DMA
    depth = features // (2 * nz) if linked else 0
    full_shapes = [jax.ShapeDtypeStruct((n_mp, features, c), BF16) for c in columns] if linked else []
    return pl.pallas_call(
        functools.partial(forward_kernel, nz, units),
        grid=(heads,),
        in_specs=[pl.BlockSpec(memory_space=pltpu.SMEM), hbm] + ([vm] * 6 if linked else [hbm] * 2),
        out_specs=[
            whole(features, own),
            pl.BlockSpec((HDIM, own), row),
            pl.BlockSpec((HDIM, rows), row),
            pl.BlockSpec((HDIM, rows), row),
            whole(HALF, rows),
            whole(HALF, rows),
            pl.BlockSpec((HDIM, own), row),
            pl.BlockSpec((1, rows, own), cube),
            pl.BlockSpec((1, 1, own), cube),
        ]
        + [hbm] * len(full_shapes),
        out_shape=[
            jax.ShapeDtypeStruct((features, own), BF16),
            jax.ShapeDtypeStruct((features, own), BF16),
            jax.ShapeDtypeStruct((features, rows), BF16),
            jax.ShapeDtypeStruct((features, rows), BF16),
            jax.ShapeDtypeStruct((HALF, rows), F32),
            jax.ShapeDtypeStruct((HALF, rows), F32),
            jax.ShapeDtypeStruct((features, own), BF16),
            jax.ShapeDtypeStruct((heads, rows, own), BF16),
            jax.ShapeDtypeStruct((heads, 1, own), F32),
        ]
        + full_shapes,
        scratch_shapes=[
            pltpu.VMEM((n_mp, features, columns[0]), BF16),
            pltpu.VMEM((n_mp, features, columns[1]), BF16),
            pltpu.VMEM((features, 3 * HDIM), BF16),
            pltpu.VMEM((features, rows), BF16),
            pltpu.VMEM((AUG, rows), BF16),
            pltpu.VMEM((AUG, own), BF16),
            pltpu.VMEM((AUG, rows), BF16),
            pltpu.VMEM((8, rows), F32),
            pltpu.VMEM((rows, features), BF16),
            dma((3,)),
        ]
        + (
            [pltpu.VMEM((depth, c), BF16) for c in columns] + [dma((n,)), dma((n,)), dma] * 3
            if linked
            else []
        ),
        compiler_params=pltpu.CompilerParams(
            dimension_semantics=("arbitrary",),
            vmem_limit_bytes=VMEM_BYTES,
            **({"collective_id": 1, "has_side_effects": True} if linked else {}),
        ),
        name="forward",
    )(lengths, tokens, *weights)


def middle(len_ref, me, tok_ref, cot_ref, heads_ref, inv_ref, w_ref, gain, units, out_ref, mcot_ref, do_ref, keep, sent, done, later):
    own, features = tok_ref.shape
    parts = w_ref.shape[0]
    width = features // parts
    heads = width // HDIM
    pair = 2 * units
    _, _, live = layout_rows(len_ref, len_ref.shape[1], me * own, own)

    def w_gu(m):
        return w_ref[m, :, :pair]

    def w_out(m):
        return w_ref[m, :, pair : pair + width]

    def w_down(m):
        return w_ref[m, :, pair + width : pair + width + units]

    total = dot(w_out(0), heads_ref[:width], NN)
    for m in range(1, parts):
        total += dot(w_out(m), heads_ref[m * width : (m + 1) * width], NN)
    middle = tok_ref[...].T.astype(F32) + total
    hat, inv_sigma = normalize(middle)
    normed = (hat * gain).astype(BF16)
    total = middle
    kept = []
    for m in range(parts):
        gate_up = dot(w_gu(m), normed, TN)
        gate, up = gate_up[:units], gate_up[units:]
        phi, slope = gelu_parts(gate)
        act = gate * phi
        hidden = (act * up).astype(BF16)
        total += dot(w_down(m), hidden, NN)
        kept.append((hidden, (up * (phi + slope)).astype(BF16), act.astype(BF16)))
    out_ref[...] = total.astype(BF16).T
    sent()
    branch = jnp.where(live, cot_ref[...].T.astype(F32), 0.0).astype(BF16)
    back = jnp.zeros((features, own), F32)
    for m in range(parts):
        hidden, one, two = kept[m]
        hidden_cot = dot(w_down(m), branch, TN)
        keep("down", m, dot(branch, hidden, NT).astype(BF16))
        cots = jnp.concatenate([hidden_cot * one.astype(F32), hidden_cot * two.astype(F32)], axis=0).astype(BF16)
        keep("gu", m, dot(normed, cots, NT).astype(BF16))
        back += dot(w_gu(m), cots, NN)
    done()
    keep("gain", 0, jnp.sum(back * hat, axis=1, keepdims=True))
    d = back * gain
    middle_cot = branch.astype(F32) + inv_sigma * (
        d - jnp.mean(d, axis=0, keepdims=True) - hat * jnp.mean(d * hat, axis=0, keepdims=True)
    )
    mcot_ref[...] = middle_cot
    attn_cot = middle_cot.astype(BF16)
    for m in range(parts):
        back_heads = dot(w_out(m), attn_cot, TN)
        for h in range(heads):
            head = m * heads + h
            rows = slice(h * HDIM, (h + 1) * HDIM)
            cot = back_heads[rows] * inv_ref[head]
            inner = jnp.sum(cot * heads_ref[head * HDIM : (head + 1) * HDIM].astype(F32), axis=0, keepdims=True)
            high = inner.astype(BF16).astype(F32)
            pad = jnp.zeros((AUG - HDIM - 2, own), F32)
            do_ref[head] = jnp.concatenate([cot, high, inner - high, pad], axis=0).astype(BF16)
    later()
    for m in range(parts):
        keep("out", m, dot(attn_cot, heads_ref[m * width : (m + 1) * width], NT).astype(BF16))


def mid_kernel(
    units, len_ref, tok_hbm, cot_hbm, heads_ref, inv_ref, two_ref, w_hbm,
    out_ref, mcot_ref, do_ref, g_ref, o_ref, gain_ref, tok_ref, cot_ref, w_ref, load,
):
    own = tok_ref.shape[0]
    me = lax.axis_index("mp")
    mine = pl.ds(pl.multiple_of(me * own, own), own)
    loads = [
        pltpu.make_async_copy(tok_hbm.at[mine], tok_ref, load.at[0]),
        pltpu.make_async_copy(cot_hbm.at[mine], cot_ref, load.at[1]),
        pltpu.make_async_copy(w_hbm, w_ref, load.at[2]),
    ]
    for copy in loads:
        copy.start()
    for copy in loads:
        copy.wait()
    pair = 2 * units

    def keep(what, m, made):
        if what == "gu":
            g_ref[m, :, :pair] = made
        elif what == "down":
            g_ref[m, :, pair:] = made
        elif what == "out":
            o_ref[m] = made
        else:
            gain_ref[...] = made

    nothing = lambda: None
    middle(
        len_ref, me, tok_ref, cot_ref, heads_ref, inv_ref, w_ref, two_ref[...].astype(F32), units, out_ref, mcot_ref, do_ref,
        keep, nothing, nothing, nothing,
    )


def mid(n_mp, lengths, tokens, out_grad, heads_out, inv, gain, w_rest, units):
    features, own = heads_out.shape
    heads = inv.shape[0]
    vm = pl.BlockSpec(memory_space=pltpu.VMEM)
    hbm = pl.BlockSpec(memory_space=pl.ANY)
    return pl.pallas_call(
        functools.partial(mid_kernel, units),
        in_specs=[pl.BlockSpec(memory_space=pltpu.SMEM), hbm, hbm, vm, vm, vm, hbm],
        out_specs=[vm] * 6,
        out_shape=[
            jax.ShapeDtypeStruct((own, features), BF16),
            jax.ShapeDtypeStruct((features, own), F32),
            jax.ShapeDtypeStruct((heads, AUG, own), BF16),
            jax.ShapeDtypeStruct((n_mp, features, 3 * units), BF16),
            jax.ShapeDtypeStruct((n_mp, features, features // n_mp), BF16),
            jax.ShapeDtypeStruct((features, 1), F32),
        ],
        scratch_shapes=[
            pltpu.VMEM((own, features), BF16),
            pltpu.VMEM((own, features), BF16),
            pltpu.VMEM(w_rest.shape, BF16),
            pltpu.SemaphoreType.DMA((3,)),
        ],
        compiler_params=pltpu.CompilerParams(vmem_limit_bytes=VMEM_BYTES),
        name="mid",
    )(lengths, tokens, out_grad, heads_out, inv, gain, w_rest)


SLOTS = 7
LAG = 4
PIECES = 4


def backward_kernel(nz, units, *refs):
    len_ref, q_ref, k_ref, v_ref, p_ref, cos_ref, sin_ref, n1_ref, heads_ref, inv_ref, wa_ref, tok_hbm, cot_hbm, wb_hbm, wr_hbm = refs[:15]
    dq_ref, dr_ref, gains_ref, in_full, out_full = refs[15:20]
    wb_ref, wr_ref, gr_ref, do_ref, mcot_ref, pc_ref, qc_ref, acc_ref, gc_ref, va_ref, tok_ref, cot_ref, own_ref, load = refs[20:34]
    refs = refs[34:]
    gq_ref = wr_ref.at[:, :, pl.ds(0, dq_ref.shape[1])]
    rest = Scatter(nz, (0, 1), gr_ref, gr_ref, dr_ref, *refs[:6])
    low = Scatter(nz, (0,), gq_ref, gq_ref, dq_ref, *refs[6:12])
    high = Scatter(nz, (1,), gq_ref, gq_ref, dq_ref, *refs[12:18])
    fold = Fold(*refs[18:23])
    in_share = Share(own_ref.at[0], in_full, *refs[23:26], PIECES)
    out_share = Share(own_ref.at[1], out_full, *refs[26:29])
    gains = Everyone(*refs[29:35])
    step, heads = pl.program_id(0) - 1, pl.num_programs(0) - 1
    parts = wa_ref.shape[0]
    features, own = n1_ref.shape
    rows = k_ref.shape[1]
    width = features // parts
    per = width // HDIM
    me = lax.axis_index("mp")
    mine = pl.ds(pl.multiple_of(me * own, own), own)
    late = pltpu.make_async_copy(wb_hbm, wb_ref, load.at[3])
    three = 3 * HDIM
    depth = gains_ref.shape[1]
    shards = features // depth

    def put(row, column):
        for i in range(shards):
            gains.held[i, row : row + 1, :depth] = column[i * depth : (i + 1) * depth].T

    @pl.when(step < 0)
    def _():
        gains.held[0] = jnp.zeros(gains.held.shape[1:], F32)
        loads = [
            pltpu.make_async_copy(wr_hbm, wr_ref.at[:, :, pl.ds(0, wr_hbm.shape[2])], load.at[0]),
            pltpu.make_async_copy(tok_hbm.at[mine], tok_ref, load.at[1]),
            pltpu.make_async_copy(cot_hbm.at[mine], cot_ref, load.at[2]),
        ]
        for copy in loads:
            copy.start()
        greet(Everyone.peers(parts, 2 * nz))
        for copy in loads:
            copy.wait()
        late.start()
        pair = 2 * units

        def first():
            rest.chip(2)
            rest.cross(2)

        for m in range(parts):
            wr_ref[m, :, wr_hbm.shape[2] :] = wa_ref[m, :, 256 - units % 128 :]

        def keep(what, m, made):
            if what == "gu":
                gr_ref[m, :, :pair] = made
            elif what == "down":
                gr_ref[m, :, pair:] = made
            elif what == "out":
                wr_ref[m, :, 3 * width : 4 * width] = made
            else:
                put(1, made)

        middle(
            len_ref, me, tok_ref, cot_ref, heads_ref, inv_ref, wr_ref, wa_ref[0, :, three + 1 : three + 2].astype(F32), units,
            own_ref.at[1], mcot_ref, do_ref, keep,
            lambda: out_share.begin(0), lambda: rest.begin(2, 3), first,
        )
        va_ref[HDIM:] = jnp.full((AUG - HDIM, rows), -1.0, BF16)
        acc_ref[...] = jnp.zeros_like(acc_ref)
        gc_ref[...] = jnp.zeros_like(gc_ref)
        late.wait()

    def collect(head):
        at = lax.rem(head, per) * three
        pc_ref[pl.ds(pl.multiple_of(at + HDIM, HDIM), 2 * HDIM)] = fold.end(head)

    def close(part):
        for i in range(per):
            pc_ref[i * three : i * three + HDIM] = qc_ref[lax.rem(part, 3), i * HDIM : (i + 1) * HDIM]
        made = dot(n1_ref[...], pc_ref[...], NT)
        wr_ref[part, :, : 3 * width] = made.astype(BF16)
        weights = jnp.concatenate([wa_ref[part, :, :three], wb_ref[part]], axis=1)
        gc_ref[...] += jnp.sum(made * weights.astype(F32), axis=1, keepdims=True)
        acc_ref[...] += dot(weights, pc_ref[...], NN)

    @pl.when(step >= 0)
    def _():
        va_ref[:HDIM] = v_ref[...]
        cot = dot(va_ref[...], do_ref[step], TN)
        probs = p_ref[0]
        score_cot = probs * cot.astype(BF16)
        dv = dot(do_ref[step, :HDIM], probs, NT).astype(BF16)
        dk = turn(dot(q_ref[...], score_cot, NT) * LN2, cos_ref[...], sin_ref[...], 1, True).astype(BF16)
        dq = turn(dot(k_ref[...], score_cot, NN) * SCALE, cos_ref[:, mine], sin_ref[:, mine], 1, True)
        slot = lax.rem(step, SLOTS)
        for m in range(parts):
            fold.part[slot, m, :HDIM] = dk[:, m * own : (m + 1) * own]
            fold.part[slot, m, HDIM:] = dv[:, m * own : (m + 1) * own]
        at = pl.ds(pl.multiple_of(lax.rem(step, per) * HDIM, HDIM), HDIM)
        qc_ref[lax.rem(step // per, 3), at] = dq.astype(BF16)

        @pl.when(step >= LAG)
        def _():
            collect(step - LAG)

        @pl.when(step >= 1)
        def _():
            fold.chip(step - 1)

        fold.begin(step)

        @pl.when((step >= LAG) & (lax.rem(step - LAG, per) == per - 1))
        def _():
            close((step - LAG) // per)

    sums = {"rest": rest, "low": low, "high": high, "out": out_share, "in": in_share, "gains": gains}
    for at, which, name, *d in SUM_STEPS:
        pl.when(step == at)(functools.partial(getattr(sums[which], name), *d))

    @pl.when(step == heads - 1)
    def _():
        fold.chip(step)
        for which, name, *d in FLUSH_STEPS:
            getattr(sums[which], name)(*d)
        for back in range(LAG - 1, -1, -1):
            collect(step - back)
            if (features // HDIM - 1 - back) % per == per - 1:
                close((step - back) // per)
        high.begin(2, 3, 1, 0)
        gain = wa_ref[0, :, three : three + 1].astype(F32)
        put(0, gc_ref[...] / gain)
        gains.begin()
        size = own // PIECES
        for i in range(PIECES):
            at = slice(i * size, (i + 1) * size)
            own_ref[0, at] = finish(tok_ref[at], gain, acc_ref[:, at], mcot_ref[:, at])
            in_share.begin(i)
        for which, name, *d in LAST_STEPS:
            getattr(sums[which], name)(*d)
        high.along()
        for which in (rest, low, high):
            which.end()
        out_share.end()
        in_share.end()
        gains_ref[...] = gains.end()[:2, :depth]


SUM_STEPS = (
    (-1, "rest", "begin", 1, 0),
    (-1, "rest", "chip", 3),
    (0, "rest", "cross", 3),
    (0, "rest", "chip", 1),
    (0, "rest", "chip", 0),
    (1, "rest", "over", 2),
    (1, "out", "on", 0),
    (3, "rest", "cross", 1),
    (4, "rest", "over", 3),
    (6, "rest", "cross", 0),
    (7, "rest", "over", 1),
    (9, "low", "begin", 2, 3, 1, 0),
    (10, "low", "chip", 2),
    (10, "low", "chip", 3),
    (10, "low", "chip", 1),
    (10, "low", "chip", 0),
    (10, "low", "cross", 2),
    (10, "low", "cross", 3),
    (10, "low", "cross", 1),
    (10, "low", "cross", 0),
    (9, "rest", "over", 0),
)
FLUSH_STEPS = (
    ("rest", "along"),
    ("low", "over", 2),
    ("low", "over", 3),
)
LAST_STEPS = (
    ("high", "chip", 2),
    ("high", "cross", 2),
    ("high", "chip", 3),
    ("high", "cross", 3),
    ("high", "chip", 1),
    ("high", "cross", 1),
    ("high", "chip", 0),
    ("high", "cross", 0),
    ("low", "over", 1),
    ("low", "over", 0),
    ("gains", "pass_on"),
    ("high", "over", 2),
    ("in", "on", 0),
    ("high", "over", 3),
    ("in", "on", 1),
    ("high", "over", 1),
    ("low", "along"),
    ("high", "over", 0),
    ("in", "on", 2),
    ("in", "on", 3),
)


def backward(nz, lengths, q, k, v, p, cos, sin, n1, heads_out, inv, tokens, out_grad, w_a, w_b, w_rest, units):
    (features, own), rows = q.shape, k.shape[1]
    n_mp = w_a.shape[0]
    heads = features // HDIM
    width = features // n_mp
    depth = features // (2 * nz)
    columns = 4 * width, 3 * units
    hbm = pl.BlockSpec(memory_space=pl.ANY)
    vm = pl.BlockSpec(memory_space=pltpu.VMEM)
    row = lambda h: (jnp.maximum(h - 1, 0), 0)
    cube = lambda h: (jnp.maximum(h - 1, 0), 0, 0)
    dma = pltpu.SemaphoreType.DMA
    return pl.pallas_call(
        functools.partial(backward_kernel, nz, units),
        grid=(heads + 1,),
        in_specs=[
            pl.BlockSpec(memory_space=pltpu.SMEM),
            pl.BlockSpec((HDIM, own), row),
            pl.BlockSpec((HDIM, rows), row),
            pl.BlockSpec((HDIM, rows), row),
            pl.BlockSpec((1, rows, own), cube),
        ]
        + [vm] * 6
        + [hbm] * 4,
        out_specs=[vm, vm, vm, hbm, hbm],
        out_shape=[
            jax.ShapeDtypeStruct((depth, columns[0]), F32),
            jax.ShapeDtypeStruct((depth, columns[1]), F32),
            jax.ShapeDtypeStruct((2, depth), F32),
            jax.ShapeDtypeStruct((rows, features), BF16),
            jax.ShapeDtypeStruct((rows, features), BF16),
        ],
        scratch_shapes=[
            pltpu.VMEM(w_b.shape, BF16),
            pltpu.VMEM((n_mp, features, width + 3 * units), BF16),
            pltpu.VMEM((n_mp, features, 3 * units), BF16),
            pltpu.VMEM((heads, AUG, own), BF16),
            pltpu.VMEM((features, own), F32),
            pltpu.VMEM((3 * width, own), BF16),
            pltpu.VMEM((3, width, own), BF16),
            pltpu.VMEM((features, own), F32),
            pltpu.VMEM((features, 1), F32),
            pltpu.VMEM((AUG, rows), BF16),
            pltpu.VMEM((own, features), BF16),
            pltpu.VMEM((own, features), BF16),
            pltpu.VMEM((2, own, features), BF16),
            dma((4,)),
        ]
        + Scatter.scratch(nz, (0, 1), depth, columns[1])
        + Scatter.scratch(nz, (0,), depth, columns[0])
        + Scatter.scratch(nz, (1,), depth, columns[0])
        + Fold.scratch(n_mp, own, SLOTS)
        + Share.sems(PIECES)
        + Share.sems(1)
        + Everyone.scratch(n_mp, 2 * nz),
        compiler_params=pltpu.CompilerParams(
            dimension_semantics=("arbitrary",), collective_id=3, has_side_effects=True, vmem_limit_bytes=VMEM_BYTES
        ),
        name="backward",
    )(lengths, q, k, v, p, cos, sin, n1, heads_out, inv, w_a, tokens, out_grad, w_b, w_rest)


def deliver_kernel(units, in_ref, out_ref, dq_ref, dr_ref, gains_ref, grad_ref, to_ref, gq_ref, go_ref, gg_ref, gd_ref, one_ref, two_ref):
    @pl.when(pl.program_id(0) == 0)
    def _():
        width = go_ref.shape[0]
        pair = 2 * units
        for r in range(width // HDIM):
            for i in range(3):
                at = (3 * r + i) * HDIM
                gq_ref[i, :, r * HDIM : (r + 1) * HDIM] = dq_ref[:, at : at + HDIM]
        go_ref[...] = dq_ref[:, 3 * width : 4 * width].T
        one_ref[...] = gains_ref[0:1]
        two_ref[...] = gains_ref[1:2]
        for i in range(2):
            gg_ref[:, i, :] = dr_ref[:, i * units : (i + 1) * units]
        gd_ref[...] = dr_ref[:, pair : pair + units].T

    grad_ref[...] = in_ref[...].astype(F32)
    to_ref[...] = out_ref[...]


def deliver(layer_out, input_grad, d_qkv, d_rest, gains, width, units):
    rows, features = input_grad.shape
    depth = d_qkv.shape[0]
    shape = lambda *s: jax.ShapeDtypeStruct(s, F32)
    shapes = [(3, depth, width), (width, depth), (depth, 2, units), (units, depth), (1, depth), (1, depth)]
    steps = 2
    slab = pl.BlockSpec((rows // steps, features), lambda i: (i, 0))
    return pl.pallas_call(
        functools.partial(deliver_kernel, units),
        grid=(steps,),
        in_specs=[slab, slab, whole(*d_qkv.shape), whole(*d_rest.shape), whole(*gains.shape)],
        out_specs=[slab, slab] + [whole(*s) for s in shapes],
        out_shape=[shape(rows, features), jax.ShapeDtypeStruct((rows, features), BF16)] + [shape(*s) for s in shapes],
        compiler_params=params("arbitrary"),
        name="deliver",
    )(input_grad, layer_out, d_qkv, d_rest, gains)


def per_device(n_dp, n_mp, tokens, out_grad, w_qkv, w_out, w_gu, w_down, gain_attn, gain_mlp, lengths):
    rows, features = tokens.shape
    depth = w_qkv.shape[0]
    units, width = w_down.shape[0], w_out.shape[0]
    everyone = ("mp", "dp")
    linked = n_mp == 4 and n_dp == 8 and depth % 32 == 0 and features // HDIM == 12
    nz = n_dp // 2 if linked else 0
    three = 3 * HDIM
    loose = units % 128
    columns = 256, 3 * width - three, 3 * units + width - loose
    wq = w_qkv.transpose(1, 0, 2)
    if linked:
        weights = wq, w_gu, w_out, w_down, gain_attn[None], gain_mlp[None]
        n1, q, k, v, cos, sin, heads_out, probs, inv, w_a, w_b, w_c = forward(
            nz, n_mp, units, lengths, tokens, weights, columns
        )
        d_qkv, d_rest, gains, in_full, layer_out = backward(
            nz, lengths, q, k, v, probs, cos, sin, n1, heads_out, inv, tokens, out_grad, w_a, w_b, w_c, units
        )
    else:
        by_head = w_qkv.reshape(depth, 3, width // HDIM, HDIM).transpose(0, 2, 1, 3).reshape(depth, 3 * width)
        blank = jnp.zeros((depth, columns[0] - three - 2), BF16)
        shards = [
            jnp.concatenate([by_head[:, :three], gain_attn[:, None], gain_mlp[:, None], blank], axis=1),
            by_head[:, three:],
            jnp.concatenate([w_gu.reshape(depth, -1), w_out.T, w_down.T], axis=1),
        ]
        w_a, w_b, w_c = (
            lax.all_gather(s, everyone, axis=0, tiled=True).reshape(n_mp, features, s.shape[1]) for s in shards
        )
        n1, q, k, v, cos, sin, heads_out, probs, inv = forward(nz, n_mp, units, lengths, tokens, [w_a, w_b], columns)
        layer_out, middle_cot, do, g_rest, g_out, gain_two = mid(
            n_mp, lengths, tokens, out_grad, heads_out, inv, w_a[0, :, three + 1 : three + 2], w_c, units
        )
        own = middle_cot.shape[1]
        swap = lambda g, a, b: g.reshape(n_mp, features, a, b, HDIM).swapaxes(2, 3).reshape(n_mp, features, 3 * width)
        natural = jnp.concatenate([w_a[..., :three], w_b], axis=2)
        natural = jnp.concatenate([swap(natural, width // HDIM, 3), w_a[..., three : three + 1]], axis=2)
        g_qkv, nc = last(q, k, v, do, probs, cos, sin, lax.all_gather(n1, "mp", axis=1, tiled=True), natural)
        gain_one = w_a[0, :, three : three + 1].astype(F32)
        tok = lax.dynamic_slice_in_dim(tokens, lax.axis_index("mp") * own, own, 0)
        nc_own = lax.psum_scatter(nc, "mp", scatter_dimension=0, tiled=True)[0]
        in_own = finish(tok, gain_one, nc_own.astype(F32), middle_cot)
        layer_out, in_full = (lax.all_gather(v, "mp", axis=0, tiled=True) for v in (layer_out, in_own))
        both = jnp.stack([g_qkv[0, :, -1].astype(F32), gain_two[:, 0]])
        both = lax.psum(both, everyone)
        gains = lax.dynamic_slice_in_dim(both, lax.axis_index("dp") * depth, depth, 1)
        g_qkv = jnp.concatenate([swap(g_qkv[..., : 3 * width], 3, width // HDIM), g_out], axis=2)
        d_qkv, d_rest = (
            lax.psum_scatter(
                g.reshape(n_mp * features, -1), everyone, scatter_dimension=0, tiled=True
            ).astype(F32)
            for g in (g_qkv, g_rest)
        )
    input_grad, layer_out, g_q, g_o, g_g, g_d, one, two = deliver(
        layer_out, in_full, d_qkv, d_rest, gains, width, units
    )
    return layer_out, input_grad, g_q.transpose(1, 0, 2), g_o, g_g, g_d, one[0], two[0]


def solution(mesh):
    n_dp, n_mp = mesh.shape["dp"], mesh.shape["mp"]
    return jax.shard_map(
        functools.partial(per_device, n_dp, n_mp),
        mesh=mesh,
        in_specs=(
            P("dp", None),
            P("dp", None),
            P("dp", None, "mp"),
            P("mp", "dp"),
            P("dp", None, "mp"),
            P("mp", "dp"),
            P("dp"),
            P("dp"),
            P("dp", None),
        ),
        out_specs=(
            P("dp", None),
            P("dp", None),
            P("dp", None, "mp"),
            P("mp", "dp"),
            P("dp", None, "mp"),
            P("mp", "dp"),
            P("dp"),
            P("dp"),
        ),
        check_vma=False,
    )
```
